32 devices in a mesh: dp: 16 (over z, y, core), tensor: 2 (over x).
Axes of the slice: x: 2, y: 2, z: 4, core: 2. Of those that a mesh axis runs over, the one named last changes fastest.
Arguments:
- tokens: bfloat16 [32768, 768], P('dp'), may hold values from -6 to 6
- cotangent: bfloat16 [32768, 768], P('dp'), may hold values from -6 to 6
- pair_lengths: int32 [64, 4], P('dp'), may hold values from 1 to 256, 512 in all within a row
- block_of_slot: int32 [224], replicated, may hold values from 0 to 216, as said below
- masters: float32 [2, 224, 128, 128], P('tensor', 'dp'), may hold values from -4 to 4
- mom_first: float32 [2, 224, 128, 128], P('tensor', 'dp'), may hold values from -0.078125 to 0.078125
- mom_second: float32 [2, 224, 128, 128], P('tensor', 'dp'), may hold values from 3.0517579e-06 to 6.1035156e-05
- left_bases: float32 [2, 224, 128, 128], P('tensor', 'dp'), may hold values from -1 to 1, as said below
- right_bases: float32 [2, 224, 128, 128], P('tensor', 'dp'), may hold values from -1 to 1, as said below
- split_vec: float32 [2, 2304], P('tensor'), may hold values from -4 to 4
- split_first: float32 [2, 2304], P('tensor'), may hold values from -0.078125 to 0.078125
- split_second: float32 [2, 2304], P('tensor'), may hold values from 3.0517579e-06 to 6.1035156e-05
- row_vec: float32 [6, 768], replicated, may hold values from -2 to 2
- row_first: float32 [6, 768], replicated, may hold values from -0.078125 to 0.078125
- row_second: float32 [6, 768], replicated, may hold values from 3.0517579e-06 to 6.1035156e-05
Outputs:
- layer_out: bfloat16 [32768, 768], P('dp')
- input_grad: float32 [32768, 768], P('dp')
- weight_grads: float32 [2, 224, 128, 128], P('tensor', 'dp')
- new_masters: float32 [2, 224, 128, 128], P('tensor', 'dp')
- new_first: float32 [2, 224, 128, 128], P('tensor', 'dp')
- new_second: float32 [2, 224, 128, 128], P('tensor', 'dp')
- weight_copies: bfloat16 [2, 224, 128, 128], P('tensor', 'dp')
- split_grad: float32 [2, 2304], P('tensor')
- new_split: float32 [2, 2304], P('tensor')
- new_split_first: float32 [2, 2304], P('tensor')
- new_split_second: float32 [2, 2304], P('tensor')
- row_grad: float32 [6, 768], replicated
- new_row: float32 [6, 768], replicated
- new_row_first: float32 [6, 768], replicated
- new_row_second: float32 [6, 768], replicated
The draws below stay inside these ranges and needn't reach their ends.
Inputs may be any that keep to these rules, and one draw needn't show every extreme that they name: `block_of_slot`: each block number 0 to 215 stands in exactly one slot and 216 marks an empty slot; index d of dp owns slots d * 14 to (d + 1) * 14 - 1. `left_bases`: each [128, 128] matrix is orthogonal. `right_bases`: each [128, 128] matrix is orthogonal.
All inputs are finite; a program needn't handle non-finite values.
Results may differ from the reference program's by a relative error of at most 0.018.
Values may be sent and summed in bfloat16 or wider, within the bound.
A program may use at most 192 MiB of HBM per device.

```python
import math
import jax
import jax.numpy as jnp
import numpy as np
from jax import lax

D = 768
HEADS = 12
HEAD = 64
FF = 3072
S = 512
PAIRS = 4
MAXLEN = 256
B = 128
PIECES = 2
ROWS = 64
TOKENS = 32768
NBLK = 216
SLOTS = 224
VSPLIT = 2304


def slot_layout(key):
    ordering = jax.random.permutation(jax.random.fold_in(key, 7), SLOTS)
    return jnp.minimum(ordering, NBLK).astype(jnp.int32)


def draw_block_of_slot(key, part):
    return slot_layout(key)


def draw_masters(key, part):
    table = slot_layout(key)
    head_width = HEADS * HEAD // PIECES
    ffn_width = FF // PIECES
    first_end = D // B * (3 * head_width // B)
    second_end = first_end + head_width // B * (D // B)
    third_end = second_end + D // B * (ffn_width // B)
    narrow_fan = max(D // 48, 1)
    spread = jnp.where(table < first_end, D ** (-0.5), jnp.where(table < second_end, narrow_fan ** (-0.5), jnp.where(table < third_end, D ** (-0.5), jnp.where(table < NBLK, FF ** (-0.5), D ** (-0.5)))))
    noise = jnp.clip(jax.random.normal(jax.random.fold_in(key, 11), (PIECES, SLOTS, B, B), jnp.float32), -4.0, 4.0)
    return noise * spread.astype(jnp.float32)[None, :, None, None]


def permute_one(sub_key):
    return jax.random.permutation(sub_key, B)


def orthogonal_blocks(key):
    block_total = PIECES * SLOTS
    frequency = jax.vmap(permute_one)(jax.random.split(jax.random.fold_in(key, 1), block_total)).astype(jnp.float32)
    position = jax.vmap(permute_one)(jax.random.split(jax.random.fold_in(key, 2), block_total)).astype(jnp.float32)
    signs_row = jnp.where(jax.random.bernoulli(jax.random.fold_in(key, 3), 0.5, (block_total, B)), 1.0, -1.0)
    signs_col = jnp.where(jax.random.bernoulli(jax.random.fold_in(key, 4), 0.5, (block_total, B)), 1.0, -1.0)
    angles = math.pi / B * (position[:, None, :] + 0.5) * frequency[:, :, None]
    norming = jnp.where(frequency == 0.0, math.sqrt(1.0 / B), math.sqrt(2.0 / B))
    result = jnp.cos(angles) * norming[:, :, None] * signs_row[:, :, None] * signs_col[:, None, :]
    return result.astype(jnp.float32).reshape(PIECES, SLOTS, B, B)


def draw_left_bases(key, part):
    return orthogonal_blocks(jax.random.fold_in(key, 21))


def draw_right_bases(key, part):
    return orthogonal_blocks(jax.random.fold_in(key, 22))


def draw_row_vec(key, part):
    noise = jnp.clip(jax.random.normal(jax.random.fold_in(key, 31), (6, D), jnp.float32), -4.0, 4.0)
    row_number = jnp.arange(6)[:, None]
    is_gain = (row_number == 1) | (row_number == 4)
    return jnp.where(is_gain, 1.0 + 0.2 * noise, 0.5 * noise).astype(jnp.float32)


def shard_levels(key, dims, pieces, least, high):
    factor_of, own = 1.0, jax.random.fold_in(key, 6)
    for dim, shards_of in pieces:
        draws = jnp.exp(jax.random.uniform(jax.random.fold_in(own, dim), (shards_of,), jnp.float32, least / len(pieces), high / len(pieces)))
        factor_of = factor_of * jnp.repeat(draws, dims[dim] // shards_of).reshape([-1 if axis == dim else 1 for axis in range(len(dims))])
    return factor_of


def split_up(number_of, total, most, slope):
    loads = [(1 << 20) // math.isqrt(rank ** slope) + 1 for rank in range(2, number_of + 1)]
    spare, counts = total - most - (number_of - 1), [1] * (number_of - 1)
    while spare > 0:
        movable = [i for i in range(number_of - 1) if counts[i] < most]
        mass, budget = sum([loads[i] for i in movable]), spare
        for i in movable:
            extra = min(most - counts[i], max(1, budget * loads[i] // mass), spare)
            counts[i] = counts[i] + extra
            spare = spare - extra
    return np.array([most] + counts)


def uneven_parts(key, count, total, most, slope):
    if count == 2:
        one = jax.random.randint(key, (), max(1, total - most), min(most, total - 1) + 1)
        return jnp.stack([one, total - one])
    tallies = jnp.asarray(split_up(count, total, most, slope), jnp.int32)
    pairs = (count - 1) // 2
    source_of, sink = tallies[1:1 + 2 * pairs:2], tallies[2:2 + 2 * pairs:2]
    margin = jnp.minimum(source_of - 1, most - sink)
    shifted = jax.random.randint(jax.random.fold_in(key, 1), (pairs,), 0, 1 << 20) % (margin + 1)
    tallies = tallies.at[1:1 + 2 * pairs:2].set(source_of - shifted).at[2:2 + 2 * pairs:2].set(sink + shifted)
    return tallies[jax.random.permutation(jax.random.fold_in(key, 2), count)]


def gaussian(stream_key, extent, width, reach, cuts=(), kind=jnp.bfloat16):
    values = jax.random.normal(stream_key, extent, jnp.float32) * width
    if len(cuts) > 0:
        values = shard_levels(stream_key, extent, cuts, -0.22, 0.18) * values
    return jnp.clip(values, min=-reach, max=reach).astype(kind)


def setup_inputs(seed: int = 0) -> dict:
    keys = jax.random.split(jax.random.key(seed), 16)
    return {
        "tokens": gaussian(keys[0], (TOKENS, D), 1.0, 6.0, ((0, 16),)),
        "cotangent": gaussian(keys[1], (TOKENS, D), 1.0, 6.0, ((0, 16),)),
        "pair_lengths": jax.vmap(lambda own: uneven_parts(own, PAIRS, S, MAXLEN, 2))(jax.random.split(keys[2], ROWS)).reshape((ROWS, PAIRS)).astype(jnp.int32),
        "block_of_slot": draw_block_of_slot(jax.random.fold_in(keys[15], 71), 0),
        "masters": draw_masters(jax.random.fold_in(keys[15], 71), 0),
        "mom_first": gaussian(keys[5], (PIECES, SLOTS, B, B), (TOKENS ** -0.5), 0.078125, ((0, 2), (1, 16)), jnp.float32),
        "mom_second": jnp.clip(jnp.exp(math.log(6.103515625e-05) - 2.9957323 * jax.random.uniform(keys[6], (PIECES, SLOTS, B, B), jnp.float32) ** shard_levels(keys[6], (PIECES, SLOTS, B, B), ((0, 2), (1, 16)), -0.2, 0.2)), 3.051757857974735e-06, 6.103515625e-05),
        "left_bases": draw_left_bases(jax.random.fold_in(keys[15], 71), 0),
        "right_bases": draw_right_bases(jax.random.fold_in(keys[15], 71), 0),
        "split_vec": gaussian(keys[9], (PIECES, VSPLIT), 0.5, 4.0, ((0, 2),), jnp.float32),
        "split_first": gaussian(keys[10], (PIECES, VSPLIT), (TOKENS ** -0.5), 0.078125, ((0, 2),), jnp.float32),
        "split_second": jnp.clip(jnp.exp(math.log(6.103515625e-05) - 2.9957323 * jax.random.uniform(keys[11], (PIECES, VSPLIT), jnp.float32) ** shard_levels(keys[11], (PIECES, VSPLIT), ((0, 2),), -0.2, 0.2)), 3.051757857974735e-06, 6.103515625e-05),
        "row_vec": draw_row_vec(jax.random.fold_in(keys[15], 71), 0),
        "row_first": gaussian(keys[13], (6, D), (TOKENS ** -0.5), 0.078125, (), jnp.float32),
        "row_second": jnp.clip(jnp.exp(jax.random.uniform(keys[14], (6, D), jnp.float32, math.log(3.051757857974735e-06), math.log(6.103515625e-05))), 3.051757857974735e-06, 6.103515625e-05),
    }


@jax.custom_vjp
def low(v):
    return lax.optimization_barrier(v.astype(jnp.bfloat16)).astype(jnp.float32)

@jax.custom_vjp
def low_back(v):
    return v

def low_keep(v):
    return (low(v), None)

def low_pass(kept, grad):
    return (grad,)

def back_keep(v):
    return (v, None)

def back_low(kept, grad):
    return (low(grad),)
low.defvjp(low_keep, low_pass)
low_back.defvjp(back_keep, back_low)
EPS_NORM = 1e-05
EPS_ADAM = 1e-08
LEARN_RATE = 0.01
VECTOR_RATE = 0.15
MOMENT_DECAY = 0.5
MASKED_SCORE = -1e+30
HIGHEST_PRECISION = lax.Precision.HIGHEST

def both_ways(operand):
    return low(low_back(operand))

def norm_row(hidden, gain_vec, shift_vec):
    row_mean = lax.optimization_barrier(jnp.mean(hidden, axis=-1, keepdims=True))
    centred = hidden - row_mean
    row_var = lax.optimization_barrier(jnp.mean(centred * centred, axis=-1, keepdims=True))
    return centred * lax.rsqrt(row_var + EPS_NORM) * gain_vec + shift_vec

def segment_ids(pair_sizes, seq_len):
    pair_ends = jnp.cumsum(pair_sizes, axis=-1).astype(jnp.int32)
    position = jnp.arange(seq_len, dtype=jnp.int32)
    hits = (position[None, :, None] >= pair_ends[:, None, :-1]).astype(jnp.int32)
    return lax.optimization_barrier(jnp.sum(hits, axis=-1)).astype(jnp.int32)

def slot_table(block_of_slot, block_total):
    slot_numbers = jnp.arange(block_of_slot.shape[0], dtype=jnp.int32)
    matches = block_of_slot[:, None] == jnp.arange(block_total, dtype=jnp.int32)[None, :]
    return lax.optimization_barrier(jnp.sum(jnp.where(matches, slot_numbers[:, None], 0), axis=0)).astype(jnp.int32)

def to_blocks(matrix, block_edge):
    row_total, col_total = matrix.shape
    shaped = matrix.reshape(row_total // block_edge, block_edge, col_total // block_edge, block_edge)
    return shaped.transpose(0, 2, 1, 3).reshape(-1, block_edge, block_edge)

def from_blocks(blocks, row_total, col_total):
    block_edge = blocks.shape[-1]
    shaped = blocks.reshape(row_total // block_edge, col_total // block_edge, block_edge, block_edge)
    return shaped.transpose(0, 2, 1, 3).reshape(row_total, col_total)

def block_counts(block_edge, head_width, ffn_width):
    return (D // block_edge * (3 * head_width // block_edge), head_width // block_edge * (D // block_edge), D // block_edge * (ffn_width // block_edge), ffn_width // block_edge * (D // block_edge))

def unpack(blocks, block_edge, head_width, ffn_width):
    counts_list = block_counts(block_edge, head_width, ffn_width)
    first_end = counts_list[0]
    second_end = first_end + counts_list[1]
    third_end = second_end + counts_list[2]
    fourth_end = third_end + counts_list[3]
    return (from_blocks(blocks[:first_end], D, 3 * head_width), from_blocks(blocks[first_end:second_end], head_width, D), from_blocks(blocks[second_end:third_end], D, ffn_width), from_blocks(blocks[third_end:fourth_end], ffn_width, D))

def pack(qkv_matrix, out_matrix, up_matrix, down_matrix, block_edge):
    return jnp.concatenate([to_blocks(qkv_matrix, block_edge), to_blocks(out_matrix, block_edge), to_blocks(up_matrix, block_edge), to_blocks(down_matrix, block_edge)], axis=0)

def rotate_update(gradient, moment_one, moment_two, left, right, master):
    turned = jnp.einsum('psji,psjk->psik', left, gradient, precision=HIGHEST_PRECISION)
    turned = jnp.einsum('psik,pskl->psil', turned, right, precision=HIGHEST_PRECISION)
    first_new = MOMENT_DECAY * moment_one + (1.0 - MOMENT_DECAY) * turned
    second_new = MOMENT_DECAY * moment_two + (1.0 - MOMENT_DECAY) * turned * turned
    stepped = first_new / (jnp.sqrt(second_new) + EPS_ADAM)
    turned_back = jnp.einsum('psij,psjk->psik', left, stepped, precision=HIGHEST_PRECISION)
    turned_back = jnp.einsum('psik,pslk->psil', turned_back, right, precision=HIGHEST_PRECISION)
    return (master - LEARN_RATE * turned_back, first_new, second_new)

def adam_vector(gradient, moment_one, moment_two, current):
    first_new = MOMENT_DECAY * moment_one + (1.0 - MOMENT_DECAY) * gradient
    second_new = MOMENT_DECAY * moment_two + (1.0 - MOMENT_DECAY) * gradient * gradient
    return (current - VECTOR_RATE * first_new / (jnp.sqrt(second_new) + EPS_ADAM), first_new, second_new)

def matmul(left_op, right_op):
    return jnp.dot(left_op, right_op, precision=HIGHEST_PRECISION, preferred_element_type=jnp.float32)

def layer(inputs, seg_rows, params):
    w_query, w_key, w_value, w_out, w_up, w_down, query_bias, value_bias, up_bias, row_vec = params
    row_count = seg_rows.shape[0]
    queries = both_ways(matmul(inputs, w_query) + query_bias)
    keys_proj = both_ways(matmul(inputs, w_key))
    values = both_ways(matmul(inputs, w_value) + value_bias)

    def heads_of(matrix):
        return matrix.reshape(row_count, S, HEADS, HEAD)
    raw_scores = jnp.einsum('rqhd,rkhd->rhqk', heads_of(queries), heads_of(keys_proj), precision=HIGHEST_PRECISION) * HEAD ** (-0.5)
    same_pair = seg_rows[:, :, None] == seg_rows[:, None, :]
    scores = low_back(jnp.where(same_pair[:, None], raw_scores, MASKED_SCORE))
    probabilities = low(jax.nn.softmax(scores, axis=-1))
    mixed = jnp.einsum('rhqk,rkhd->rqhd', probabilities, heads_of(values), precision=HIGHEST_PRECISION)
    attended = both_ways(mixed.reshape(row_count * S, D))
    hidden_one = inputs + low_back(matmul(attended, w_out)) + row_vec[0]
    normed_one = norm_row(hidden_one, row_vec[1], row_vec[2])
    up_pre = low_back(matmul(low(normed_one), w_up) + up_bias)
    active = low(jax.nn.gelu(up_pre, approximate=False))
    hidden_two = normed_one + low_back(matmul(active, w_down)) + row_vec[3]
    return norm_row(hidden_two, row_vec[4], row_vec[5])

def slot_blocks(block_of_slot, qkv_grad, out_grad, up_grad, down_grad):
    blocks = pack(qkv_grad, out_grad, up_grad, down_grad, B)
    padded = jnp.concatenate([blocks, jnp.zeros((1, B, B), jnp.float32)], axis=0)
    return jnp.take(padded, block_of_slot, axis=0)

def reference(tokens, cotangent, pair_lengths, block_of_slot, masters, mom_first, mom_second, left_bases, right_bases, split_vec, split_first, split_second, row_vec, row_first, row_second):
    head_width = HEADS * HEAD // PIECES
    ffn_width = FF // PIECES
    slot_of = slot_table(block_of_slot, NBLK)
    rounded = masters.astype(jnp.bfloat16).astype(jnp.float32)
    piece_mats = [unpack(jnp.take(rounded[piece_index], slot_of, axis=0), B, head_width, ffn_width) for piece_index in range(PIECES)]
    w_query = jnp.concatenate([piece_mat[0][:, :head_width] for piece_mat in piece_mats], axis=1)
    w_key = jnp.concatenate([piece_mat[0][:, head_width:2 * head_width] for piece_mat in piece_mats], axis=1)
    w_value = jnp.concatenate([piece_mat[0][:, 2 * head_width:] for piece_mat in piece_mats], axis=1)
    w_out = jnp.concatenate([piece_mat[1] for piece_mat in piece_mats], axis=0)
    w_up = jnp.concatenate([piece_mat[2] for piece_mat in piece_mats], axis=1)
    w_down = jnp.concatenate([piece_mat[3] for piece_mat in piece_mats], axis=0)
    query_bias = split_vec[:, :head_width].reshape(-1)
    value_bias = split_vec[:, head_width:2 * head_width].reshape(-1)
    up_bias = split_vec[:, 2 * head_width:].reshape(-1)
    params = (w_query, w_key, w_value, w_out, w_up, w_down, query_bias, value_bias, up_bias, row_vec)
    group_rows = 8
    group_count = ROWS // group_rows
    seg_all = segment_ids(pair_lengths, S).reshape(group_count, group_rows, S)
    inputs_all = tokens.astype(jnp.float32).reshape(group_count, group_rows * S, D)
    cot_all = cotangent.astype(jnp.float32).reshape(group_count, group_rows * S, D)

    def one_group(totals, group_items):
        inputs, seg_rows, cot_rows = group_items

        def forward(inner_rows, inner_params):
            return layer(inner_rows, seg_rows, inner_params)
        outputs, pullback = jax.vjp(forward, inputs, params)
        input_part, param_part = pullback(cot_rows)
        return (jax.tree.map(jnp.add, totals, param_part), (outputs.astype(jnp.bfloat16), input_part))
    zero_totals = jax.tree.map(jnp.zeros_like, params)
    totals, (outputs, input_grads) = lax.scan(one_group, zero_totals, (inputs_all, seg_all, cot_all))
    grad_query, grad_key, grad_value, grad_out, grad_up, grad_down, grad_qbias, grad_vbias, grad_ubias, grad_rowvec = totals
    mean_scale = 1.0 / TOKENS
    slot_list = []
    split_list = []
    for piece_index in range(PIECES):
        head_start = piece_index * head_width
        head_stop = head_start + head_width
        ffn_start = piece_index * ffn_width
        ffn_stop = ffn_start + ffn_width
        qkv_part = jnp.concatenate([grad_query[:, head_start:head_stop], grad_key[:, head_start:head_stop], grad_value[:, head_start:head_stop]], axis=1)
        slot_list.append(slot_blocks(block_of_slot, qkv_part, grad_out[head_start:head_stop], grad_up[:, ffn_start:ffn_stop], grad_down[ffn_start:ffn_stop]))
        split_list.append(jnp.concatenate([grad_qbias[head_start:head_stop], grad_vbias[head_start:head_stop], grad_ubias[ffn_start:ffn_stop]]))
    weight_grads = jnp.stack(slot_list) * mean_scale
    split_grad = jnp.stack(split_list) * mean_scale
    row_grad = grad_rowvec * mean_scale
    new_masters, new_first, new_second = rotate_update(weight_grads, mom_first, mom_second, left_bases, right_bases, masters)
    new_split, new_split_first, new_split_second = adam_vector(split_grad, split_first, split_second, split_vec)
    new_row, new_row_first, new_row_second = adam_vector(row_grad, row_first, row_second, row_vec)
    return (outputs.reshape(TOKENS, D), input_grads.reshape(TOKENS, D), weight_grads, new_masters, new_first, new_second, new_masters.astype(jnp.bfloat16), split_grad, new_split, new_split_first, new_split_second, row_grad, new_row, new_row_first, new_row_second)
```

```python
import jax
import jax.numpy as jnp
from jax import lax
from jax.sharding import PartitionSpec as P

D = 768
HEADS = 12
HEAD = 64
FF = 3072


EPS_NORM = 1e-05
EPS_ADAM = 1e-08
LEARN_RATE = 0.01
VECTOR_RATE = 0.15
MOMENT_DECAY = 0.5
MASKED_SCORE = -1e30
HIGHEST_PRECISION = lax.Precision.HIGHEST


def norm_row(hidden, gain_vec, shift_vec):
    row_mean = jnp.mean(hidden, axis=-1, keepdims=True)
    centred = hidden - row_mean
    row_var = jnp.mean(centred * centred, axis=-1, keepdims=True)
    return centred * lax.rsqrt(row_var + EPS_NORM) * gain_vec + shift_vec


def gelu_exact(operand):
    return jax.nn.gelu(operand, approximate=False)


def segment_ids(pair_sizes, seq_len):
    pair_ends = jnp.cumsum(pair_sizes, axis=-1)
    position = jnp.arange(seq_len, dtype=jnp.int32)
    hits = (position[None, :, None] >= pair_ends[:, None, :-1]).astype(jnp.int32)
    return jnp.sum(hits, axis=-1)


def slot_table(block_of_slot, block_total):
    slot_numbers = jnp.arange(block_of_slot.shape[0], dtype=jnp.int32)
    matches = block_of_slot[:, None] == jnp.arange(block_total, dtype=jnp.int32)[None, :]
    return jnp.sum(jnp.where(matches, slot_numbers[:, None], 0), axis=0)


def to_blocks(matrix, block_edge):
    row_total, col_total = matrix.shape
    shaped = matrix.reshape(
        row_total // block_edge, block_edge, col_total // block_edge, block_edge
    )
    return shaped.transpose(0, 2, 1, 3).reshape(-1, block_edge, block_edge)


def from_blocks(blocks, row_total, col_total):
    block_edge = blocks.shape[-1]
    shaped = blocks.reshape(
        row_total // block_edge, col_total // block_edge, block_edge, block_edge
    )
    return shaped.transpose(0, 2, 1, 3).reshape(row_total, col_total)


def block_counts(block_edge, head_width, ffn_width):
    return (
        D // block_edge * (3 * head_width // block_edge),
        head_width // block_edge * (D // block_edge),
        D // block_edge * (ffn_width // block_edge),
        ffn_width // block_edge * (D // block_edge),
    )


def unpack(blocks, block_edge, head_width, ffn_width):
    counts_list = block_counts(block_edge, head_width, ffn_width)
    first_end = counts_list[0]
    second_end = first_end + counts_list[1]
    third_end = second_end + counts_list[2]
    fourth_end = third_end + counts_list[3]
    return (
        from_blocks(blocks[:first_end], D, 3 * head_width),
        from_blocks(blocks[first_end:second_end], head_width, D),
        from_blocks(blocks[second_end:third_end], D, ffn_width),
        from_blocks(blocks[third_end:fourth_end], ffn_width, D),
    )


def pack(qkv_matrix, out_matrix, up_matrix, down_matrix, block_edge):
    return jnp.concatenate(
        [
            to_blocks(qkv_matrix, block_edge),
            to_blocks(out_matrix, block_edge),
            to_blocks(up_matrix, block_edge),
            to_blocks(down_matrix, block_edge),
        ],
        axis=0,
    )


def rotate_update(gradient, moment_one, moment_two, left, right, master):
    turned = jnp.einsum("psji,psjk->psik", left, gradient, precision=HIGHEST_PRECISION)
    turned = jnp.einsum("psik,pskl->psil", turned, right, precision=HIGHEST_PRECISION)
    first_new = MOMENT_DECAY * moment_one + (1.0 - MOMENT_DECAY) * turned
    second_new = MOMENT_DECAY * moment_two + (1.0 - MOMENT_DECAY) * turned * turned
    stepped = first_new / (jnp.sqrt(second_new) + EPS_ADAM)
    turned_back = jnp.einsum("psij,psjk->psik", left, stepped, precision=HIGHEST_PRECISION)
    turned_back = jnp.einsum("psik,pslk->psil", turned_back, right, precision=HIGHEST_PRECISION)
    return (master - LEARN_RATE * turned_back, first_new, second_new)


def adam_vector(gradient, moment_one, moment_two, current):
    first_new = MOMENT_DECAY * moment_one + (1.0 - MOMENT_DECAY) * gradient
    second_new = MOMENT_DECAY * moment_two + (1.0 - MOMENT_DECAY) * gradient * gradient
    return (
        current - VECTOR_RATE * first_new / (jnp.sqrt(second_new) + EPS_ADAM),
        first_new,
        second_new,
    )


def masked_scores(query_row, key_row, seg_row):
    raw_scores = jnp.einsum(
        "qhd,khd->hqk", query_row, key_row, preferred_element_type=jnp.float32
    ) * HEAD ** (-0.5)
    same_pair = seg_row[:, None] == seg_row[None, :]
    return jnp.where(same_pair[None], raw_scores, MASKED_SCORE)


def split_heads(matrix, row_count, seq_len, local_heads):
    return matrix.reshape(row_count, seq_len, local_heads, HEAD)


def body(
    tokens,
    cotangent,
    pair_lengths,
    block_of_slot,
    masters,
    mom_first,
    mom_second,
    left_bases,
    right_bases,
    split_vec,
    split_first,
    split_second,
    row_vec,
    row_first,
    row_second,
):
    pieces = lax.axis_size("tensor")
    piece = lax.axis_index("tensor")
    piece_width = HEADS * HEAD // pieces
    piece_ffn = FF // pieces
    block_edge = masters.shape[-1]
    block_total = sum(block_counts(block_edge, piece_width, piece_ffn))
    slots = block_of_slot.shape[0]
    full_seq = tokens.shape[0] // pair_lengths.shape[0]
    row_count = pair_lengths.shape[0] // pieces
    token_count = row_count * full_seq
    tokens_own = lax.dynamic_slice_in_dim(tokens, piece * token_count, token_count, 0)
    cotangent_own = lax.dynamic_slice_in_dim(cotangent, piece * token_count, token_count, 0)
    pairs_own = lax.dynamic_slice_in_dim(pair_lengths, piece * row_count, row_count, 0)
    everyone = lax.all_gather(
        masters[0].astype(jnp.bfloat16), ("tensor", "dp"), axis=0, tiled=True
    ).reshape(pieces, slots, block_edge, block_edge)
    slot_of = slot_table(block_of_slot, block_total)
    unpacked = [
        unpack(jnp.take(everyone[index], slot_of, axis=0), block_edge, piece_width, piece_ffn)
        for index in range(pieces)
    ]
    w_qkv = jnp.concatenate(
        [
            one_piece[0][:, part_index * piece_width : (part_index + 1) * piece_width]
            for part_index in range(3)
            for one_piece in unpacked
        ],
        axis=1,
    )
    w_out = jnp.concatenate([one_piece[1] for one_piece in unpacked], axis=0)
    w_up = jnp.concatenate([one_piece[2] for one_piece in unpacked], axis=1)
    w_down = jnp.concatenate([one_piece[3] for one_piece in unpacked], axis=0)
    split_all = lax.all_gather(split_vec[0], "tensor", axis=0)
    query_bias = split_all[:, :piece_width].reshape(-1)
    value_bias = split_all[:, piece_width : 2 * piece_width].reshape(-1)
    up_bias = split_all[:, 2 * piece_width :].reshape(-1)
    out_bias, gain_one, shift_one, down_bias, gain_two, shift_two = (
        row_vec[row_number] for row_number in range(6)
    )
    seg_rows = segment_ids(pairs_own, full_seq)
    inputs = tokens_own.astype(jnp.float32)
    projected = jnp.dot(tokens_own, w_qkv, preferred_element_type=jnp.float32)
    queries = (projected[:, :D] + query_bias).astype(jnp.bfloat16)
    keys_proj = projected[:, D : 2 * D].astype(jnp.bfloat16)
    values = (projected[:, 2 * D :] + value_bias).astype(jnp.bfloat16)
    query_rows = split_heads(queries, row_count, full_seq, HEADS)
    key_rows = split_heads(keys_proj, row_count, full_seq, HEADS)
    value_rows = split_heads(values, row_count, full_seq, HEADS)

    def forward_row(row_items):
        query_row, key_row, value_row, seg_row = row_items
        scores = masked_scores(query_row, key_row, seg_row)
        row_top = jnp.max(scores, axis=-1, keepdims=True)
        log_total = row_top + jnp.log(jnp.sum(jnp.exp(scores - row_top), axis=-1, keepdims=True))
        probabilities = jnp.exp(scores - log_total)
        mixed = jnp.einsum(
            "hqk,khd->qhd",
            probabilities.astype(jnp.bfloat16),
            value_row,
            preferred_element_type=jnp.float32,
        )
        return (mixed.astype(jnp.bfloat16), log_total)

    mapped = lax.map(forward_row, (query_rows, key_rows, value_rows, seg_rows))
    attended = mapped[0].reshape(token_count, D)
    attn_sum = jnp.dot(attended, w_out, preferred_element_type=jnp.float32)
    hidden_one = inputs + attn_sum + out_bias
    normed_one, norm_one_back = jax.vjp(norm_row, hidden_one, gain_one, shift_one)
    normed_low = normed_one.astype(jnp.bfloat16)
    up_pre = jnp.dot(normed_low, w_up, preferred_element_type=jnp.float32) + up_bias
    active, gelu_back = jax.vjp(gelu_exact, up_pre)
    active_low = active.astype(jnp.bfloat16)
    down_sum = jnp.dot(active_low, w_down, preferred_element_type=jnp.float32)
    hidden_two = normed_one + down_sum + down_bias
    output, norm_two_back = jax.vjp(norm_row, hidden_two, gain_two, shift_two)
    layer_own = output.astype(jnp.bfloat16)
    layer_out = lax.all_gather(layer_own, "tensor", axis=0, tiled=True)
    grad_two, gain_two_grad, shift_two_grad = norm_two_back(cotangent_own.astype(jnp.float32))
    down_low = grad_two.astype(jnp.bfloat16)
    down_bias_grad = jnp.sum(grad_two, axis=0)
    down_weight_grad = jnp.dot(active_low.T, down_low, preferred_element_type=jnp.float32)
    grad_active = jnp.dot(down_low, w_down.T, preferred_element_type=jnp.float32)
    up_low = gelu_back(grad_active)[0].astype(jnp.bfloat16)
    up_bias_grad = jnp.sum(up_low.astype(jnp.float32), axis=0)
    up_weight_grad = jnp.dot(normed_low.T, up_low, preferred_element_type=jnp.float32)
    back_sum = jnp.dot(up_low, w_up.T, preferred_element_type=jnp.float32)
    grad_normed = grad_two + back_sum
    grad_one, gain_one_grad, shift_one_grad = norm_one_back(grad_normed)
    out_bias_grad = jnp.sum(grad_one, axis=0)
    attn_low = grad_one.astype(jnp.bfloat16)
    out_weight_grad = jnp.dot(attended.T, attn_low, preferred_element_type=jnp.float32)
    mixed_low = jnp.dot(attn_low, w_out.T, preferred_element_type=jnp.float32).astype(jnp.bfloat16)
    grad_rows = split_heads(mixed_low, row_count, full_seq, HEADS)

    def backward_row(row_items):
        query_row, key_row, value_row, seg_row, grad_row, log_total = row_items
        probabilities = jnp.exp(masked_scores(query_row, key_row, seg_row) - log_total)
        grad_probs = jnp.einsum(
            "qhd,khd->hqk", grad_row, value_row, preferred_element_type=jnp.float32
        )
        value_grad = jnp.einsum(
            "hqk,qhd->khd",
            probabilities.astype(jnp.bfloat16),
            grad_row,
            preferred_element_type=jnp.float32,
        )
        spread = jnp.sum(probabilities * grad_probs, axis=-1, keepdims=True)
        score_low = (probabilities * (grad_probs - spread)).astype(jnp.bfloat16)
        query_grad = jnp.einsum(
            "hqk,khd->qhd", score_low, key_row, preferred_element_type=jnp.float32
        ) * HEAD ** (-0.5)
        key_grad = jnp.einsum(
            "hqk,qhd->khd", score_low, query_row, preferred_element_type=jnp.float32
        ) * HEAD ** (-0.5)
        return (
            query_grad.astype(jnp.bfloat16),
            key_grad.astype(jnp.bfloat16),
            value_grad.astype(jnp.bfloat16),
        )

    query_low, key_low, value_low = lax.map(
        backward_row, (query_rows, key_rows, value_rows, seg_rows, grad_rows, mapped[1])
    )
    merged = jnp.concatenate(
        [
            query_low.reshape(token_count, D),
            key_low.reshape(token_count, D),
            value_low.reshape(token_count, D),
        ],
        axis=1,
    )
    qkv_weight_grad = jnp.dot(tokens_own.T, merged, preferred_element_type=jnp.float32)
    input_own = grad_one + jnp.dot(merged, w_qkv.T, preferred_element_type=jnp.float32)
    input_grad = lax.all_gather(
        input_own.astype(jnp.bfloat16), "tensor", axis=0, tiled=True
    ).astype(jnp.float32)
    query_bias_grad = jnp.sum(merged[:, :D].astype(jnp.float32), axis=0)
    value_bias_grad = jnp.sum(merged[:, 2 * D :].astype(jnp.float32), axis=0)
    block_list = []
    split_list = []
    for index in range(pieces):
        heads_at = slice(index * piece_width, (index + 1) * piece_width)
        ffn_at = slice(index * piece_ffn, (index + 1) * piece_ffn)
        qkv_piece = jnp.concatenate(
            [qkv_weight_grad[:, part * D : (part + 1) * D][:, heads_at] for part in range(3)],
            axis=1,
        )
        block_list.append(
            pack(
                qkv_piece,
                out_weight_grad[heads_at],
                up_weight_grad[:, ffn_at],
                down_weight_grad[ffn_at],
                block_edge,
            )
        )
        split_list.append(
            jnp.concatenate(
                [query_bias_grad[heads_at], value_bias_grad[heads_at], up_bias_grad[ffn_at]]
            )
        )
    padded = jnp.concatenate(
        [
            jnp.stack(block_list).astype(jnp.bfloat16),
            jnp.zeros((pieces, 1, block_edge, block_edge), jnp.bfloat16),
        ],
        axis=1,
    )
    split_local = jnp.stack(split_list)
    row_local = jnp.stack(
        [
            out_bias_grad,
            gain_one_grad,
            shift_one_grad,
            down_bias_grad,
            gain_two_grad,
            shift_two_grad,
        ]
    )
    token_total = tokens.shape[0] * lax.axis_size("dp")
    mean_scale = 1.0 / token_total
    slot_terms = jnp.take(padded, block_of_slot, axis=1)
    owned_sum = lax.psum_scatter(
        slot_terms.reshape(pieces * slots, block_edge, block_edge),
        ("tensor", "dp"),
        scatter_dimension=0,
        tiled=True,
    ).astype(jnp.float32)
    split_total, row_total = lax.psum((split_local, row_local), ("tensor", "dp"))
    weight_grads = (owned_sum * mean_scale)[None]
    split_grad = lax.dynamic_slice_in_dim(split_total, piece, 1, 0) * mean_scale
    row_grad = row_total * mean_scale
    new_masters, new_first, new_second = rotate_update(
        weight_grads, mom_first, mom_second, left_bases, right_bases, masters
    )
    new_split, new_split_first, new_split_second = adam_vector(
        split_grad, split_first, split_second, split_vec
    )
    new_row, new_row_first, new_row_second = adam_vector(row_grad, row_first, row_second, row_vec)
    return (
        layer_out,
        input_grad,
        weight_grads,
        new_masters,
        new_first,
        new_second,
        new_masters.astype(jnp.bfloat16),
        split_grad,
        new_split,
        new_split_first,
        new_split_second,
        row_grad,
        new_row,
        new_row_first,
        new_row_second,
    )


def solution(mesh):
    in_specs = (
        P("dp", None),
        P("dp", None),
        P("dp", None),
        P(),
        P("tensor", "dp", None, None),
        P("tensor", "dp", None, None),
        P("tensor", "dp", None, None),
        P("tensor", "dp", None, None),
        P("tensor", "dp", None, None),
        P("tensor", None),
        P("tensor", None),
        P("tensor", None),
        P(),
        P(),
        P(),
    )
    out_specs = (
        P("dp", None),
        P("dp", None),
        P("tensor", "dp", None, None),
        P("tensor", "dp", None, None),
        P("tensor", "dp", None, None),
        P("tensor", "dp", None, None),
        P("tensor", "dp", None, None),
        P("tensor", None),
        P("tensor", None),
        P("tensor", None),
        P("tensor", None),
        P(),
        P(),
        P(),
        P(),
    )
    return jax.shard_map(body, mesh=mesh, in_specs=in_specs, out_specs=out_specs, check_vma=False)
```

```python
import jax
import jax.numpy as jnp
from jax import lax
from jax.experimental import pallas as pl
from jax.experimental.pallas import tpu as pltpu
from jax.sharding import PartitionSpec as P
import numpy as np

D = 768
HEADS = 12
HEAD = 64
FF = 3072


EPS_NORM = 1e-05
EPS_ADAM = 1e-08
LEARN_RATE = 0.01
VECTOR_RATE = 0.15
MOMENT_DECAY = 0.5
MASKED_SCORE = -1e30
HIGHEST_PRECISION = lax.Precision.HIGHEST


def slot_table(block_of_slot, block_total):
    slot_numbers = jnp.arange(block_of_slot.shape[0], dtype=jnp.int32)
    matches = block_of_slot[:, None] == jnp.arange(block_total, dtype=jnp.int32)[None, :]
    return jnp.sum(jnp.where(matches, slot_numbers[:, None], 0), axis=0)


def block_counts(block_edge, head_width, ffn_width):
    return (
        D // block_edge * (3 * head_width // block_edge),
        head_width // block_edge * (D // block_edge),
        D // block_edge * (ffn_width // block_edge),
        ffn_width // block_edge * (D // block_edge),
    )


def rotate_update(gradient, moment_one, moment_two, left, right, master):
    turned = jnp.einsum("psji,psjk->psik", left, gradient, precision=HIGHEST_PRECISION)
    turned = jnp.einsum("psik,pskl->psil", turned, right, precision=HIGHEST_PRECISION)
    first_new = MOMENT_DECAY * moment_one + (1.0 - MOMENT_DECAY) * turned
    second_new = MOMENT_DECAY * moment_two + (1.0 - MOMENT_DECAY) * turned * turned
    stepped = first_new / (jnp.sqrt(second_new) + EPS_ADAM)
    turned_back = jnp.einsum("psij,psjk->psik", left, stepped, precision=HIGHEST_PRECISION)
    turned_back = jnp.einsum("psik,pslk->psil", turned_back, right, precision=HIGHEST_PRECISION)
    return (master - LEARN_RATE * turned_back, first_new, second_new)


def adam_vector(gradient, moment_one, moment_two, current):
    first_new = MOMENT_DECAY * moment_one + (1.0 - MOMENT_DECAY) * gradient
    second_new = MOMENT_DECAY * moment_two + (1.0 - MOMENT_DECAY) * gradient * gradient
    return (
        current - VECTOR_RATE * first_new / (jnp.sqrt(second_new) + EPS_ADAM),
        first_new,
        second_new,
    )


LOG2E = 1.4426950408889634
LN_TWO = 0.6931471805599453
ROOT_HALF = 0.7071067811865476
PHI_SCALE = 0.3989422804014327
ERF_P = 0.3275911
ERF_A = (0.254829592, -0.284496736, 1.421413741, -1.453152027, 1.061405429)
VMEM_LIMIT = 60 * 1024 * 1024
LANES = 128
BF16 = jnp.bfloat16
F32 = jnp.float32


def dot_nn(left, right):
    return lax.dot_general(left, right, (((1,), (0,)), ((), ())), preferred_element_type=F32)


def dot_nt(left, right):
    return lax.dot_general(left, right, (((1,), (1,)), ((), ())), preferred_element_type=F32)


def dot_tn(left, right):
    return lax.dot_general(left, right, (((0,), (0,)), ((), ())), preferred_element_type=F32)


def block_home(pieces):
    d_b, f_b = D // LANES, FF // LANES
    d_p, f_p = d_b // pieces, f_b // pieces
    first = d_b * 3 * d_p
    second = first + d_p * d_b
    third = second + d_b * f_p
    qkv = [
        (n % d_b // d_p, k * 3 * d_p + n // d_b * d_p + n % d_p)
        for k in range(d_b)
        for n in range(3 * d_b)
    ]
    out = [(k // d_p, first + k % d_p * d_b + n) for k in range(d_b) for n in range(d_b)]
    up = [(n // f_p, second + k * f_p + n % f_p) for k in range(d_b) for n in range(f_b)]
    down = [(k // f_p, third + k % f_p * d_b + n) for k in range(f_b) for n in range(d_b)]
    return qkv, out, up, down


def grad_order(pieces):
    d_b, f_b = D // LANES, FF // LANES
    qkv, out, up, down = block_home(pieces)
    f_s, q_s = f_b // d_b, 3
    order = []
    for j in range(d_b):
        order += [down[(j * f_s + k) * d_b + n] for k in range(f_s) for n in range(d_b)]
        order += [up[k * f_b + j * f_s + n] for k in range(d_b) for n in range(f_s)]
        order += [qkv[k * 3 * d_b + j * q_s + n] for k in range(d_b) for n in range(q_s)]
        order += [out[j * d_b + n] for n in range(d_b)]
    return order


def start_blocks(homes, base, rows, cols, source, target, sem):
    def step(index, carry):
        k, n = index // cols, index % cols
        pltpu.make_async_copy(
            source.at[homes[base + index]],
            target.at[pl.ds(pl.multiple_of(k * LANES, LANES), LANES), pl.ds(pl.multiple_of(n * LANES, LANES), LANES)],
            sem,
        ).start()
        return carry

    lax.fori_loop(0, rows * cols, step, 0, unroll=6)


def wait_blocks(target, sem):
    pltpu.make_async_copy(target, target, sem).wait()


def mask_bias(ends_ref, row, seq, bias_ref):
    col = lax.broadcasted_iota(jnp.int32, (seq, 1), 0)
    lane = lax.broadcasted_iota(jnp.int32, (1, seq), 1)
    seg_col = jnp.zeros((seq, 1), jnp.int32)
    seg_lane = jnp.zeros((1, seq), jnp.int32)
    end = 0
    for k in range(ends_ref.shape[1] - 1):
        end = end + ends_ref[row, k]
        seg_col = seg_col + (col >= end).astype(jnp.int32)
        seg_lane = seg_lane + (lane >= end).astype(jnp.int32)
    bias_ref[...] = jnp.where(seg_col == seg_lane, 0.0, MASKED_SCORE)


def attend_kernel(homes, pairs, offset, x_ref, every, qb_ref, vb_ref, qkv_ref, att_ref, lse_ref, w_ref, bias_ref, sem):
    d_b = D // LANES
    row = pl.program_id(0)
    seq = x_ref.shape[0]

    @pl.when(row == 0)
    def _():
        start_blocks(homes, 0, d_b, 3 * d_b, every, w_ref, sem)

    mask_bias(pairs, offset[0] + row, seq, bias_ref)

    @pl.when(row == 0)
    def _():
        wait_blocks(w_ref, sem)

    x = x_ref[...]
    wide = 2 * LANES
    for part in range(3):
        for c in range(0, D, wide):
            y = dot_nn(x, w_ref[:, part * D + c : part * D + c + wide])
            if part == 0:
                y = (y + qb_ref[:, c : c + wide]).astype(BF16).astype(F32) * HEAD ** (-0.5)
            if part == 2:
                y = y + vb_ref[:, c : c + wide]
            y = y.astype(BF16)
            for n in range(2):
                qkv_ref[part * d_b + c // LANES + n] = y[:, n * LANES : (n + 1) * LANES]
    lane = lax.broadcasted_iota(jnp.int32, (1, LANES), 1)

    def pair(n, carry):
        q = qkv_ref[n]
        k = qkv_ref[d_b + n]
        v_t = qkv_ref[2 * d_b + n].T
        halves = []
        for h in range(2):
            keep = (lane < HEAD) if h == 0 else (lane >= HEAD)
            scores = dot_nt(jnp.where(keep, k, jnp.zeros_like(k)), q) + bias_ref[...]
            top = jnp.max(scores, axis=0, keepdims=True)
            p = jnp.exp(scores - top)
            total = jnp.sum(p, axis=0, keepdims=True)
            lse_ref[0, 2 * n + h] = (top + jnp.log(total)).reshape(1, seq)
            mixed = dot_nn(v_t[h * HEAD : (h + 1) * HEAD], p.astype(BF16))
            halves.append(mixed * (1.0 / total))
        att_ref[n] = jnp.concatenate(halves, axis=0).T.astype(BF16)
        return carry

    lax.fori_loop(0, d_b, pair, 0)


def norm_parts(hidden):
    mean = jnp.mean(hidden, axis=-1, keepdims=True)
    centred = hidden - mean
    var = jnp.mean(centred * centred, axis=-1, keepdims=True)
    inv = lax.rsqrt(var + EPS_NORM)
    return centred * inv, inv


def norm_back(grad, gain, normed, inv):
    scaled = grad * gain
    mean = jnp.mean(scaled, axis=-1, keepdims=True)
    along = jnp.mean(scaled * normed, axis=-1, keepdims=True)
    return inv * (scaled - mean - normed * along)


def put_blocks(ref, value):
    for n in range(ref.shape[0]):
        ref[n] = value[:, n * LANES : (n + 1) * LANES]


def get_blocks(ref):
    return jnp.concatenate([ref[n] for n in range(ref.shape[0])], axis=1)


def gelu_parts(u):
    e = jnp.exp(u * u * -0.5)
    t = 1.0 / (1.0 + (ERF_P * ROOT_HALF) * jnp.abs(u))
    a1, a2, a3, a4, a5 = (0.5 * a for a in ERF_A)
    tail = ((((a5 * t + a4) * t + a3) * t + a2) * t + a1) * t * e
    cdf = jnp.where(u >= 0, 1.0 - tail, tail)
    return u * cdf, cdf + u * e * PHI_SCALE


def token_kernel(
    homes, att_ref, x_ref, cot_ref, every, bu_ref, rv_ref,
    out_ref, nl_ref, act_ref, dl_ref, up_ref, al_ref, ml_ref, g1_ref, rg_ref, bg_ref,
    wo_ref, wu_ref, wd_ref, dg_ref, sem,
):
    d_b, f_b = D // LANES, FF // LANES
    step = pl.program_id(0)

    @pl.when(step == 0)
    def _():
        start_blocks(homes, 3 * d_b * d_b, d_b, d_b, every, wo_ref, sem.at[0])
        start_blocks(homes, 4 * d_b * d_b, d_b, f_b, every, wu_ref, sem.at[1])
        start_blocks(homes, 4 * d_b * d_b + d_b * f_b, f_b, d_b, every, wd_ref, sem.at[2])
        rg_ref[...] = jnp.zeros_like(rg_ref)
        bg_ref[...] = jnp.zeros_like(bg_ref)
        wait_blocks(wo_ref, sem.at[0])
        wait_blocks(wu_ref, sem.at[1])
        wait_blocks(wd_ref, sem.at[2])

    out_bias, gain_one, shift_one, down_bias, gain_two, shift_two = (
        rv_ref[i : i + 1] for i in range(6)
    )
    hidden = dot_nn(get_blocks(att_ref), wo_ref[...]) + x_ref[...].astype(F32) + out_bias
    n_one, inv_one = norm_parts(hidden)
    normed = n_one * gain_one + shift_one
    normed_low = normed.astype(BF16)
    put_blocks(nl_ref, normed_low)
    wide = 512
    total = normed + down_bias
    for c in range(0, FF, wide):
        u = dot_nn(normed_low, wu_ref[:, c : c + wide]) + bu_ref[:, c : c + wide]
        active, slope = gelu_parts(u)
        active = active.astype(BF16)
        dg_ref[:, c : c + wide] = slope.astype(BF16)
        for n in range(wide // LANES):
            act_ref[c // LANES + n] = active[:, n * LANES : (n + 1) * LANES]
        total = total + dot_nn(active, wd_ref[c : c + wide, :])
    n_two, inv_two = norm_parts(total)
    out_ref[...] = (n_two * gain_two + shift_two).astype(BF16)
    dy = cot_ref[...].astype(F32)
    grad_two = norm_back(dy, gain_two, n_two, inv_two)
    down_low = grad_two.astype(BF16)
    put_blocks(dl_ref, down_low)
    rg_ref[3:4] += jnp.sum(grad_two, axis=0, keepdims=True)
    rg_ref[4:5] += jnp.sum(dy * n_two, axis=0, keepdims=True)
    rg_ref[5:6] += jnp.sum(dy, axis=0, keepdims=True)
    grad_normed = grad_two
    for c in range(0, FF, wide):
        ga = dot_nt(down_low, wd_ref[c : c + wide, :]) * dg_ref[:, c : c + wide].astype(F32)
        up = ga.astype(BF16)
        for n in range(wide // LANES):
            up_ref[c // LANES + n] = up[:, n * LANES : (n + 1) * LANES]
        bg_ref[:, c : c + wide] += jnp.sum(up.astype(F32), axis=0, keepdims=True)
        grad_normed = grad_normed + dot_nt(up, wu_ref[:, c : c + wide])
    rg_ref[1:2] += jnp.sum(grad_normed * n_one, axis=0, keepdims=True)
    rg_ref[2:3] += jnp.sum(grad_normed, axis=0, keepdims=True)
    grad_one = norm_back(grad_normed, gain_one, n_one, inv_one)
    rg_ref[0:1] += jnp.sum(grad_one, axis=0, keepdims=True)
    g1_ref[...] = grad_one
    attn_low = grad_one.astype(BF16)
    put_blocks(al_ref, attn_low)
    put_blocks(ml_ref, dot_nt(attn_low, wo_ref[...]).astype(BF16))


def attend_back_kernel(
    homes, pairs, offset, qkv_ref, att_ref, ml_ref, lse_ref, g1_ref, every,
    merged_ref, ig_ref, sg_ref, w_ref, bias_ref, sem,
):
    d_b = D // LANES
    row = pl.program_id(0)
    seq = g1_ref.shape[0]

    @pl.when(row == 0)
    def _():
        start_blocks(homes, 0, d_b, 3 * d_b, every, w_ref, sem)
        sg_ref[...] = jnp.zeros_like(sg_ref)

    mask_bias(pairs, offset[0] + row, seq, bias_ref)
    lane = lax.broadcasted_iota(jnp.int32, (1, LANES), 1)

    def pair(n, carry):
        q = qkv_ref[n]
        k = qkv_ref[d_b + n]
        v = qkv_ref[2 * d_b + n]
        g = ml_ref[n]
        k_t = k.T
        both = g.T.astype(F32) * att_ref[n].T.astype(F32)
        zero = jnp.zeros_like(k)
        parts = []
        for h in range(2):
            keep = (lane < HEAD) if h == 0 else (lane >= HEAD)
            spread = jnp.sum(both[h * HEAD : (h + 1) * HEAD], axis=0, keepdims=True)
            scores = dot_nt(jnp.where(keep, k, zero), q) + bias_ref[...]
            p = jnp.exp(scores - lse_ref[0, 2 * n + h].reshape(1, seq))
            gp = dot_nt(jnp.where(keep, v, zero), g)
            low = (p * (gp - spread)).astype(BF16)
            gv = dot_nn(p.astype(BF16), g)
            gk = dot_nn(low, q)
            gq = dot_nn(k_t[h * HEAD : (h + 1) * HEAD], low)
            parts.append((gq, gk, gv))
        gq = (jnp.concatenate([parts[0][0], parts[1][0]], axis=0) * HEAD ** (-0.5)).T
        merged_ref[n] = gq.astype(BF16)
        merged_ref[d_b + n] = jnp.where(lane < HEAD, parts[0][1], parts[1][1]).astype(BF16)
        merged_ref[2 * d_b + n] = jnp.where(lane < HEAD, parts[0][2], parts[1][2]).astype(BF16)
        return carry

    lax.fori_loop(0, d_b, pair, 0)

    @pl.when(row == 0)
    def _():
        wait_blocks(w_ref, sem)

    for n in range(d_b):
        at = slice(n * LANES, (n + 1) * LANES)
        sg_ref[0:1, at] += jnp.sum(merged_ref[n].astype(F32), axis=0, keepdims=True)
        sg_ref[1:2, at] += jnp.sum(merged_ref[2 * d_b + n].astype(F32), axis=0, keepdims=True)
    merged = get_blocks(merged_ref)
    ig_ref[...] = (g1_ref[...] + dot_nt(merged, w_ref[...])).astype(BF16)


def grad_kernel(act_ref, dl_ref, nl_ref, up_ref, x_ref, merged_ref, att_ref, al_ref, g_ref):
    d_b = D // LANES
    f_s = act_ref.shape[0]
    at = 0

    def store(value, at):
        value = value.astype(BF16)
        for k in range(value.shape[0] // LANES):
            for n in range(value.shape[1] // LANES):
                g_ref[at] = value[k * LANES : (k + 1) * LANES, n * LANES : (n + 1) * LANES]
                at += 1
        return at

    at = store(dot_tn(get_blocks(act_ref), get_blocks(dl_ref)), at)
    at = store(dot_tn(get_blocks(nl_ref), get_blocks(up_ref)), at)
    at = store(dot_tn(x_ref[...], get_blocks(merged_ref)), at)
    at = store(dot_tn(att_ref[0], get_blocks(al_ref)), at)


def slot_kernel(places, g_ref, zero_ref, out_ref, sem):
    def step(s, carry):
        @pl.when(places[s] >= 0)
        def _():
            pltpu.make_async_copy(g_ref.at[jnp.maximum(places[s], 0)], out_ref.at[s], sem).start()

        @pl.when(places[s] < 0)
        def _():
            pltpu.make_async_copy(zero_ref.at[0], out_ref.at[s], sem).start()

        return carry

    lax.fori_loop(0, places.shape[0], step, 0)
    pltpu.make_async_copy(out_ref, out_ref, sem).wait()


def smem():
    return pl.BlockSpec(memory_space=pltpu.SMEM)


def anywhere():
    return pl.BlockSpec(memory_space=pl.ANY)


def params():
    return pltpu.CompilerParams(vmem_limit_bytes=VMEM_LIMIT, dimension_semantics=("arbitrary",))


def layer_passes(tokens, cotangent, pair_lengths, piece, homes, every, query_bias, value_bias, up_bias, row_vec, row_count, seq):
    d_b, f_b = D // LANES, FF // LANES
    total = row_count * seq
    shape = jax.ShapeDtypeStruct
    offset = (piece * row_count).astype(jnp.int32).reshape(1)
    stack = lambda n: pl.BlockSpec((n, seq, LANES), lambda r, *_: (0, r, 0))
    rows = pl.BlockSpec((seq, D), lambda r, *_: (r, 0))
    own = lambda at: pl.BlockSpec((seq, D), lambda r, *pre: (pre[at][0] + r, 0))
    whole = lambda s: pl.BlockSpec(s, lambda *_: tuple(0 for _ in s))
    lse_spec = pl.BlockSpec((1, HEADS, 1, seq), lambda r, *_: (r, 0, 0, 0))
    qkv, att, lse = pl.pallas_call(
        attend_kernel,
        grid_spec=pltpu.PrefetchScalarGridSpec(
            num_scalar_prefetch=3,
            grid=(row_count,),
            in_specs=[own(2), anywhere(), whole((1, D)), whole((1, D))],
            out_specs=[stack(3 * d_b), stack(d_b), lse_spec],
            scratch_shapes=[
                pltpu.VMEM((D, 3 * D), BF16),
                pltpu.VMEM((seq, seq), F32),
                pltpu.SemaphoreType.DMA,
            ],
        ),
        out_shape=[
            shape((3 * d_b, total, LANES), BF16),
            shape((d_b, total, LANES), BF16),
            shape((row_count, HEADS, 1, seq), F32),
        ],
        compiler_params=params(),
        name="attend",
    )(homes, pair_lengths, offset, tokens, every, query_bias, value_bias)
    token_outs = pl.pallas_call(
        lambda homes, off, *refs: token_kernel(homes, *refs),
        grid_spec=pltpu.PrefetchScalarGridSpec(
            num_scalar_prefetch=2,
            grid=(row_count,),
            in_specs=[stack(d_b), own(1), own(1), anywhere(), whole((1, FF)), whole((6, D))],
            out_specs=[
                rows, stack(d_b), stack(f_b), stack(d_b), stack(f_b), stack(d_b), stack(d_b), rows,
                whole((6, D)), whole((1, FF)),
            ],
            scratch_shapes=[
                pltpu.VMEM((D, D), BF16),
                pltpu.VMEM((D, FF), BF16),
                pltpu.VMEM((FF, D), BF16),
                pltpu.VMEM((seq, FF), BF16),
                pltpu.SemaphoreType.DMA((3,)),
            ],
        ),
        out_shape=[
            shape((total, D), BF16),
            shape((d_b, total, LANES), BF16),
            shape((f_b, total, LANES), BF16),
            shape((d_b, total, LANES), BF16),
            shape((f_b, total, LANES), BF16),
            shape((d_b, total, LANES), BF16),
            shape((d_b, total, LANES), BF16),
            shape((total, D), F32),
            shape((6, D), F32),
            shape((1, FF), F32),
        ],
        compiler_params=params(),
        name="tokenwise",
    )(homes, offset, att, tokens, cotangent, every, up_bias, row_vec)
    layer_own, normed_low, active_low, down_low, up_low, attn_low, mixed_low, grad_one, row_grad, up_grad = token_outs
    merged, input_own, split_grad = pl.pallas_call(
        attend_back_kernel,
        grid_spec=pltpu.PrefetchScalarGridSpec(
            num_scalar_prefetch=3,
            grid=(row_count,),
            in_specs=[stack(3 * d_b), stack(d_b), stack(d_b), lse_spec, rows, anywhere()],
            out_specs=[stack(3 * d_b), rows, whole((2, D))],
            scratch_shapes=[
                pltpu.VMEM((D, 3 * D), BF16),
                pltpu.VMEM((seq, seq), F32),
                pltpu.SemaphoreType.DMA,
            ],
        ),
        out_shape=[
            shape((3 * d_b, total, LANES), BF16),
            shape((total, D), BF16),
            shape((2, D), F32),
        ],
        compiler_params=params(),
        name="attend_back",
    )(homes, pair_lengths, offset, qkv, att, mixed_low, lse, grad_one, every)
    f_s = f_b // d_b
    part = lambda n: pl.BlockSpec((n, total, LANES), lambda j, *_: (j, 0, 0))
    blocks = 2 * f_s * d_b + 4 * d_b
    grads = pl.pallas_call(
        lambda pc, *refs: grad_kernel(*refs),
        grid_spec=pltpu.PrefetchScalarGridSpec(
            num_scalar_prefetch=1,
            grid=(d_b,),
            in_specs=[
                part(f_s), whole((d_b, total, LANES)), whole((d_b, total, LANES)), part(f_s),
                pl.BlockSpec((total, D), lambda j, pc: (pc[0], 0)),
                part(3), part(1), whole((d_b, total, LANES)),
            ],
            out_specs=pl.BlockSpec((blocks, LANES, LANES), lambda j, *_: (j, 0, 0)),
        ),
        out_shape=shape((d_b * blocks, LANES, LANES), BF16),
        compiler_params=params(),
        name="weight_grads",
    )(piece.astype(jnp.int32).reshape(1), active_low, down_low, normed_low, up_low, tokens, merged, att, attn_low)
    return layer_own, input_own, grads, row_grad, up_grad, split_grad


def body(
    tokens,
    cotangent,
    pair_lengths,
    block_of_slot,
    masters,
    mom_first,
    mom_second,
    left_bases,
    right_bases,
    split_vec,
    split_first,
    split_second,
    row_vec,
    row_first,
    row_second,
):
    pieces = lax.axis_size("tensor")
    piece = lax.axis_index("tensor")
    piece_width = HEADS * HEAD // pieces
    piece_ffn = FF // pieces
    block_edge = masters.shape[-1]
    block_total = sum(block_counts(block_edge, piece_width, piece_ffn))
    slots = block_of_slot.shape[0]
    full_seq = tokens.shape[0] // pair_lengths.shape[0]
    row_count = pair_lengths.shape[0] // pieces
    every = lax.all_gather(masters[0].astype(BF16), ("tensor", "dp"), axis=0, tiled=True)
    slot_of = slot_table(block_of_slot, block_total)
    order = np.array(sum(block_home(pieces), []), np.int32)
    homes = slot_of[order[:, 1]] + order[:, 0] * slots
    split_all = lax.all_gather(split_vec[0], "tensor", axis=0)
    query_bias = split_all[:, :piece_width].reshape(1, -1)
    value_bias = split_all[:, piece_width : 2 * piece_width].reshape(1, -1)
    up_bias = split_all[:, 2 * piece_width :].reshape(1, -1)
    layer_own, input_own, grads, row_local, up_grad, qv_grad = layer_passes(
        tokens, cotangent, pair_lengths, piece, homes, every, query_bias, value_bias, up_bias, row_vec, row_count, full_seq
    )
    layer_out = lax.all_gather(layer_own, "tensor", axis=0, tiled=True)
    input_grad = lax.all_gather(input_own, "tensor", axis=0, tiled=True).astype(F32)
    place_table = np.full((pieces, block_total + 1), -1, np.int32)
    for index, (at_piece, number) in enumerate(grad_order(pieces)):
        place_table[at_piece, number] = index
    places = jnp.asarray(place_table)[:, block_of_slot].reshape(-1)
    slot_terms = pl.pallas_call(
        slot_kernel,
        in_specs=[smem(), anywhere(), anywhere()],
        out_specs=anywhere(),
        out_shape=jax.ShapeDtypeStruct((pieces * slots, block_edge, block_edge), BF16),
        scratch_shapes=[pltpu.SemaphoreType.DMA],
        name="slots",
    )(places, grads, jnp.zeros((1, block_edge, block_edge), BF16))
    split_local = jnp.concatenate(
        [
            qv_grad[0].reshape(pieces, piece_width),
            qv_grad[1].reshape(pieces, piece_width),
            up_grad.reshape(pieces, piece_ffn),
        ],
        axis=1,
    )
    token_total = tokens.shape[0] * lax.axis_size("dp")
    mean_scale = 1.0 / token_total
    owned_sum = lax.psum_scatter(
        slot_terms, ("tensor", "dp"), scatter_dimension=0, tiled=True
    ).astype(F32)
    split_total, row_total = lax.psum((split_local, row_local), ("tensor", "dp"))
    weight_grads = (owned_sum * mean_scale)[None]
    split_grad = lax.dynamic_slice_in_dim(split_total, piece, 1, 0) * mean_scale
    row_grad = row_total * mean_scale
    new_masters, new_first, new_second = rotate_update(
        weight_grads, mom_first, mom_second, left_bases, right_bases, masters
    )
    new_split, new_split_first, new_split_second = adam_vector(
        split_grad, split_first, split_second, split_vec
    )
    new_row, new_row_first, new_row_second = adam_vector(row_grad, row_first, row_second, row_vec)
    return (
        layer_out,
        input_grad,
        weight_grads,
        new_masters,
        new_first,
        new_second,
        new_masters.astype(jnp.bfloat16),
        split_grad,
        new_split,
        new_split_first,
        new_split_second,
        row_grad,
        new_row,
        new_row_first,
        new_row_second,
    )


def solution(mesh):
    in_specs = (
        P("dp", None),
        P("dp", None),
        P("dp", None),
        P(),
        P("tensor", "dp", None, None),
        P("tensor", "dp", None, None),
        P("tensor", "dp", None, None),
        P("tensor", "dp", None, None),
        P("tensor", "dp", None, None),
        P("tensor", None),
        P("tensor", None),
        P("tensor", None),
        P(),
        P(),
        P(),
    )
    out_specs = (
        P("dp", None),
        P("dp", None),
        P("tensor", "dp", None, None),
        P("tensor", "dp", None, None),
        P("tensor", "dp", None, None),
        P("tensor", "dp", None, None),
        P("tensor", "dp", None, None),
        P("tensor", None),
        P("tensor", None),
        P("tensor", None),
        P("tensor", None),
        P(),
        P(),
        P(),
        P(),
    )
    return jax.shard_map(body, mesh=mesh, in_specs=in_specs, out_specs=out_specs, check_vma=False)
```

```python
import functools

import jax
import jax.numpy as jnp
from jax import lax
from jax.experimental import pallas as pl
from jax.experimental.pallas import tpu as pltpu
from jax.sharding import PartitionSpec as P
import numpy as np

D = 768
HEADS = 12
HEAD = 64
FF = 3072


EPS_NORM = 1e-05
EPS_ADAM = 1e-08
LEARN_RATE = 0.01
VECTOR_RATE = 0.15
MOMENT_DECAY = 0.5
MASKED_SCORE = -1e30
HIGHEST_PRECISION = lax.Precision.HIGHEST


def slot_table(block_of_slot, block_total):
    slot_numbers = jnp.arange(block_of_slot.shape[0], dtype=jnp.int32)
    matches = block_of_slot[:, None] == jnp.arange(block_total, dtype=jnp.int32)[None, :]
    return jnp.sum(jnp.where(matches, slot_numbers[:, None], 0), axis=0)


def block_counts(block_edge, head_width, ffn_width):
    return (
        D // block_edge * (3 * head_width // block_edge),
        head_width // block_edge * (D // block_edge),
        D // block_edge * (ffn_width // block_edge),
        ffn_width // block_edge * (D // block_edge),
    )


def adam_vector(gradient, moment_one, moment_two, current):
    first_new = MOMENT_DECAY * moment_one + (1.0 - MOMENT_DECAY) * gradient
    second_new = MOMENT_DECAY * moment_two + (1.0 - MOMENT_DECAY) * gradient * gradient
    return (
        current - VECTOR_RATE * first_new / (jnp.sqrt(second_new) + EPS_ADAM),
        first_new,
        second_new,
    )


LOG2E = 1.4426950408889634
LN_TWO = 0.6931471805599453
ROOT_HALF = 0.7071067811865476
PHI_SCALE = 0.3989422804014327
ERF_P = 0.3275911
ERF_A = (0.254829592, -0.284496736, 1.421413741, -1.453152027, 1.061405429)
VMEM_LIMIT = 60 * 1024 * 1024
LANES = 128
BF16 = jnp.bfloat16
F32 = jnp.float32


def dot_nn(left, right):
    return lax.dot_general(left, right, (((1,), (0,)), ((), ())), preferred_element_type=F32)


def dot_nt(left, right):
    return lax.dot_general(left, right, (((1,), (1,)), ((), ())), preferred_element_type=F32)


def dot_tn(left, right):
    return lax.dot_general(left, right, (((0,), (0,)), ((), ())), preferred_element_type=F32)


def block_home(pieces):
    d_b, f_b = D // LANES, FF // LANES
    d_p, f_p = d_b // pieces, f_b // pieces
    first = d_b * 3 * d_p
    second = first + d_p * d_b
    third = second + d_b * f_p
    qkv = [
        (n % d_b // d_p, k * 3 * d_p + n // d_b * d_p + n % d_p)
        for k in range(d_b)
        for n in range(3 * d_b)
    ]
    out = [(k // d_p, first + k % d_p * d_b + n) for k in range(d_b) for n in range(d_b)]
    up = [(n // f_p, second + k * f_p + n % f_p) for k in range(d_b) for n in range(f_b)]
    down = [(k // f_p, third + k % f_p * d_b + n) for k in range(f_b) for n in range(d_b)]
    return qkv, out, up, down


def grad_order(pieces):
    d_b, f_b = D // LANES, FF // LANES
    qkv, out, up, down = block_home(pieces)
    f_s, q_s = f_b // d_b, 3
    order = []
    for j in range(d_b):
        order += [down[(j * f_s + k) * d_b + n] for k in range(f_s) for n in range(d_b)]
        order += [up[k * f_b + j * f_s + n] for k in range(d_b) for n in range(f_s)]
        order += [qkv[k * 3 * d_b + j * q_s + n] for k in range(d_b) for n in range(q_s)]
        order += [out[j * d_b + n] for n in range(d_b)]
    return order


def start_blocks(homes, base, rows, cols, source, target, sem):
    def step(index, carry):
        k, n = index // cols, index % cols
        pltpu.make_async_copy(
            source.at[homes[base + index]],
            target.at[pl.ds(pl.multiple_of(k * LANES, LANES), LANES), pl.ds(pl.multiple_of(n * LANES, LANES), LANES)],
            sem,
        ).start()
        return carry

    lax.fori_loop(0, rows * cols, step, 0, unroll=6)


def wait_blocks(target, sem):
    pltpu.make_async_copy(target, target, sem).wait()


def mask_bias(ends_ref, row, seq, bias_ref):
    col = lax.broadcasted_iota(jnp.int32, (seq, 1), 0)
    lane = lax.broadcasted_iota(jnp.int32, (1, seq), 1)
    seg_col = jnp.zeros((seq, 1), jnp.int32)
    seg_lane = jnp.zeros((1, seq), jnp.int32)
    end = 0
    for k in range(ends_ref.shape[1] - 1):
        end = end + ends_ref[row, k]
        seg_col = seg_col + (col >= end).astype(jnp.int32)
        seg_lane = seg_lane + (lane >= end).astype(jnp.int32)
    bias_ref[...] = jnp.where(seg_col == seg_lane, 0.0, MASKED_SCORE)


def attend_kernel(homes, pairs, offset, x_ref, every, qb_ref, vb_ref, qkv_ref, att_ref, lse_ref, w_ref, bias_ref, sem):
    d_b = D // LANES
    row = pl.program_id(0)
    seq = x_ref.shape[0]

    @pl.when(row == 0)
    def _():
        start_blocks(homes, 0, d_b, 3 * d_b, every, w_ref, sem)

    mask_bias(pairs, offset[0] + row, seq, bias_ref)

    @pl.when(row == 0)
    def _():
        wait_blocks(w_ref, sem)

    x = x_ref[...]
    wide = 2 * LANES
    for part in range(3):
        for c in range(0, D, wide):
            y = dot_nn(x, w_ref[:, part * D + c : part * D + c + wide])
            if part == 0:
                y = (y + qb_ref[:, c : c + wide]).astype(BF16).astype(F32) * HEAD ** (-0.5)
            if part == 2:
                y = y + vb_ref[:, c : c + wide]
            y = y.astype(BF16)
            for n in range(2):
                qkv_ref[part * d_b + c // LANES + n] = y[:, n * LANES : (n + 1) * LANES]
    lane = lax.broadcasted_iota(jnp.int32, (1, LANES), 1)

    def pair(n, carry):
        q = qkv_ref[n]
        k = qkv_ref[d_b + n]
        v_t = qkv_ref[2 * d_b + n].T
        halves = []
        for h in range(2):
            keep = (lane < HEAD) if h == 0 else (lane >= HEAD)
            scores = dot_nt(jnp.where(keep, k, jnp.zeros_like(k)), q) + bias_ref[...]
            top = jnp.max(scores, axis=0, keepdims=True)
            p = jnp.exp(scores - top)
            total = jnp.sum(p, axis=0, keepdims=True)
            lse_ref[0, 2 * n + h] = (top + jnp.log(total)).reshape(1, seq)
            mixed = dot_nn(v_t[h * HEAD : (h + 1) * HEAD], p.astype(BF16))
            halves.append(mixed * (1.0 / total))
        att_ref[n] = jnp.concatenate(halves, axis=0).T.astype(BF16)
        return carry

    lax.fori_loop(0, d_b, pair, 0)


def norm_parts(hidden):
    mean = jnp.mean(hidden, axis=-1, keepdims=True)
    centred = hidden - mean
    var = jnp.mean(centred * centred, axis=-1, keepdims=True)
    inv = lax.rsqrt(var + EPS_NORM)
    return centred * inv, inv


def norm_back(grad, gain, normed, inv):
    scaled = grad * gain
    mean = jnp.mean(scaled, axis=-1, keepdims=True)
    along = jnp.mean(scaled * normed, axis=-1, keepdims=True)
    return inv * (scaled - mean - normed * along)


def put_blocks(ref, value):
    for n in range(ref.shape[0]):
        ref[n] = value[:, n * LANES : (n + 1) * LANES]


def get_blocks(ref):
    return jnp.concatenate([ref[n] for n in range(ref.shape[0])], axis=1)


def gelu_parts(u):
    e = jnp.exp(u * u * -0.5)
    t = 1.0 / (1.0 + (ERF_P * ROOT_HALF) * jnp.abs(u))
    a1, a2, a3, a4, a5 = (0.5 * a for a in ERF_A)
    tail = ((((a5 * t + a4) * t + a3) * t + a2) * t + a1) * t * e
    cdf = jnp.where(u >= 0, 1.0 - tail, tail)
    return u * cdf, cdf + u * e * PHI_SCALE


def token_kernel(
    homes, att_ref, x_ref, cot_ref, every, bu_ref, rv_ref,
    out_ref, nl_ref, act_ref, dl_ref, up_ref, al_ref, ml_ref, g1_ref, rg_ref, bg_ref,
    wo_ref, wu_ref, wd_ref, dg_ref, sem,
):
    d_b, f_b = D // LANES, FF // LANES
    step = pl.program_id(0)

    @pl.when(step == 0)
    def _():
        start_blocks(homes, 3 * d_b * d_b, d_b, d_b, every, wo_ref, sem.at[0])
        start_blocks(homes, 4 * d_b * d_b, d_b, f_b, every, wu_ref, sem.at[1])
        start_blocks(homes, 4 * d_b * d_b + d_b * f_b, f_b, d_b, every, wd_ref, sem.at[2])
        rg_ref[...] = jnp.zeros_like(rg_ref)
        bg_ref[...] = jnp.zeros_like(bg_ref)
        wait_blocks(wo_ref, sem.at[0])
        wait_blocks(wu_ref, sem.at[1])
        wait_blocks(wd_ref, sem.at[2])

    out_bias, gain_one, shift_one, down_bias, gain_two, shift_two = (
        rv_ref[i : i + 1] for i in range(6)
    )
    hidden = dot_nn(get_blocks(att_ref), wo_ref[...]) + x_ref[...].astype(F32) + out_bias
    n_one, inv_one = norm_parts(hidden)
    normed = n_one * gain_one + shift_one
    normed_low = normed.astype(BF16)
    put_blocks(nl_ref, normed_low)
    wide = 512
    total = normed + down_bias
    for c in range(0, FF, wide):
        u = dot_nn(normed_low, wu_ref[:, c : c + wide]) + bu_ref[:, c : c + wide]
        active, slope = gelu_parts(u)
        active = active.astype(BF16)
        dg_ref[:, c : c + wide] = slope.astype(BF16)
        for n in range(wide // LANES):
            act_ref[c // LANES + n] = active[:, n * LANES : (n + 1) * LANES]
        total = total + dot_nn(active, wd_ref[c : c + wide, :])
    n_two, inv_two = norm_parts(total)
    out_ref[...] = (n_two * gain_two + shift_two).astype(BF16)
    dy = cot_ref[...].astype(F32)
    grad_two = norm_back(dy, gain_two, n_two, inv_two)
    down_low = grad_two.astype(BF16)
    put_blocks(dl_ref, down_low)
    rg_ref[3:4] += jnp.sum(grad_two, axis=0, keepdims=True)
    rg_ref[4:5] += jnp.sum(dy * n_two, axis=0, keepdims=True)
    rg_ref[5:6] += jnp.sum(dy, axis=0, keepdims=True)
    grad_normed = grad_two
    for c in range(0, FF, wide):
        ga = dot_nt(down_low, wd_ref[c : c + wide, :]) * dg_ref[:, c : c + wide].astype(F32)
        up = ga.astype(BF16)
        for n in range(wide // LANES):
            up_ref[c // LANES + n] = up[:, n * LANES : (n + 1) * LANES]
        bg_ref[:, c : c + wide] += jnp.sum(up.astype(F32), axis=0, keepdims=True)
        grad_normed = grad_normed + dot_nt(up, wu_ref[:, c : c + wide])
    rg_ref[1:2] += jnp.sum(grad_normed * n_one, axis=0, keepdims=True)
    rg_ref[2:3] += jnp.sum(grad_normed, axis=0, keepdims=True)
    grad_one = norm_back(grad_normed, gain_one, n_one, inv_one)
    rg_ref[0:1] += jnp.sum(grad_one, axis=0, keepdims=True)
    g1_ref[...] = grad_one
    attn_low = grad_one.astype(BF16)
    put_blocks(al_ref, attn_low)
    put_blocks(ml_ref, dot_nt(attn_low, wo_ref[...]).astype(BF16))


def attend_back_kernel(
    homes, pairs, offset, qkv_ref, att_ref, ml_ref, lse_ref, g1_ref, every,
    merged_ref, ig_ref, sg_ref, w_ref, bias_ref, sem,
):
    d_b = D // LANES
    row = pl.program_id(0)
    seq = g1_ref.shape[0]

    @pl.when(row == 0)
    def _():
        start_blocks(homes, 0, d_b, 3 * d_b, every, w_ref, sem)
        sg_ref[...] = jnp.zeros_like(sg_ref)

    mask_bias(pairs, offset[0] + row, seq, bias_ref)
    lane = lax.broadcasted_iota(jnp.int32, (1, LANES), 1)

    def pair(n, carry):
        q = qkv_ref[n]
        k = qkv_ref[d_b + n]
        v = qkv_ref[2 * d_b + n]
        g = ml_ref[n]
        k_t = k.T
        both = g.T.astype(F32) * att_ref[n].T.astype(F32)
        zero = jnp.zeros_like(k)
        parts = []
        for h in range(2):
            keep = (lane < HEAD) if h == 0 else (lane >= HEAD)
            spread = jnp.sum(both[h * HEAD : (h + 1) * HEAD], axis=0, keepdims=True)
            scores = dot_nt(jnp.where(keep, k, zero), q) + bias_ref[...]
            p = jnp.exp(scores - lse_ref[0, 2 * n + h].reshape(1, seq))
            gp = dot_nt(jnp.where(keep, v, zero), g)
            low = (p * (gp - spread)).astype(BF16)
            gv = dot_nn(p.astype(BF16), g)
            gk = dot_nn(low, q)
            gq = dot_nn(k_t[h * HEAD : (h + 1) * HEAD], low)
            parts.append((gq, gk, gv))
        gq = (jnp.concatenate([parts[0][0], parts[1][0]], axis=0) * HEAD ** (-0.5)).T
        merged_ref[n] = gq.astype(BF16)
        merged_ref[d_b + n] = jnp.where(lane < HEAD, parts[0][1], parts[1][1]).astype(BF16)
        merged_ref[2 * d_b + n] = jnp.where(lane < HEAD, parts[0][2], parts[1][2]).astype(BF16)
        return carry

    lax.fori_loop(0, d_b, pair, 0)

    @pl.when(row == 0)
    def _():
        wait_blocks(w_ref, sem)

    for n in range(d_b):
        at = slice(n * LANES, (n + 1) * LANES)
        sg_ref[0:1, at] += jnp.sum(merged_ref[n].astype(F32), axis=0, keepdims=True)
        sg_ref[1:2, at] += jnp.sum(merged_ref[2 * d_b + n].astype(F32), axis=0, keepdims=True)
    merged = get_blocks(merged_ref)
    ig_ref[...] = (g1_ref[...] + dot_nt(merged, w_ref[...])).astype(BF16)


def grad_kernel(act_ref, dl_ref, nl_ref, up_ref, x_ref, merged_ref, att_ref, al_ref, g_ref):
    d_b = D // LANES
    f_s = act_ref.shape[0]
    at = 0

    def store(value, at):
        value = value.astype(BF16)
        for k in range(value.shape[0] // LANES):
            for n in range(value.shape[1] // LANES):
                g_ref[at] = value[k * LANES : (k + 1) * LANES, n * LANES : (n + 1) * LANES]
                at += 1
        return at

    at = store(dot_tn(get_blocks(act_ref), get_blocks(dl_ref)), at)
    at = store(dot_tn(get_blocks(nl_ref), get_blocks(up_ref)), at)
    at = store(dot_tn(x_ref[...], get_blocks(merged_ref)), at)
    at = store(dot_tn(att_ref[0], get_blocks(al_ref)), at)


def smem():
    return pl.BlockSpec(memory_space=pltpu.SMEM)


def anywhere():
    return pl.BlockSpec(memory_space=pl.ANY)


def params():
    return pltpu.CompilerParams(vmem_limit_bytes=VMEM_LIMIT, dimension_semantics=("arbitrary",))


def layer_passes(tokens, cotangent, pair_lengths, piece, homes, every, query_bias, value_bias, up_bias, row_vec, row_count, seq):
    d_b, f_b = D // LANES, FF // LANES
    total = row_count * seq
    shape = jax.ShapeDtypeStruct
    offset = (piece * row_count).astype(jnp.int32).reshape(1)
    stack = lambda n: pl.BlockSpec((n, seq, LANES), lambda r, *_: (0, r, 0))
    rows = pl.BlockSpec((seq, D), lambda r, *_: (r, 0))
    own = lambda at: pl.BlockSpec((seq, D), lambda r, *pre: (pre[at][0] + r, 0))
    whole = lambda s: pl.BlockSpec(s, lambda *_: tuple(0 for _ in s))
    lse_spec = pl.BlockSpec((1, HEADS, 1, seq), lambda r, *_: (r, 0, 0, 0))
    qkv, att, lse = pl.pallas_call(
        attend_kernel,
        grid_spec=pltpu.PrefetchScalarGridSpec(
            num_scalar_prefetch=3,
            grid=(row_count,),
            in_specs=[own(2), anywhere(), whole((1, D)), whole((1, D))],
            out_specs=[stack(3 * d_b), stack(d_b), lse_spec],
            scratch_shapes=[
                pltpu.VMEM((D, 3 * D), BF16),
                pltpu.VMEM((seq, seq), F32),
                pltpu.SemaphoreType.DMA,
            ],
        ),
        out_shape=[
            shape((3 * d_b, total, LANES), BF16),
            shape((d_b, total, LANES), BF16),
            shape((row_count, HEADS, 1, seq), F32),
        ],
        compiler_params=params(),
        name="attend",
    )(homes, pair_lengths, offset, tokens, every, query_bias, value_bias)
    token_outs = pl.pallas_call(
        lambda homes, off, *refs: token_kernel(homes, *refs),
        grid_spec=pltpu.PrefetchScalarGridSpec(
            num_scalar_prefetch=2,
            grid=(row_count,),
            in_specs=[stack(d_b), own(1), own(1), anywhere(), whole((1, FF)), whole((6, D))],
            out_specs=[
                rows, stack(d_b), stack(f_b), stack(d_b), stack(f_b), stack(d_b), stack(d_b), rows,
                whole((6, D)), whole((1, FF)),
            ],
            scratch_shapes=[
                pltpu.VMEM((D, D), BF16),
                pltpu.VMEM((D, FF), BF16),
                pltpu.VMEM((FF, D), BF16),
                pltpu.VMEM((seq, FF), BF16),
                pltpu.SemaphoreType.DMA((3,)),
            ],
        ),
        out_shape=[
            shape((total, D), BF16),
            shape((d_b, total, LANES), BF16),
            shape((f_b, total, LANES), BF16),
            shape((d_b, total, LANES), BF16),
            shape((f_b, total, LANES), BF16),
            shape((d_b, total, LANES), BF16),
            shape((d_b, total, LANES), BF16),
            shape((total, D), F32),
            shape((6, D), F32),
            shape((1, FF), F32),
        ],
        compiler_params=params(),
        name="tokenwise",
    )(homes, offset, att, tokens, cotangent, every, up_bias, row_vec)
    layer_own, normed_low, active_low, down_low, up_low, attn_low, mixed_low, grad_one, row_grad, up_grad = token_outs
    merged, input_own, split_grad = pl.pallas_call(
        attend_back_kernel,
        grid_spec=pltpu.PrefetchScalarGridSpec(
            num_scalar_prefetch=3,
            grid=(row_count,),
            in_specs=[stack(3 * d_b), stack(d_b), stack(d_b), lse_spec, rows, anywhere()],
            out_specs=[stack(3 * d_b), rows, whole((2, D))],
            scratch_shapes=[
                pltpu.VMEM((D, 3 * D), BF16),
                pltpu.VMEM((seq, seq), F32),
                pltpu.SemaphoreType.DMA,
            ],
        ),
        out_shape=[
            shape((3 * d_b, total, LANES), BF16),
            shape((total, D), BF16),
            shape((2, D), F32),
        ],
        compiler_params=params(),
        name="attend_back",
    )(homes, pair_lengths, offset, qkv, att, mixed_low, lse, grad_one, every)
    f_s = f_b // d_b
    part = lambda n: pl.BlockSpec((n, total, LANES), lambda j, *_: (j, 0, 0))
    blocks = 2 * f_s * d_b + 4 * d_b
    grads = pl.pallas_call(
        lambda pc, *refs: grad_kernel(*refs),
        grid_spec=pltpu.PrefetchScalarGridSpec(
            num_scalar_prefetch=1,
            grid=(d_b,),
            in_specs=[
                part(f_s), whole((d_b, total, LANES)), whole((d_b, total, LANES)), part(f_s),
                pl.BlockSpec((total, D), lambda j, pc: (pc[0], 0)),
                part(3), part(1), whole((d_b, total, LANES)),
            ],
            out_specs=pl.BlockSpec((blocks, LANES, LANES), lambda j, *_: (j, 0, 0)),
        ),
        out_shape=shape((d_b * blocks, LANES, LANES), BF16),
        compiler_params=params(),
        name="weight_grads",
    )(piece.astype(jnp.int32).reshape(1), active_low, down_low, normed_low, up_low, tokens, merged, att, attn_low)
    return layer_own, input_own, grads, row_grad, up_grad, split_grad


def bit_orders(n_dp, spd):
    dp_bits = list(range(1, n_dp.bit_length() - 1))
    near, far = dp_bits[:1], dp_bits[1:]
    third = spd * 4 // 14
    first = (spd - third) // 2
    counts = (first, spd - third - first, third)
    orders = ([-1] + near + far, near + [-1] + far, far + [-1] + near)
    parts, at = [], 0
    for order, count in zip(orders, counts):
        if count:
            parts.append((order, at, count))
        at += count
    return parts


def bit_of(number, bit):
    return number // (1 << bit) % 2


def across(bit):
    if bit < 0:
        return {"tensor": 1 - lax.axis_index("tensor")}
    me = lax.axis_index("dp")
    return {"dp": me + (1 - 2 * bit_of(me, bit)) * (1 << bit)}


def first_slot(order, code, core, n_dp, spd):
    dp, tensor = lax.axis_index("dp"), lax.axis_index("tensor")
    place = len(order) - 1
    dev = core
    for bit in order:
        flip = bit_of(code, place)
        mine = tensor if bit < 0 else bit_of(dp, bit)
        dev = dev + (mine + flip) % 2 * (n_dp if bit < 0 else 1 << bit)
        place -= 1
    return dev * spd


def greet(bits):
    barrier = pltpu.get_barrier_semaphore()
    for bit in bits:
        pl.semaphore_signal(barrier, inc=1, device_id=across(bit), device_id_type=pl.DeviceIdType.MESH)
    pl.semaphore_wait(barrier, len(bits))


def remote(source, target, send, recv, bit):
    return pltpu.make_async_remote_copy(
        src_ref=source, dst_ref=target, send_sem=send, recv_sem=recv,
        device_id=across(bit), device_id_type=pl.DeviceIdType.MESH,
    )


def gather_kernel(n_dp, spd, own_ref, vec_ref, all_ref, both_ref, local_sem, send_sem, recv_sem, core_send, core_recv, vec_send, vec_recv):
    parts = bit_orders(n_dp, spd)
    n_bits = len(parts[0][0])
    core = bit_of(lax.axis_index("dp"), 0)
    tensor = lax.axis_index("tensor")
    greet([0] + parts[0][0])
    mine = first_slot(parts[0][0], 0, core, n_dp, spd)
    keep = pltpu.make_async_copy(own_ref, all_ref.at[pl.ds(mine, spd)], local_sem.at[0])
    keep.start()
    keep_vec = pltpu.make_async_copy(vec_ref, both_ref.at[pl.ds(tensor, 1)], local_sem.at[1])
    keep_vec.start()
    vec = remote(vec_ref, both_ref.at[pl.ds(tensor, 1)], vec_send, vec_recv, -1)
    vec.start()

    def piece(part, code, core_of):
        order, at, count = part
        return all_ref.at[pl.ds(first_slot(order, code, core_of, n_dp, spd) + at, count)]

    def forward(p, code, level, source):
        order = parts[p][0]
        for stage in range(level, n_bits):
            remote(
                source, piece(parts[p], code, core), send_sem.at[p, stage, code],
                recv_sem.at[p, code + (1 << stage)], order[n_bits - 1 - stage],
            ).start()
        remote(source, piece(parts[p], code, core), core_send.at[p, code], core_recv.at[p, code], 0).start()

    for p, part in enumerate(parts):
        forward(p, 0, 0, own_ref.at[pl.ds(part[1], part[2])])
    for level in range(n_bits):
        def arrive(j, carry):
            code = (1 << level) + j
            for p, part in enumerate(parts):
                here = piece(part, code, core)
                pltpu.make_async_copy(here, here, recv_sem.at[p, code]).wait()
                forward(p, code, level + 1, here)
            return carry

        lax.fori_loop(0, 1 << level, arrive, 0)

    def drain(code, carry):
        for p, part in enumerate(parts):
            here = piece(part, code, core)
            there = piece(part, code, 1 - core)
            pltpu.make_async_copy(here, here, core_send.at[p, code]).wait()
            pltpu.make_async_copy(there, there, core_recv.at[p, code]).wait()
        return carry

    for stage in range(n_bits):
        def sent(code, carry):
            for p, part in enumerate(parts):
                here = piece(part, code, core)
                pltpu.make_async_copy(here, here, send_sem.at[p, stage, code]).wait()
            return carry

        lax.fori_loop(0, 1 << stage, sent, 0)
    lax.fori_loop(0, 1 << n_bits, drain, 0)
    keep.wait()
    keep_vec.wait()
    vec.wait()


def gather_all(own, vec, n_dp, pieces, space):
    spd, edge = own.shape[0], own.shape[-1]
    parts = bit_orders(n_dp, spd)
    n, n_bits = len(parts), len(parts[0][0])
    dma = pltpu.SemaphoreType.DMA
    return pl.pallas_call(
        functools.partial(gather_kernel, n_dp, spd),
        in_specs=[pl.BlockSpec(memory_space=pltpu.VMEM)] * 2,
        out_specs=[pl.BlockSpec(memory_space=space), pl.BlockSpec(memory_space=pltpu.VMEM)],
        out_shape=[
            jax.ShapeDtypeStruct((pieces * n_dp * spd, edge, edge), BF16),
            jax.ShapeDtypeStruct((pieces, vec.shape[1]), F32),
        ],
        scratch_shapes=[
            dma((2,)), dma((n, n_bits, 1 << n_bits)), dma((n, 1 << n_bits)),
            dma((n, 1 << n_bits)), dma((n, 1 << n_bits)), dma, dma,
        ],
        compiler_params=pltpu.CompilerParams(
            vmem_limit_bytes=VMEM_LIMIT, collective_id=0, has_side_effects=True
        ),
        name="gather",
    )(own, vec)


def scatter_kernel(
    n_dp, spd, scale, places, g_ref, vec_ref, out_ref, vec_out,
    give_ref, sum_ref, in_ref, vec_sum, vec_in,
    core_send, core_recv, send_sem, recv_sem, vec_send, vec_recv,
):
    parts = bit_orders(n_dp, spd)
    n_bits = len(parts[0][0])
    codes = 1 << n_bits
    core = bit_of(lax.axis_index("dp"), 0)
    vec_bits = [0] + parts[0][0]
    greet(vec_bits)

    def term(slot):
        place = places[slot]
        return jnp.where(place >= 0, g_ref[jnp.maximum(place, 0)], jnp.zeros(g_ref.shape[1:], BF16))

    def vec_copy(stage):
        return remote(vec_sum.at[stage], vec_in.at[stage], vec_send.at[stage], vec_recv.at[stage], vec_bits[stage])

    def vec_step(stage):
        vec_copy(stage).wait_recv()
        total = vec_sum[stage] + vec_in[stage]
        if stage + 1 < len(vec_bits):
            vec_sum[stage + 1] = total
            vec_copy(stage + 1).start()
        else:
            vec_out[...] = total * scale

    vec_sum[0] = vec_ref[...]
    vec_copy(0).start()

    def give(p, code):
        order, at, count = parts[p]
        where = pl.ds(at, count)
        return remote(
            give_ref.at[code, where], sum_ref.at[code, where], core_send.at[p, code], core_recv.at[p, code], 0
        )

    def passed(p, level, code):
        order, at, count = parts[p]
        where = pl.ds(at, count)
        return remote(
            sum_ref.at[code, where], in_ref.at[code - 1, where],
            send_sem.at[p, code], recv_sem.at[p, code - 1], order[n_bits - 1 - level],
        )

    def hand(j, carry):
        code = codes - 1 - j
        for p, (order, at, count) in enumerate(parts):
            start = first_slot(order, code, 1 - core, n_dp, spd) + at
            for s in range(count):
                give_ref[code, at + s] = term(start + s)
            give(p, code).start()
        return carry

    lax.fori_loop(0, codes, hand, 0)
    vec_step(0)

    def total_of(p, code, level, finish):
        order, at, count = parts[p]
        start = first_slot(order, code, core, n_dp, spd) + at
        give(p, code).wait_recv()
        sources = []
        for stage in range(level + 1, n_bits):
            entry = (1 << stage) - 1 + code
            here = in_ref.at[entry, pl.ds(at, count)]
            pltpu.make_async_copy(here, here, recv_sem.at[p, entry]).wait()
            sources.append(entry)
        for s in range(count):
            value = term(start + s).astype(F32) + sum_ref[code, at + s].astype(F32)
            for entry in sources:
                value = value + in_ref[entry, at + s].astype(F32)
            if finish:
                out_ref[at + s] = value * scale
            else:
                sum_ref[code, at + s] = value.astype(BF16)

    for level in reversed(range(n_bits)):
        def onward(j, carry):
            code = (2 << level) - 1 - j
            for p in range(len(parts)):
                total_of(p, code, level, False)
                passed(p, level, code).start()
            return carry

        lax.fori_loop(0, 1 << level, onward, 0)
        vec_step(n_bits - level)
    for p in range(len(parts)):
        total_of(p, 0, -1, True)
    for stage in range(len(vec_bits)):
        vec_copy(stage).wait_send()

    def drain(code, carry):
        for p in range(len(parts)):
            give(p, code).wait_send()
        return carry

    lax.fori_loop(0, codes, drain, 0)
    for level in range(n_bits):
        def drain_level(j, carry):
            for p in range(len(parts)):
                passed(p, level, (1 << level) + j).wait_send()
            return carry

        lax.fori_loop(0, 1 << level, drain_level, 0)


def scatter_all(places, grads, vec, n_dp, scale):
    edge = grads.shape[-1]
    spd = places.shape[0] // (2 * n_dp)
    parts = bit_orders(n_dp, spd)
    n, n_bits = len(parts), len(parts[0][0])
    codes = 1 << n_bits
    dma = pltpu.SemaphoreType.DMA
    vmem = pl.BlockSpec(memory_space=pltpu.VMEM)
    return pl.pallas_call(
        functools.partial(scatter_kernel, n_dp, spd, scale),
        in_specs=[smem(), vmem, vmem],
        out_specs=[vmem, vmem],
        out_shape=[
            jax.ShapeDtypeStruct((spd, edge, edge), F32),
            jax.ShapeDtypeStruct(vec.shape, F32),
        ],
        scratch_shapes=[
            pltpu.VMEM((codes, spd, edge, edge), BF16),
            pltpu.VMEM((codes, spd, edge, edge), BF16),
            pltpu.VMEM((codes - 1, spd, edge, edge), BF16),
            pltpu.VMEM((n_bits + 1,) + vec.shape, F32),
            pltpu.VMEM((n_bits + 1,) + vec.shape, F32),
            dma((n, codes)), dma((n, codes)), dma((n, codes)), dma((n, codes)),
            dma((n_bits + 1,)), dma((n_bits + 1,)),
        ],
        compiler_params=pltpu.CompilerParams(
            vmem_limit_bytes=VMEM_LIMIT, collective_id=1, has_side_effects=True
        ),
        name="scatter",
    )(places, grads, vec)


def update_kernel(grad_ref, master_ref, first_ref, second_ref, left_ref, right_ref, new_ref, nf_ref, ns_ref, low_ref):
    for s in range(grad_ref.shape[0]):
        left, right = left_ref[0, s].astype(BF16), right_ref[0, s].astype(BF16)
        turned = dot_nn(dot_tn(left, grad_ref[s].astype(BF16)).astype(BF16), right)
        first = MOMENT_DECAY * first_ref[0, s] + (1.0 - MOMENT_DECAY) * turned
        second = MOMENT_DECAY * second_ref[0, s] + (1.0 - MOMENT_DECAY) * turned * turned
        stepped = first / (jnp.sqrt(second) + EPS_ADAM)
        back = dot_nt(dot_nn(left, stepped.astype(BF16)).astype(BF16), right)
        new = master_ref[0, s] - LEARN_RATE * back
        new_ref[0, s] = new
        nf_ref[0, s] = first
        ns_ref[0, s] = second
        low_ref[0, s] = new.astype(BF16)


def update_blocks(grads, masters, first, second, left, right):
    spd, edge = grads.shape[0], grads.shape[-1]
    group = 2 if spd % 2 == 0 else 1
    spec = pl.BlockSpec((1, group, edge, edge), lambda i: (0, i, 0, 0))
    return pl.pallas_call(
        update_kernel,
        grid=(spd // group,),
        in_specs=[pl.BlockSpec((group, edge, edge), lambda i: (i, 0, 0))] + [spec] * 5,
        out_specs=[spec] * 4,
        out_shape=[jax.ShapeDtypeStruct(masters.shape, F32)] * 3 + [jax.ShapeDtypeStruct(masters.shape, BF16)],
        compiler_params=params(),
        name="update",
    )(grads, masters, first, second, left, right)


def body(
    tokens,
    cotangent,
    pair_lengths,
    block_of_slot,
    masters,
    mom_first,
    mom_second,
    left_bases,
    right_bases,
    split_vec,
    split_first,
    split_second,
    row_vec,
    row_first,
    row_second,
):
    pieces = lax.axis_size("tensor")
    piece = lax.axis_index("tensor")
    piece_width = HEADS * HEAD // pieces
    piece_ffn = FF // pieces
    block_edge = masters.shape[-1]
    block_total = sum(block_counts(block_edge, piece_width, piece_ffn))
    slots = block_of_slot.shape[0]
    full_seq = tokens.shape[0] // pair_lengths.shape[0]
    row_count = pair_lengths.shape[0] // pieces
    n_dp = lax.axis_size("dp")
    every, split_all = gather_all(masters[0].astype(BF16), split_vec, n_dp, pieces, pl.ANY)
    slot_of = slot_table(block_of_slot, block_total)
    order = np.array(sum(block_home(pieces), []), np.int32)
    homes = slot_of[order[:, 1]] + order[:, 0] * slots
    query_bias = split_all[:, :piece_width].reshape(1, -1)
    value_bias = split_all[:, piece_width : 2 * piece_width].reshape(1, -1)
    up_bias = split_all[:, 2 * piece_width :].reshape(1, -1)
    layer_own, input_own, grads, row_local, up_grad, qv_grad = layer_passes(
        tokens, cotangent, pair_lengths, piece, homes, every, query_bias, value_bias, up_bias, row_vec, row_count, full_seq
    )
    layer_out = lax.all_gather(layer_own, "tensor", axis=0, tiled=True)
    input_grad = lax.all_gather(input_own, "tensor", axis=0, tiled=True).astype(F32)
    place_table = np.full((pieces, block_total + 1), -1, np.int32)
    for index, (at_piece, number) in enumerate(grad_order(pieces)):
        place_table[at_piece, number] = index
    places = jnp.asarray(place_table)[:, block_of_slot].reshape(-1)
    split_local = jnp.concatenate(
        [
            qv_grad[0].reshape(pieces, piece_width),
            qv_grad[1].reshape(pieces, piece_width),
            up_grad.reshape(pieces, piece_ffn),
        ],
        axis=1,
    )
    mean_scale = 1.0 / (tokens.shape[0] * n_dp)
    vectors = jnp.concatenate([split_local.reshape(-1, LANES), row_local.reshape(-1, LANES)], axis=0)
    owned, summed = scatter_all(places, grads, vectors, n_dp, mean_scale)
    weight_grads = owned[None]
    split_rows = split_local.size // LANES
    split_grad = lax.dynamic_slice_in_dim(summed[:split_rows].reshape(pieces, -1), piece, 1, 0)
    row_grad = summed[split_rows:].reshape(row_local.shape)
    new_masters, new_first, new_second, copies = update_blocks(
        owned, masters, mom_first, mom_second, left_bases, right_bases
    )
    new_split, new_split_first, new_split_second = adam_vector(
        split_grad, split_first, split_second, split_vec
    )
    new_row, new_row_first, new_row_second = adam_vector(row_grad, row_first, row_second, row_vec)
    return (
        layer_out,
        input_grad,
        weight_grads,
        new_masters,
        new_first,
        new_second,
        copies,
        split_grad,
        new_split,
        new_split_first,
        new_split_second,
        row_grad,
        new_row,
        new_row_first,
        new_row_second,
    )


def solution(mesh):
    in_specs = (
        P("dp", None),
        P("dp", None),
        P("dp", None),
        P(),
        P("tensor", "dp", None, None),
        P("tensor", "dp", None, None),
        P("tensor", "dp", None, None),
        P("tensor", "dp", None, None),
        P("tensor", "dp", None, None),
        P("tensor", None),
        P("tensor", None),
        P("tensor", None),
        P(),
        P(),
        P(),
    )
    out_specs = (
        P("dp", None),
        P("dp", None),
        P("tensor", "dp", None, None),
        P("tensor", "dp", None, None),
        P("tensor", "dp", None, None),
        P("tensor", "dp", None, None),
        P("tensor", "dp", None, None),
        P("tensor", None),
        P("tensor", None),
        P("tensor", None),
        P("tensor", None),
        P(),
        P(),
        P(),
        P(),
    )
    return jax.shard_map(body, mesh=mesh, in_specs=in_specs, out_specs=out_specs, check_vma=False)
```

```python
import functools

import jax
import jax.numpy as jnp
from jax import lax
from jax.experimental import pallas as pl
from jax.experimental.pallas import tpu as pltpu
from jax.sharding import PartitionSpec as P
import numpy as np

D = 768
HEADS = 12
HEAD = 64
FF = 3072


EPS_NORM = 1e-05
EPS_ADAM = 1e-08
LEARN_RATE = 0.01
VECTOR_RATE = 0.15
MOMENT_DECAY = 0.5
MASKED_SCORE = -1e30
HIGHEST_PRECISION = lax.Precision.HIGHEST


def block_counts(block_edge, head_width, ffn_width):
    return (
        D // block_edge * (3 * head_width // block_edge),
        head_width // block_edge * (D // block_edge),
        D // block_edge * (ffn_width // block_edge),
        ffn_width // block_edge * (D // block_edge),
    )


LOG2E = 1.4426950408889634
LN_TWO = 0.6931471805599453
ROOT_HALF = 0.7071067811865476
PHI_SCALE = 0.3989422804014327
ERF_P = 0.3275911
ERF_A = (0.254829592, -0.284496736, 1.421413741, -1.453152027, 1.061405429)
VMEM_LIMIT = 60 * 1024 * 1024
LANES = 128
VEC_ROWS = 16
BF16 = jnp.bfloat16
F32 = jnp.float32


def dot_nn(left, right):
    return lax.dot_general(left, right, (((1,), (0,)), ((), ())), preferred_element_type=F32)


def dot_nt(left, right):
    return lax.dot_general(left, right, (((1,), (1,)), ((), ())), preferred_element_type=F32)


def dot_tn(left, right):
    return lax.dot_general(left, right, (((0,), (0,)), ((), ())), preferred_element_type=F32)


def block_home(pieces):
    d_b, f_b = D // LANES, FF // LANES
    d_p, f_p = d_b // pieces, f_b // pieces
    first = d_b * 3 * d_p
    second = first + d_p * d_b
    third = second + d_b * f_p
    qkv = [
        (n % d_b // d_p, k * 3 * d_p + n // d_b * d_p + n % d_p)
        for k in range(d_b)
        for n in range(3 * d_b)
    ]
    out = [(k // d_p, first + k % d_p * d_b + n) for k in range(d_b) for n in range(d_b)]
    up = [(n // f_p, second + k * f_p + n % f_p) for k in range(d_b) for n in range(f_b)]
    down = [(k // f_p, third + k % f_p * d_b + n) for k in range(f_b) for n in range(d_b)]
    return qkv, out, up, down


def grad_order(pieces):
    d_b, f_b = D // LANES, FF // LANES
    qkv, out, up, down = block_home(pieces)
    f_s, q_s = f_b // d_b, 3
    order = []
    for j in range(d_b):
        order += [down[(j * f_s + k) * d_b + n] for k in range(f_s) for n in range(d_b)]
        order += [up[k * f_b + j * f_s + n] for k in range(d_b) for n in range(f_s)]
        order += [qkv[k * 3 * d_b + j * q_s + n] for k in range(d_b) for n in range(q_s)]
        order += [out[j * d_b + n] for n in range(d_b)]
    return order


def start_blocks(homes, base, rows, cols, source, target, sem):
    def step(index, carry):
        k, n = index // cols, index % cols
        pltpu.make_async_copy(
            source.at[homes[base + index]],
            target.at[pl.ds(pl.multiple_of(k * LANES, LANES), LANES), pl.ds(pl.multiple_of(n * LANES, LANES), LANES)],
            sem,
        ).start()
        return carry

    lax.fori_loop(0, rows * cols, step, 0, unroll=6)


def wait_blocks(target, sem):
    pltpu.make_async_copy(target, target, sem).wait()


def mask_bias(ends_ref, row, seq, bias_ref):
    col = lax.broadcasted_iota(jnp.int32, (seq, 1), 0)
    lane = lax.broadcasted_iota(jnp.int32, (1, seq), 1)
    seg_col = jnp.zeros((seq, 1), jnp.int32)
    seg_lane = jnp.zeros((1, seq), jnp.int32)
    end = 0
    for k in range(ends_ref.shape[1] - 1):
        end = end + ends_ref[row, k]
        seg_col = seg_col + (col >= end).astype(jnp.int32)
        seg_lane = seg_lane + (lane >= end).astype(jnp.int32)
    bias_ref[...] = jnp.where(seg_col == seg_lane, 0.0, MASKED_SCORE)


def attend_kernel(homes, pairs, offset, x_ref, every, qb_ref, vb_ref, qkv_ref, att_ref, lse_ref, w_ref, bias_ref, sem):
    d_b = D // LANES
    row = pl.program_id(0)
    seq = x_ref.shape[0]

    @pl.when(row == 0)
    def _():
        start_blocks(homes, 0, d_b, 3 * d_b, every, w_ref, sem)

    mask_bias(pairs, offset[0] + row, seq, bias_ref)

    @pl.when(row == 0)
    def _():
        wait_blocks(w_ref, sem)

    x = x_ref[...]
    wide = 2 * LANES
    for part in range(3):
        for c in range(0, D, wide):
            y = dot_nn(x, w_ref[:, part * D + c : part * D + c + wide])
            if part == 0:
                y = (y + qb_ref[:, c : c + wide]).astype(BF16).astype(F32) * HEAD ** (-0.5)
            if part == 2:
                y = y + vb_ref[:, c : c + wide]
            y = y.astype(BF16)
            for n in range(2):
                qkv_ref[part * d_b + c // LANES + n] = y[:, n * LANES : (n + 1) * LANES]
    lane = lax.broadcasted_iota(jnp.int32, (1, LANES), 1)

    def pair(n, carry):
        q = qkv_ref[n]
        k = qkv_ref[d_b + n]
        v_t = qkv_ref[2 * d_b + n].T
        halves = []
        for h in range(2):
            keep = (lane < HEAD) if h == 0 else (lane >= HEAD)
            scores = dot_nt(jnp.where(keep, k, jnp.zeros_like(k)), q) + bias_ref[...]
            top = jnp.max(scores, axis=0, keepdims=True)
            p = jnp.exp(scores - top)
            total = jnp.sum(p, axis=0, keepdims=True)
            lse_ref[0, 2 * n + h] = (top + jnp.log(total)).reshape(1, seq)
            mixed = dot_nn(v_t[h * HEAD : (h + 1) * HEAD], p.astype(BF16))
            halves.append(mixed * (1.0 / total))
        att_ref[n] = jnp.concatenate(halves, axis=0).T.astype(BF16)
        return carry

    lax.fori_loop(0, d_b, pair, 0)


def norm_parts(hidden):
    mean = jnp.mean(hidden, axis=-1, keepdims=True)
    centred = hidden - mean
    var = jnp.mean(centred * centred, axis=-1, keepdims=True)
    inv = lax.rsqrt(var + EPS_NORM)
    return centred * inv, inv


def norm_back(grad, gain, normed, inv):
    scaled = grad * gain
    mean = jnp.mean(scaled, axis=-1, keepdims=True)
    along = jnp.mean(scaled * normed, axis=-1, keepdims=True)
    return inv * (scaled - mean - normed * along)


def put_blocks(ref, value):
    for n in range(ref.shape[0]):
        ref[n] = value[:, n * LANES : (n + 1) * LANES]


def get_blocks(ref):
    return jnp.concatenate([ref[n] for n in range(ref.shape[0])], axis=1)


def gelu_parts(u):
    e = jnp.exp(u * u * -0.5)
    t = 1.0 / (1.0 + (ERF_P * ROOT_HALF) * jnp.abs(u))
    a1, a2, a3, a4, a5 = (0.5 * a for a in ERF_A)
    tail = ((((a5 * t + a4) * t + a3) * t + a2) * t + a1) * t * e
    cdf = jnp.where(u >= 0, 1.0 - tail, tail)
    return u * cdf, cdf + u * e * PHI_SCALE


def token_kernel(
    homes, att_ref, x_ref, cot_ref, every, bu_ref, rv_ref,
    out_ref, nl_ref, act_ref, dl_ref, up_ref, al_ref, ml_ref, g1_ref, rg_ref, bg_ref,
    wo_ref, wu_ref, wd_ref, dg_ref, sem,
):
    d_b, f_b = D // LANES, FF // LANES
    step = pl.program_id(0)

    @pl.when(step == 0)
    def _():
        start_blocks(homes, 3 * d_b * d_b, d_b, d_b, every, wo_ref, sem.at[0])
        start_blocks(homes, 4 * d_b * d_b, d_b, f_b, every, wu_ref, sem.at[1])
        start_blocks(homes, 4 * d_b * d_b + d_b * f_b, f_b, d_b, every, wd_ref, sem.at[2])
        rg_ref[...] = jnp.zeros_like(rg_ref)
        bg_ref[...] = jnp.zeros_like(bg_ref)
        wait_blocks(wo_ref, sem.at[0])
        wait_blocks(wu_ref, sem.at[1])
        wait_blocks(wd_ref, sem.at[2])

    out_bias, gain_one, shift_one, down_bias, gain_two, shift_two = (
        rv_ref[i : i + 1] for i in range(6)
    )
    hidden = dot_nn(get_blocks(att_ref), wo_ref[...]) + x_ref[...].astype(F32) + out_bias
    n_one, inv_one = norm_parts(hidden)
    normed = n_one * gain_one + shift_one
    normed_low = normed.astype(BF16)
    put_blocks(nl_ref, normed_low)
    wide = 512
    total = normed + down_bias
    for c in range(0, FF, wide):
        u = dot_nn(normed_low, wu_ref[:, c : c + wide]) + bu_ref[:, c : c + wide]
        active, slope = gelu_parts(u)
        active = active.astype(BF16)
        dg_ref[:, c : c + wide] = slope.astype(BF16)
        for n in range(wide // LANES):
            act_ref[c // LANES + n] = active[:, n * LANES : (n + 1) * LANES]
        total = total + dot_nn(active, wd_ref[c : c + wide, :])
    n_two, inv_two = norm_parts(total)
    out_ref[...] = (n_two * gain_two + shift_two).astype(BF16)
    dy = cot_ref[...].astype(F32)
    grad_two = norm_back(dy, gain_two, n_two, inv_two)
    down_low = grad_two.astype(BF16)
    put_blocks(dl_ref, down_low)
    rg_ref[3:4] += jnp.sum(grad_two, axis=0, keepdims=True)
    rg_ref[4:5] += jnp.sum(dy * n_two, axis=0, keepdims=True)
    rg_ref[5:6] += jnp.sum(dy, axis=0, keepdims=True)
    grad_normed = grad_two
    for c in range(0, FF, wide):
        ga = dot_nt(down_low, wd_ref[c : c + wide, :]) * dg_ref[:, c : c + wide].astype(F32)
        up = ga.astype(BF16)
        for n in range(wide // LANES):
            up_ref[c // LANES + n] = up[:, n * LANES : (n + 1) * LANES]
        bg_ref[:, c : c + wide] += jnp.sum(up.astype(F32), axis=0, keepdims=True)
        grad_normed = grad_normed + dot_nt(up, wu_ref[:, c : c + wide])
    rg_ref[1:2] += jnp.sum(grad_normed * n_one, axis=0, keepdims=True)
    rg_ref[2:3] += jnp.sum(grad_normed, axis=0, keepdims=True)
    grad_one = norm_back(grad_normed, gain_one, n_one, inv_one)
    rg_ref[0:1] += jnp.sum(grad_one, axis=0, keepdims=True)
    g1_ref[...] = grad_one
    attn_low = grad_one.astype(BF16)
    put_blocks(al_ref, attn_low)
    put_blocks(ml_ref, dot_nt(attn_low, wo_ref[...]).astype(BF16))


def attend_back_kernel(
    homes, pairs, offset, qkv_ref, att_ref, ml_ref, lse_ref, g1_ref, every,
    merged_ref, ig_ref, il_ref, sg_ref, w_ref, bias_ref, sem,
):
    d_b = D // LANES
    row = pl.program_id(0)
    seq = g1_ref.shape[0]

    @pl.when(row == 0)
    def _():
        start_blocks(homes, 0, d_b, 3 * d_b, every, w_ref, sem)
        sg_ref[...] = jnp.zeros_like(sg_ref)

    mask_bias(pairs, offset[0] + row, seq, bias_ref)
    lane = lax.broadcasted_iota(jnp.int32, (1, LANES), 1)

    def pair(n, carry):
        q = qkv_ref[n]
        k = qkv_ref[d_b + n]
        v = qkv_ref[2 * d_b + n]
        g = ml_ref[n]
        k_t = k.T
        both = g.T.astype(F32) * att_ref[n].T.astype(F32)
        zero = jnp.zeros_like(k)
        parts = []
        for h in range(2):
            keep = (lane < HEAD) if h == 0 else (lane >= HEAD)
            spread = jnp.sum(both[h * HEAD : (h + 1) * HEAD], axis=0, keepdims=True)
            scores = dot_nt(jnp.where(keep, k, zero), q) + bias_ref[...]
            p = jnp.exp(scores - lse_ref[0, 2 * n + h].reshape(1, seq))
            gp = dot_nt(jnp.where(keep, v, zero), g)
            low = (p * (gp - spread)).astype(BF16)
            gv = dot_nn(p.astype(BF16), g)
            gk = dot_nn(low, q)
            gq = dot_nn(k_t[h * HEAD : (h + 1) * HEAD], low)
            parts.append((gq, gk, gv))
        gq = (jnp.concatenate([parts[0][0], parts[1][0]], axis=0) * HEAD ** (-0.5)).T
        merged_ref[n] = gq.astype(BF16)
        merged_ref[d_b + n] = jnp.where(lane < HEAD, parts[0][1], parts[1][1]).astype(BF16)
        merged_ref[2 * d_b + n] = jnp.where(lane < HEAD, parts[0][2], parts[1][2]).astype(BF16)
        return carry

    lax.fori_loop(0, d_b, pair, 0)

    @pl.when(row == 0)
    def _():
        wait_blocks(w_ref, sem)

    for n in range(d_b):
        at = slice(n * LANES, (n + 1) * LANES)
        sg_ref[0:1, at] += jnp.sum(merged_ref[n].astype(F32), axis=0, keepdims=True)
        sg_ref[1:2, at] += jnp.sum(merged_ref[2 * d_b + n].astype(F32), axis=0, keepdims=True)
    merged = get_blocks(merged_ref)
    total = g1_ref[...] + dot_nt(merged, w_ref[...])
    ig_ref[...] = total
    il_ref[...] = total.astype(BF16)


def grad_kernel(act_ref, dl_ref, nl_ref, up_ref, x_ref, merged_ref, att_ref, al_ref, g_ref):
    d_b = D // LANES
    f_s = act_ref.shape[0]
    at = 0

    def store(value, at):
        value = value.astype(BF16)
        for k in range(value.shape[0] // LANES):
            for n in range(value.shape[1] // LANES):
                g_ref[at] = value[k * LANES : (k + 1) * LANES, n * LANES : (n + 1) * LANES]
                at += 1
        return at

    at = store(dot_tn(get_blocks(act_ref), get_blocks(dl_ref)), at)
    at = store(dot_tn(get_blocks(nl_ref), get_blocks(up_ref)), at)
    at = store(dot_tn(x_ref[...], get_blocks(merged_ref)), at)
    at = store(dot_tn(att_ref[0], get_blocks(al_ref)), at)


def smem():
    return pl.BlockSpec(memory_space=pltpu.SMEM)


def anywhere():
    return pl.BlockSpec(memory_space=pl.ANY)


def params():
    return pltpu.CompilerParams(vmem_limit_bytes=VMEM_LIMIT, dimension_semantics=("arbitrary",))


def layer_passes(tokens, cotangent, pair_lengths, piece, homes, every, query_bias, value_bias, up_bias, row_vec, row_count, seq):
    d_b, f_b = D // LANES, FF // LANES
    total = row_count * seq
    shape = jax.ShapeDtypeStruct
    offset = (piece * row_count).astype(jnp.int32).reshape(1)
    stack = lambda n: pl.BlockSpec((n, seq, LANES), lambda r, *_: (0, r, 0))
    rows = pl.BlockSpec((seq, D), lambda r, *_: (r, 0))
    own = lambda at: pl.BlockSpec((seq, D), lambda r, *pre: (pre[at][0] + r, 0))
    whole = lambda s: pl.BlockSpec(s, lambda *_: tuple(0 for _ in s))
    lse_spec = pl.BlockSpec((1, HEADS, 1, seq), lambda r, *_: (r, 0, 0, 0))
    qkv, att, lse = pl.pallas_call(
        attend_kernel,
        grid_spec=pltpu.PrefetchScalarGridSpec(
            num_scalar_prefetch=3,
            grid=(row_count,),
            in_specs=[own(2), anywhere(), whole((1, D)), whole((1, D))],
            out_specs=[stack(3 * d_b), stack(d_b), lse_spec],
            scratch_shapes=[
                pltpu.VMEM((D, 3 * D), BF16),
                pltpu.VMEM((seq, seq), F32),
                pltpu.SemaphoreType.DMA,
            ],
        ),
        out_shape=[
            shape((3 * d_b, total, LANES), BF16),
            shape((d_b, total, LANES), BF16),
            shape((row_count, HEADS, 1, seq), F32),
        ],
        compiler_params=params(),
        cost_estimate=pl.CostEstimate(flops=24 * total * D * D, bytes_accessed=32 * total * D, transcendentals=0),
        name="attend",
    )(homes, pair_lengths, offset, tokens, every, query_bias, value_bias)
    token_outs = pl.pallas_call(
        lambda homes, off, *refs: token_kernel(homes, *refs),
        grid_spec=pltpu.PrefetchScalarGridSpec(
            num_scalar_prefetch=2,
            grid=(row_count,),
            in_specs=[stack(d_b), own(1), own(1), anywhere(), whole((1, FF)), whole((6, D))],
            out_specs=[
                rows, stack(d_b), stack(f_b), stack(d_b), stack(f_b), stack(d_b), stack(d_b), rows,
                whole((6, D)), whole((1, FF)),
            ],
            scratch_shapes=[
                pltpu.VMEM((D, D), BF16),
                pltpu.VMEM((D, FF), BF16),
                pltpu.VMEM((FF, D), BF16),
                pltpu.VMEM((seq, FF), BF16),
                pltpu.SemaphoreType.DMA((3,)),
            ],
        ),
        out_shape=[
            shape((total, D), BF16),
            shape((d_b, total, LANES), BF16),
            shape((f_b, total, LANES), BF16),
            shape((d_b, total, LANES), BF16),
            shape((f_b, total, LANES), BF16),
            shape((d_b, total, LANES), BF16),
            shape((d_b, total, LANES), BF16),
            shape((total, D), F32),
            shape((6, D), F32),
            shape((1, FF), F32),
        ],
        compiler_params=params(),
        cost_estimate=pl.CostEstimate(flops=40 * total * D * D, bytes_accessed=64 * total * D, transcendentals=0),
        name="tokenwise",
    )(homes, offset, att, tokens, cotangent, every, up_bias, row_vec)
    layer_own, normed_low, active_low, down_low, up_low, attn_low, mixed_low, grad_one, row_grad, up_grad = token_outs
    swap = [(0, 1), (1, 0)]
    layer_other = lax.ppermute(layer_own, "tensor", swap)
    merged, input_own, input_low, split_grad = pl.pallas_call(
        attend_back_kernel,
        grid_spec=pltpu.PrefetchScalarGridSpec(
            num_scalar_prefetch=3,
            grid=(row_count,),
            in_specs=[stack(3 * d_b), stack(d_b), stack(d_b), lse_spec, rows, anywhere()],
            out_specs=[stack(3 * d_b), rows, rows, whole((2, D))],
            scratch_shapes=[
                pltpu.VMEM((D, 3 * D), BF16),
                pltpu.VMEM((seq, seq), F32),
                pltpu.SemaphoreType.DMA,
            ],
        ),
        out_shape=[
            shape((3 * d_b, total, LANES), BF16),
            shape((total, D), F32),
            shape((total, D), BF16),
            shape((2, D), F32),
        ],
        compiler_params=params(),
        cost_estimate=pl.CostEstimate(flops=32 * total * D * D, bytes_accessed=40 * total * D, transcendentals=0),
        name="attend_back",
    )(homes, pair_lengths, offset, qkv, att, mixed_low, lse, grad_one, every)
    input_other = lax.ppermute(input_low, "tensor", swap)
    f_s = f_b // d_b
    part = lambda n: pl.BlockSpec((n, total, LANES), lambda j, *_: (j, 0, 0))
    blocks = 2 * f_s * d_b + 4 * d_b
    grads = pl.pallas_call(
        lambda pc, *refs: grad_kernel(*refs),
        grid_spec=pltpu.PrefetchScalarGridSpec(
            num_scalar_prefetch=1,
            grid=(d_b,),
            in_specs=[
                part(f_s), whole((d_b, total, LANES)), whole((d_b, total, LANES)), part(f_s),
                pl.BlockSpec((total, D), lambda j, pc: (pc[0], 0)),
                part(3), part(1), whole((d_b, total, LANES)),
            ],
            out_specs=pl.BlockSpec((blocks, LANES, LANES), lambda j, *_: (j, 0, 0)),
        ),
        out_shape=shape((d_b * blocks, LANES, LANES), BF16),
        compiler_params=params(),
        cost_estimate=pl.CostEstimate(flops=24 * total * D * D, bytes_accessed=40 * total * D, transcendentals=0),
        name="weight_grads",
    )(piece.astype(jnp.int32).reshape(1), active_low, down_low, normed_low, up_low, tokens, merged, att, attn_low)
    return layer_own, layer_other, input_own, input_other, grads, row_grad, up_grad, split_grad


def bit_orders(n_dp, spd):
    dp_bits = list(range(1, n_dp.bit_length() - 1))
    near, far = dp_bits[:1], dp_bits[1:]
    third = spd * 4 // 14
    first = (spd - third) // 2
    counts = (first, spd - third - first, third)
    orders = ([-1] + near + far, near + [-1] + far, far + [-1] + near)
    parts, at = [], 0
    for order, count in zip(orders, counts):
        if count:
            parts.append((order, at, count))
        at += count
    return parts


def bit_of(number, bit):
    return number // (1 << bit) % 2


def across(bit):
    if bit < 0:
        return {"tensor": 1 - lax.axis_index("tensor")}
    me = lax.axis_index("dp")
    return {"dp": me + (1 - 2 * bit_of(me, bit)) * (1 << bit)}


def place_of(order, code, core):
    dp, tensor = lax.axis_index("dp"), lax.axis_index("tensor")
    place = len(order) - 1
    to_dp, to_tensor = core, tensor
    for bit in order:
        flip = bit_of(code, place)
        if bit < 0:
            to_tensor = (tensor + flip) % 2
        else:
            to_dp = to_dp + (bit_of(dp, bit) + flip) % 2 * (1 << bit)
        place -= 1
    return to_tensor, to_dp


def slot_at(order, code, core, spd, at):
    to_tensor, to_dp = place_of(order, code, core)
    return to_tensor, to_dp * spd + at


def first_slot(order, code, core, n_dp, spd):
    to_tensor, to_dp = place_of(order, code, core)
    return (to_tensor * n_dp + to_dp) * spd


def greet(bits):
    barrier = pltpu.get_barrier_semaphore()
    for bit in bits:
        pl.semaphore_signal(barrier, inc=1, device_id=across(bit), device_id_type=pl.DeviceIdType.MESH)
    pl.semaphore_wait(barrier, len(bits))


def remote(source, target, send, recv, bit):
    return pltpu.make_async_remote_copy(
        src_ref=source, dst_ref=target, send_sem=send, recv_sem=recv,
        device_id=across(bit), device_id_type=pl.DeviceIdType.MESH,
    )


def gather_kernel(n_dp, spd, master_ref, vec_ref, all_ref, qb_ref, vb_ref, bu_ref, own_ref, both_ref, local_sem, send_sem, recv_sem, core_send, core_recv, vec_send, vec_recv):
    parts = bit_orders(n_dp, spd)
    n_bits = len(parts[0][0])
    core = bit_of(lax.axis_index("dp"), 0)
    tensor = lax.axis_index("tensor")
    greet([0] + parts[0][0])
    own_ref[...] = master_ref[0].astype(BF16)
    mine = first_slot(parts[0][0], 0, core, n_dp, spd)
    keep = pltpu.make_async_copy(own_ref, all_ref.at[pl.ds(mine, spd)], local_sem.at[0])
    keep.start()
    keep_vec = pltpu.make_async_copy(vec_ref, both_ref.at[pl.ds(tensor, 1)], local_sem.at[1])
    keep_vec.start()
    vec = remote(vec_ref, both_ref.at[pl.ds(tensor, 1)], vec_send, vec_recv, -1)
    vec.start()

    def piece(part, code, core_of):
        order, at, count = part
        return all_ref.at[pl.ds(first_slot(order, code, core_of, n_dp, spd) + at, count)]

    def forward(p, code, level, source):
        order = parts[p][0]
        for stage in range(level, n_bits):
            remote(
                source, piece(parts[p], code, core), send_sem.at[p, stage, code],
                recv_sem.at[p, code + (1 << stage)], order[n_bits - 1 - stage],
            ).start()
        remote(source, piece(parts[p], code, core), core_send.at[p, code], core_recv.at[p, code], 0).start()

    for p, part in enumerate(parts):
        forward(p, 0, 0, own_ref.at[pl.ds(part[1], part[2])])
    for level in range(n_bits):
        def arrive(j, carry):
            code = (1 << level) + j
            for p, part in enumerate(parts):
                here = piece(part, code, core)
                pltpu.make_async_copy(here, here, recv_sem.at[p, code]).wait()
                forward(p, code, level + 1, here)
            return carry

        lax.fori_loop(0, 1 << level, arrive, 0)

    def drain(code, carry):
        for p, part in enumerate(parts):
            here = piece(part, code, core)
            there = piece(part, code, 1 - core)
            pltpu.make_async_copy(here, here, core_send.at[p, code]).wait()
            pltpu.make_async_copy(there, there, core_recv.at[p, code]).wait()
        return carry

    keep_vec.wait()
    vec.wait()
    pieces = both_ref.shape[0]
    head_w, ffn_w = D // pieces, FF // pieces
    for i in range(pieces):
        row = both_ref[i : i + 1]
        qb_ref[:, i * head_w : (i + 1) * head_w] = row[:, :head_w]
        vb_ref[:, i * head_w : (i + 1) * head_w] = row[:, head_w : 2 * head_w]
        bu_ref[:, i * ffn_w : (i + 1) * ffn_w] = row[:, 2 * head_w :]
    for stage in range(n_bits):
        def sent(code, carry):
            for p, part in enumerate(parts):
                here = piece(part, code, core)
                pltpu.make_async_copy(here, here, send_sem.at[p, stage, code]).wait()
            return carry

        lax.fori_loop(0, 1 << stage, sent, 0)
    lax.fori_loop(0, 1 << n_bits, drain, 0)
    keep.wait()


def gather_all(masters, vec, n_dp, pieces):
    spd, edge = masters.shape[1], masters.shape[-1]
    parts = bit_orders(n_dp, spd)
    n, n_bits = len(parts), len(parts[0][0])
    dma = pltpu.SemaphoreType.DMA
    vmem = pl.BlockSpec(memory_space=pltpu.VMEM)
    shape = jax.ShapeDtypeStruct
    return pl.pallas_call(
        functools.partial(gather_kernel, n_dp, spd),
        in_specs=[vmem] * 2,
        out_specs=[anywhere()] + [vmem] * 3,
        out_shape=[
            shape((pieces * n_dp * spd, edge, edge), BF16),
            shape((1, D), F32), shape((1, D), F32), shape((1, FF), F32),
        ],
        scratch_shapes=[
            pltpu.VMEM((spd, edge, edge), BF16),
            pltpu.VMEM((pieces, vec.shape[1]), F32),
            dma((2,)), dma((n, n_bits, 1 << n_bits)), dma((n, 1 << n_bits)),
            dma((n, 1 << n_bits)), dma((n, 1 << n_bits)), dma, dma,
        ],
        compiler_params=pltpu.CompilerParams(
            vmem_limit_bytes=VMEM_LIMIT, collective_id=0, has_side_effects=True
        ),
        name="gather",
    )(masters, vec)


def scatter_kernel(
    n_dp, spd, scale, places, g_ref, rg_ref, sg_ref, bg_ref, out_ref, vec_out,
    give_ref, sum_ref, in_ref, vec_sum, vec_in,
    core_send, core_recv, send_sem, recv_sem, vec_send, vec_recv,
):
    parts = bit_orders(n_dp, spd)
    n_bits = len(parts[0][0])
    codes = 1 << n_bits
    core = bit_of(lax.axis_index("dp"), 0)
    vec_bits = [0] + parts[0][0]
    greet(vec_bits)

    def term(slot):
        place = places[slot[0], slot[1]]
        return jnp.where(place >= 0, g_ref[jnp.maximum(place, 0)], jnp.zeros(g_ref.shape[1:], BF16))

    def vec_copy(stage):
        return remote(vec_sum.at[stage], vec_in.at[stage], vec_send.at[stage], vec_recv.at[stage], vec_bits[stage])

    def vec_step(stage):
        vec_copy(stage).wait_recv()
        total = vec_sum[stage] + vec_in[stage]
        if stage + 1 < len(vec_bits):
            vec_sum[stage + 1] = total
            vec_copy(stage + 1).start()
        else:
            vec_out[...] = total * scale

    vec_sum[0, 0:6] = rg_ref[...]
    vec_sum[0, 6:8] = sg_ref[...]
    for i in range(FF // D):
        vec_sum[0, 8 + i : 9 + i] = bg_ref[:, i * D : (i + 1) * D]
    vec_sum[0, 8 + FF // D :] = jnp.zeros((VEC_ROWS - 8 - FF // D, D), F32)
    vec_copy(0).start()

    def give(p, code):
        order, at, count = parts[p]
        where = pl.ds(at, count)
        return remote(
            give_ref.at[code, where], sum_ref.at[code, where], core_send.at[p, code], core_recv.at[p, code], 0
        )

    def passed(p, level, code):
        order, at, count = parts[p]
        where = pl.ds(at, count)
        return remote(
            sum_ref.at[code, where], in_ref.at[code - 1, where],
            send_sem.at[p, code], recv_sem.at[p, code - 1], order[n_bits - 1 - level],
        )

    def hand(code):
        for p, (order, at, count) in enumerate(parts):
            start = slot_at(order, code, 1 - core, spd, at)
            for s in range(count):
                give_ref[code, at + s] = term((start[0], start[1] + s))
            give(p, code).start()

    ahead = min(4, codes)
    def first_hands(j, carry):
        hand(codes - 1 - j)
        return carry

    lax.fori_loop(0, ahead, first_hands, 0)

    def total_of(p, code, level, finish):
        order, at, count = parts[p]
        start = slot_at(order, code, core, spd, at)
        give(p, code).wait_recv()
        sources = []
        for stage in range(level + 1, n_bits):
            entry = (1 << stage) - 1 + code
            here = in_ref.at[entry, pl.ds(at, count)]
            pltpu.make_async_copy(here, here, recv_sem.at[p, entry]).wait()
            sources.append(entry)
        for s in range(count):
            value = term((start[0], start[1] + s)).astype(F32) + sum_ref[code, at + s].astype(F32)
            for entry in sources:
                value = value + in_ref[entry, at + s].astype(F32)
            if finish:
                out_ref[at + s] = value * scale
            else:
                sum_ref[code, at + s] = value.astype(BF16)

    for level in reversed(range(n_bits)):
        def onward(j, carry):
            code = (2 << level) - 1 - j
            if (1 << level) >= ahead:
                hand(code - ahead)
            for p in range(len(parts)):
                total_of(p, code, level, False)
                passed(p, level, code).start()
            return carry

        lax.fori_loop(0, 1 << level, onward, 0)
        vec_step(n_bits - 1 - level)
    for p in range(len(parts)):
        total_of(p, 0, -1, True)
    vec_step(n_bits)
    for stage in range(len(vec_bits)):
        vec_copy(stage).wait_send()

    def drain(code, carry):
        for p in range(len(parts)):
            give(p, code).wait_send()
        return carry

    lax.fori_loop(0, codes, drain, 0)
    for level in range(n_bits):
        def drain_level(j, carry):
            for p in range(len(parts)):
                passed(p, level, (1 << level) + j).wait_send()
            return carry

        lax.fori_loop(0, 1 << level, drain_level, 0)


def scatter_all(places, grads, row_grad, qv_grad, up_grad, n_dp, scale):
    edge = grads.shape[-1]
    spd = places.shape[1] // n_dp
    parts = bit_orders(n_dp, spd)
    n, n_bits = len(parts), len(parts[0][0])
    codes = 1 << n_bits
    dma = pltpu.SemaphoreType.DMA
    vmem = pl.BlockSpec(memory_space=pltpu.VMEM)
    return pl.pallas_call(
        functools.partial(scatter_kernel, n_dp, spd, scale),
        in_specs=[smem()] + [vmem] * 4,
        out_specs=[vmem, vmem],
        out_shape=[
            jax.ShapeDtypeStruct((spd, edge, edge), F32),
            jax.ShapeDtypeStruct((VEC_ROWS, D), F32),
        ],
        scratch_shapes=[
            pltpu.VMEM((codes, spd, edge, edge), BF16),
            pltpu.VMEM((codes, spd, edge, edge), BF16),
            pltpu.VMEM((codes - 1, spd, edge, edge), BF16),
            pltpu.VMEM((n_bits + 1, VEC_ROWS, D), F32),
            pltpu.VMEM((n_bits + 1, VEC_ROWS, D), F32),
            dma((n, codes)), dma((n, codes)), dma((n, codes)), dma((n, codes)),
            dma((n_bits + 1,)), dma((n_bits + 1,)),
        ],
        compiler_params=pltpu.CompilerParams(
            vmem_limit_bytes=VMEM_LIMIT, collective_id=1, has_side_effects=True
        ),
        name="scatter",
    )(places, grads, row_grad, qv_grad, up_grad)


def adam(grad, first, second, current, outs):
    first = MOMENT_DECAY * first + (1.0 - MOMENT_DECAY) * grad
    second = MOMENT_DECAY * second + (1.0 - MOMENT_DECAY) * grad * grad
    grad_out, new_out, first_out, second_out = outs
    grad_out[...] = grad
    new_out[...] = current - VECTOR_RATE * first / (jnp.sqrt(second) + EPS_ADAM)
    first_out[...] = first
    second_out[...] = second


def update_kernel(
    piece, grad_ref, master_ref, first_ref, second_ref, left_ref, right_ref,
    layer_own, layer_other, input_own, input_other, vec_ref, split_ref, sf_ref, ss_ref, row_ref, rf_ref, rs_ref,
    wg_ref, new_ref, nf_ref, ns_ref, low_ref, layer_ref, input_ref, *vec_outs,
):
    step = pl.program_id(0)
    for s in range(grad_ref.shape[0]):
        left, right = left_ref[0, s].astype(BF16), right_ref[0, s].astype(BF16)
        grad = grad_ref[s]
        turned = dot_nn(dot_tn(left, grad.astype(BF16)).astype(BF16), right)
        first = MOMENT_DECAY * first_ref[0, s] + (1.0 - MOMENT_DECAY) * turned
        second = MOMENT_DECAY * second_ref[0, s] + (1.0 - MOMENT_DECAY) * turned * turned
        stepped = first / (jnp.sqrt(second) + EPS_ADAM)
        back = dot_nt(dot_nn(left, stepped.astype(BF16)).astype(BF16), right)
        new = master_ref[0, s] - LEARN_RATE * back
        wg_ref[0, s] = grad
        new_ref[0, s] = new
        nf_ref[0, s] = first
        ns_ref[0, s] = second
        low_ref[0, s] = new.astype(BF16)

    @pl.when(step == 0)
    def _():
        layer_ref[...] = layer_own[...]
        input_ref[...] = input_own[...]
        pieces = (2 * D + FF) // split_ref.shape[1]
        head_w, ffn_w = D // pieces, FF // pieces
        wide = jnp.concatenate([vec_ref[8 + i : 9 + i] for i in range(FF // D)], axis=1)
        grad = jnp.zeros(split_ref.shape, F32)
        for i in range(pieces):
            mine = jnp.concatenate(
                [
                    vec_ref[6:7, i * head_w : (i + 1) * head_w],
                    vec_ref[7:8, i * head_w : (i + 1) * head_w],
                    wide[:, i * ffn_w : (i + 1) * ffn_w],
                ],
                axis=1,
            )
            grad = jnp.where(piece[0] == i, mine, grad)
        adam(grad, sf_ref[...], ss_ref[...], split_ref[...], vec_outs[:4])
        adam(vec_ref[0:6], rf_ref[...], rs_ref[...], row_ref[...], vec_outs[4:])

    @pl.when(step == 1)
    def _():
        layer_ref[...] = layer_other[...]
        input_ref[...] = input_other[...].astype(F32)


def update_all(piece, owned, blocks, halves, summed, vectors):
    masters = blocks[0]
    spd, edge = masters.shape[1], masters.shape[-1]
    group = spd // 2
    whole = lambda a: pl.BlockSpec(a.shape, lambda i, p: tuple(0 for _ in a.shape))
    spec = pl.BlockSpec((1, group, edge, edge), lambda i, p: (0, i, 0, 0))
    half = pl.BlockSpec(halves[0].shape, lambda i, p: ((p[0] + i) % 2, 0))
    shape = jax.ShapeDtypeStruct
    vec_shapes = [shape(vectors[0].shape, F32)] * 4 + [shape(vectors[3].shape, F32)] * 4
    total = 2 * halves[0].shape[0]
    return pl.pallas_call(
        update_kernel,
        grid_spec=pltpu.PrefetchScalarGridSpec(
            num_scalar_prefetch=1,
            grid=(2,),
            in_specs=[pl.BlockSpec((group, edge, edge), lambda i, p: (i, 0, 0))]
            + [spec] * 5
            + [whole(a) for a in (*halves, summed, *vectors)],
            out_specs=[spec] * 5 + [half, half] + [whole(a) for a in vec_shapes],
        ),
        out_shape=[shape(masters.shape, F32)] * 4
        + [shape(masters.shape, BF16), shape((total, D), BF16), shape((total, D), F32)]
        + vec_shapes,
        compiler_params=params(),
        name="update",
    )(piece, owned, *blocks, *halves, summed, *vectors)


def body(
    tokens,
    cotangent,
    pair_lengths,
    block_of_slot,
    masters,
    mom_first,
    mom_second,
    left_bases,
    right_bases,
    split_vec,
    split_first,
    split_second,
    row_vec,
    row_first,
    row_second,
):
    pieces = lax.axis_size("tensor")
    piece = lax.axis_index("tensor")
    n_dp = lax.axis_size("dp")
    slots = block_of_slot.shape[0]
    full_seq = tokens.shape[0] // pair_lengths.shape[0]
    row_count = pair_lengths.shape[0] // pieces
    order = np.array(sum(block_home(pieces), []), np.int32)
    slot_numbers = jnp.arange(slots, dtype=jnp.int32)[:, None] + order[None, :, 0] * slots
    homes = jnp.sum(jnp.where(block_of_slot[:, None] == order[None, :, 1], slot_numbers, 0), axis=0)
    grads_at = np.array(grad_order(pieces), np.int32)
    number = np.array([np.where(grads_at[:, 0] == i, grads_at[:, 1], -1) for i in range(pieces)])
    index = jnp.arange(1, len(grads_at) + 1, dtype=jnp.int32)[None, :, None]
    places = jnp.sum(jnp.where(number[:, :, None] == block_of_slot[None, None, :], index, 0), axis=1) - 1
    every, query_bias, value_bias, up_bias = gather_all(masters, split_vec, n_dp, pieces)
    layer_own, layer_other, input_own, input_other, grads, row_local, up_grad, qv_grad = layer_passes(
        tokens, cotangent, pair_lengths, piece, homes, every, query_bias, value_bias, up_bias, row_vec, row_count, full_seq
    )
    mean_scale = 1.0 / (tokens.shape[0] * n_dp)
    owned, summed = scatter_all(places, grads, row_local, qv_grad, up_grad, n_dp, mean_scale)
    outs = update_all(
        piece.astype(jnp.int32).reshape(1),
        owned,
        (masters, mom_first, mom_second, left_bases, right_bases),
        (layer_own, layer_other, input_own, input_other),
        summed,
        (split_vec, split_first, split_second, row_vec, row_first, row_second),
    )
    return (outs[5], outs[6], *outs[:5], *outs[7:])


def solution(mesh):
    in_specs = (
        P("dp", None),
        P("dp", None),
        P("dp", None),
        P(),
        P("tensor", "dp", None, None),
        P("tensor", "dp", None, None),
        P("tensor", "dp", None, None),
        P("tensor", "dp", None, None),
        P("tensor", "dp", None, None),
        P("tensor", None),
        P("tensor", None),
        P("tensor", None),
        P(),
        P(),
        P(),
    )
    out_specs = (
        P("dp", None),
        P("dp", None),
        P("tensor", "dp", None, None),
        P("tensor", "dp", None, None),
        P("tensor", "dp", None, None),
        P("tensor", "dp", None, None),
        P("tensor", "dp", None, None),
        P("tensor", None),
        P("tensor", None),
        P("tensor", None),
        P("tensor", None),
        P(),
        P(),
        P(),
        P(),
    )
    return jax.shard_map(body, mesh=mesh, in_specs=in_specs, out_specs=out_specs, check_vma=False)
```

```python
import functools

import jax
import jax.numpy as jnp
from jax import lax
from jax.experimental import pallas as pl
from jax.experimental.pallas import tpu as pltpu
from jax.sharding import PartitionSpec as P
import numpy as np

D = 768
HEADS = 12
HEAD = 64
FF = 3072


EPS_NORM = 1e-05
EPS_ADAM = 1e-08
LEARN_RATE = 0.01
VECTOR_RATE = 0.15
MOMENT_DECAY = 0.5
MASKED_SCORE = -1e30
HIGHEST_PRECISION = lax.Precision.HIGHEST


def block_counts(block_edge, head_width, ffn_width):
    return (
        D // block_edge * (3 * head_width // block_edge),
        head_width // block_edge * (D // block_edge),
        D // block_edge * (ffn_width // block_edge),
        ffn_width // block_edge * (D // block_edge),
    )


LOG2E = 1.4426950408889634
LN_TWO = 0.6931471805599453
ROOT_HALF = 0.7071067811865476
PHI_SCALE = 0.3989422804014327
ERF_P = 0.3275911
ERF_A = (0.254829592, -0.284496736, 1.421413741, -1.453152027, 1.061405429)
VMEM_LIMIT = 60 * 1024 * 1024
LANES = 128
VEC_ROWS = 16
BF16 = jnp.bfloat16
F32 = jnp.float32


def dot_nn(left, right):
    return lax.dot_general(left, right, (((1,), (0,)), ((), ())), preferred_element_type=F32)


def dot_nt(left, right):
    return lax.dot_general(left, right, (((1,), (1,)), ((), ())), preferred_element_type=F32)


def dot_tn(left, right):
    return lax.dot_general(left, right, (((0,), (0,)), ((), ())), preferred_element_type=F32)


def block_home(pieces):
    d_b, f_b = D // LANES, FF // LANES
    d_p, f_p = d_b // pieces, f_b // pieces
    first = d_b * 3 * d_p
    second = first + d_p * d_b
    third = second + d_b * f_p
    qkv = [
        (n % d_b // d_p, k * 3 * d_p + n // d_b * d_p + n % d_p)
        for k in range(d_b)
        for n in range(3 * d_b)
    ]
    out = [(k // d_p, first + k % d_p * d_b + n) for k in range(d_b) for n in range(d_b)]
    up = [(n // f_p, second + k * f_p + n % f_p) for k in range(d_b) for n in range(f_b)]
    down = [(k // f_p, third + k % f_p * d_b + n) for k in range(f_b) for n in range(d_b)]
    return qkv, out, up, down


def grad_order(pieces):
    d_b, f_b = D // LANES, FF // LANES
    qkv, out, up, down = block_home(pieces)
    f_s, q_s = f_b // d_b, 3
    order = []
    for j in range(d_b):
        order += [down[(j * f_s + k) * d_b + n] for k in range(f_s) for n in range(d_b)]
        order += [up[k * f_b + j * f_s + n] for k in range(d_b) for n in range(f_s)]
        order += [qkv[k * 3 * d_b + j * q_s + n] for k in range(d_b) for n in range(q_s)]
        order += [out[j * d_b + n] for n in range(d_b)]
    return order


def start_blocks(homes, base, rows, cols, source, target, sem):
    def step(index, carry):
        k, n = index // cols, index % cols
        pltpu.make_async_copy(
            source.at[homes[base + index]],
            target.at[pl.ds(pl.multiple_of(k * LANES, LANES), LANES), pl.ds(pl.multiple_of(n * LANES, LANES), LANES)],
            sem,
        ).start()
        return carry

    lax.fori_loop(0, rows * cols, step, 0, unroll=6)


def wait_blocks(target, sem):
    pltpu.make_async_copy(target, target, sem).wait()


def mask_bias(ends_ref, row, seq, bias_ref):
    col = lax.broadcasted_iota(jnp.int32, (seq, 1), 0)
    lane = lax.broadcasted_iota(jnp.int32, (1, seq), 1)
    seg_col = jnp.zeros((seq, 1), jnp.int32)
    seg_lane = jnp.zeros((1, seq), jnp.int32)
    end = 0
    for k in range(ends_ref.shape[1] - 1):
        end = end + ends_ref[row, k]
        seg_col = seg_col + (col >= end).astype(jnp.int32)
        seg_lane = seg_lane + (lane >= end).astype(jnp.int32)
    bias_ref[...] = jnp.where(seg_col == seg_lane, 0.0, MASKED_SCORE)


def attend_kernel(homes, pairs, offset, x_ref, every, qb_ref, vb_ref, qkv_ref, att_ref, lse_ref, w_ref, bias_ref, sem):
    d_b = D // LANES
    row = pl.program_id(0)
    seq = x_ref.shape[0]

    @pl.when(row == 0)
    def _():
        start_blocks(homes, 0, d_b, 3 * d_b, every, w_ref, sem)

    mask_bias(pairs, offset[0] + row, seq, bias_ref)

    @pl.when(row == 0)
    def _():
        wait_blocks(w_ref, sem)

    x = x_ref[...]
    wide = 2 * LANES
    for part in range(3):
        for c in range(0, D, wide):
            y = dot_nn(x, w_ref[:, part * D + c : part * D + c + wide])
            if part == 0:
                y = (y + qb_ref[:, c : c + wide]).astype(BF16).astype(F32) * HEAD ** (-0.5)
            if part == 2:
                y = y + vb_ref[:, c : c + wide]
            y = y.astype(BF16)
            for n in range(2):
                qkv_ref[part * d_b + c // LANES + n] = y[:, n * LANES : (n + 1) * LANES]
    lane = lax.broadcasted_iota(jnp.int32, (1, LANES), 1)

    def pair(n, carry):
        q = qkv_ref[n]
        k = qkv_ref[d_b + n]
        v_t = qkv_ref[2 * d_b + n].T
        halves = []
        for h in range(2):
            keep = (lane < HEAD) if h == 0 else (lane >= HEAD)
            scores = dot_nt(jnp.where(keep, k, jnp.zeros_like(k)), q) + bias_ref[...]
            top = jnp.max(scores, axis=0, keepdims=True)
            p = jnp.exp(scores - top)
            total = jnp.sum(p, axis=0, keepdims=True)
            lse_ref[0, 2 * n + h] = (top + jnp.log(total)).reshape(1, seq)
            mixed = dot_nn(v_t[h * HEAD : (h + 1) * HEAD], p.astype(BF16))
            halves.append(mixed * (1.0 / total))
        att_ref[n] = jnp.concatenate(halves, axis=0).T.astype(BF16)
        return carry

    lax.fori_loop(0, d_b, pair, 0)


def norm_parts(hidden):
    mean = jnp.mean(hidden, axis=-1, keepdims=True)
    centred = hidden - mean
    var = jnp.mean(centred * centred, axis=-1, keepdims=True)
    inv = lax.rsqrt(var + EPS_NORM)
    return centred * inv, inv


def norm_back(grad, gain, normed, inv):
    scaled = grad * gain
    mean = jnp.mean(scaled, axis=-1, keepdims=True)
    along = jnp.mean(scaled * normed, axis=-1, keepdims=True)
    return inv * (scaled - mean - normed * along)


def put_blocks(ref, value):
    for n in range(ref.shape[0]):
        ref[n] = value[:, n * LANES : (n + 1) * LANES]


def get_blocks(ref):
    return jnp.concatenate([ref[n] for n in range(ref.shape[0])], axis=1)


def gelu_parts(u):
    e = jnp.exp(u * u * -0.5)
    t = 1.0 / (1.0 + (ERF_P * ROOT_HALF) * jnp.abs(u))
    a1, a2, a3, a4, a5 = (0.5 * a for a in ERF_A)
    tail = ((((a5 * t + a4) * t + a3) * t + a2) * t + a1) * t * e
    cdf = jnp.where(u >= 0, 1.0 - tail, tail)
    return u * cdf, cdf + u * e * PHI_SCALE


def token_kernel(
    homes, att_ref, x_ref, cot_ref, every, bu_ref, rv_ref,
    out_ref, nl_ref, act_ref, dl_ref, up_ref, al_ref, ml_ref, g1_ref, rg_ref, bg_ref,
    wo_ref, wu_ref, wd_ref, dg_ref, sem,
):
    d_b, f_b = D // LANES, FF // LANES
    step = pl.program_id(0)

    @pl.when(step == 0)
    def _():
        start_blocks(homes, 3 * d_b * d_b, d_b, d_b, every, wo_ref, sem.at[0])
        start_blocks(homes, 4 * d_b * d_b, d_b, f_b, every, wu_ref, sem.at[1])
        start_blocks(homes, 4 * d_b * d_b + d_b * f_b, f_b, d_b, every, wd_ref, sem.at[2])
        rg_ref[...] = jnp.zeros_like(rg_ref)
        bg_ref[...] = jnp.zeros_like(bg_ref)
        wait_blocks(wo_ref, sem.at[0])
        wait_blocks(wu_ref, sem.at[1])
        wait_blocks(wd_ref, sem.at[2])

    out_bias, gain_one, shift_one, down_bias, gain_two, shift_two = (
        rv_ref[i : i + 1] for i in range(6)
    )
    hidden = dot_nn(get_blocks(att_ref), wo_ref[...]) + x_ref[...].astype(F32) + out_bias
    n_one, inv_one = norm_parts(hidden)
    normed = n_one * gain_one + shift_one
    normed_low = normed.astype(BF16)
    put_blocks(nl_ref, normed_low)
    wide = 512
    total = normed + down_bias
    for c in range(0, FF, wide):
        u = dot_nn(normed_low, wu_ref[:, c : c + wide]) + bu_ref[:, c : c + wide]
        active, slope = gelu_parts(u)
        active = active.astype(BF16)
        dg_ref[:, c : c + wide] = slope.astype(BF16)
        for n in range(wide // LANES):
            act_ref[c // LANES + n] = active[:, n * LANES : (n + 1) * LANES]
        total = total + dot_nn(active, wd_ref[c : c + wide, :])
    n_two, inv_two = norm_parts(total)
    out_ref[...] = (n_two * gain_two + shift_two).astype(BF16)
    dy = cot_ref[...].astype(F32)
    grad_two = norm_back(dy, gain_two, n_two, inv_two)
    down_low = grad_two.astype(BF16)
    put_blocks(dl_ref, down_low)
    rg_ref[3:4] += jnp.sum(grad_two, axis=0, keepdims=True)
    rg_ref[4:5] += jnp.sum(dy * n_two, axis=0, keepdims=True)
    rg_ref[5:6] += jnp.sum(dy, axis=0, keepdims=True)
    grad_normed = grad_two
    for c in range(0, FF, wide):
        ga = dot_nt(down_low, wd_ref[c : c + wide, :]) * dg_ref[:, c : c + wide].astype(F32)
        up = ga.astype(BF16)
        for n in range(wide // LANES):
            up_ref[c // LANES + n] = up[:, n * LANES : (n + 1) * LANES]
        bg_ref[:, c : c + wide] += jnp.sum(up.astype(F32), axis=0, keepdims=True)
        grad_normed = grad_normed + dot_nt(up, wu_ref[:, c : c + wide])
    rg_ref[1:2] += jnp.sum(grad_normed * n_one, axis=0, keepdims=True)
    rg_ref[2:3] += jnp.sum(grad_normed, axis=0, keepdims=True)
    grad_one = norm_back(grad_normed, gain_one, n_one, inv_one)
    rg_ref[0:1] += jnp.sum(grad_one, axis=0, keepdims=True)
    g1_ref[...] = grad_one
    attn_low = grad_one.astype(BF16)
    put_blocks(al_ref, attn_low)
    put_blocks(ml_ref, dot_nt(attn_low, wo_ref[...]).astype(BF16))


def attend_back_kernel(
    homes, pairs, offset, qkv_ref, att_ref, ml_ref, lse_ref, g1_ref, every,
    merged_ref, ig_ref, il_ref, sg_ref, w_ref, bias_ref, sem,
):
    d_b = D // LANES
    row = pl.program_id(0)
    seq = g1_ref.shape[0]

    @pl.when(row == 0)
    def _():
        start_blocks(homes, 0, d_b, 3 * d_b, every, w_ref, sem)
        sg_ref[...] = jnp.zeros_like(sg_ref)

    mask_bias(pairs, offset[0] + row, seq, bias_ref)
    lane = lax.broadcasted_iota(jnp.int32, (1, LANES), 1)

    def pair(n, carry):
        q = qkv_ref[n]
        k = qkv_ref[d_b + n]
        v = qkv_ref[2 * d_b + n]
        g = ml_ref[n]
        k_t = k.T
        both = g.T.astype(F32) * att_ref[n].T.astype(F32)
        zero = jnp.zeros_like(k)
        parts = []
        for h in range(2):
            keep = (lane < HEAD) if h == 0 else (lane >= HEAD)
            spread = jnp.sum(both[h * HEAD : (h + 1) * HEAD], axis=0, keepdims=True)
            scores = dot_nt(jnp.where(keep, k, zero), q) + bias_ref[...]
            p = jnp.exp(scores - lse_ref[0, 2 * n + h].reshape(1, seq))
            gp = dot_nt(jnp.where(keep, v, zero), g)
            low = (p * (gp - spread)).astype(BF16)
            gv = dot_nn(p.astype(BF16), g)
            gk = dot_nn(low, q)
            gq = dot_nn(k_t[h * HEAD : (h + 1) * HEAD], low)
            parts.append((gq, gk, gv))
        gq = (jnp.concatenate([parts[0][0], parts[1][0]], axis=0) * HEAD ** (-0.5)).T
        merged_ref[n] = gq.astype(BF16)
        merged_ref[d_b + n] = jnp.where(lane < HEAD, parts[0][1], parts[1][1]).astype(BF16)
        merged_ref[2 * d_b + n] = jnp.where(lane < HEAD, parts[0][2], parts[1][2]).astype(BF16)
        return carry

    lax.fori_loop(0, d_b, pair, 0)

    @pl.when(row == 0)
    def _():
        wait_blocks(w_ref, sem)

    for n in range(d_b):
        at = slice(n * LANES, (n + 1) * LANES)
        sg_ref[0:1, at] += jnp.sum(merged_ref[n].astype(F32), axis=0, keepdims=True)
        sg_ref[1:2, at] += jnp.sum(merged_ref[2 * d_b + n].astype(F32), axis=0, keepdims=True)
    merged = get_blocks(merged_ref)
    total = g1_ref[...] + dot_nt(merged, w_ref[...])
    ig_ref[...] = total
    il_ref[...] = total.astype(BF16)


def grad_kernel(act_ref, dl_ref, nl_ref, up_ref, x_ref, merged_ref, att_ref, al_ref, g_ref):
    d_b = D // LANES
    f_s = act_ref.shape[0]
    at = 0

    def store(value, at):
        value = value.astype(BF16)
        for k in range(value.shape[0] // LANES):
            for n in range(value.shape[1] // LANES):
                g_ref[at] = value[k * LANES : (k + 1) * LANES, n * LANES : (n + 1) * LANES]
                at += 1
        return at

    at = store(dot_tn(get_blocks(act_ref), get_blocks(dl_ref)), at)
    at = store(dot_tn(get_blocks(nl_ref), get_blocks(up_ref)), at)
    at = store(dot_tn(x_ref[...], get_blocks(merged_ref)), at)
    at = store(dot_tn(att_ref[0], get_blocks(al_ref)), at)


def smem():
    return pl.BlockSpec(memory_space=pltpu.SMEM)


def anywhere():
    return pl.BlockSpec(memory_space=pl.ANY)


def params():
    return pltpu.CompilerParams(vmem_limit_bytes=VMEM_LIMIT, dimension_semantics=("arbitrary",))


def layer_passes(tokens, cotangent, pair_lengths, piece, homes, every, query_bias, value_bias, up_bias, row_vec, row_count, seq):
    d_b, f_b = D // LANES, FF // LANES
    total = row_count * seq
    shape = jax.ShapeDtypeStruct
    offset = (piece * row_count).astype(jnp.int32).reshape(1)
    stack = lambda n: pl.BlockSpec((n, seq, LANES), lambda r, *_: (0, r, 0))
    rows = pl.BlockSpec((seq, D), lambda r, *_: (r, 0))
    own = lambda at: pl.BlockSpec((seq, D), lambda r, *pre: (pre[at][0] + r, 0))
    whole = lambda s: pl.BlockSpec(s, lambda *_: tuple(0 for _ in s))
    lse_spec = pl.BlockSpec((1, HEADS, 1, seq), lambda r, *_: (r, 0, 0, 0))
    qkv, att, lse = pl.pallas_call(
        attend_kernel,
        grid_spec=pltpu.PrefetchScalarGridSpec(
            num_scalar_prefetch=3,
            grid=(row_count,),
            in_specs=[own(2), anywhere(), whole((1, D)), whole((1, D))],
            out_specs=[stack(3 * d_b), stack(d_b), lse_spec],
            scratch_shapes=[
                pltpu.VMEM((D, 3 * D), BF16),
                pltpu.VMEM((seq, seq), F32),
                pltpu.SemaphoreType.DMA,
            ],
        ),
        out_shape=[
            shape((3 * d_b, total, LANES), BF16),
            shape((d_b, total, LANES), BF16),
            shape((row_count, HEADS, 1, seq), F32),
        ],
        compiler_params=params(),
        cost_estimate=pl.CostEstimate(flops=24 * total * D * D, bytes_accessed=32 * total * D, transcendentals=0),
        name="attend",
    )(homes, pair_lengths, offset, tokens, every, query_bias, value_bias)
    token_outs = pl.pallas_call(
        lambda homes, off, *refs: token_kernel(homes, *refs),
        grid_spec=pltpu.PrefetchScalarGridSpec(
            num_scalar_prefetch=2,
            grid=(row_count,),
            in_specs=[stack(d_b), own(1), own(1), anywhere(), whole((1, FF)), whole((6, D))],
            out_specs=[
                rows, stack(d_b), stack(f_b), stack(d_b), stack(f_b), stack(d_b), stack(d_b), rows,
                whole((6, D)), whole((1, FF)),
            ],
            scratch_shapes=[
                pltpu.VMEM((D, D), BF16),
                pltpu.VMEM((D, FF), BF16),
                pltpu.VMEM((FF, D), BF16),
                pltpu.VMEM((seq, FF), BF16),
                pltpu.SemaphoreType.DMA((3,)),
            ],
        ),
        out_shape=[
            shape((total, D), BF16),
            shape((d_b, total, LANES), BF16),
            shape((f_b, total, LANES), BF16),
            shape((d_b, total, LANES), BF16),
            shape((f_b, total, LANES), BF16),
            shape((d_b, total, LANES), BF16),
            shape((d_b, total, LANES), BF16),
            shape((total, D), F32),
            shape((6, D), F32),
            shape((1, FF), F32),
        ],
        compiler_params=params(),
        cost_estimate=pl.CostEstimate(flops=40 * total * D * D, bytes_accessed=64 * total * D, transcendentals=0),
        name="tokenwise",
    )(homes, offset, att, tokens, cotangent, every, up_bias, row_vec)
    layer_own, normed_low, active_low, down_low, up_low, attn_low, mixed_low, grad_one, row_grad, up_grad = token_outs
    swap = [(0, 1), (1, 0)]
    layer_other = lax.ppermute(layer_own, "tensor", swap)
    merged, input_own, input_low, split_grad = pl.pallas_call(
        attend_back_kernel,
        grid_spec=pltpu.PrefetchScalarGridSpec(
            num_scalar_prefetch=3,
            grid=(row_count,),
            in_specs=[stack(3 * d_b), stack(d_b), stack(d_b), lse_spec, rows, anywhere()],
            out_specs=[stack(3 * d_b), rows, rows, whole((2, D))],
            scratch_shapes=[
                pltpu.VMEM((D, 3 * D), BF16),
                pltpu.VMEM((seq, seq), F32),
                pltpu.SemaphoreType.DMA,
            ],
        ),
        out_shape=[
            shape((3 * d_b, total, LANES), BF16),
            shape((total, D), F32),
            shape((total, D), BF16),
            shape((2, D), F32),
        ],
        compiler_params=params(),
        cost_estimate=pl.CostEstimate(flops=32 * total * D * D, bytes_accessed=40 * total * D, transcendentals=0),
        name="attend_back",
    )(homes, pair_lengths, offset, qkv, att, mixed_low, lse, grad_one, every)
    input_other = lax.ppermute(input_low, "tensor", swap)
    f_s = f_b // d_b
    part = lambda n: pl.BlockSpec((n, total, LANES), lambda j, *_: (j, 0, 0))
    blocks = 2 * f_s * d_b + 4 * d_b
    grads = pl.pallas_call(
        lambda pc, wait, *refs: grad_kernel(*refs),
        grid_spec=pltpu.PrefetchScalarGridSpec(
            num_scalar_prefetch=1,
            grid=(d_b,),
            in_specs=[
                anywhere(), part(f_s), whole((d_b, total, LANES)), whole((d_b, total, LANES)), part(f_s),
                pl.BlockSpec((total, D), lambda j, pc: (pc[0], 0)),
                part(3), part(1), whole((d_b, total, LANES)),
            ],
            out_specs=pl.BlockSpec((blocks, LANES, LANES), lambda j, *_: (j, 0, 0)),
        ),
        out_shape=shape((d_b * blocks, LANES, LANES), BF16),
        compiler_params=params(),
        cost_estimate=pl.CostEstimate(flops=24 * total * D * D, bytes_accessed=40 * total * D, transcendentals=0),
        name="weight_grads",
    )(piece.astype(jnp.int32).reshape(1), layer_other, active_low, down_low, normed_low, up_low, tokens, merged, att, attn_low)
    return layer_own, layer_other, input_own, input_other, grads, row_grad, up_grad, split_grad


def split_slots(orders, counts):
    parts, at = [], 0
    for order, count in zip(orders, counts):
        if count:
            parts.append((order, at, count))
        at += count
    return parts


def index_bits(n_dp):
    dp_bits = list(range(1, n_dp.bit_length() - 1))
    return dp_bits[:1], dp_bits[1:]


def gather_orders(n_dp, spd):
    near, far = index_bits(n_dp)
    third = spd * 4 // 14
    first = (spd - third) // 2
    return split_slots(
        ([-1] + near + far, near + [-1] + far, far + [-1] + near), (first, spd - third - first, third)
    )


def scatter_orders(n_dp, spd):
    near, far = index_bits(n_dp)
    first, third = spd * 4 // 14, spd * 2 // 14
    return split_slots(
        ([-1] + far + near, near + [-1] + far, far + near + [-1]), (first, spd - third - first, third)
    )


def bit_of(number, bit):
    return number // (1 << bit) % 2


def across(bit):
    if bit < 0:
        return {"tensor": 1 - lax.axis_index("tensor")}
    me = lax.axis_index("dp")
    return {"dp": me + (1 - 2 * bit_of(me, bit)) * (1 << bit)}


def place_of(order, code, core):
    dp, tensor = lax.axis_index("dp"), lax.axis_index("tensor")
    place = len(order) - 1
    to_dp, to_tensor = core, tensor
    for bit in order:
        flip = bit_of(code, place)
        if bit < 0:
            to_tensor = (tensor + flip) % 2
        else:
            to_dp = to_dp + (bit_of(dp, bit) + flip) % 2 * (1 << bit)
        place -= 1
    return to_tensor, to_dp


def slot_at(order, code, core, spd, at):
    to_tensor, to_dp = place_of(order, code, core)
    return to_tensor, to_dp * spd + at


def first_slot(order, code, core, n_dp, spd):
    to_tensor, to_dp = place_of(order, code, core)
    return (to_tensor * n_dp + to_dp) * spd


def greet(bits):
    barrier = pltpu.get_barrier_semaphore()
    for bit in bits:
        pl.semaphore_signal(barrier, inc=1, device_id=across(bit), device_id_type=pl.DeviceIdType.MESH)
    pl.semaphore_wait(barrier, len(bits))


def remote(source, target, send, recv, bit):
    return pltpu.make_async_remote_copy(
        src_ref=source, dst_ref=target, send_sem=send, recv_sem=recv,
        device_id=across(bit), device_id_type=pl.DeviceIdType.MESH,
    )


def gather_kernel(n_dp, spd, master_ref, vec_ref, all_ref, qb_ref, vb_ref, bu_ref, own_ref, both_ref, local_sem, send_sem, recv_sem, core_send, core_recv, vec_send, vec_recv):
    parts = gather_orders(n_dp, spd)
    n_bits = len(parts[0][0])
    core = bit_of(lax.axis_index("dp"), 0)
    tensor = lax.axis_index("tensor")
    greet([0] + parts[0][0])
    own_ref[...] = master_ref[0].astype(BF16)
    mine = first_slot(parts[0][0], 0, core, n_dp, spd)
    keep = pltpu.make_async_copy(own_ref, all_ref.at[pl.ds(mine, spd)], local_sem.at[0])
    keep.start()
    keep_vec = pltpu.make_async_copy(vec_ref, both_ref.at[pl.ds(tensor, 1)], local_sem.at[1])
    keep_vec.start()
    vec = remote(vec_ref, both_ref.at[pl.ds(tensor, 1)], vec_send, vec_recv, -1)
    vec.start()

    def piece(part, code, core_of):
        order, at, count = part
        return all_ref.at[pl.ds(first_slot(order, code, core_of, n_dp, spd) + at, count)]

    def forward(p, code, level, source):
        order = parts[p][0]
        for stage in range(level, n_bits):
            remote(
                source, piece(parts[p], code, core), send_sem.at[p, stage, code],
                recv_sem.at[p, code + (1 << stage)], order[n_bits - 1 - stage],
            ).start()
        remote(source, piece(parts[p], code, core), core_send.at[p, code], core_recv.at[p, code], 0).start()

    for p, part in enumerate(parts):
        forward(p, 0, 0, own_ref.at[pl.ds(part[1], part[2])])
    for level in range(n_bits):
        def arrive(j, carry):
            code = (1 << level) + j
            for p, part in enumerate(parts):
                here = piece(part, code, core)
                pltpu.make_async_copy(here, here, recv_sem.at[p, code]).wait()
                forward(p, code, level + 1, here)
            return carry

        lax.fori_loop(0, 1 << level, arrive, 0)

    def drain(code, carry):
        for p, part in enumerate(parts):
            here = piece(part, code, core)
            there = piece(part, code, 1 - core)
            pltpu.make_async_copy(here, here, core_send.at[p, code]).wait()
            pltpu.make_async_copy(there, there, core_recv.at[p, code]).wait()
        return carry

    keep_vec.wait()
    vec.wait()
    pieces = both_ref.shape[0]
    head_w, ffn_w = D // pieces, FF // pieces
    for i in range(pieces):
        row = both_ref[i : i + 1]
        qb_ref[:, i * head_w : (i + 1) * head_w] = row[:, :head_w]
        vb_ref[:, i * head_w : (i + 1) * head_w] = row[:, head_w : 2 * head_w]
        bu_ref[:, i * ffn_w : (i + 1) * ffn_w] = row[:, 2 * head_w :]
    for stage in range(n_bits):
        def sent(code, carry):
            for p, part in enumerate(parts):
                here = piece(part, code, core)
                pltpu.make_async_copy(here, here, send_sem.at[p, stage, code]).wait()
            return carry

        lax.fori_loop(0, 1 << stage, sent, 0)
    lax.fori_loop(0, 1 << n_bits, drain, 0)
    keep.wait()


def gather_all(masters, vec, n_dp, pieces):
    spd, edge = masters.shape[1], masters.shape[-1]
    parts = gather_orders(n_dp, spd)
    n, n_bits = len(parts), len(parts[0][0])
    dma = pltpu.SemaphoreType.DMA
    vmem = pl.BlockSpec(memory_space=pltpu.VMEM)
    shape = jax.ShapeDtypeStruct
    return pl.pallas_call(
        functools.partial(gather_kernel, n_dp, spd),
        in_specs=[vmem] * 2,
        out_specs=[anywhere()] + [vmem] * 3,
        out_shape=[
            shape((pieces * n_dp * spd, edge, edge), BF16),
            shape((1, D), F32), shape((1, D), F32), shape((1, FF), F32),
        ],
        scratch_shapes=[
            pltpu.VMEM((spd, edge, edge), BF16),
            pltpu.VMEM((pieces, vec.shape[1]), F32),
            dma((2,)), dma((n, n_bits, 1 << n_bits)), dma((n, 1 << n_bits)),
            dma((n, 1 << n_bits)), dma((n, 1 << n_bits)), dma, dma,
        ],
        compiler_params=pltpu.CompilerParams(
            vmem_limit_bytes=VMEM_LIMIT, collective_id=0, has_side_effects=True
        ),
        name="gather",
    )(masters, vec)


def scatter_kernel(
    n_dp, spd, scale, places, g_ref, rg_ref, sg_ref, bg_ref, out_ref, vec_out,
    give_ref, sum_ref, in_ref, vec_sum, vec_in,
    core_send, core_recv, send_sem, recv_sem, vec_send, vec_recv,
):
    parts = scatter_orders(n_dp, spd)
    n_bits = len(parts[0][0])
    codes = 1 << n_bits
    core = bit_of(lax.axis_index("dp"), 0)
    vec_bits = [0] + parts[0][0]
    greet(vec_bits)

    def term(slot):
        place = places[slot[0], slot[1]]
        return jnp.where(place >= 0, g_ref[jnp.maximum(place, 0)], jnp.zeros(g_ref.shape[1:], BF16))

    def vec_copy(stage):
        return remote(vec_sum.at[stage], vec_in.at[stage], vec_send.at[stage], vec_recv.at[stage], vec_bits[stage])

    def vec_step(stage):
        vec_copy(stage).wait_recv()
        total = vec_sum[stage] + vec_in[stage]
        if stage + 1 < len(vec_bits):
            vec_sum[stage + 1] = total
            vec_copy(stage + 1).start()
        else:
            vec_out[...] = total * scale

    vec_sum[0, 0:6] = rg_ref[...]
    vec_sum[0, 6:8] = sg_ref[...]
    for i in range(FF // D):
        vec_sum[0, 8 + i : 9 + i] = bg_ref[:, i * D : (i + 1) * D]
    vec_sum[0, 8 + FF // D :] = jnp.zeros((VEC_ROWS - 8 - FF // D, D), F32)
    vec_copy(0).start()

    def give(p, code):
        order, at, count = parts[p]
        where = pl.ds(at, count)
        return remote(
            give_ref.at[code, where], sum_ref.at[code, where], core_send.at[p, code], core_recv.at[p, code], 0
        )

    def passed(p, level, code):
        order, at, count = parts[p]
        where = pl.ds(at, count)
        return remote(
            sum_ref.at[code, where], in_ref.at[code - 1, where],
            send_sem.at[p, code], recv_sem.at[p, code - 1], order[n_bits - 1 - level],
        )

    def hand(code):
        for p, (order, at, count) in enumerate(parts):
            start = slot_at(order, code, 1 - core, spd, at)
            for s in range(count):
                give_ref[code, at + s] = term((start[0], start[1] + s))
            give(p, code).start()

    ahead = min(4, codes)
    def first_hands(j, carry):
        hand(codes - 1 - j)
        return carry

    lax.fori_loop(0, ahead, first_hands, 0)
    vec_step(0)
    stage = 1

    def total_of(p, code, level, finish):
        order, at, count = parts[p]
        start = slot_at(order, code, core, spd, at)
        give(p, code).wait_recv()
        sources = []
        for stage in range(level + 1, n_bits):
            entry = (1 << stage) - 1 + code
            here = in_ref.at[entry, pl.ds(at, count)]
            pltpu.make_async_copy(here, here, recv_sem.at[p, entry]).wait()
            sources.append(entry)
        for s in range(count):
            value = term((start[0], start[1] + s)).astype(F32) + sum_ref[code, at + s].astype(F32)
            for entry in sources:
                value = value + in_ref[entry, at + s].astype(F32)
            if finish:
                out_ref[at + s] = value * scale
            else:
                sum_ref[code, at + s] = value.astype(BF16)

    for level in reversed(range(n_bits)):
        def onward(j, carry):
            code = (2 << level) - 1 - j
            if (1 << level) >= ahead:
                hand(code - ahead)
            for p in range(len(parts)):
                total_of(p, code, level, False)
                passed(p, level, code).start()
            return carry

        count = 1 << level
        if level == n_bits - 1 and count >= 4:
            lax.fori_loop(0, 1, onward, 0)
            vec_step(1)
            lax.fori_loop(1, 3, onward, 0)
            vec_step(2)
            lax.fori_loop(3, count, onward, 0)
            stage = 3
        else:
            lax.fori_loop(0, count, onward, 0)
        if stage < n_bits:
            vec_step(stage)
            stage += 1
    for p in range(len(parts)):
        total_of(p, 0, -1, True)
    for last in range(stage, n_bits + 1):
        vec_step(last)
    for stage in range(len(vec_bits)):
        vec_copy(stage).wait_send()

    def drain(code, carry):
        for p in range(len(parts)):
            give(p, code).wait_send()
        return carry

    lax.fori_loop(0, codes, drain, 0)
    for level in range(n_bits):
        def drain_level(j, carry):
            for p in range(len(parts)):
                passed(p, level, (1 << level) + j).wait_send()
            return carry

        lax.fori_loop(0, 1 << level, drain_level, 0)


def scatter_all(places, grads, row_grad, qv_grad, up_grad, n_dp, scale):
    edge = grads.shape[-1]
    spd = places.shape[1] // n_dp
    parts = scatter_orders(n_dp, spd)
    n, n_bits = len(parts), len(parts[0][0])
    codes = 1 << n_bits
    dma = pltpu.SemaphoreType.DMA
    vmem = pl.BlockSpec(memory_space=pltpu.VMEM)
    return pl.pallas_call(
        functools.partial(scatter_kernel, n_dp, spd, scale),
        in_specs=[smem()] + [vmem] * 4,
        out_specs=[vmem, vmem],
        out_shape=[
            jax.ShapeDtypeStruct((spd, edge, edge), F32),
            jax.ShapeDtypeStruct((VEC_ROWS, D), F32),
        ],
        scratch_shapes=[
            pltpu.VMEM((codes, spd, edge, edge), BF16),
            pltpu.VMEM((codes, spd, edge, edge), BF16),
            pltpu.VMEM((codes - 1, spd, edge, edge), BF16),
            pltpu.VMEM((n_bits + 1, VEC_ROWS, D), F32),
            pltpu.VMEM((n_bits + 1, VEC_ROWS, D), F32),
            dma((n, codes)), dma((n, codes)), dma((n, codes)), dma((n, codes)),
            dma((n_bits + 1,)), dma((n_bits + 1,)),
        ],
        compiler_params=pltpu.CompilerParams(
            vmem_limit_bytes=VMEM_LIMIT, collective_id=1, has_side_effects=True
        ),
        name="scatter",
    )(places, grads, row_grad, qv_grad, up_grad)


def adam(grad, first, second, current, outs):
    first = MOMENT_DECAY * first + (1.0 - MOMENT_DECAY) * grad
    second = MOMENT_DECAY * second + (1.0 - MOMENT_DECAY) * grad * grad
    grad_out, new_out, first_out, second_out = outs
    grad_out[...] = grad
    new_out[...] = current - VECTOR_RATE * first / (jnp.sqrt(second) + EPS_ADAM)
    first_out[...] = first
    second_out[...] = second


def update_kernel(
    piece, grad_ref, master_ref, first_ref, second_ref, left_ref, right_ref,
    layer_own, layer_other, input_own, input_other, vec_ref, split_ref, sf_ref, ss_ref, row_ref, rf_ref, rs_ref,
    wg_ref, new_ref, nf_ref, ns_ref, low_ref, layer_ref, input_ref, *vec_outs,
):
    step = pl.program_id(0)
    for s in range(grad_ref.shape[0]):
        left, right = left_ref[0, s].astype(BF16), right_ref[0, s].astype(BF16)
        grad = grad_ref[s]
        turned = dot_nn(dot_tn(left, grad.astype(BF16)).astype(BF16), right)
        first = MOMENT_DECAY * first_ref[0, s] + (1.0 - MOMENT_DECAY) * turned
        second = MOMENT_DECAY * second_ref[0, s] + (1.0 - MOMENT_DECAY) * turned * turned
        stepped = first / (jnp.sqrt(second) + EPS_ADAM)
        back = dot_nt(dot_nn(left, stepped.astype(BF16)).astype(BF16), right)
        new = master_ref[0, s] - LEARN_RATE * back
        wg_ref[0, s] = grad
        new_ref[0, s] = new
        nf_ref[0, s] = first
        ns_ref[0, s] = second
        low_ref[0, s] = new.astype(BF16)

    @pl.when(step == 0)
    def _():
        layer_ref[...] = layer_own[...]
        input_ref[...] = input_own[...]
        pieces = (2 * D + FF) // split_ref.shape[1]
        head_w, ffn_w = D // pieces, FF // pieces
        wide = jnp.concatenate([vec_ref[8 + i : 9 + i] for i in range(FF // D)], axis=1)
        grad = jnp.zeros(split_ref.shape, F32)
        for i in range(pieces):
            mine = jnp.concatenate(
                [
                    vec_ref[6:7, i * head_w : (i + 1) * head_w],
                    vec_ref[7:8, i * head_w : (i + 1) * head_w],
                    wide[:, i * ffn_w : (i + 1) * ffn_w],
                ],
                axis=1,
            )
            grad = jnp.where(piece[0] == i, mine, grad)
        adam(grad, sf_ref[...], ss_ref[...], split_ref[...], vec_outs[:4])
        adam(vec_ref[0:6], rf_ref[...], rs_ref[...], row_ref[...], vec_outs[4:])

    @pl.when(step == 1)
    def _():
        layer_ref[...] = layer_other[...]
        input_ref[...] = input_other[...].astype(F32)


def update_all(piece, owned, blocks, halves, summed, vectors):
    masters = blocks[0]
    spd, edge = masters.shape[1], masters.shape[-1]
    group = spd // 2
    whole = lambda a: pl.BlockSpec(a.shape, lambda i, p: tuple(0 for _ in a.shape))
    spec = pl.BlockSpec((1, group, edge, edge), lambda i, p: (0, i, 0, 0))
    half = pl.BlockSpec(halves[0].shape, lambda i, p: ((p[0] + i) % 2, 0))
    shape = jax.ShapeDtypeStruct
    vec_shapes = [shape(vectors[0].shape, F32)] * 4 + [shape(vectors[3].shape, F32)] * 4
    total = 2 * halves[0].shape[0]
    return pl.pallas_call(
        update_kernel,
        grid_spec=pltpu.PrefetchScalarGridSpec(
            num_scalar_prefetch=1,
            grid=(2,),
            in_specs=[pl.BlockSpec((group, edge, edge), lambda i, p: (i, 0, 0))]
            + [spec] * 5
            + [whole(a) for a in (*halves, summed, *vectors)],
            out_specs=[spec] * 5 + [half, half] + [whole(a) for a in vec_shapes],
        ),
        out_shape=[shape(masters.shape, F32)] * 4
        + [shape(masters.shape, BF16), shape((total, D), BF16), shape((total, D), F32)]
        + vec_shapes,
        compiler_params=params(),
        name="update",
    )(piece, owned, *blocks, *halves, summed, *vectors)


def body(
    tokens,
    cotangent,
    pair_lengths,
    block_of_slot,
    masters,
    mom_first,
    mom_second,
    left_bases,
    right_bases,
    split_vec,
    split_first,
    split_second,
    row_vec,
    row_first,
    row_second,
):
    pieces = lax.axis_size("tensor")
    piece = lax.axis_index("tensor")
    n_dp = lax.axis_size("dp")
    slots = block_of_slot.shape[0]
    full_seq = tokens.shape[0] // pair_lengths.shape[0]
    row_count = pair_lengths.shape[0] // pieces
    order = np.array(sum(block_home(pieces), []), np.int32)
    slot_numbers = jnp.arange(slots, dtype=jnp.int32)[:, None] + order[None, :, 0] * slots
    homes = jnp.sum(jnp.where(block_of_slot[:, None] == order[None, :, 1], slot_numbers, 0), axis=0)
    grads_at = np.array(grad_order(pieces), np.int32)
    number = np.array([np.where(grads_at[:, 0] == i, grads_at[:, 1], -1) for i in range(pieces)])
    index = jnp.arange(1, len(grads_at) + 1, dtype=jnp.int32)[None, :, None]
    places = jnp.sum(jnp.where(number[:, :, None] == block_of_slot[None, None, :], index, 0), axis=1) - 1
    every, query_bias, value_bias, up_bias = gather_all(masters, split_vec, n_dp, pieces)
    layer_own, layer_other, input_own, input_other, grads, row_local, up_grad, qv_grad = layer_passes(
        tokens, cotangent, pair_lengths, piece, homes, every, query_bias, value_bias, up_bias, row_vec, row_count, full_seq
    )
    mean_scale = 1.0 / (tokens.shape[0] * n_dp)
    owned, summed = scatter_all(places, grads, row_local, qv_grad, up_grad, n_dp, mean_scale)
    outs = update_all(
        piece.astype(jnp.int32).reshape(1),
        owned,
        (masters, mom_first, mom_second, left_bases, right_bases),
        (layer_own, layer_other, input_own, input_other),
        summed,
        (split_vec, split_first, split_second, row_vec, row_first, row_second),
    )
    return (outs[5], outs[6], *outs[:5], *outs[7:])


def solution(mesh):
    in_specs = (
        P("dp", None),
        P("dp", None),
        P("dp", None),
        P(),
        P("tensor", "dp", None, None),
        P("tensor", "dp", None, None),
        P("tensor", "dp", None, None),
        P("tensor", "dp", None, None),
        P("tensor", "dp", None, None),
        P("tensor", None),
        P("tensor", None),
        P("tensor", None),
        P(),
        P(),
        P(),
    )
    out_specs = (
        P("dp", None),
        P("dp", None),
        P("tensor", "dp", None, None),
        P("tensor", "dp", None, None),
        P("tensor", "dp", None, None),
        P("tensor", "dp", None, None),
        P("tensor", "dp", None, None),
        P("tensor", None),
        P("tensor", None),
        P("tensor", None),
        P("tensor", None),
        P(),
        P(),
        P(),
        P(),
    )
    return jax.shard_map(body, mesh=mesh, in_specs=in_specs, out_specs=out_specs, check_vma=False)
```

```python
import functools

import jax
import jax.numpy as jnp
from jax import lax
from jax.experimental import pallas as pl
from jax.experimental.pallas import tpu as pltpu
from jax.sharding import PartitionSpec as P
import numpy as np

D = 768
HEADS = 12
HEAD = 64
FF = 3072


EPS_NORM = 1e-05
EPS_ADAM = 1e-08
LEARN_RATE = 0.01
VECTOR_RATE = 0.15
MOMENT_DECAY = 0.5
MASKED_SCORE = -1e30
HIGHEST_PRECISION = lax.Precision.HIGHEST


def block_counts(block_edge, head_width, ffn_width):
    return (
        D // block_edge * (3 * head_width // block_edge),
        head_width // block_edge * (D // block_edge),
        D // block_edge * (ffn_width // block_edge),
        ffn_width // block_edge * (D // block_edge),
    )


LOG2E = 1.4426950408889634
LN_TWO = 0.6931471805599453
ROOT_HALF = 0.7071067811865476
PHI_SCALE = 0.3989422804014327
ERF_P = 0.3275911
ERF_A = (0.254829592, -0.284496736, 1.421413741, -1.453152027, 1.061405429)
VMEM_LIMIT = 61 * 1024 * 1024
LANES = 128
VEC_ROWS = 16
BF16 = jnp.bfloat16
F32 = jnp.float32


def dot_nn(left, right):
    return lax.dot_general(left, right, (((1,), (0,)), ((), ())), preferred_element_type=F32)


def dot_nt(left, right):
    return lax.dot_general(left, right, (((1,), (1,)), ((), ())), preferred_element_type=F32)


def dot_tn(left, right):
    return lax.dot_general(left, right, (((0,), (0,)), ((), ())), preferred_element_type=F32)


def block_home(pieces):
    d_b, f_b = D // LANES, FF // LANES
    d_p, f_p = d_b // pieces, f_b // pieces
    first = d_b * 3 * d_p
    second = first + d_p * d_b
    third = second + d_b * f_p
    qkv = [
        (n % d_b // d_p, k * 3 * d_p + n // d_b * d_p + n % d_p)
        for k in range(d_b)
        for n in range(3 * d_b)
    ]
    out = [(k // d_p, first + k % d_p * d_b + n) for k in range(d_b) for n in range(d_b)]
    up = [(n // f_p, second + k * f_p + n % f_p) for k in range(d_b) for n in range(f_b)]
    down = [(k // f_p, third + k % f_p * d_b + n) for k in range(f_b) for n in range(d_b)]
    return qkv, out, up, down


def grad_order(pieces):
    d_b, f_b = D // LANES, FF // LANES
    qkv, out, up, down = block_home(pieces)
    f_s, q_s = f_b // d_b, 3
    order = []
    for j in range(d_b):
        order += [down[(j * f_s + k) * d_b + n] for k in range(f_s) for n in range(d_b)]
        order += [up[k * f_b + j * f_s + n] for k in range(d_b) for n in range(f_s)]
        order += [qkv[k * 3 * d_b + j * q_s + n] for k in range(d_b) for n in range(q_s)]
        order += [out[j * d_b + n] for n in range(d_b)]
    return order


def start_blocks(homes, base, rows, cols, source, target, sem):
    def step(index, carry):
        k, n = index // cols, index % cols
        pltpu.make_async_copy(
            source.at[homes[base + index]],
            target.at[pl.ds(pl.multiple_of(k * LANES, LANES), LANES), pl.ds(pl.multiple_of(n * LANES, LANES), LANES)],
            sem,
        ).start()
        return carry

    lax.fori_loop(0, rows * cols, step, 0, unroll=6)


def wait_blocks(target, sem):
    pltpu.make_async_copy(target, target, sem).wait()


def mask_bias(ends_ref, row, seq, bias_ref):
    col = lax.broadcasted_iota(jnp.int32, (seq, 1), 0)
    lane = lax.broadcasted_iota(jnp.int32, (1, seq), 1)
    seg_col = jnp.zeros((seq, 1), jnp.int32)
    seg_lane = jnp.zeros((1, seq), jnp.int32)
    end = 0
    for k in range(ends_ref.shape[1] - 1):
        end = end + ends_ref[row, k]
        seg_col = seg_col + (col >= end).astype(jnp.int32)
        seg_lane = seg_lane + (lane >= end).astype(jnp.int32)
    bias_ref[...] = jnp.where(seg_col == seg_lane, 0.0, MASKED_SCORE)


def norm_parts(hidden):
    mean = jnp.mean(hidden, axis=-1, keepdims=True)
    centred = hidden - mean
    var = jnp.mean(centred * centred, axis=-1, keepdims=True)
    inv = lax.rsqrt(var + EPS_NORM)
    return centred * inv, inv


def norm_back(grad, gain, normed, inv):
    scaled = grad * gain
    mean = jnp.mean(scaled, axis=-1, keepdims=True)
    along = jnp.mean(scaled * normed, axis=-1, keepdims=True)
    return inv * (scaled - mean - normed * along)


def put_blocks(ref, value):
    for n in range(ref.shape[0]):
        ref[n] = value[:, n * LANES : (n + 1) * LANES]


def get_blocks(ref):
    return jnp.concatenate([ref[n] for n in range(ref.shape[0])], axis=1)


def gelu_parts(u):
    e = jnp.exp(u * u * -0.5)
    t = 1.0 / (1.0 + (ERF_P * ROOT_HALF) * jnp.abs(u))
    a1, a2, a3, a4, a5 = (0.5 * a for a in ERF_A)
    tail = ((((a5 * t + a4) * t + a3) * t + a2) * t + a1) * t * e
    cdf = jnp.where(u >= 0, 1.0 - tail, tail)
    return u * cdf, cdf + u * e * PHI_SCALE


def forward_kernel(
    homes, pairs, offset, x_any, cot_any, every, qb_ref, vb_ref, bu_ref, rv_ref,
    qkv_out, att_out, lse_ref, out_out, nl_out, act_out, dl_out, up_out, al_out, ml_out, g1_out, rg_ref, bg_ref,
    w_ref, wo_ref, wu_ref, wd_ref, x_ref, cot_ref, qkv_ref, att_ref, bias_ref,
    nl_ref, act_ref, dl_ref, up_ref, al_ref, ml_ref, n_ref, inv_ref, acc_ref, in_sem, out_sem,
):
    d_b, f_b = D // LANES, FF // LANES
    total = x_ref.shape[0]
    seq = bias_ref.shape[0]
    row_count = total // seq
    steps = row_count * d_b
    first = pl.multiple_of(offset[0] * seq, seq)
    x_copy = pltpu.make_async_copy(x_any.at[pl.ds(first, total)], x_ref, in_sem.at[0])
    cot_copy = pltpu.make_async_copy(cot_any.at[pl.ds(first, total)], cot_ref, in_sem.at[1])
    x_copy.start()
    start_blocks(homes, 0, d_b, 3 * d_b, every, w_ref, in_sem.at[2])
    cot_copy.start()
    x_copy.wait()
    wait_blocks(w_ref, in_sem.at[2])

    outs = []

    def send(source, target):
        copy = pltpu.make_async_copy(source, target, out_sem.at[len(outs)])
        copy.start()
        outs.append(copy)

    wide = 2 * LANES
    for part in range(3):
        for c in range(0, D, wide):
            y = dot_nn(x_ref[...], w_ref[:, part * D + c : part * D + c + wide])
            if part == 0:
                y = (y + qb_ref[:, c : c + wide]).astype(BF16).astype(F32) * HEAD ** (-0.5)
            if part == 2:
                y = y + vb_ref[:, c : c + wide]
            y = y.astype(BF16)
            for n in range(2):
                qkv_ref[part * d_b + c // LANES + n] = y[:, n * LANES : (n + 1) * LANES]
    send(qkv_ref, qkv_out)
    lane = lax.broadcasted_iota(jnp.int32, (1, LANES), 1)

    def block(base, rows, cols, source, target, sem, index):
        k, n = index // cols, index % cols
        pltpu.make_async_copy(
            every.at[homes[base + index]],
            target.at[pl.ds(pl.multiple_of(k * LANES, LANES), LANES), pl.ds(pl.multiple_of(n * LANES, LANES), LANES)],
            sem,
        ).start()

    def fetch(step):
        for base, rows, cols, target, sem in (
            (3 * d_b * d_b, d_b, d_b, wo_ref, 3),
            (4 * d_b * d_b, d_b, f_b, wu_ref, 4),
            (4 * d_b * d_b + d_b * f_b, f_b, d_b, wd_ref, 5),
        ):
            each = rows * cols // steps
            for i in range(each):
                block(base, rows, cols, every, target, in_sem.at[sem], step * each + i)

    for r in range(row_count):
        at = slice(r * seq, (r + 1) * seq)
        mask_bias(pairs, offset[0] + r, seq, bias_ref)

        def pair(n, carry):
            fetch(r * d_b + n)
            q = qkv_ref[n, at]
            k = qkv_ref[d_b + n, at]
            v_t = qkv_ref[2 * d_b + n, at].T
            halves = []
            for h in range(2):
                keep = (lane < HEAD) if h == 0 else (lane >= HEAD)
                scores = dot_nt(jnp.where(keep, k, jnp.zeros_like(k)), q) + bias_ref[...]
                top = jnp.max(scores, axis=0, keepdims=True)
                p = jnp.exp(scores - top)
                sums = jnp.sum(p, axis=0, keepdims=True)
                lse_ref[r, 2 * n + h] = (top + jnp.log(sums)).reshape(1, seq)
                mixed = dot_nn(v_t[h * HEAD : (h + 1) * HEAD], p.astype(BF16))
                halves.append(mixed * (1.0 / sums))
            att_ref[n, at] = jnp.concatenate(halves, axis=0).T.astype(BF16)
            return carry

        lax.fori_loop(0, d_b, pair, 0)
    send(att_ref, att_out)
    out_bias, gain_one, shift_one, down_bias, gain_two, shift_two = (
        rv_ref[i : i + 1] for i in range(6)
    )
    rg_ref[...] = jnp.zeros_like(rg_ref)
    tile = total // 4
    tiles = [slice(t * tile, (t + 1) * tile) for t in range(4)]

    def put(ref, at, value):
        for n in range(ref.shape[0]):
            ref[n, at] = value[:, n * LANES : (n + 1) * LANES]

    def get(ref, at):
        return jnp.concatenate([ref[n, at] for n in range(ref.shape[0])], axis=1)

    wait_blocks(wo_ref, in_sem.at[3])
    for at in tiles:
        hidden = dot_nn(get(att_ref, at), wo_ref[...]) + x_ref[at].astype(F32) + out_bias
        n_one, inv_one = norm_parts(hidden)
        n_ref[at] = n_one
        inv_ref[at] = inv_one
        normed = n_one * gain_one + shift_one
        put(nl_ref, at, normed.astype(BF16))
        acc_ref[at] = normed + down_bias
    send(nl_ref, nl_out)
    wait_blocks(wu_ref, in_sem.at[4])
    wait_blocks(wd_ref, in_sem.at[5])
    wide = 768
    per = wide // LANES
    normed_low = get_blocks(nl_ref)
    for c in range(0, FF, wide):
        u = dot_nn(normed_low, wu_ref[:, c : c + wide]) + bu_ref[:, c : c + wide]
        active, slope = gelu_parts(u)
        active = active.astype(BF16)
        slope = slope.astype(BF16)
        for n in range(per):
            act_ref[c // LANES + n] = active[:, n * LANES : (n + 1) * LANES]
            up_ref[c // LANES + n] = slope[:, n * LANES : (n + 1) * LANES]
        acc_ref[...] += dot_nn(active, wd_ref[c : c + wide, :])
    send(act_ref, act_out)
    cot_copy.wait()
    for at in tiles:
        n_two, inv_two = norm_parts(acc_ref[at])
        x_ref[at] = (n_two * gain_two + shift_two).astype(BF16)
        dy = cot_ref[at].astype(F32)
        grad_two = norm_back(dy, gain_two, n_two, inv_two)
        put(dl_ref, at, grad_two.astype(BF16))
        acc_ref[at] = grad_two
        rg_ref[3:4] += jnp.sum(grad_two, axis=0, keepdims=True)
        rg_ref[4:5] += jnp.sum(dy * n_two, axis=0, keepdims=True)
        rg_ref[5:6] += jnp.sum(dy, axis=0, keepdims=True)
    send(x_ref, out_out)
    send(dl_ref, dl_out)
    down_low = get_blocks(dl_ref)
    for c in range(0, FF, wide):
        blocks = range(c // LANES, c // LANES + per)
        slope = jnp.concatenate([up_ref[n] for n in blocks], axis=1).astype(F32)
        up = (dot_nt(down_low, wd_ref[c : c + wide, :]) * slope).astype(BF16)
        for i, n in enumerate(blocks):
            up_ref[n] = up[:, i * LANES : (i + 1) * LANES]
        bg_ref[:, c : c + wide] = jnp.sum(up.astype(F32), axis=0, keepdims=True)
        acc_ref[...] += dot_nt(up, wu_ref[:, c : c + wide])
    send(up_ref, up_out)
    for at in tiles:
        grad_normed = acc_ref[at]
        n_one = n_ref[at]
        rg_ref[1:2] += jnp.sum(grad_normed * n_one, axis=0, keepdims=True)
        rg_ref[2:3] += jnp.sum(grad_normed, axis=0, keepdims=True)
        grad_one = norm_back(grad_normed, gain_one, n_one, inv_ref[at])
        rg_ref[0:1] += jnp.sum(grad_one, axis=0, keepdims=True)
        acc_ref[at] = grad_one
        attn_low = grad_one.astype(BF16)
        put(al_ref, at, attn_low)
        put(ml_ref, at, dot_nt(attn_low, wo_ref[...]).astype(BF16))
    send(acc_ref, g1_out)
    send(al_ref, al_out)
    send(ml_ref, ml_out)
    for copy in outs:
        copy.wait()


def attend_back_kernel(
    homes, pairs, offset, qkv_ref, att_ref, ml_ref, lse_ref, g1_ref, every,
    merged_ref, ig_ref, il_ref, sg_ref, w_ref, bias_ref, sem,
):
    d_b = D // LANES
    row = pl.program_id(0)
    seq = g1_ref.shape[0]

    @pl.when(row == 0)
    def _():
        start_blocks(homes, 0, d_b, 3 * d_b, every, w_ref, sem)
        sg_ref[...] = jnp.zeros_like(sg_ref)

    mask_bias(pairs, offset[0] + row, seq, bias_ref)
    lane = lax.broadcasted_iota(jnp.int32, (1, LANES), 1)

    def pair(n, carry):
        q = qkv_ref[n]
        k = qkv_ref[d_b + n]
        v = qkv_ref[2 * d_b + n]
        g = ml_ref[n]
        k_t = k.T
        both = g.T.astype(F32) * att_ref[n].T.astype(F32)
        zero = jnp.zeros_like(k)
        parts = []
        for h in range(2):
            keep = (lane < HEAD) if h == 0 else (lane >= HEAD)
            spread = jnp.sum(both[h * HEAD : (h + 1) * HEAD], axis=0, keepdims=True)
            scores = dot_nt(jnp.where(keep, k, zero), q) + bias_ref[...]
            p = jnp.exp(scores - lse_ref[0, 2 * n + h].reshape(1, seq))
            gp = dot_nt(jnp.where(keep, v, zero), g)
            low = (p * (gp - spread)).astype(BF16)
            gv = dot_nn(p.astype(BF16), g)
            gk = dot_nn(low, q)
            gq = dot_nn(k_t[h * HEAD : (h + 1) * HEAD], low)
            parts.append((gq, gk, gv))
        gq = (jnp.concatenate([parts[0][0], parts[1][0]], axis=0) * HEAD ** (-0.5)).T
        merged_ref[n] = gq.astype(BF16)
        merged_ref[d_b + n] = jnp.where(lane < HEAD, parts[0][1], parts[1][1]).astype(BF16)
        merged_ref[2 * d_b + n] = jnp.where(lane < HEAD, parts[0][2], parts[1][2]).astype(BF16)
        return carry

    lax.fori_loop(0, d_b, pair, 0, unroll=2)

    @pl.when(row == 0)
    def _():
        wait_blocks(w_ref, sem)

    for n in range(d_b):
        at = slice(n * LANES, (n + 1) * LANES)
        sg_ref[0:1, at] += jnp.sum(merged_ref[n].astype(F32), axis=0, keepdims=True)
        sg_ref[1:2, at] += jnp.sum(merged_ref[2 * d_b + n].astype(F32), axis=0, keepdims=True)
    merged = get_blocks(merged_ref)
    total = g1_ref[...] + dot_nt(merged, w_ref[...])
    ig_ref[...] = total
    il_ref[...] = total.astype(BF16)


def grad_kernel(act_ref, dl_ref, nl_ref, up_ref, x_ref, merged_ref, att_ref, al_ref, g_ref):
    d_b = D // LANES
    f_s = act_ref.shape[0]
    at = 0

    def store(value, at):
        value = value.astype(BF16)
        for k in range(value.shape[0] // LANES):
            for n in range(value.shape[1] // LANES):
                g_ref[at] = value[k * LANES : (k + 1) * LANES, n * LANES : (n + 1) * LANES]
                at += 1
        return at

    at = store(dot_tn(get_blocks(act_ref), get_blocks(dl_ref)), at)
    at = store(dot_tn(get_blocks(nl_ref), get_blocks(up_ref)), at)
    at = store(dot_tn(x_ref[...], get_blocks(merged_ref)), at)
    at = store(dot_tn(att_ref[0], get_blocks(al_ref)), at)


def smem():
    return pl.BlockSpec(memory_space=pltpu.SMEM)


def anywhere():
    return pl.BlockSpec(memory_space=pl.ANY)


def params():
    return pltpu.CompilerParams(vmem_limit_bytes=VMEM_LIMIT, dimension_semantics=("arbitrary",))


def layer_passes(tokens, cotangent, pair_lengths, piece, homes, every, query_bias, value_bias, up_bias, row_vec, row_count, seq):
    d_b, f_b = D // LANES, FF // LANES
    total = row_count * seq
    shape = jax.ShapeDtypeStruct
    offset = (piece * row_count).astype(jnp.int32).reshape(1)
    stack = lambda n: pl.BlockSpec((n, seq, LANES), lambda r, *_: (0, r, 0))
    rows = pl.BlockSpec((seq, D), lambda r, *_: (r, 0))
    own = lambda at: pl.BlockSpec((seq, D), lambda r, *pre: (pre[at][0] + r, 0))
    whole = lambda s: pl.BlockSpec(s, lambda *_: tuple(0 for _ in s))
    lse_spec = pl.BlockSpec((1, HEADS, 1, seq), lambda r, *_: (r, 0, 0, 0))
    vmem = pl.BlockSpec(memory_space=pltpu.VMEM)
    tokens_bf = shape((total, D), BF16)
    stacked = lambda n: shape((n, total, LANES), BF16)
    kept = lambda n: pltpu.VMEM((n, total, LANES), BF16)
    (
        qkv, att, lse, layer_own, normed_low, active_low, down_low, up_low, attn_low, mixed_low, grad_one, row_grad, up_grad
    ) = pl.pallas_call(
        forward_kernel,
        in_specs=[smem()] * 3 + [anywhere()] * 3 + [vmem] * 4,
        out_specs=[anywhere()] * 2 + [vmem] + [anywhere()] * 8 + [vmem] * 2,
        out_shape=[
            stacked(3 * d_b), stacked(d_b), shape((row_count, HEADS, 1, seq), F32), tokens_bf,
            stacked(d_b), stacked(f_b), stacked(d_b), stacked(f_b), stacked(d_b), stacked(d_b),
            shape((total, D), F32), shape((6, D), F32), shape((1, FF), F32),
        ],
        scratch_shapes=[
            pltpu.VMEM((D, 3 * D), BF16), pltpu.VMEM((D, D), BF16), pltpu.VMEM((D, FF), BF16), pltpu.VMEM((FF, D), BF16),
            pltpu.VMEM((total, D), BF16), pltpu.VMEM((total, D), BF16), kept(3 * d_b), kept(d_b),
            pltpu.VMEM((seq, seq), F32), kept(d_b), kept(f_b), kept(d_b), kept(f_b), kept(d_b), kept(d_b),
            pltpu.VMEM((total, D), F32), pltpu.VMEM((total, 1), F32), pltpu.VMEM((total, D), F32),
            pltpu.SemaphoreType.DMA((6,)), pltpu.SemaphoreType.DMA((10,)),
        ],
        compiler_params=pltpu.CompilerParams(vmem_limit_bytes=VMEM_LIMIT),
        cost_estimate=pl.CostEstimate(flops=64 * total * D * D, bytes_accessed=96 * total * D, transcendentals=0),
        name="forward",
    )(homes, pair_lengths, offset, tokens, cotangent, every, query_bias, value_bias, up_bias, row_vec)
    swap = [(0, 1), (1, 0)]
    layer_other = lax.ppermute(layer_own, "tensor", swap)
    merged, input_own, input_low, split_grad = pl.pallas_call(
        attend_back_kernel,
        grid_spec=pltpu.PrefetchScalarGridSpec(
            num_scalar_prefetch=3,
            grid=(row_count,),
            in_specs=[stack(3 * d_b), stack(d_b), stack(d_b), lse_spec, rows, anywhere()],
            out_specs=[stack(3 * d_b), rows, rows, whole((2, D))],
            scratch_shapes=[
                pltpu.VMEM((D, 3 * D), BF16),
                pltpu.VMEM((seq, seq), F32),
                pltpu.SemaphoreType.DMA,
            ],
        ),
        out_shape=[
            shape((3 * d_b, total, LANES), BF16),
            shape((total, D), F32),
            shape((total, D), BF16),
            shape((2, D), F32),
        ],
        compiler_params=params(),
        cost_estimate=pl.CostEstimate(flops=32 * total * D * D, bytes_accessed=40 * total * D, transcendentals=0),
        name="attend_back",
    )(homes, pair_lengths, offset, qkv, att, mixed_low, lse, grad_one, every)
    input_other = lax.ppermute(input_low, "tensor", swap)
    f_s = f_b // d_b
    part = lambda n: pl.BlockSpec((n, total, LANES), lambda j, *_: (j, 0, 0))
    blocks = 2 * f_s * d_b + 4 * d_b
    grads = pl.pallas_call(
        lambda pc, *refs: grad_kernel(*refs),
        grid_spec=pltpu.PrefetchScalarGridSpec(
            num_scalar_prefetch=1,
            grid=(d_b,),
            in_specs=[
                part(f_s), whole((d_b, total, LANES)), whole((d_b, total, LANES)), part(f_s),
                pl.BlockSpec((total, D), lambda j, pc: (pc[0], 0)),
                part(3), part(1), whole((d_b, total, LANES)),
            ],
            out_specs=pl.BlockSpec((blocks, LANES, LANES), lambda j, *_: (j, 0, 0)),
        ),
        out_shape=shape((d_b * blocks, LANES, LANES), BF16),
        compiler_params=params(),
        cost_estimate=pl.CostEstimate(flops=24 * total * D * D, bytes_accessed=40 * total * D, transcendentals=0),
        name="weight_grads",
    )(piece.astype(jnp.int32).reshape(1), active_low, down_low, normed_low, up_low, tokens, merged, att, attn_low)
    return layer_own, layer_other, input_own, input_other, grads, row_grad, up_grad, split_grad


def split_slots(orders, counts):
    parts, at = [], 0
    for order, count in zip(orders, counts):
        if count:
            parts.append((order, at, count))
        at += count
    return parts


def index_bits(n_dp):
    dp_bits = list(range(1, n_dp.bit_length() - 1))
    return dp_bits[:1], dp_bits[1:]


def gather_orders(n_dp, spd):
    near, far = index_bits(n_dp)
    third = spd * 4 // 14
    first = (spd - third) // 2
    return split_slots(
        ([-1] + near + far, near + [-1] + far, far + [-1] + near), (first, spd - third - first, third)
    )


def scatter_orders(n_dp, spd):
    near, far = index_bits(n_dp)
    first, third = spd * 4 // 14, spd * 2 // 14
    return split_slots(
        ([-1] + far + near, near + [-1] + far, far + near + [-1]), (first, spd - third - first, third)
    )


def bit_of(number, bit):
    return number // (1 << bit) % 2


def across(bit):
    if bit < 0:
        return {"tensor": 1 - lax.axis_index("tensor")}
    me = lax.axis_index("dp")
    return {"dp": me + (1 - 2 * bit_of(me, bit)) * (1 << bit)}


def place_of(order, code, core):
    dp, tensor = lax.axis_index("dp"), lax.axis_index("tensor")
    place = len(order) - 1
    to_dp, to_tensor = core, tensor
    for bit in order:
        flip = bit_of(code, place)
        if bit < 0:
            to_tensor = (tensor + flip) % 2
        else:
            to_dp = to_dp + (bit_of(dp, bit) + flip) % 2 * (1 << bit)
        place -= 1
    return to_tensor, to_dp


def slot_at(order, code, core, spd, at):
    to_tensor, to_dp = place_of(order, code, core)
    return to_tensor, to_dp * spd + at


def first_slot(order, code, core, n_dp, spd):
    to_tensor, to_dp = place_of(order, code, core)
    return (to_tensor * n_dp + to_dp) * spd


def greet(bits):
    barrier = pltpu.get_barrier_semaphore()
    for bit in bits:
        pl.semaphore_signal(barrier, inc=1, device_id=across(bit), device_id_type=pl.DeviceIdType.MESH)
    pl.semaphore_wait(barrier, len(bits))


def remote(source, target, send, recv, bit):
    return pltpu.make_async_remote_copy(
        src_ref=source, dst_ref=target, send_sem=send, recv_sem=recv,
        device_id=across(bit), device_id_type=pl.DeviceIdType.MESH,
    )


def gather_kernel(n_dp, spd, master_ref, vec_ref, all_ref, qb_ref, vb_ref, bu_ref, own_ref, both_ref, local_sem, send_sem, recv_sem, core_send, core_recv, vec_send, vec_recv):
    parts = gather_orders(n_dp, spd)
    n_bits = len(parts[0][0])
    core = bit_of(lax.axis_index("dp"), 0)
    tensor = lax.axis_index("tensor")
    greet([0] + parts[0][0])
    own_ref[...] = master_ref[0].astype(BF16)
    mine = first_slot(parts[0][0], 0, core, n_dp, spd)
    keep = pltpu.make_async_copy(own_ref, all_ref.at[pl.ds(mine, spd)], local_sem.at[0])
    keep.start()
    keep_vec = pltpu.make_async_copy(vec_ref, both_ref.at[pl.ds(tensor, 1)], local_sem.at[1])
    keep_vec.start()
    vec = remote(vec_ref, both_ref.at[pl.ds(tensor, 1)], vec_send, vec_recv, -1)
    vec.start()

    def piece(part, code, core_of):
        order, at, count = part
        return all_ref.at[pl.ds(first_slot(order, code, core_of, n_dp, spd) + at, count)]

    def forward(p, code, level, source):
        order = parts[p][0]
        for stage in range(level, n_bits):
            remote(
                source, piece(parts[p], code, core), send_sem.at[p, stage, code],
                recv_sem.at[p, code + (1 << stage)], order[n_bits - 1 - stage],
            ).start()
        remote(source, piece(parts[p], code, core), core_send.at[p, code], core_recv.at[p, code], 0).start()

    for p, part in enumerate(parts):
        forward(p, 0, 0, own_ref.at[pl.ds(part[1], part[2])])
    for level in range(n_bits):
        def arrive(j, carry):
            code = (1 << level) + j
            for p, part in enumerate(parts):
                here = piece(part, code, core)
                pltpu.make_async_copy(here, here, recv_sem.at[p, code]).wait()
                forward(p, code, level + 1, here)
            return carry

        lax.fori_loop(0, 1 << level, arrive, 0)

    def drain(code, carry):
        for p, part in enumerate(parts):
            here = piece(part, code, core)
            there = piece(part, code, 1 - core)
            pltpu.make_async_copy(here, here, core_send.at[p, code]).wait()
            pltpu.make_async_copy(there, there, core_recv.at[p, code]).wait()
        return carry

    keep_vec.wait()
    vec.wait()
    pieces = both_ref.shape[0]
    head_w, ffn_w = D // pieces, FF // pieces
    for i in range(pieces):
        row = both_ref[i : i + 1]
        qb_ref[:, i * head_w : (i + 1) * head_w] = row[:, :head_w]
        vb_ref[:, i * head_w : (i + 1) * head_w] = row[:, head_w : 2 * head_w]
        bu_ref[:, i * ffn_w : (i + 1) * ffn_w] = row[:, 2 * head_w :]
    for stage in range(n_bits):
        def sent(code, carry):
            for p, part in enumerate(parts):
                here = piece(part, code, core)
                pltpu.make_async_copy(here, here, send_sem.at[p, stage, code]).wait()
            return carry

        lax.fori_loop(0, 1 << stage, sent, 0)
    lax.fori_loop(0, 1 << n_bits, drain, 0)
    keep.wait()


def gather_all(masters, vec, n_dp, pieces):
    spd, edge = masters.shape[1], masters.shape[-1]
    parts = gather_orders(n_dp, spd)
    n, n_bits = len(parts), len(parts[0][0])
    dma = pltpu.SemaphoreType.DMA
    vmem = pl.BlockSpec(memory_space=pltpu.VMEM)
    shape = jax.ShapeDtypeStruct
    return pl.pallas_call(
        functools.partial(gather_kernel, n_dp, spd),
        in_specs=[vmem] * 2,
        out_specs=[anywhere()] + [vmem] * 3,
        out_shape=[
            shape((pieces * n_dp * spd, edge, edge), BF16),
            shape((1, D), F32), shape((1, D), F32), shape((1, FF), F32),
        ],
        scratch_shapes=[
            pltpu.VMEM((spd, edge, edge), BF16),
            pltpu.VMEM((pieces, vec.shape[1]), F32),
            dma((2,)), dma((n, n_bits, 1 << n_bits)), dma((n, 1 << n_bits)),
            dma((n, 1 << n_bits)), dma((n, 1 << n_bits)), dma, dma,
        ],
        compiler_params=pltpu.CompilerParams(
            vmem_limit_bytes=VMEM_LIMIT, collective_id=0, has_side_effects=True
        ),
        name="gather",
    )(masters, vec)


def scatter_kernel(
    n_dp, spd, scale, places, g_ref, rg_ref, sg_ref, bg_ref, swapped, out_ref, vec_out,
    give_ref, sum_ref, in_ref, vec_sum, vec_in,
    core_send, core_recv, send_sem, recv_sem, vec_send, vec_recv,
):
    parts = scatter_orders(n_dp, spd)
    n_bits = len(parts[0][0])
    codes = 1 << n_bits
    core = bit_of(lax.axis_index("dp"), 0)
    vec_bits = [0] + parts[0][0]
    greet(vec_bits)

    def term(slot):
        place = places[slot[0], slot[1]]
        return jnp.where(place >= 0, g_ref[jnp.maximum(place, 0)], jnp.zeros(g_ref.shape[1:], BF16))

    def vec_copy(stage):
        return remote(vec_sum.at[stage], vec_in.at[stage], vec_send.at[stage], vec_recv.at[stage], vec_bits[stage])

    def vec_step(stage):
        vec_copy(stage).wait_recv()
        total = vec_sum[stage] + vec_in[stage]
        if stage + 1 < len(vec_bits):
            vec_sum[stage + 1] = total
            vec_copy(stage + 1).start()
        else:
            vec_out[...] = total * scale

    vec_sum[0, 0:6] = rg_ref[...]
    vec_sum[0, 6:8] = sg_ref[...]
    for i in range(FF // D):
        vec_sum[0, 8 + i : 9 + i] = bg_ref[:, i * D : (i + 1) * D]
    vec_sum[0, 8 + FF // D :] = jnp.zeros((VEC_ROWS - 8 - FF // D, D), F32)
    vec_copy(0).start()

    def give(p, code):
        order, at, count = parts[p]
        where = pl.ds(at, count)
        return remote(
            give_ref.at[code, where], sum_ref.at[code, where], core_send.at[p, code], core_recv.at[p, code], 0
        )

    def passed(p, level, code):
        order, at, count = parts[p]
        where = pl.ds(at, count)
        return remote(
            sum_ref.at[code, where], in_ref.at[code - 1, where],
            send_sem.at[p, code], recv_sem.at[p, code - 1], order[n_bits - 1 - level],
        )

    def hand(code):
        for p, (order, at, count) in enumerate(parts):
            start = slot_at(order, code, 1 - core, spd, at)
            for s in range(count):
                give_ref[code, at + s] = term((start[0], start[1] + s))
            give(p, code).start()

    ahead = min(4, codes)
    def first_hands(j, carry):
        hand(codes - 1 - j)
        return carry

    lax.fori_loop(0, ahead, first_hands, 0)
    vec_step(0)
    stage = 1

    def total_of(p, code, level, finish):
        order, at, count = parts[p]
        start = slot_at(order, code, core, spd, at)
        give(p, code).wait_recv()
        sources = []
        for stage in range(level + 1, n_bits):
            entry = (1 << stage) - 1 + code
            here = in_ref.at[entry, pl.ds(at, count)]
            pltpu.make_async_copy(here, here, recv_sem.at[p, entry]).wait()
            sources.append(entry)
        for s in range(count):
            value = term((start[0], start[1] + s)).astype(F32) + sum_ref[code, at + s].astype(F32)
            for entry in sources:
                value = value + in_ref[entry, at + s].astype(F32)
            if finish:
                out_ref[at + s] = value * scale
            else:
                sum_ref[code, at + s] = value.astype(BF16)

    for level in reversed(range(n_bits)):
        def onward(j, carry):
            code = (2 << level) - 1 - j
            if (1 << level) >= ahead:
                hand(code - ahead)
            for p in range(len(parts)):
                total_of(p, code, level, False)
                passed(p, level, code).start()
            return carry

        count = 1 << level
        if level == n_bits - 1 and count >= 4:
            lax.fori_loop(0, 1, onward, 0)
            vec_step(1)
            lax.fori_loop(1, 3, onward, 0)
            vec_step(2)
            lax.fori_loop(3, count, onward, 0)
            stage = 3
        else:
            lax.fori_loop(0, count, onward, 0)
        if stage < n_bits:
            vec_step(stage)
            stage += 1
    for p in range(len(parts)):
        total_of(p, 0, -1, True)
    for last in range(stage, n_bits + 1):
        vec_step(last)
    for stage in range(len(vec_bits)):
        vec_copy(stage).wait_send()

    def drain(code, carry):
        for p in range(len(parts)):
            give(p, code).wait_send()
        return carry

    lax.fori_loop(0, codes, drain, 0)
    for level in range(n_bits):
        def drain_level(j, carry):
            for p in range(len(parts)):
                passed(p, level, (1 << level) + j).wait_send()
            return carry

        lax.fori_loop(0, 1 << level, drain_level, 0)


def scatter_all(places, grads, row_grad, qv_grad, up_grad, swapped, n_dp, scale):
    edge = grads.shape[-1]
    spd = places.shape[1] // n_dp
    parts = scatter_orders(n_dp, spd)
    n, n_bits = len(parts), len(parts[0][0])
    codes = 1 << n_bits
    dma = pltpu.SemaphoreType.DMA
    vmem = pl.BlockSpec(memory_space=pltpu.VMEM)
    return pl.pallas_call(
        functools.partial(scatter_kernel, n_dp, spd, scale),
        in_specs=[smem()] + [vmem] * 4 + [anywhere()],
        out_specs=[vmem, vmem],
        out_shape=[
            jax.ShapeDtypeStruct((spd, edge, edge), F32),
            jax.ShapeDtypeStruct((VEC_ROWS, D), F32),
        ],
        scratch_shapes=[
            pltpu.VMEM((codes, spd, edge, edge), BF16),
            pltpu.VMEM((codes, spd, edge, edge), BF16),
            pltpu.VMEM((codes - 1, spd, edge, edge), BF16),
            pltpu.VMEM((n_bits + 1, VEC_ROWS, D), F32),
            pltpu.VMEM((n_bits + 1, VEC_ROWS, D), F32),
            dma((n, codes)), dma((n, codes)), dma((n, codes)), dma((n, codes)),
            dma((n_bits + 1,)), dma((n_bits + 1,)),
        ],
        compiler_params=pltpu.CompilerParams(
            vmem_limit_bytes=VMEM_LIMIT, collective_id=1, has_side_effects=True
        ),
        name="scatter",
    )(places, grads, row_grad, qv_grad, up_grad, swapped)


def adam(grad, first, second, current, outs):
    first = MOMENT_DECAY * first + (1.0 - MOMENT_DECAY) * grad
    second = MOMENT_DECAY * second + (1.0 - MOMENT_DECAY) * grad * grad
    grad_out, new_out, first_out, second_out = outs
    grad_out[...] = grad
    new_out[...] = current - VECTOR_RATE * first / (jnp.sqrt(second) + EPS_ADAM)
    first_out[...] = first
    second_out[...] = second


def update_kernel(
    piece, grad_ref, master_ref, first_ref, second_ref, left_ref, right_ref,
    layer_own, layer_other, input_own, input_other, vec_ref, split_ref, sf_ref, ss_ref, row_ref, rf_ref, rs_ref,
    wg_ref, new_ref, nf_ref, ns_ref, low_ref, layer_ref, input_ref, *vec_outs,
):
    step = pl.program_id(0)
    for s in range(grad_ref.shape[0]):
        left, right = left_ref[0, s].astype(BF16), right_ref[0, s].astype(BF16)
        grad = grad_ref[s]
        turned = dot_nn(dot_tn(left, grad.astype(BF16)).astype(BF16), right)
        first = MOMENT_DECAY * first_ref[0, s] + (1.0 - MOMENT_DECAY) * turned
        second = MOMENT_DECAY * second_ref[0, s] + (1.0 - MOMENT_DECAY) * turned * turned
        stepped = first / (jnp.sqrt(second) + EPS_ADAM)
        back = dot_nt(dot_nn(left, stepped.astype(BF16)).astype(BF16), right)
        new = master_ref[0, s] - LEARN_RATE * back
        wg_ref[0, s] = grad
        new_ref[0, s] = new
        nf_ref[0, s] = first
        ns_ref[0, s] = second
        low_ref[0, s] = new.astype(BF16)

    @pl.when(step == 0)
    def _():
        layer_ref[...] = layer_own[...]
        input_ref[...] = input_own[...]
        pieces = (2 * D + FF) // split_ref.shape[1]
        head_w, ffn_w = D // pieces, FF // pieces
        wide = jnp.concatenate([vec_ref[8 + i : 9 + i] for i in range(FF // D)], axis=1)
        grad = jnp.zeros(split_ref.shape, F32)
        for i in range(pieces):
            mine = jnp.concatenate(
                [
                    vec_ref[6:7, i * head_w : (i + 1) * head_w],
                    vec_ref[7:8, i * head_w : (i + 1) * head_w],
                    wide[:, i * ffn_w : (i + 1) * ffn_w],
                ],
                axis=1,
            )
            grad = jnp.where(piece[0] == i, mine, grad)
        adam(grad, sf_ref[...], ss_ref[...], split_ref[...], vec_outs[:4])
        adam(vec_ref[0:6], rf_ref[...], rs_ref[...], row_ref[...], vec_outs[4:])

    @pl.when(step == 1)
    def _():
        layer_ref[...] = layer_other[...]
        input_ref[...] = input_other[...].astype(F32)


def update_all(piece, owned, blocks, halves, summed, vectors):
    masters = blocks[0]
    spd, edge = masters.shape[1], masters.shape[-1]
    group = spd // 2
    whole = lambda a: pl.BlockSpec(a.shape, lambda i, p: tuple(0 for _ in a.shape))
    spec = pl.BlockSpec((1, group, edge, edge), lambda i, p: (0, i, 0, 0))
    half = pl.BlockSpec(halves[0].shape, lambda i, p: ((p[0] + i) % 2, 0))
    shape = jax.ShapeDtypeStruct
    vec_shapes = [shape(vectors[0].shape, F32)] * 4 + [shape(vectors[3].shape, F32)] * 4
    total = 2 * halves[0].shape[0]
    return pl.pallas_call(
        update_kernel,
        grid_spec=pltpu.PrefetchScalarGridSpec(
            num_scalar_prefetch=1,
            grid=(2,),
            in_specs=[pl.BlockSpec((group, edge, edge), lambda i, p: (i, 0, 0))]
            + [spec] * 5
            + [whole(a) for a in (*halves, summed, *vectors)],
            out_specs=[spec] * 5 + [half, half] + [whole(a) for a in vec_shapes],
        ),
        out_shape=[shape(masters.shape, F32)] * 4
        + [shape(masters.shape, BF16), shape((total, D), BF16), shape((total, D), F32)]
        + vec_shapes,
        compiler_params=params(),
        name="update",
    )(piece, owned, *blocks, *halves, summed, *vectors)


def body(
    tokens,
    cotangent,
    pair_lengths,
    block_of_slot,
    masters,
    mom_first,
    mom_second,
    left_bases,
    right_bases,
    split_vec,
    split_first,
    split_second,
    row_vec,
    row_first,
    row_second,
):
    pieces = lax.axis_size("tensor")
    piece = lax.axis_index("tensor")
    n_dp = lax.axis_size("dp")
    slots = block_of_slot.shape[0]
    full_seq = tokens.shape[0] // pair_lengths.shape[0]
    row_count = pair_lengths.shape[0] // pieces
    order = np.array(sum(block_home(pieces), []), np.int32)
    slot_numbers = jnp.arange(slots, dtype=jnp.int32)[:, None] + order[None, :, 0] * slots
    homes = jnp.sum(jnp.where(block_of_slot[:, None] == order[None, :, 1], slot_numbers, 0), axis=0)
    grads_at = np.array(grad_order(pieces), np.int32)
    number = np.array([np.where(grads_at[:, 0] == i, grads_at[:, 1], -1) for i in range(pieces)])
    index = jnp.arange(1, len(grads_at) + 1, dtype=jnp.int32)[None, :, None]
    places = jnp.sum(jnp.where(number[:, :, None] == block_of_slot[None, None, :], index, 0), axis=1) - 1
    every, query_bias, value_bias, up_bias = gather_all(masters, split_vec, n_dp, pieces)
    layer_own, layer_other, input_own, input_other, grads, row_local, up_grad, qv_grad = layer_passes(
        tokens, cotangent, pair_lengths, piece, homes, every, query_bias, value_bias, up_bias, row_vec, row_count, full_seq
    )
    mean_scale = 1.0 / (tokens.shape[0] * n_dp)
    owned, summed = scatter_all(places, grads, row_local, qv_grad, up_grad, layer_other, n_dp, mean_scale)
    outs = update_all(
        piece.astype(jnp.int32).reshape(1),
        owned,
        (masters, mom_first, mom_second, left_bases, right_bases),
        (layer_own, layer_other, input_own, input_other),
        summed,
        (split_vec, split_first, split_second, row_vec, row_first, row_second),
    )
    return (outs[5], outs[6], *outs[:5], *outs[7:])


def solution(mesh):
    in_specs = (
        P("dp", None),
        P("dp", None),
        P("dp", None),
        P(),
        P("tensor", "dp", None, None),
        P("tensor", "dp", None, None),
        P("tensor", "dp", None, None),
        P("tensor", "dp", None, None),
        P("tensor", "dp", None, None),
        P("tensor", None),
        P("tensor", None),
        P("tensor", None),
        P(),
        P(),
        P(),
    )
    out_specs = (
        P("dp", None),
        P("dp", None),
        P("tensor", "dp", None, None),
        P("tensor", "dp", None, None),
        P("tensor", "dp", None, None),
        P("tensor", "dp", None, None),
        P("tensor", "dp", None, None),
        P("tensor", None),
        P("tensor", None),
        P("tensor", None),
        P("tensor", None),
        P(),
        P(),
        P(),
        P(),
    )
    return jax.shard_map(body, mesh=mesh, in_specs=in_specs, out_specs=out_specs, check_vma=False)
```

```python
import functools

import jax
import jax.numpy as jnp
from jax import lax
from jax.experimental import pallas as pl
from jax.experimental.pallas import tpu as pltpu
from jax.sharding import PartitionSpec as P
import numpy as np

D = 768
HEADS = 12
HEAD = 64
FF = 3072


EPS_NORM = 1e-05
EPS_ADAM = 1e-08
LEARN_RATE = 0.01
VECTOR_RATE = 0.15
MOMENT_DECAY = 0.5
MASKED_SCORE = -1e30
HIGHEST_PRECISION = lax.Precision.HIGHEST


def block_counts(block_edge, head_width, ffn_width):
    return (
        D // block_edge * (3 * head_width // block_edge),
        head_width // block_edge * (D // block_edge),
        D // block_edge * (ffn_width // block_edge),
        ffn_width // block_edge * (D // block_edge),
    )


LOG2E = 1.4426950408889634
LN_TWO = 0.6931471805599453
ROOT_HALF = 0.7071067811865476
PHI_SCALE = 0.3989422804014327
ERF_P = 0.3275911
ERF_A = (0.254829592, -0.284496736, 1.421413741, -1.453152027, 1.061405429)
VMEM_LIMIT = 61 * 1024 * 1024
LANES = 128
VEC_ROWS = 16
BF16 = jnp.bfloat16
F32 = jnp.float32


def dot_nn(left, right):
    return lax.dot_general(left, right, (((1,), (0,)), ((), ())), preferred_element_type=F32)


def dot_nt(left, right):
    return lax.dot_general(left, right, (((1,), (1,)), ((), ())), preferred_element_type=F32)


def dot_tn(left, right):
    return lax.dot_general(left, right, (((0,), (0,)), ((), ())), preferred_element_type=F32)


def block_home(pieces):
    d_b, f_b = D // LANES, FF // LANES
    d_p, f_p = d_b // pieces, f_b // pieces
    first = d_b * 3 * d_p
    second = first + d_p * d_b
    third = second + d_b * f_p
    qkv = [
        (n % d_b // d_p, k * 3 * d_p + n // d_b * d_p + n % d_p)
        for k in range(d_b)
        for n in range(3 * d_b)
    ]
    out = [(k // d_p, first + k % d_p * d_b + n) for k in range(d_b) for n in range(d_b)]
    up = [(n // f_p, second + k * f_p + n % f_p) for k in range(d_b) for n in range(f_b)]
    down = [(k // f_p, third + k % f_p * d_b + n) for k in range(f_b) for n in range(d_b)]
    return qkv, out, up, down


def grad_order(pieces):
    d_b, f_b = D // LANES, FF // LANES
    qkv, out, up, down = block_home(pieces)
    f_s, q_s = f_b // d_b, 3
    order = []
    for j in range(d_b):
        order += [down[(j * f_s + k) * d_b + n] for k in range(f_s) for n in range(d_b)]
        order += [up[k * f_b + j * f_s + n] for k in range(d_b) for n in range(f_s)]
        order += [qkv[k * 3 * d_b + j * q_s + n] for k in range(d_b) for n in range(q_s)]
        order += [out[j * d_b + n] for n in range(d_b)]
    return order


def start_blocks(homes, base, rows, cols, source, target, sem):
    def step(index, carry):
        k, n = index // cols, index % cols
        pltpu.make_async_copy(
            source.at[homes[0, base + index]],
            target.at[pl.ds(pl.multiple_of(k * LANES, LANES), LANES), pl.ds(pl.multiple_of(n * LANES, LANES), LANES)],
            sem,
        ).start()
        return carry

    lax.fori_loop(0, rows * cols, step, 0, unroll=6)


def wait_blocks(target, sem):
    pltpu.make_async_copy(target, target, sem).wait()


def mask_bias(ends_ref, row, seq, bias_ref):
    col = lax.broadcasted_iota(jnp.int32, (seq, 1), 0)
    lane = lax.broadcasted_iota(jnp.int32, (1, seq), 1)
    seg_col = jnp.zeros((seq, 1), jnp.int32)
    seg_lane = jnp.zeros((1, seq), jnp.int32)
    end = 0
    for k in range(ends_ref.shape[1] - 1):
        end = end + ends_ref[row, k]
        seg_col = seg_col + (col >= end).astype(jnp.int32)
        seg_lane = seg_lane + (lane >= end).astype(jnp.int32)
    bias_ref[...] = jnp.where(seg_col == seg_lane, 0.0, MASKED_SCORE)


def norm_parts(hidden):
    mean = jnp.mean(hidden, axis=-1, keepdims=True)
    centred = hidden - mean
    var = jnp.mean(centred * centred, axis=-1, keepdims=True)
    inv = lax.rsqrt(var + EPS_NORM)
    return centred * inv, inv


def norm_back(grad, gain, normed, inv):
    scaled = grad * gain
    mean = jnp.mean(scaled, axis=-1, keepdims=True)
    along = jnp.mean(scaled * normed, axis=-1, keepdims=True)
    return inv * (scaled - mean - normed * along)


def put_blocks(ref, value):
    for n in range(ref.shape[0]):
        ref[n] = value[:, n * LANES : (n + 1) * LANES]


def get_blocks(ref):
    return jnp.concatenate([ref[n] for n in range(ref.shape[0])], axis=1)


def gelu_parts(u):
    e = jnp.exp(u * u * -0.5)
    t = 1.0 / (1.0 + (ERF_P * ROOT_HALF) * jnp.abs(u))
    a1, a2, a3, a4, a5 = (0.5 * a for a in ERF_A)
    tail = ((((a5 * t + a4) * t + a3) * t + a2) * t + a1) * t * e
    cdf = jnp.where(u >= 0, 1.0 - tail, tail)
    return u * cdf, cdf + u * e * PHI_SCALE


def forward_kernel(
    homes, pairs, offset, x_any, cot_any, every, qb_ref, vb_ref, bu_ref, rv_ref,
    qkv_out, att_out, lse_ref, out_out, whole_out, nl_out, act_out, dl_out, up_out, al_out, ml_out, g1_out, rg_ref, bg_ref,
    w_ref, wo_ref, wu_ref, wd_ref, x_ref, cot_ref, qkv_ref, att_ref, bias_ref,
    nl_ref, act_ref, dl_ref, up_ref, al_ref, ml_ref, n_ref, inv_ref, acc_ref, in_sem, out_sem,
):
    d_b, f_b = D // LANES, FF // LANES
    total = x_ref.shape[0]
    seq = bias_ref.shape[0]
    row_count = total // seq
    steps = row_count * d_b
    first = pl.multiple_of(offset[0] * seq, seq)
    x_copy = pltpu.make_async_copy(x_any.at[pl.ds(first, total)], x_ref, in_sem.at[0])
    cot_copy = pltpu.make_async_copy(cot_any.at[pl.ds(first, total)], cot_ref, in_sem.at[1])
    x_copy.start()
    start_blocks(homes, 0, d_b, 3 * d_b, every, w_ref, in_sem.at[2])
    cot_copy.start()
    x_copy.wait()
    wait_blocks(w_ref, in_sem.at[2])

    outs = []

    def send(source, target):
        copy = pltpu.make_async_copy(source, target, out_sem.at[len(outs)])
        copy.start()
        outs.append(copy)

    wide = 2 * LANES
    for part in range(3):
        for c in range(0, D, wide):
            y = dot_nn(x_ref[...], w_ref[:, part * D + c : part * D + c + wide])
            if part == 0:
                y = (y + qb_ref[:, c : c + wide]).astype(BF16).astype(F32) * HEAD ** (-0.5)
            if part == 2:
                y = y + vb_ref[:, c : c + wide]
            y = y.astype(BF16)
            for n in range(2):
                qkv_ref[part * d_b + c // LANES + n] = y[:, n * LANES : (n + 1) * LANES]
    send(qkv_ref, qkv_out)
    lane = lax.broadcasted_iota(jnp.int32, (1, LANES), 1)

    def block(base, rows, cols, source, target, sem, index):
        k, n = index // cols, index % cols
        pltpu.make_async_copy(
            every.at[homes[0, base + index]],
            target.at[pl.ds(pl.multiple_of(k * LANES, LANES), LANES), pl.ds(pl.multiple_of(n * LANES, LANES), LANES)],
            sem,
        ).start()

    def fetch(step):
        for base, rows, cols, target, sem in (
            (3 * d_b * d_b, d_b, d_b, wo_ref, 3),
            (4 * d_b * d_b, d_b, f_b, wu_ref, 4),
            (4 * d_b * d_b + d_b * f_b, f_b, d_b, wd_ref, 5),
        ):
            each = rows * cols // steps
            for i in range(each):
                block(base, rows, cols, every, target, in_sem.at[sem], step * each + i)

    for r in range(row_count):
        at = slice(r * seq, (r + 1) * seq)
        mask_bias(pairs, offset[0] + r, seq, bias_ref)

        def pair(n, carry):
            fetch(r * d_b + n)
            q = qkv_ref[n, at]
            k = qkv_ref[d_b + n, at]
            v_t = qkv_ref[2 * d_b + n, at].T
            halves, all_scores = [], []
            for h in range(2):
                keep = (lane < HEAD) if h == 0 else (lane >= HEAD)
                all_scores.append(dot_nt(jnp.where(keep, k, jnp.zeros_like(k)), q) + bias_ref[...])
            for h in range(2):
                scores = all_scores[h]
                top = jnp.max(scores, axis=0, keepdims=True)
                p = jnp.exp(scores - top)
                sums = jnp.sum(p, axis=0, keepdims=True)
                lse_ref[r, 2 * n + h] = (top + jnp.log(sums)).reshape(1, seq)
                mixed = dot_nn(v_t[h * HEAD : (h + 1) * HEAD], p.astype(BF16))
                halves.append(mixed * (1.0 / sums))
            att_ref[n, at] = jnp.concatenate(halves, axis=0).T.astype(BF16)
            return carry

        lax.fori_loop(0, d_b, pair, 0, unroll=2)
    send(att_ref, att_out)
    out_bias, gain_one, shift_one, down_bias, gain_two, shift_two = (
        rv_ref[i : i + 1] for i in range(6)
    )
    rg_ref[...] = jnp.zeros_like(rg_ref)
    tile = total // 4
    tiles = [slice(t * tile, (t + 1) * tile) for t in range(4)]

    def put(ref, at, value):
        for n in range(ref.shape[0]):
            ref[n, at] = value[:, n * LANES : (n + 1) * LANES]

    def get(ref, at):
        return jnp.concatenate([ref[n, at] for n in range(ref.shape[0])], axis=1)

    wait_blocks(wo_ref, in_sem.at[3])
    for at in tiles:
        hidden = dot_nn(get(att_ref, at), wo_ref[...]) + x_ref[at].astype(F32) + out_bias
        n_one, inv_one = norm_parts(hidden)
        n_ref[at] = n_one
        inv_ref[at] = inv_one
        normed = n_one * gain_one + shift_one
        put(nl_ref, at, normed.astype(BF16))
        acc_ref[at] = normed + down_bias
    send(nl_ref, nl_out)
    wait_blocks(wu_ref, in_sem.at[4])
    wait_blocks(wd_ref, in_sem.at[5])
    wide = 768
    per = wide // LANES
    normed_low = get_blocks(nl_ref)
    for c in range(0, FF, wide):
        u = dot_nn(normed_low, wu_ref[:, c : c + wide]) + bu_ref[:, c : c + wide]
        active, slope = gelu_parts(u)
        active = active.astype(BF16)
        slope = slope.astype(BF16)
        for n in range(per):
            act_ref[c // LANES + n] = active[:, n * LANES : (n + 1) * LANES]
            up_ref[c // LANES + n] = slope[:, n * LANES : (n + 1) * LANES]
        acc_ref[...] += dot_nn(active, wd_ref[c : c + wide, :])
    send(act_ref, act_out)
    cot_copy.wait()
    for at in tiles:
        n_two, inv_two = norm_parts(acc_ref[at])
        x_ref[at] = (n_two * gain_two + shift_two).astype(BF16)
        dy = cot_ref[at].astype(F32)
        grad_two = norm_back(dy, gain_two, n_two, inv_two)
        put(dl_ref, at, grad_two.astype(BF16))
        acc_ref[at] = grad_two
        rg_ref[3:4] += jnp.sum(grad_two, axis=0, keepdims=True)
        rg_ref[4:5] += jnp.sum(dy * n_two, axis=0, keepdims=True)
        rg_ref[5:6] += jnp.sum(dy, axis=0, keepdims=True)
    send(x_ref, out_out)
    send(x_ref, whole_out.at[pl.ds(first, total)])
    send(dl_ref, dl_out)
    down_low = get_blocks(dl_ref)
    for c in range(0, FF, wide):
        blocks = range(c // LANES, c // LANES + per)
        slope = jnp.concatenate([up_ref[n] for n in blocks], axis=1).astype(F32)
        up = (dot_nt(down_low, wd_ref[c : c + wide, :]) * slope).astype(BF16)
        for i, n in enumerate(blocks):
            up_ref[n] = up[:, i * LANES : (i + 1) * LANES]
        bg_ref[:, c : c + wide] = jnp.sum(up.astype(F32), axis=0, keepdims=True)
        acc_ref[...] += dot_nt(up, wu_ref[:, c : c + wide])
    send(up_ref, up_out)
    for at in tiles:
        grad_normed = acc_ref[at]
        n_one = n_ref[at]
        rg_ref[1:2] += jnp.sum(grad_normed * n_one, axis=0, keepdims=True)
        rg_ref[2:3] += jnp.sum(grad_normed, axis=0, keepdims=True)
        grad_one = norm_back(grad_normed, gain_one, n_one, inv_ref[at])
        rg_ref[0:1] += jnp.sum(grad_one, axis=0, keepdims=True)
        acc_ref[at] = grad_one
        attn_low = grad_one.astype(BF16)
        put(al_ref, at, attn_low)
        put(ml_ref, at, dot_nt(attn_low, wo_ref[...]).astype(BF16))
    send(acc_ref, g1_out)
    send(al_ref, al_out)
    send(ml_ref, ml_out)
    for copy in outs:
        copy.wait()


def attend_back_kernel(
    homes, pairs, offset, qkv_ref, att_ref, ml_ref, lse_ref, g1_ref, every,
    merged_ref, ig_ref, il_ref, sg_ref, w_ref, bias_ref, sem,
):
    d_b = D // LANES
    row = pl.program_id(0)
    seq = g1_ref.shape[0]

    @pl.when(row == 0)
    def _():
        start_blocks(homes, 0, d_b, 3 * d_b, every, w_ref, sem)
        sg_ref[...] = jnp.zeros_like(sg_ref)

    mask_bias(pairs, offset[0] + row, seq, bias_ref)
    lane = lax.broadcasted_iota(jnp.int32, (1, LANES), 1)

    def pair(n, carry):
        q = qkv_ref[n]
        k = qkv_ref[d_b + n]
        v = qkv_ref[2 * d_b + n]
        g = ml_ref[n]
        k_t = k.T
        both = g.T.astype(F32) * att_ref[n].T.astype(F32)
        zero = jnp.zeros_like(k)
        parts, firsts = [], []
        for h in range(2):
            keep = (lane < HEAD) if h == 0 else (lane >= HEAD)
            scores = dot_nt(jnp.where(keep, k, zero), q) + bias_ref[...]
            firsts.append((scores, dot_nt(jnp.where(keep, v, zero), g)))
        for h in range(2):
            scores, gp = firsts[h]
            spread = jnp.sum(both[h * HEAD : (h + 1) * HEAD], axis=0, keepdims=True)
            p = jnp.exp(scores - lse_ref[0, 2 * n + h].reshape(1, seq))
            low = (p * (gp - spread)).astype(BF16)
            gv = dot_nn(p.astype(BF16), g)
            gk = dot_nn(low, q)
            gq = dot_nn(k_t[h * HEAD : (h + 1) * HEAD], low)
            parts.append((gq, gk, gv))
        gq = (jnp.concatenate([parts[0][0], parts[1][0]], axis=0) * HEAD ** (-0.5)).T
        merged_ref[n] = gq.astype(BF16)
        merged_ref[d_b + n] = jnp.where(lane < HEAD, parts[0][1], parts[1][1]).astype(BF16)
        merged_ref[2 * d_b + n] = jnp.where(lane < HEAD, parts[0][2], parts[1][2]).astype(BF16)
        return carry

    lax.fori_loop(0, d_b, pair, 0, unroll=2)

    @pl.when(row == 0)
    def _():
        wait_blocks(w_ref, sem)

    for n in range(d_b):
        at = slice(n * LANES, (n + 1) * LANES)
        sg_ref[0:1, at] += jnp.sum(merged_ref[n].astype(F32), axis=0, keepdims=True)
        sg_ref[1:2, at] += jnp.sum(merged_ref[2 * d_b + n].astype(F32), axis=0, keepdims=True)
    merged = get_blocks(merged_ref)
    total = g1_ref[...] + dot_nt(merged, w_ref[...])
    ig_ref[...] = total
    il_ref[...] = total.astype(BF16)


def grad_kernel(act_ref, dl_ref, nl_ref, up_ref, x_ref, merged_ref, att_ref, al_ref, g_ref):
    d_b = D // LANES
    f_s = act_ref.shape[0]
    at = 0

    def store(value, at):
        value = value.astype(BF16)
        for k in range(value.shape[0] // LANES):
            for n in range(value.shape[1] // LANES):
                g_ref[at] = value[k * LANES : (k + 1) * LANES, n * LANES : (n + 1) * LANES]
                at += 1
        return at

    at = store(dot_tn(get_blocks(act_ref), get_blocks(dl_ref)), at)
    at = store(dot_tn(get_blocks(nl_ref), get_blocks(up_ref)), at)
    at = store(dot_tn(x_ref[...], get_blocks(merged_ref)), at)
    at = store(dot_tn(att_ref[0], get_blocks(al_ref)), at)


def smem():
    return pl.BlockSpec(memory_space=pltpu.SMEM)


def anywhere():
    return pl.BlockSpec(memory_space=pl.ANY)


def params():
    return pltpu.CompilerParams(vmem_limit_bytes=VMEM_LIMIT, dimension_semantics=("arbitrary",))


def layer_passes(tokens, cotangent, pair_lengths, piece, homes, every, query_bias, value_bias, up_bias, row_vec, row_count, seq):
    d_b, f_b = D // LANES, FF // LANES
    total = row_count * seq
    shape = jax.ShapeDtypeStruct
    offset = (piece * row_count).astype(jnp.int32).reshape(1)
    stack = lambda n: pl.BlockSpec((n, seq, LANES), lambda r, *_: (0, r, 0))
    rows = pl.BlockSpec((seq, D), lambda r, *_: (r, 0))
    own = lambda at: pl.BlockSpec((seq, D), lambda r, *pre: (pre[at][0] + r, 0))
    whole = lambda s: pl.BlockSpec(s, lambda *_: tuple(0 for _ in s))
    lse_spec = pl.BlockSpec((1, HEADS, 1, seq), lambda r, *_: (r, 0, 0, 0))
    vmem = pl.BlockSpec(memory_space=pltpu.VMEM)
    tokens_bf = shape((total, D), BF16)
    stacked = lambda n: shape((n, total, LANES), BF16)
    kept = lambda n: pltpu.VMEM((n, total, LANES), BF16)
    (
        qkv, att, lse, layer_own, layer_whole, normed_low, active_low, down_low, up_low, attn_low, mixed_low, grad_one, row_grad, up_grad
    ) = pl.pallas_call(
        forward_kernel,
        in_specs=[smem()] * 3 + [anywhere()] * 3 + [vmem] * 4,
        out_specs=[anywhere()] * 2 + [vmem] + [anywhere()] * 9 + [vmem] * 2,
        out_shape=[
            stacked(3 * d_b), stacked(d_b), shape((row_count, HEADS, 1, seq), F32), tokens_bf,
            shape(tokens.shape, BF16),
            stacked(d_b), stacked(f_b), stacked(d_b), stacked(f_b), stacked(d_b), stacked(d_b),
            shape((total, D), F32), shape((6, D), F32), shape((1, FF), F32),
        ],
        scratch_shapes=[
            pltpu.VMEM((D, 3 * D), BF16), pltpu.VMEM((D, D), BF16), pltpu.VMEM((D, FF), BF16), pltpu.VMEM((FF, D), BF16),
            pltpu.VMEM((total, D), BF16), pltpu.VMEM((total, D), BF16), kept(3 * d_b), kept(d_b),
            pltpu.VMEM((seq, seq), F32), kept(d_b), kept(f_b), kept(d_b), kept(f_b), kept(d_b), kept(d_b),
            pltpu.VMEM((total, D), F32), pltpu.VMEM((total, 1), F32), pltpu.VMEM((total, D), F32),
            pltpu.SemaphoreType.DMA((6,)), pltpu.SemaphoreType.DMA((11,)),
        ],
        compiler_params=pltpu.CompilerParams(vmem_limit_bytes=VMEM_LIMIT),
        cost_estimate=pl.CostEstimate(flops=64 * total * D * D, bytes_accessed=96 * total * D, transcendentals=0),
        name="forward",
    )(homes, pair_lengths, offset, tokens, cotangent, every, query_bias, value_bias, up_bias, row_vec)
    swap = [(0, 1), (1, 0)]
    layer_other = lax.ppermute(layer_own, "tensor", swap)
    merged, input_whole, input_low, split_grad = pl.pallas_call(
        attend_back_kernel,
        grid_spec=pltpu.PrefetchScalarGridSpec(
            num_scalar_prefetch=3,
            grid=(row_count,),
            in_specs=[stack(3 * d_b), stack(d_b), stack(d_b), lse_spec, rows, anywhere()],
            out_specs=[stack(3 * d_b), own(2), rows, whole((2, D))],
            scratch_shapes=[
                pltpu.VMEM((D, 3 * D), BF16),
                pltpu.VMEM((seq, seq), F32),
                pltpu.SemaphoreType.DMA,
            ],
        ),
        out_shape=[
            shape((3 * d_b, total, LANES), BF16),
            shape(tokens.shape, F32),
            shape((total, D), BF16),
            shape((2, D), F32),
        ],
        compiler_params=params(),
        cost_estimate=pl.CostEstimate(flops=32 * total * D * D, bytes_accessed=40 * total * D, transcendentals=0),
        name="attend_back",
    )(homes, pair_lengths, offset, qkv, att, mixed_low, lse, grad_one, every)
    input_other = lax.ppermute(input_low, "tensor", swap)
    f_s = f_b // d_b
    part = lambda n: pl.BlockSpec((n, total, LANES), lambda j, *_: (j, 0, 0))
    blocks = 2 * f_s * d_b + 4 * d_b
    grads = pl.pallas_call(
        lambda pc, *refs: grad_kernel(*refs),
        grid_spec=pltpu.PrefetchScalarGridSpec(
            num_scalar_prefetch=1,
            grid=(d_b,),
            in_specs=[
                part(f_s), whole((d_b, total, LANES)), whole((d_b, total, LANES)), part(f_s),
                pl.BlockSpec((total, D), lambda j, pc: (pc[0], 0)),
                part(3), part(1), whole((d_b, total, LANES)),
            ],
            out_specs=pl.BlockSpec((blocks, LANES, LANES), lambda j, *_: (j, 0, 0)),
        ),
        out_shape=shape((d_b * blocks, LANES, LANES), BF16),
        compiler_params=params(),
        cost_estimate=pl.CostEstimate(flops=24 * total * D * D, bytes_accessed=40 * total * D, transcendentals=0),
        name="weight_grads",
    )(piece.astype(jnp.int32).reshape(1), active_low, down_low, normed_low, up_low, tokens, merged, att, attn_low)
    return layer_whole, layer_other, input_whole, input_other, grads, row_grad, up_grad, split_grad


def split_slots(orders, counts):
    parts, at = [], 0
    for order, count in zip(orders, counts):
        if count:
            parts.append((order, at, count))
        at += count
    return parts


def index_bits(n_dp):
    dp_bits = list(range(1, n_dp.bit_length() - 1))
    return dp_bits[:1], dp_bits[1:]


def gather_orders(n_dp, spd):
    near, far = index_bits(n_dp)
    third = spd * 4 // 14
    first = (spd - third) // 2
    return split_slots(
        ([-1] + near + far, near + [-1] + far, far + [-1] + near), (first, spd - third - first, third)
    )


def scatter_orders(n_dp, spd):
    near, far = index_bits(n_dp)
    first = spd * 5 // 14
    return split_slots((far[:1] + [-1] + far[1:] + near, near + [-1] + far), (first, spd - first))


def bit_of(number, bit):
    return number // (1 << bit) % 2


def across(bit):
    if bit < 0:
        return {"tensor": 1 - lax.axis_index("tensor")}
    me = lax.axis_index("dp")
    return {"dp": me + (1 - 2 * bit_of(me, bit)) * (1 << bit)}


def place_of(order, code, core):
    dp, tensor = lax.axis_index("dp"), lax.axis_index("tensor")
    place = len(order) - 1
    to_dp, to_tensor = core, tensor
    for bit in order:
        flip = bit_of(code, place)
        if bit < 0:
            to_tensor = (tensor + flip) % 2
        else:
            to_dp = to_dp + (bit_of(dp, bit) + flip) % 2 * (1 << bit)
        place -= 1
    return to_tensor, to_dp


def slot_at(order, code, core, spd, at):
    to_tensor, to_dp = place_of(order, code, core)
    return to_tensor, to_dp * spd + at


def first_slot(order, code, core, n_dp, spd):
    to_tensor, to_dp = place_of(order, code, core)
    return (to_tensor * n_dp + to_dp) * spd


def greet(bits):
    barrier = pltpu.get_barrier_semaphore()
    for bit in bits:
        pl.semaphore_signal(barrier, inc=1, device_id=across(bit), device_id_type=pl.DeviceIdType.MESH)
    pl.semaphore_wait(barrier, len(bits))


def remote(source, target, send, recv, bit):
    return pltpu.make_async_remote_copy(
        src_ref=source, dst_ref=target, send_sem=send, recv_sem=recv,
        device_id=across(bit), device_id_type=pl.DeviceIdType.MESH,
    )


def gather_kernel(
    n_dp, spd, master_ref, vec_ref, col_ref, row_ref, order_ref, grads_ref,
    all_ref, qb_ref, vb_ref, bu_ref, homes_ref, places_ref, own_ref, both_ref, local_sem, send_sem, recv_sem, core_send, core_recv, vec_send, vec_recv):
    parts = gather_orders(n_dp, spd)
    n_bits = len(parts[0][0])
    core = bit_of(lax.axis_index("dp"), 0)
    tensor = lax.axis_index("tensor")
    greet([0] + parts[0][0])
    own_ref[...] = master_ref[0].astype(BF16)
    mine = first_slot(parts[0][0], 0, core, n_dp, spd)
    keep = pltpu.make_async_copy(own_ref, all_ref.at[pl.ds(mine, spd)], local_sem.at[0])
    keep.start()
    keep_vec = pltpu.make_async_copy(vec_ref, both_ref.at[pl.ds(tensor, 1)], local_sem.at[1])
    keep_vec.start()
    vec = remote(vec_ref, both_ref.at[pl.ds(tensor, 1)], vec_send, vec_recv, -1)
    vec.start()

    def piece(part, code, core_of):
        order, at, count = part
        return all_ref.at[pl.ds(first_slot(order, code, core_of, n_dp, spd) + at, count)]

    def forward(p, code, level, source):
        order = parts[p][0]
        for stage in range(level, n_bits):
            remote(
                source, piece(parts[p], code, core), send_sem.at[p, stage, code],
                recv_sem.at[p, code + (1 << stage)], order[n_bits - 1 - stage],
            ).start()
        remote(source, piece(parts[p], code, core), core_send.at[p, code], core_recv.at[p, code], 0).start()

    for p, part in enumerate(parts):
        forward(p, 0, 0, own_ref.at[pl.ds(part[1], part[2])])
    slots = n_dp * spd
    match = col_ref[...] == order_ref[1:2]
    slot = lax.broadcasted_iota(jnp.int32, match.shape, 0).astype(F32)
    found = jnp.sum(jnp.where(match, slot, 0.0), axis=0, keepdims=True)
    homes_ref[...] = found.astype(jnp.int32) + order_ref[0:1] * slots
    for i in range(places_ref.shape[0]):
        match = (grads_ref[:, 1:2] == row_ref[...]) & (grads_ref[:, 0:1] == i)
        index = lax.broadcasted_iota(jnp.int32, match.shape, 0).astype(F32) + 1.0
        found = jnp.sum(jnp.where(match, index, 0.0), axis=0, keepdims=True)
        places_ref[i : i + 1] = found.astype(jnp.int32) - 1
    for level in range(n_bits):
        def arrive(j, carry):
            code = (1 << level) + j
            for p, part in enumerate(parts):
                here = piece(part, code, core)
                pltpu.make_async_copy(here, here, recv_sem.at[p, code]).wait()
                forward(p, code, level + 1, here)
            return carry

        lax.fori_loop(0, 1 << level, arrive, 0)

    def drain(code, carry):
        for p, part in enumerate(parts):
            here = piece(part, code, core)
            there = piece(part, code, 1 - core)
            pltpu.make_async_copy(here, here, core_send.at[p, code]).wait()
            pltpu.make_async_copy(there, there, core_recv.at[p, code]).wait()
        return carry

    keep_vec.wait()
    vec.wait()
    pieces = both_ref.shape[0]
    head_w, ffn_w = D // pieces, FF // pieces
    for i in range(pieces):
        row = both_ref[i : i + 1]
        qb_ref[:, i * head_w : (i + 1) * head_w] = row[:, :head_w]
        vb_ref[:, i * head_w : (i + 1) * head_w] = row[:, head_w : 2 * head_w]
        bu_ref[:, i * ffn_w : (i + 1) * ffn_w] = row[:, 2 * head_w :]
    for stage in range(n_bits):
        def sent(code, carry):
            for p, part in enumerate(parts):
                here = piece(part, code, core)
                pltpu.make_async_copy(here, here, send_sem.at[p, stage, code]).wait()
            return carry

        lax.fori_loop(0, 1 << stage, sent, 0)
    lax.fori_loop(0, 1 << n_bits, drain, 0)
    keep.wait()


def gather_all(masters, vec, block_of_slot, n_dp, pieces):
    order = np.array(sum(block_home(pieces), []), np.int32)
    grads_at = np.array(grad_order(pieces), np.int32)
    spd, edge = masters.shape[1], masters.shape[-1]
    parts = gather_orders(n_dp, spd)
    n, n_bits = len(parts), len(parts[0][0])
    dma = pltpu.SemaphoreType.DMA
    vmem = pl.BlockSpec(memory_space=pltpu.VMEM)
    shape = jax.ShapeDtypeStruct
    return pl.pallas_call(
        functools.partial(gather_kernel, n_dp, spd),
        in_specs=[vmem] * 6,
        out_specs=[anywhere()] + [vmem] * 5,
        out_shape=[
            shape((pieces * n_dp * spd, edge, edge), BF16),
            shape((1, D), F32), shape((1, D), F32), shape((1, FF), F32),
            shape((1, len(order)), jnp.int32), shape((pieces, n_dp * spd), jnp.int32),
        ],
        scratch_shapes=[
            pltpu.VMEM((spd, edge, edge), BF16),
            pltpu.VMEM((pieces, vec.shape[1]), F32),
            dma((2,)), dma((n, n_bits, 1 << n_bits)), dma((n, 1 << n_bits)),
            dma((n, 1 << n_bits)), dma((n, 1 << n_bits)), dma, dma,
        ],
        compiler_params=pltpu.CompilerParams(
            vmem_limit_bytes=VMEM_LIMIT, collective_id=0, has_side_effects=True
        ),
        name="gather",
    )(masters, vec, block_of_slot[:, None], block_of_slot[None, :], jnp.asarray(order.T), jnp.asarray(grads_at))


def scatter_kernel(
    n_dp, spd, scale, places, g_ref, rg_ref, sg_ref, bg_ref, swapped, out_ref, vec_out,
    give_ref, sum_ref, in_ref, vec_sum, vec_in,
    core_send, core_recv, send_sem, recv_sem, vec_send, vec_recv,
):
    parts = scatter_orders(n_dp, spd)
    n_bits = len(parts[0][0])
    codes = 1 << n_bits
    core = bit_of(lax.axis_index("dp"), 0)
    vec_bits = [0] + parts[0][0]
    greet(vec_bits)

    def term(slot):
        place = places[slot[0], slot[1]]
        return jnp.where(place >= 0, g_ref[jnp.maximum(place, 0)], jnp.zeros(g_ref.shape[1:], BF16))

    def vec_copy(stage):
        return remote(vec_sum.at[stage], vec_in.at[stage], vec_send.at[stage], vec_recv.at[stage], vec_bits[stage])

    def vec_step(stage):
        vec_copy(stage).wait_recv()
        total = vec_sum[stage] + vec_in[stage]
        if stage + 1 < len(vec_bits):
            vec_sum[stage + 1] = total
            vec_copy(stage + 1).start()
        else:
            vec_out[...] = total * scale

    vec_sum[0, 0:6] = rg_ref[...]
    vec_sum[0, 6:8] = sg_ref[...]
    for i in range(FF // D):
        vec_sum[0, 8 + i : 9 + i] = bg_ref[:, i * D : (i + 1) * D]
    vec_sum[0, 8 + FF // D :] = jnp.zeros((VEC_ROWS - 8 - FF // D, D), F32)
    vec_copy(0).start()

    def give(p, code):
        order, at, count = parts[p]
        where = pl.ds(at, count)
        return remote(
            give_ref.at[code, where], sum_ref.at[code, where], core_send.at[p, code], core_recv.at[p, code], 0
        )

    def passed(p, level, code):
        order, at, count = parts[p]
        where = pl.ds(at, count)
        return remote(
            sum_ref.at[code, where], in_ref.at[code - 1, where],
            send_sem.at[p, code], recv_sem.at[p, code - 1], order[n_bits - 1 - level],
        )

    def hand(code):
        for p, (order, at, count) in enumerate(parts):
            start = slot_at(order, code, 1 - core, spd, at)
            for s in range(count):
                give_ref[code, at + s] = term((start[0], start[1] + s))
            give(p, code).start()

    ahead = min(4, codes)
    def first_hands(j, carry):
        hand(codes - 1 - j)
        return carry

    lax.fori_loop(0, ahead, first_hands, 0)
    vec_step(0)
    stage = 1

    def total_of(p, code, level, finish):
        order, at, count = parts[p]
        start = slot_at(order, code, core, spd, at)
        give(p, code).wait_recv()
        sources = []
        for stage in range(level + 1, n_bits):
            entry = (1 << stage) - 1 + code
            here = in_ref.at[entry, pl.ds(at, count)]
            pltpu.make_async_copy(here, here, recv_sem.at[p, entry]).wait()
            sources.append(entry)
        for s in range(count):
            value = term((start[0], start[1] + s)).astype(F32) + sum_ref[code, at + s].astype(F32)
            for entry in sources:
                value = value + in_ref[entry, at + s].astype(F32)
            if finish:
                out_ref[at + s] = value * scale
            else:
                sum_ref[code, at + s] = value.astype(BF16)

    for level in reversed(range(n_bits)):
        def onward(j, carry):
            code = (2 << level) - 1 - j
            if (1 << level) >= ahead:
                hand(code - ahead)
            for p in range(len(parts)):
                total_of(p, code, level, False)
                passed(p, level, code).start()
            return carry

        count = 1 << level
        if level == n_bits - 1 and count >= 4:
            lax.fori_loop(0, 1, onward, 0)
            vec_step(1)
            lax.fori_loop(1, 3, onward, 0)
            vec_step(2)
            lax.fori_loop(3, count, onward, 0)
            stage = 3
        else:
            lax.fori_loop(0, count, onward, 0)
        if stage < n_bits:
            vec_step(stage)
            stage += 1
    for p in range(len(parts)):
        total_of(p, 0, -1, True)
    for last in range(stage, n_bits + 1):
        vec_step(last)
    for stage in range(len(vec_bits)):
        vec_copy(stage).wait_send()

    def drain(code, carry):
        for p in range(len(parts)):
            give(p, code).wait_send()
        return carry

    lax.fori_loop(0, codes, drain, 0)
    for level in range(n_bits):
        def drain_level(j, carry):
            for p in range(len(parts)):
                passed(p, level, (1 << level) + j).wait_send()
            return carry

        lax.fori_loop(0, 1 << level, drain_level, 0)


def scatter_all(places, grads, row_grad, qv_grad, up_grad, swapped, n_dp, scale):
    edge = grads.shape[-1]
    spd = places.shape[1] // n_dp
    parts = scatter_orders(n_dp, spd)
    n, n_bits = len(parts), len(parts[0][0])
    codes = 1 << n_bits
    dma = pltpu.SemaphoreType.DMA
    vmem = pl.BlockSpec(memory_space=pltpu.VMEM)
    return pl.pallas_call(
        functools.partial(scatter_kernel, n_dp, spd, scale),
        in_specs=[smem()] + [vmem] * 4 + [anywhere()],
        out_specs=[vmem, vmem],
        out_shape=[
            jax.ShapeDtypeStruct((spd, edge, edge), F32),
            jax.ShapeDtypeStruct((VEC_ROWS, D), F32),
        ],
        scratch_shapes=[
            pltpu.VMEM((codes, spd, edge, edge), BF16),
            pltpu.VMEM((codes, spd, edge, edge), BF16),
            pltpu.VMEM((codes - 1, spd, edge, edge), BF16),
            pltpu.VMEM((n_bits + 1, VEC_ROWS, D), F32),
            pltpu.VMEM((n_bits + 1, VEC_ROWS, D), F32),
            dma((n, codes)), dma((n, codes)), dma((n, codes)), dma((n, codes)),
            dma((n_bits + 1,)), dma((n_bits + 1,)),
        ],
        compiler_params=pltpu.CompilerParams(
            vmem_limit_bytes=VMEM_LIMIT, collective_id=1, has_side_effects=True
        ),
        name="scatter",
    )(places, grads, row_grad, qv_grad, up_grad, swapped)


def adam(grad, first, second, current, outs):
    first = MOMENT_DECAY * first + (1.0 - MOMENT_DECAY) * grad
    second = MOMENT_DECAY * second + (1.0 - MOMENT_DECAY) * grad * grad
    grad_out, new_out, first_out, second_out = outs
    grad_out[...] = grad
    new_out[...] = current - VECTOR_RATE * first / (jnp.sqrt(second) + EPS_ADAM)
    first_out[...] = first
    second_out[...] = second


def update_kernel(
    piece, grad_ref, master_ref, first_ref, second_ref, left_ref, right_ref,
    layer_whole, input_whole, layer_other, input_other, vec_ref, split_ref, sf_ref, ss_ref, row_ref, rf_ref, rs_ref,
    wg_ref, new_ref, nf_ref, ns_ref, low_ref, layer_ref, input_ref, *vec_outs,
):
    step = pl.program_id(0)
    for s in range(grad_ref.shape[0]):
        left, right = left_ref[0, s].astype(BF16), right_ref[0, s].astype(BF16)
        grad = grad_ref[s]
        turned = dot_nn(dot_tn(left, grad.astype(BF16)).astype(BF16), right)
        first = MOMENT_DECAY * first_ref[0, s] + (1.0 - MOMENT_DECAY) * turned
        second = MOMENT_DECAY * second_ref[0, s] + (1.0 - MOMENT_DECAY) * turned * turned
        stepped = first / (jnp.sqrt(second) + EPS_ADAM)
        back = dot_nt(dot_nn(left, stepped.astype(BF16)).astype(BF16), right)
        new = master_ref[0, s] - LEARN_RATE * back
        wg_ref[0, s] = grad
        new_ref[0, s] = new
        nf_ref[0, s] = first
        ns_ref[0, s] = second
        low_ref[0, s] = new.astype(BF16)

    layer_ref[...] = layer_other[...]
    input_ref[...] = input_other[...].astype(F32)

    @pl.when(step == 0)
    def _():
        pieces = (2 * D + FF) // split_ref.shape[1]
        head_w, ffn_w = D // pieces, FF // pieces
        wide = jnp.concatenate([vec_ref[8 + i : 9 + i] for i in range(FF // D)], axis=1)
        grad = jnp.zeros(split_ref.shape, F32)
        for i in range(pieces):
            mine = jnp.concatenate(
                [
                    vec_ref[6:7, i * head_w : (i + 1) * head_w],
                    vec_ref[7:8, i * head_w : (i + 1) * head_w],
                    wide[:, i * ffn_w : (i + 1) * ffn_w],
                ],
                axis=1,
            )
            grad = jnp.where(piece[0] == i, mine, grad)
        adam(grad, sf_ref[...], ss_ref[...], split_ref[...], vec_outs[:4])
        adam(vec_ref[0:6], rf_ref[...], rs_ref[...], row_ref[...], vec_outs[4:])


def update_all(piece, owned, blocks, halves, summed, vectors):
    masters = blocks[0]
    spd, edge = masters.shape[1], masters.shape[-1]
    group = spd // 2
    whole = lambda a: pl.BlockSpec(a.shape, lambda i, p: tuple(0 for _ in a.shape))
    spec = pl.BlockSpec((1, group, edge, edge), lambda i, p: (0, i, 0, 0))
    rows = halves[2].shape[0] // 2
    given = pl.BlockSpec((rows, D), lambda i, p: (i, 0))
    taken = pl.BlockSpec((rows, D), lambda i, p: ((1 - p[0]) * 2 + i, 0))
    shape = jax.ShapeDtypeStruct
    vec_shapes = [shape(vectors[0].shape, F32)] * 4 + [shape(vectors[3].shape, F32)] * 4
    total = halves[0].shape[0]
    return pl.pallas_call(
        update_kernel,
        grid_spec=pltpu.PrefetchScalarGridSpec(
            num_scalar_prefetch=1,
            grid=(2,),
            in_specs=[pl.BlockSpec((group, edge, edge), lambda i, p: (i, 0, 0))]
            + [spec] * 5
            + [anywhere(), anywhere(), given, given]
            + [whole(a) for a in (summed, *vectors)],
            out_specs=[spec] * 5 + [taken, taken] + [whole(a) for a in vec_shapes],
        ),
        out_shape=[shape(masters.shape, F32)] * 4
        + [shape(masters.shape, BF16), shape((total, D), BF16), shape((total, D), F32)]
        + vec_shapes,
        input_output_aliases={7: 5, 8: 6},
        compiler_params=params(),
        name="update",
    )(piece, owned, *blocks, *halves, summed, *vectors)


def body(
    tokens,
    cotangent,
    pair_lengths,
    block_of_slot,
    masters,
    mom_first,
    mom_second,
    left_bases,
    right_bases,
    split_vec,
    split_first,
    split_second,
    row_vec,
    row_first,
    row_second,
):
    pieces = lax.axis_size("tensor")
    piece = lax.axis_index("tensor")
    n_dp = lax.axis_size("dp")
    full_seq = tokens.shape[0] // pair_lengths.shape[0]
    row_count = pair_lengths.shape[0] // pieces
    every, query_bias, value_bias, up_bias, homes, places = gather_all(
        masters, split_vec, block_of_slot, n_dp, pieces
    )
    layer_whole, layer_other, input_whole, input_other, grads, row_local, up_grad, qv_grad = layer_passes(
        tokens, cotangent, pair_lengths, piece, homes, every, query_bias, value_bias, up_bias, row_vec, row_count, full_seq
    )
    mean_scale = 1.0 / (tokens.shape[0] * n_dp)
    owned, summed = scatter_all(places, grads, row_local, qv_grad, up_grad, layer_other, n_dp, mean_scale)
    outs = update_all(
        piece.astype(jnp.int32).reshape(1),
        owned,
        (masters, mom_first, mom_second, left_bases, right_bases),
        (layer_whole, input_whole, layer_other, input_other),
        summed,
        (split_vec, split_first, split_second, row_vec, row_first, row_second),
    )
    return (outs[5], outs[6], *outs[:5], *outs[7:])


def solution(mesh):
    in_specs = (
        P("dp", None),
        P("dp", None),
        P("dp", None),
        P(),
        P("tensor", "dp", None, None),
        P("tensor", "dp", None, None),
        P("tensor", "dp", None, None),
        P("tensor", "dp", None, None),
        P("tensor", "dp", None, None),
        P("tensor", None),
        P("tensor", None),
        P("tensor", None),
        P(),
        P(),
        P(),
    )
    out_specs = (
        P("dp", None),
        P("dp", None),
        P("tensor", "dp", None, None),
        P("tensor", "dp", None, None),
        P("tensor", "dp", None, None),
        P("tensor", "dp", None, None),
        P("tensor", "dp", None, None),
        P("tensor", None),
        P("tensor", None),
        P("tensor", None),
        P("tensor", None),
        P(),
        P(),
        P(),
        P(),
    )
    return jax.shard_map(body, mesh=mesh, in_specs=in_specs, out_specs=out_specs, check_vma=False)
```

```python
import functools

import jax
import jax.numpy as jnp
from jax import lax
from jax.experimental import pallas as pl
from jax.experimental.pallas import tpu as pltpu
from jax.sharding import PartitionSpec as P
import numpy as np

D = 768
HEADS = 12
HEAD = 64
FF = 3072


EPS_NORM = 1e-05
EPS_ADAM = 1e-08
LEARN_RATE = 0.01
VECTOR_RATE = 0.15
MOMENT_DECAY = 0.5
MASKED_SCORE = -1e30
HIGHEST_PRECISION = lax.Precision.HIGHEST


def block_counts(block_edge, head_width, ffn_width):
    return (
        D // block_edge * (3 * head_width // block_edge),
        head_width // block_edge * (D // block_edge),
        D // block_edge * (ffn_width // block_edge),
        ffn_width // block_edge * (D // block_edge),
    )


LOG2E = 1.4426950408889634
LN_TWO = 0.6931471805599453
ROOT_HALF = 0.7071067811865476
PHI_SCALE = 0.3989422804014327
ERF_P = 0.3275911
ERF_A = (0.254829592, -0.284496736, 1.421413741, -1.453152027, 1.061405429)
VMEM_LIMIT = 61 * 1024 * 1024
LANES = 128
VEC_ROWS = 16
GATHER_TURNS = (
    (0, 0), (2, 0), (0, 4), (0, 2), (2, 4), (1, 0), (2, 2), (0, 1), (2, 1), (0, 3), (1, 2), (1, 1), (2, 6), (1,
    6), (1, 3), (2, 3), (1, 5), (1, 7), (2, 5), (2, 8), (2, 7), (1, 11), (2, 10), (1, 9), (0, 5), (0, 7), (1, 8),
    (0, 15), (1, 10), (2, 11), (1, 13), (0, 11), (0, 12), (2, 14), (1, 4), (0, 8), (0, 13), (1, 15), (0, 6), (2,
    9), (2, 12), (0, 10), (1, 14), (0, 9), (0, 14), (1, 12), (2, 13), (2, 15),
)
BF16 = jnp.bfloat16
F32 = jnp.float32


def dot_nn(left, right):
    return lax.dot_general(left, right, (((1,), (0,)), ((), ())), preferred_element_type=F32)


def dot_nt(left, right):
    return lax.dot_general(left, right, (((1,), (1,)), ((), ())), preferred_element_type=F32)


def dot_tn(left, right):
    return lax.dot_general(left, right, (((0,), (0,)), ((), ())), preferred_element_type=F32)


def block_home(pieces):
    d_b, f_b = D // LANES, FF // LANES
    d_p, f_p = d_b // pieces, f_b // pieces
    first = d_b * 3 * d_p
    second = first + d_p * d_b
    third = second + d_b * f_p
    qkv = [
        (n % d_b // d_p, k * 3 * d_p + n // d_b * d_p + n % d_p)
        for k in range(d_b)
        for n in range(3 * d_b)
    ]
    out = [(k // d_p, first + k % d_p * d_b + n) for k in range(d_b) for n in range(d_b)]
    up = [(n // f_p, second + k * f_p + n % f_p) for k in range(d_b) for n in range(f_b)]
    down = [(k // f_p, third + k % f_p * d_b + n) for k in range(f_b) for n in range(d_b)]
    return qkv, out, up, down


def grad_order(pieces):
    d_b, f_b = D // LANES, FF // LANES
    qkv, out, up, down = block_home(pieces)
    f_s, q_s = f_b // d_b, 3
    order = []
    for j in range(d_b):
        order += [down[(j * f_s + k) * d_b + n] for k in range(f_s) for n in range(d_b)]
        order += [up[k * f_b + j * f_s + n] for k in range(d_b) for n in range(f_s)]
        order += [qkv[k * 3 * d_b + j * q_s + n] for k in range(d_b) for n in range(q_s)]
        order += [out[j * d_b + n] for n in range(d_b)]
    return order


def start_blocks(homes, base, rows, cols, source, target, sem):
    def step(index, carry):
        k, n = index // cols, index % cols
        pltpu.make_async_copy(
            source.at[homes[0, base + index]],
            target.at[pl.ds(pl.multiple_of(k * LANES, LANES), LANES), pl.ds(pl.multiple_of(n * LANES, LANES), LANES)],
            sem,
        ).start()
        return carry

    lax.fori_loop(0, rows * cols, step, 0, unroll=6)


def wait_blocks(target, sem):
    pltpu.make_async_copy(target, target, sem).wait()


def mask_bias(ends_ref, row, seq, bias_ref):
    col = lax.broadcasted_iota(jnp.int32, (seq, 1), 0)
    lane = lax.broadcasted_iota(jnp.int32, (1, seq), 1)
    seg_col = jnp.zeros((seq, 1), jnp.int32)
    seg_lane = jnp.zeros((1, seq), jnp.int32)
    end = 0
    for k in range(ends_ref.shape[1] - 1):
        end = end + ends_ref[row, k]
        seg_col = seg_col + (col >= end).astype(jnp.int32)
        seg_lane = seg_lane + (lane >= end).astype(jnp.int32)
    bias_ref[...] = jnp.where(seg_col == seg_lane, 0.0, MASKED_SCORE)


def norm_parts(hidden):
    mean = jnp.mean(hidden, axis=-1, keepdims=True)
    centred = hidden - mean
    var = jnp.mean(centred * centred, axis=-1, keepdims=True)
    inv = lax.rsqrt(var + EPS_NORM)
    return centred * inv, inv


def norm_back(grad, gain, normed, inv):
    scaled = grad * gain
    mean = jnp.mean(scaled, axis=-1, keepdims=True)
    along = jnp.mean(scaled * normed, axis=-1, keepdims=True)
    return inv * (scaled - mean - normed * along)


def put_blocks(ref, value):
    for n in range(ref.shape[0]):
        ref[n] = value[:, n * LANES : (n + 1) * LANES]


def get_blocks(ref):
    return jnp.concatenate([ref[n] for n in range(ref.shape[0])], axis=1)


def gelu_parts(u):
    e = jnp.exp(u * u * -0.5)
    t = 1.0 / (1.0 + (ERF_P * ROOT_HALF) * jnp.abs(u))
    a1, a2, a3, a4, a5 = (0.5 * a for a in ERF_A)
    tail = ((((a5 * t + a4) * t + a3) * t + a2) * t + a1) * t * e
    cdf = jnp.where(u >= 0, 1.0 - tail, tail)
    return u * cdf, cdf + u * e * PHI_SCALE


def forward_kernel(
    homes, pairs, offset, x_any, cot_any, every, qb_ref, vb_ref, bu_ref, rv_ref,
    qkv_out, att_out, lse_ref, out_out, whole_out, nl_out, act_out, dl_out, up_out, al_out, ml_out, g1_out, rg_ref, bg_ref,
    w_ref, wo_ref, wu_ref, wd_ref, x_ref, cot_ref, qkv_ref, att_ref, bias_ref,
    nl_ref, act_ref, dl_ref, up_ref, al_ref, ml_ref, n_ref, inv_ref, acc_ref, in_sem, out_sem,
):
    d_b, f_b = D // LANES, FF // LANES
    total = x_ref.shape[0]
    seq = bias_ref.shape[0]
    row_count = total // seq
    steps = row_count * d_b
    first = pl.multiple_of(offset[0] * seq, seq)
    x_copy = pltpu.make_async_copy(x_any.at[pl.ds(first, total)], x_ref, in_sem.at[0])
    cot_copy = pltpu.make_async_copy(cot_any.at[pl.ds(first, total)], cot_ref, in_sem.at[1])
    x_copy.start()
    start_blocks(homes, 0, d_b, 3 * d_b, every, w_ref, in_sem.at[2])
    cot_copy.start()
    x_copy.wait()
    wait_blocks(w_ref, in_sem.at[2])

    outs = []

    def send(source, target):
        copy = pltpu.make_async_copy(source, target, out_sem.at[len(outs)])
        copy.start()
        outs.append(copy)

    wide = 2 * LANES
    for part in range(3):
        for c in range(0, D, wide):
            y = dot_nn(x_ref[...], w_ref[:, part * D + c : part * D + c + wide])
            if part == 0:
                y = (y + qb_ref[:, c : c + wide]).astype(BF16).astype(F32) * HEAD ** (-0.5)
            if part == 2:
                y = y + vb_ref[:, c : c + wide]
            y = y.astype(BF16)
            for n in range(2):
                qkv_ref[part * d_b + c // LANES + n] = y[:, n * LANES : (n + 1) * LANES]
    send(qkv_ref, qkv_out)
    lane = lax.broadcasted_iota(jnp.int32, (1, LANES), 1)

    def block(base, rows, cols, source, target, sem, index):
        k, n = index // cols, index % cols
        pltpu.make_async_copy(
            every.at[homes[0, base + index]],
            target.at[pl.ds(pl.multiple_of(k * LANES, LANES), LANES), pl.ds(pl.multiple_of(n * LANES, LANES), LANES)],
            sem,
        ).start()

    def fetch(step):
        for base, rows, cols, target, sem in (
            (3 * d_b * d_b, d_b, d_b, wo_ref, 3),
            (4 * d_b * d_b, d_b, f_b, wu_ref, 4),
            (4 * d_b * d_b + d_b * f_b, f_b, d_b, wd_ref, 5),
        ):
            each = rows * cols // steps
            for i in range(each):
                block(base, rows, cols, every, target, in_sem.at[sem], step * each + i)

    for r in range(row_count):
        at = slice(r * seq, (r + 1) * seq)
        mask_bias(pairs, offset[0] + r, seq, bias_ref)

        def pair(n, carry):
            fetch(r * d_b + n)
            q = qkv_ref[n, at]
            k = qkv_ref[d_b + n, at]
            v_t = qkv_ref[2 * d_b + n, at].T
            halves, all_scores = [], []
            for h in range(2):
                keep = (lane < HEAD) if h == 0 else (lane >= HEAD)
                all_scores.append(dot_nt(jnp.where(keep, k, jnp.zeros_like(k)), q) + bias_ref[...])
            for h in range(2):
                scores = all_scores[h]
                top = jnp.max(scores, axis=0, keepdims=True)
                p = jnp.exp(scores - top)
                sums = jnp.sum(p, axis=0, keepdims=True)
                lse_ref[r, 2 * n + h] = (top + jnp.log(sums)).reshape(1, seq)
                mixed = dot_nn(v_t[h * HEAD : (h + 1) * HEAD], p.astype(BF16))
                halves.append(mixed * (1.0 / sums))
            att_ref[n, at] = jnp.concatenate(halves, axis=0).T.astype(BF16)
            return carry

        lax.fori_loop(0, d_b, pair, 0, unroll=2)
    send(att_ref, att_out)
    out_bias, gain_one, shift_one, down_bias, gain_two, shift_two = (
        rv_ref[i : i + 1] for i in range(6)
    )
    rg_ref[...] = jnp.zeros_like(rg_ref)
    tile = total // 4
    tiles = [slice(t * tile, (t + 1) * tile) for t in range(4)]

    def put(ref, at, value):
        for n in range(ref.shape[0]):
            ref[n, at] = value[:, n * LANES : (n + 1) * LANES]

    def get(ref, at):
        return jnp.concatenate([ref[n, at] for n in range(ref.shape[0])], axis=1)

    wait_blocks(wo_ref, in_sem.at[3])
    for at in tiles:
        hidden = dot_nn(get(att_ref, at), wo_ref[...]) + x_ref[at].astype(F32) + out_bias
        n_one, inv_one = norm_parts(hidden)
        n_ref[at] = n_one
        inv_ref[at] = inv_one
        normed = n_one * gain_one + shift_one
        put(nl_ref, at, normed.astype(BF16))
        acc_ref[at] = normed + down_bias
    send(nl_ref, nl_out)
    wait_blocks(wu_ref, in_sem.at[4])
    wait_blocks(wd_ref, in_sem.at[5])
    wide = 768
    per = wide // LANES
    normed_low = get_blocks(nl_ref)
    for c in range(0, FF, wide):
        u = dot_nn(normed_low, wu_ref[:, c : c + wide]) + bu_ref[:, c : c + wide]
        active, slope = gelu_parts(u)
        active = active.astype(BF16)
        slope = slope.astype(BF16)
        for n in range(per):
            act_ref[c // LANES + n] = active[:, n * LANES : (n + 1) * LANES]
            up_ref[c // LANES + n] = slope[:, n * LANES : (n + 1) * LANES]
        acc_ref[...] += dot_nn(active, wd_ref[c : c + wide, :])
    send(act_ref, act_out)
    cot_copy.wait()
    for at in tiles:
        n_two, inv_two = norm_parts(acc_ref[at])
        x_ref[at] = (n_two * gain_two + shift_two).astype(BF16)
        dy = cot_ref[at].astype(F32)
        grad_two = norm_back(dy, gain_two, n_two, inv_two)
        put(dl_ref, at, grad_two.astype(BF16))
        acc_ref[at] = grad_two
        rg_ref[3:4] += jnp.sum(grad_two, axis=0, keepdims=True)
        rg_ref[4:5] += jnp.sum(dy * n_two, axis=0, keepdims=True)
        rg_ref[5:6] += jnp.sum(dy, axis=0, keepdims=True)
    send(x_ref, out_out)
    send(x_ref, whole_out.at[pl.ds(first, total)])
    send(dl_ref, dl_out)
    down_low = get_blocks(dl_ref)
    for c in range(0, FF, wide):
        blocks = range(c // LANES, c // LANES + per)
        slope = jnp.concatenate([up_ref[n] for n in blocks], axis=1).astype(F32)
        up = (dot_nt(down_low, wd_ref[c : c + wide, :]) * slope).astype(BF16)
        for i, n in enumerate(blocks):
            up_ref[n] = up[:, i * LANES : (i + 1) * LANES]
        bg_ref[:, c : c + wide] = jnp.sum(up.astype(F32), axis=0, keepdims=True)
        acc_ref[...] += dot_nt(up, wu_ref[:, c : c + wide])
    send(up_ref, up_out)
    for at in tiles:
        grad_normed = acc_ref[at]
        n_one = n_ref[at]
        rg_ref[1:2] += jnp.sum(grad_normed * n_one, axis=0, keepdims=True)
        rg_ref[2:3] += jnp.sum(grad_normed, axis=0, keepdims=True)
        grad_one = norm_back(grad_normed, gain_one, n_one, inv_ref[at])
        rg_ref[0:1] += jnp.sum(grad_one, axis=0, keepdims=True)
        acc_ref[at] = grad_one
        attn_low = grad_one.astype(BF16)
        put(al_ref, at, attn_low)
        put(ml_ref, at, dot_nt(attn_low, wo_ref[...]).astype(BF16))
    send(acc_ref, g1_out)
    send(al_ref, al_out)
    send(ml_ref, ml_out)
    for copy in outs:
        copy.wait()


def attend_back_kernel(
    homes, pairs, offset, qkv_ref, att_ref, ml_ref, lse_ref, g1_ref, every,
    merged_ref, ig_ref, il_ref, sg_ref, w_ref, bias_ref, sem,
):
    d_b = D // LANES
    row = pl.program_id(0)
    seq = g1_ref.shape[0]

    @pl.when(row == 0)
    def _():
        start_blocks(homes, 0, d_b, 3 * d_b, every, w_ref, sem)
        sg_ref[...] = jnp.zeros_like(sg_ref)

    mask_bias(pairs, offset[0] + row, seq, bias_ref)
    lane = lax.broadcasted_iota(jnp.int32, (1, LANES), 1)

    def pair(n, carry):
        q = qkv_ref[n]
        k = qkv_ref[d_b + n]
        v = qkv_ref[2 * d_b + n]
        g = ml_ref[n]
        k_t = k.T
        both = g.T.astype(F32) * att_ref[n].T.astype(F32)
        zero = jnp.zeros_like(k)
        parts, firsts = [], []
        for h in range(2):
            keep = (lane < HEAD) if h == 0 else (lane >= HEAD)
            scores = dot_nt(jnp.where(keep, k, zero), q) + bias_ref[...]
            firsts.append((scores, dot_nt(jnp.where(keep, v, zero), g)))
        for h in range(2):
            scores, gp = firsts[h]
            spread = jnp.sum(both[h * HEAD : (h + 1) * HEAD], axis=0, keepdims=True)
            p = jnp.exp(scores - lse_ref[0, 2 * n + h].reshape(1, seq))
            low = (p * (gp - spread)).astype(BF16)
            gv = dot_nn(p.astype(BF16), g)
            gk = dot_nn(low, q)
            gq = dot_nn(k_t[h * HEAD : (h + 1) * HEAD], low)
            parts.append((gq, gk, gv))
        gq = (jnp.concatenate([parts[0][0], parts[1][0]], axis=0) * HEAD ** (-0.5)).T
        merged_ref[n] = gq.astype(BF16)
        merged_ref[d_b + n] = jnp.where(lane < HEAD, parts[0][1], parts[1][1]).astype(BF16)
        merged_ref[2 * d_b + n] = jnp.where(lane < HEAD, parts[0][2], parts[1][2]).astype(BF16)
        return carry

    lax.fori_loop(0, d_b, pair, 0, unroll=2)

    @pl.when(row == 0)
    def _():
        wait_blocks(w_ref, sem)

    for n in range(d_b):
        at = slice(n * LANES, (n + 1) * LANES)
        sg_ref[0:1, at] += jnp.sum(merged_ref[n].astype(F32), axis=0, keepdims=True)
        sg_ref[1:2, at] += jnp.sum(merged_ref[2 * d_b + n].astype(F32), axis=0, keepdims=True)
    merged = get_blocks(merged_ref)
    total = g1_ref[...] + dot_nt(merged, w_ref[...])
    ig_ref[...] = total
    il_ref[...] = total.astype(BF16)


def grad_kernel(act_ref, dl_ref, nl_ref, up_ref, x_ref, merged_ref, att_ref, al_ref, g_ref):
    d_b = D // LANES
    f_s = act_ref.shape[0]
    at = 0

    def store(value, at):
        value = value.astype(BF16)
        for k in range(value.shape[0] // LANES):
            for n in range(value.shape[1] // LANES):
                g_ref[at] = value[k * LANES : (k + 1) * LANES, n * LANES : (n + 1) * LANES]
                at += 1
        return at

    at = store(dot_tn(get_blocks(act_ref), get_blocks(dl_ref)), at)
    at = store(dot_tn(get_blocks(nl_ref), get_blocks(up_ref)), at)
    at = store(dot_tn(x_ref[...], get_blocks(merged_ref)), at)
    at = store(dot_tn(att_ref[0], get_blocks(al_ref)), at)


def smem():
    return pl.BlockSpec(memory_space=pltpu.SMEM)


def anywhere():
    return pl.BlockSpec(memory_space=pl.ANY)


def params():
    return pltpu.CompilerParams(vmem_limit_bytes=VMEM_LIMIT, dimension_semantics=("arbitrary",))


def layer_passes(tokens, cotangent, pair_lengths, piece, homes, every, query_bias, value_bias, up_bias, row_vec, row_count, seq):
    d_b, f_b = D // LANES, FF // LANES
    total = row_count * seq
    shape = jax.ShapeDtypeStruct
    offset = (piece * row_count).astype(jnp.int32).reshape(1)
    stack = lambda n: pl.BlockSpec((n, seq, LANES), lambda r, *_: (0, r, 0))
    rows = pl.BlockSpec((seq, D), lambda r, *_: (r, 0))
    own = lambda at: pl.BlockSpec((seq, D), lambda r, *pre: (pre[at][0] + r, 0))
    whole = lambda s: pl.BlockSpec(s, lambda *_: tuple(0 for _ in s))
    lse_spec = pl.BlockSpec((1, HEADS, 1, seq), lambda r, *_: (r, 0, 0, 0))
    vmem = pl.BlockSpec(memory_space=pltpu.VMEM)
    tokens_bf = shape((total, D), BF16)
    stacked = lambda n: shape((n, total, LANES), BF16)
    kept = lambda n: pltpu.VMEM((n, total, LANES), BF16)
    (
        qkv, att, lse, layer_own, layer_whole, normed_low, active_low, down_low, up_low, attn_low, mixed_low, grad_one, row_grad, up_grad
    ) = pl.pallas_call(
        forward_kernel,
        in_specs=[smem()] * 3 + [anywhere()] * 3 + [vmem] * 4,
        out_specs=[anywhere()] * 2 + [vmem] + [anywhere()] * 9 + [vmem] * 2,
        out_shape=[
            stacked(3 * d_b), stacked(d_b), shape((row_count, HEADS, 1, seq), F32), tokens_bf,
            shape(tokens.shape, BF16),
            stacked(d_b), stacked(f_b), stacked(d_b), stacked(f_b), stacked(d_b), stacked(d_b),
            shape((total, D), F32), shape((6, D), F32), shape((1, FF), F32),
        ],
        scratch_shapes=[
            pltpu.VMEM((D, 3 * D), BF16), pltpu.VMEM((D, D), BF16), pltpu.VMEM((D, FF), BF16), pltpu.VMEM((FF, D), BF16),
            pltpu.VMEM((total, D), BF16), pltpu.VMEM((total, D), BF16), kept(3 * d_b), kept(d_b),
            pltpu.VMEM((seq, seq), F32), kept(d_b), kept(f_b), kept(d_b), kept(f_b), kept(d_b), kept(d_b),
            pltpu.VMEM((total, D), F32), pltpu.VMEM((total, 1), F32), pltpu.VMEM((total, D), F32),
            pltpu.SemaphoreType.DMA((6,)), pltpu.SemaphoreType.DMA((11,)),
        ],
        compiler_params=pltpu.CompilerParams(vmem_limit_bytes=VMEM_LIMIT),
        cost_estimate=pl.CostEstimate(flops=64 * total * D * D, bytes_accessed=96 * total * D, transcendentals=0),
        name="forward",
    )(homes, pair_lengths, offset, tokens, cotangent, every, query_bias, value_bias, up_bias, row_vec)
    swap = [(0, 1), (1, 0)]
    layer_other = lax.ppermute(layer_own, "tensor", swap)
    merged, input_whole, input_low, split_grad = pl.pallas_call(
        attend_back_kernel,
        grid_spec=pltpu.PrefetchScalarGridSpec(
            num_scalar_prefetch=3,
            grid=(row_count,),
            in_specs=[stack(3 * d_b), stack(d_b), stack(d_b), lse_spec, rows, anywhere()],
            out_specs=[stack(3 * d_b), own(2), rows, whole((2, D))],
            scratch_shapes=[
                pltpu.VMEM((D, 3 * D), BF16),
                pltpu.VMEM((seq, seq), F32),
                pltpu.SemaphoreType.DMA,
            ],
        ),
        out_shape=[
            shape((3 * d_b, total, LANES), BF16),
            shape(tokens.shape, F32),
            shape((total, D), BF16),
            shape((2, D), F32),
        ],
        compiler_params=params(),
        cost_estimate=pl.CostEstimate(flops=32 * total * D * D, bytes_accessed=40 * total * D, transcendentals=0),
        name="attend_back",
    )(homes, pair_lengths, offset, qkv, att, mixed_low, lse, grad_one, every)
    input_other = lax.ppermute(input_low, "tensor", swap)
    f_s = f_b // d_b
    part = lambda n: pl.BlockSpec((n, total, LANES), lambda j, *_: (j, 0, 0))
    blocks = 2 * f_s * d_b + 4 * d_b
    grads = pl.pallas_call(
        lambda pc, *refs: grad_kernel(*refs),
        grid_spec=pltpu.PrefetchScalarGridSpec(
            num_scalar_prefetch=1,
            grid=(d_b,),
            in_specs=[
                part(f_s), whole((d_b, total, LANES)), whole((d_b, total, LANES)), part(f_s),
                pl.BlockSpec((total, D), lambda j, pc: (pc[0], 0)),
                part(3), part(1), whole((d_b, total, LANES)),
            ],
            out_specs=pl.BlockSpec((blocks, LANES, LANES), lambda j, *_: (j, 0, 0)),
        ),
        out_shape=shape((d_b * blocks, LANES, LANES), BF16),
        compiler_params=params(),
        cost_estimate=pl.CostEstimate(flops=24 * total * D * D, bytes_accessed=40 * total * D, transcendentals=0),
        name="weight_grads",
    )(piece.astype(jnp.int32).reshape(1), active_low, down_low, normed_low, up_low, tokens, merged, att, attn_low)
    return layer_whole, layer_other, input_whole, input_other, grads, row_grad, up_grad, split_grad


def split_slots(orders, counts):
    parts, at = [], 0
    for order, count in zip(orders, counts):
        if count:
            parts.append((order, at, count))
        at += count
    return parts


def index_bits(n_dp):
    dp_bits = list(range(1, n_dp.bit_length() - 1))
    return dp_bits[:1], dp_bits[1:]


def gather_orders(n_dp, spd):
    near, far = index_bits(n_dp)
    first, second = spd * 3 // 14, spd * 4 // 14
    return split_slots(
        ([-1] + near + far, far[:1] + [-1] + far[1:] + near, near + [-1] + far), (first, second, spd - first - second)
    )


def scatter_orders(n_dp, spd):
    near, far = index_bits(n_dp)
    first, third = spd * 4 // 14, spd * 2 // 14
    return split_slots(
        ([-1] + far + near, near + [-1] + far, far + near + [-1]), (first, spd - third - first, third)
    )


def bit_of(number, bit):
    return number // (1 << bit) % 2


def across(bit):
    if bit < 0:
        return {"tensor": 1 - lax.axis_index("tensor")}
    me = lax.axis_index("dp")
    return {"dp": me + (1 - 2 * bit_of(me, bit)) * (1 << bit)}


def place_of(order, code, core):
    dp, tensor = lax.axis_index("dp"), lax.axis_index("tensor")
    place = len(order) - 1
    to_dp, to_tensor = core, tensor
    for bit in order:
        flip = bit_of(code, place)
        if bit < 0:
            to_tensor = (tensor + flip) % 2
        else:
            to_dp = to_dp + (bit_of(dp, bit) + flip) % 2 * (1 << bit)
        place -= 1
    return to_tensor, to_dp


def slot_at(order, code, core, spd, at):
    to_tensor, to_dp = place_of(order, code, core)
    return to_tensor, to_dp * spd + at


def first_slot(order, code, core, n_dp, spd):
    to_tensor, to_dp = place_of(order, code, core)
    return (to_tensor * n_dp + to_dp) * spd


def greet(bits):
    barrier = pltpu.get_barrier_semaphore()
    for bit in bits:
        pl.semaphore_signal(barrier, inc=1, device_id=across(bit), device_id_type=pl.DeviceIdType.MESH)
    pl.semaphore_wait(barrier, len(bits))


def remote(source, target, send, recv, bit):
    return pltpu.make_async_remote_copy(
        src_ref=source, dst_ref=target, send_sem=send, recv_sem=recv,
        device_id=across(bit), device_id_type=pl.DeviceIdType.MESH,
    )


def gather_kernel(
    n_dp, spd, master_ref, vec_ref, col_ref, row_ref, order_ref, grads_ref,
    all_ref, qb_ref, vb_ref, bu_ref, homes_ref, places_ref, own_ref, both_ref, local_sem, send_sem, recv_sem, core_send, core_recv, vec_send, vec_recv):
    parts = gather_orders(n_dp, spd)
    n_bits = len(parts[0][0])
    core = bit_of(lax.axis_index("dp"), 0)
    tensor = lax.axis_index("tensor")
    greet([0] + parts[0][0])
    own_ref[...] = master_ref[0].astype(BF16)
    mine = first_slot(parts[0][0], 0, core, n_dp, spd)
    keep = pltpu.make_async_copy(own_ref, all_ref.at[pl.ds(mine, spd)], local_sem.at[0])
    keep.start()
    keep_vec = pltpu.make_async_copy(vec_ref, both_ref.at[pl.ds(tensor, 1)], local_sem.at[1])
    keep_vec.start()
    vec = remote(vec_ref, both_ref.at[pl.ds(tensor, 1)], vec_send, vec_recv, -1)
    vec.start()

    def piece(part, code, core_of):
        order, at, count = part
        return all_ref.at[pl.ds(first_slot(order, code, core_of, n_dp, spd) + at, count)]

    def forward(p, code, level, source):
        order = parts[p][0]
        for stage in range(level, n_bits):
            remote(
                source, piece(parts[p], code, core), send_sem.at[p, stage, code],
                recv_sem.at[p, code + (1 << stage)], order[n_bits - 1 - stage],
            ).start()
        remote(source, piece(parts[p], code, core), core_send.at[p, code], core_recv.at[p, code], 0).start()

    def turn(p, code, level):
        if isinstance(code, int) and code == 0:
            forward(p, 0, 0, own_ref.at[pl.ds(parts[p][1], parts[p][2])])
        else:
            here = piece(parts[p], code, core)
            pltpu.make_async_copy(here, here, recv_sem.at[p, code]).wait()
            forward(p, code, level + 1, here)

    listed = n_bits == 4 and len(parts) == 3
    opening = [at for at in GATHER_TURNS if at[1] == 0][-1] if listed else None
    if listed:
        cut = GATHER_TURNS.index(opening) + 1
        for p, code in GATHER_TURNS[:cut]:
            turn(p, code, code.bit_length() - 1)
    else:
        for p in range(len(parts)):
            turn(p, 0, -1)
    slots = n_dp * spd
    match = col_ref[...] == order_ref[1:2]
    slot = lax.broadcasted_iota(jnp.int32, match.shape, 0).astype(F32)
    found = jnp.sum(jnp.where(match, slot, 0.0), axis=0, keepdims=True)
    homes_ref[...] = found.astype(jnp.int32) + order_ref[0:1] * slots
    for i in range(places_ref.shape[0]):
        match = (grads_ref[:, 1:2] == row_ref[...]) & (grads_ref[:, 0:1] == i)
        index = lax.broadcasted_iota(jnp.int32, match.shape, 0).astype(F32) + 1.0
        found = jnp.sum(jnp.where(match, index, 0.0), axis=0, keepdims=True)
        places_ref[i : i + 1] = found.astype(jnp.int32) - 1
    if listed:
        for p, code in GATHER_TURNS[cut:]:
            turn(p, code, code.bit_length() - 1)
    for level in range(0 if listed else n_bits):
        def arrive(j, carry):
            for p in range(len(parts)):
                turn(p, (1 << level) + j, level)
            return carry

        lax.fori_loop(0, 1 << level, arrive, 0)

    def drain(code, carry):
        for p, part in enumerate(parts):
            here = piece(part, code, core)
            there = piece(part, code, 1 - core)
            pltpu.make_async_copy(here, here, core_send.at[p, code]).wait()
            pltpu.make_async_copy(there, there, core_recv.at[p, code]).wait()
        return carry

    keep_vec.wait()
    vec.wait()
    pieces = both_ref.shape[0]
    head_w, ffn_w = D // pieces, FF // pieces
    for i in range(pieces):
        row = both_ref[i : i + 1]
        qb_ref[:, i * head_w : (i + 1) * head_w] = row[:, :head_w]
        vb_ref[:, i * head_w : (i + 1) * head_w] = row[:, head_w : 2 * head_w]
        bu_ref[:, i * ffn_w : (i + 1) * ffn_w] = row[:, 2 * head_w :]
    for stage in range(n_bits):
        def sent(code, carry):
            for p, part in enumerate(parts):
                here = piece(part, code, core)
                pltpu.make_async_copy(here, here, send_sem.at[p, stage, code]).wait()
            return carry

        lax.fori_loop(0, 1 << stage, sent, 0)
    lax.fori_loop(0, 1 << n_bits, drain, 0)
    keep.wait()


def gather_all(masters, vec, block_of_slot, n_dp, pieces):
    order = np.array(sum(block_home(pieces), []), np.int32)
    grads_at = np.array(grad_order(pieces), np.int32)
    spd, edge = masters.shape[1], masters.shape[-1]
    parts = gather_orders(n_dp, spd)
    n, n_bits = len(parts), len(parts[0][0])
    dma = pltpu.SemaphoreType.DMA
    vmem = pl.BlockSpec(memory_space=pltpu.VMEM)
    shape = jax.ShapeDtypeStruct
    return pl.pallas_call(
        functools.partial(gather_kernel, n_dp, spd),
        in_specs=[vmem] * 6,
        out_specs=[anywhere()] + [vmem] * 5,
        out_shape=[
            shape((pieces * n_dp * spd, edge, edge), BF16),
            shape((1, D), F32), shape((1, D), F32), shape((1, FF), F32),
            shape((1, len(order)), jnp.int32), shape((pieces, n_dp * spd), jnp.int32),
        ],
        scratch_shapes=[
            pltpu.VMEM((spd, edge, edge), BF16),
            pltpu.VMEM((pieces, vec.shape[1]), F32),
            dma((2,)), dma((n, n_bits, 1 << n_bits)), dma((n, 1 << n_bits)),
            dma((n, 1 << n_bits)), dma((n, 1 << n_bits)), dma, dma,
        ],
        compiler_params=pltpu.CompilerParams(
            vmem_limit_bytes=VMEM_LIMIT, collective_id=0, has_side_effects=True
        ),
        name="gather",
    )(masters, vec, block_of_slot[:, None], block_of_slot[None, :], jnp.asarray(order.T), jnp.asarray(grads_at))


def scatter_kernel(
    n_dp, spd, scale, places, g_any, rg_ref, sg_ref, bg_ref, swapped, out_ref, vec_out,
    g_ref, g_sem, give_ref, sum_ref, in_ref, vec_sum, vec_in,
    core_send, core_recv, send_sem, recv_sem, vec_send, vec_recv,
):
    parts = scatter_orders(n_dp, spd)
    n_bits = len(parts[0][0])
    codes = 1 << n_bits
    core = bit_of(lax.axis_index("dp"), 0)
    vec_bits = [0] + parts[0][0]
    grads = pltpu.make_async_copy(g_any, g_ref, g_sem)
    grads.start()
    greet(vec_bits)

    def term(slot):
        place = places[slot[0], slot[1]]
        return jnp.where(place >= 0, g_ref[jnp.maximum(place, 0)], jnp.zeros(g_ref.shape[1:], BF16))

    def vec_copy(stage):
        return remote(vec_sum.at[stage], vec_in.at[stage], vec_send.at[stage], vec_recv.at[stage], vec_bits[stage])

    def vec_step(stage):
        vec_copy(stage).wait_recv()
        total = vec_sum[stage] + vec_in[stage]
        if stage + 1 < len(vec_bits):
            vec_sum[stage + 1] = total
            vec_copy(stage + 1).start()
        else:
            vec_out[...] = total * scale

    vec_sum[0, 0:6] = rg_ref[...]
    vec_sum[0, 6:8] = sg_ref[...]
    for i in range(FF // D):
        vec_sum[0, 8 + i : 9 + i] = bg_ref[:, i * D : (i + 1) * D]
    vec_sum[0, 8 + FF // D :] = jnp.zeros((VEC_ROWS - 8 - FF // D, D), F32)
    vec_copy(0).start()

    def give(p, code):
        order, at, count = parts[p]
        where = pl.ds(at, count)
        return remote(
            give_ref.at[code, where], sum_ref.at[code, where], core_send.at[p, code], core_recv.at[p, code], 0
        )

    def passed(p, level, code):
        order, at, count = parts[p]
        where = pl.ds(at, count)
        return remote(
            sum_ref.at[code, where], in_ref.at[code - 1, where],
            send_sem.at[p, code], recv_sem.at[p, code - 1], order[n_bits - 1 - level],
        )

    def hand(code):
        for p, (order, at, count) in enumerate(parts):
            start = slot_at(order, code, 1 - core, spd, at)
            for s in range(count):
                give_ref[code, at + s] = term((start[0], start[1] + s))
            give(p, code).start()

    ahead = min(4, codes)
    grads.wait()

    def first_hands(j, carry):
        hand(codes - 1 - j)
        return carry

    lax.fori_loop(0, ahead, first_hands, 0)
    vec_step(0)
    stage = 1

    def total_of(p, code, level, finish):
        order, at, count = parts[p]
        start = slot_at(order, code, core, spd, at)
        give(p, code).wait_recv()
        sources = []
        for stage in range(level + 1, n_bits):
            entry = (1 << stage) - 1 + code
            here = in_ref.at[entry, pl.ds(at, count)]
            pltpu.make_async_copy(here, here, recv_sem.at[p, entry]).wait()
            sources.append(entry)
        for s in range(count):
            value = term((start[0], start[1] + s)).astype(F32) + sum_ref[code, at + s].astype(F32)
            for entry in sources:
                value = value + in_ref[entry, at + s].astype(F32)
            if finish:
                out_ref[at + s] = value * scale
            else:
                sum_ref[code, at + s] = value.astype(BF16)

    for level in reversed(range(n_bits)):
        def onward(j, carry):
            code = (2 << level) - 1 - j
            if (1 << level) >= ahead:
                hand(code - ahead)
            for p in range(len(parts)):
                total_of(p, code, level, False)
                passed(p, level, code).start()
            return carry

        count = 1 << level
        if level == n_bits - 1 and count >= 4:
            lax.fori_loop(0, 1, onward, 0)
            vec_step(1)
            lax.fori_loop(1, 3, onward, 0)
            vec_step(2)
            lax.fori_loop(3, count, onward, 0)
            stage = 3
        else:
            lax.fori_loop(0, count, onward, 0)
        if stage < n_bits:
            vec_step(stage)
            stage += 1
    for p in range(len(parts)):
        total_of(p, 0, -1, True)
    for last in range(stage, n_bits + 1):
        vec_step(last)
    for stage in range(len(vec_bits)):
        vec_copy(stage).wait_send()

    def drain(code, carry):
        for p in range(len(parts)):
            give(p, code).wait_send()
        return carry

    lax.fori_loop(0, codes, drain, 0)
    for level in range(n_bits):
        def drain_level(j, carry):
            for p in range(len(parts)):
                passed(p, level, (1 << level) + j).wait_send()
            return carry

        lax.fori_loop(0, 1 << level, drain_level, 0)


def scatter_all(places, grads, row_grad, qv_grad, up_grad, swapped, n_dp, scale):
    edge = grads.shape[-1]
    spd = places.shape[1] // n_dp
    parts = scatter_orders(n_dp, spd)
    n, n_bits = len(parts), len(parts[0][0])
    codes = 1 << n_bits
    dma = pltpu.SemaphoreType.DMA
    vmem = pl.BlockSpec(memory_space=pltpu.VMEM)
    return pl.pallas_call(
        functools.partial(scatter_kernel, n_dp, spd, scale),
        in_specs=[smem(), anywhere()] + [vmem] * 3 + [anywhere()],
        out_specs=[vmem, vmem],
        out_shape=[
            jax.ShapeDtypeStruct((spd, edge, edge), F32),
            jax.ShapeDtypeStruct((VEC_ROWS, D), F32),
        ],
        scratch_shapes=[
            pltpu.VMEM(grads.shape, BF16),
            dma,
            pltpu.VMEM((codes, spd, edge, edge), BF16),
            pltpu.VMEM((codes, spd, edge, edge), BF16),
            pltpu.VMEM((codes - 1, spd, edge, edge), BF16),
            pltpu.VMEM((n_bits + 1, VEC_ROWS, D), F32),
            pltpu.VMEM((n_bits + 1, VEC_ROWS, D), F32),
            dma((n, codes)), dma((n, codes)), dma((n, codes)), dma((n, codes)),
            dma((n_bits + 1,)), dma((n_bits + 1,)),
        ],
        compiler_params=pltpu.CompilerParams(
            vmem_limit_bytes=VMEM_LIMIT, collective_id=1, has_side_effects=True
        ),
        name="scatter",
    )(places, grads, row_grad, qv_grad, up_grad, swapped)


def adam(grad, first, second, current, outs):
    first = MOMENT_DECAY * first + (1.0 - MOMENT_DECAY) * grad
    second = MOMENT_DECAY * second + (1.0 - MOMENT_DECAY) * grad * grad
    grad_out, new_out, first_out, second_out = outs
    grad_out[...] = grad
    new_out[...] = current - VECTOR_RATE * first / (jnp.sqrt(second) + EPS_ADAM)
    first_out[...] = first
    second_out[...] = second


def update_kernel(
    piece, grad_ref, master_ref, first_ref, second_ref, left_ref, right_ref,
    layer_whole, input_whole, layer_other, input_other, vec_ref, split_ref, sf_ref, ss_ref, row_ref, rf_ref, rs_ref,
    wg_ref, new_ref, nf_ref, ns_ref, low_ref, layer_ref, input_ref, *vec_outs,
):
    step = pl.program_id(0)
    for s in range(grad_ref.shape[0]):
        left, right = left_ref[0, s].astype(BF16), right_ref[0, s].astype(BF16)
        grad = grad_ref[s]
        turned = dot_nn(dot_tn(left, grad.astype(BF16)).astype(BF16), right)
        first = MOMENT_DECAY * first_ref[0, s] + (1.0 - MOMENT_DECAY) * turned
        second = MOMENT_DECAY * second_ref[0, s] + (1.0 - MOMENT_DECAY) * turned * turned
        stepped = first / (jnp.sqrt(second) + EPS_ADAM)
        back = dot_nt(dot_nn(left, stepped.astype(BF16)).astype(BF16), right)
        new = master_ref[0, s] - LEARN_RATE * back
        wg_ref[0, s] = grad
        new_ref[0, s] = new
        nf_ref[0, s] = first
        ns_ref[0, s] = second
        low_ref[0, s] = new.astype(BF16)

    layer_ref[...] = layer_other[...]
    input_ref[...] = input_other[...].astype(F32)

    @pl.when(step == 0)
    def _():
        pieces = (2 * D + FF) // split_ref.shape[1]
        head_w, ffn_w = D // pieces, FF // pieces
        wide = jnp.concatenate([vec_ref[8 + i : 9 + i] for i in range(FF // D)], axis=1)
        grad = jnp.zeros(split_ref.shape, F32)
        for i in range(pieces):
            mine = jnp.concatenate(
                [
                    vec_ref[6:7, i * head_w : (i + 1) * head_w],
                    vec_ref[7:8, i * head_w : (i + 1) * head_w],
                    wide[:, i * ffn_w : (i + 1) * ffn_w],
                ],
                axis=1,
            )
            grad = jnp.where(piece[0] == i, mine, grad)
        adam(grad, sf_ref[...], ss_ref[...], split_ref[...], vec_outs[:4])
        adam(vec_ref[0:6], rf_ref[...], rs_ref[...], row_ref[...], vec_outs[4:])


def update_all(piece, owned, blocks, halves, summed, vectors):
    masters = blocks[0]
    spd, edge = masters.shape[1], masters.shape[-1]
    group = spd // 2
    whole = lambda a: pl.BlockSpec(a.shape, lambda i, p: tuple(0 for _ in a.shape))
    spec = pl.BlockSpec((1, group, edge, edge), lambda i, p: (0, i, 0, 0))
    rows = halves[2].shape[0] // 2
    given = pl.BlockSpec((rows, D), lambda i, p: (i, 0))
    taken = pl.BlockSpec((rows, D), lambda i, p: ((1 - p[0]) * 2 + i, 0))
    shape = jax.ShapeDtypeStruct
    vec_shapes = [shape(vectors[0].shape, F32)] * 4 + [shape(vectors[3].shape, F32)] * 4
    total = halves[0].shape[0]
    return pl.pallas_call(
        update_kernel,
        grid_spec=pltpu.PrefetchScalarGridSpec(
            num_scalar_prefetch=1,
            grid=(2,),
            in_specs=[pl.BlockSpec((group, edge, edge), lambda i, p: (i, 0, 0))]
            + [spec] * 5
            + [anywhere(), anywhere(), given, given]
            + [whole(a) for a in (summed, *vectors)],
            out_specs=[spec] * 5 + [taken, taken] + [whole(a) for a in vec_shapes],
        ),
        out_shape=[shape(masters.shape, F32)] * 4
        + [shape(masters.shape, BF16), shape((total, D), BF16), shape((total, D), F32)]
        + vec_shapes,
        input_output_aliases={7: 5, 8: 6},
        compiler_params=params(),
        name="update",
    )(piece, owned, *blocks, *halves, summed, *vectors)


def body(
    tokens,
    cotangent,
    pair_lengths,
    block_of_slot,
    masters,
    mom_first,
    mom_second,
    left_bases,
    right_bases,
    split_vec,
    split_first,
    split_second,
    row_vec,
    row_first,
    row_second,
):
    pieces = lax.axis_size("tensor")
    piece = lax.axis_index("tensor")
    n_dp = lax.axis_size("dp")
    full_seq = tokens.shape[0] // pair_lengths.shape[0]
    row_count = pair_lengths.shape[0] // pieces
    every, query_bias, value_bias, up_bias, homes, places = gather_all(
        masters, split_vec, block_of_slot, n_dp, pieces
    )
    layer_whole, layer_other, input_whole, input_other, grads, row_local, up_grad, qv_grad = layer_passes(
        tokens, cotangent, pair_lengths, piece, homes, every, query_bias, value_bias, up_bias, row_vec, row_count, full_seq
    )
    mean_scale = 1.0 / (tokens.shape[0] * n_dp)
    owned, summed = scatter_all(places, grads, row_local, qv_grad, up_grad, layer_other, n_dp, mean_scale)
    outs = update_all(
        piece.astype(jnp.int32).reshape(1),
        owned,
        (masters, mom_first, mom_second, left_bases, right_bases),
        (layer_whole, input_whole, layer_other, input_other),
        summed,
        (split_vec, split_first, split_second, row_vec, row_first, row_second),
    )
    return (outs[5], outs[6], *outs[:5], *outs[7:])


def solution(mesh):
    in_specs = (
        P("dp", None),
        P("dp", None),
        P("dp", None),
        P(),
        P("tensor", "dp", None, None),
        P("tensor", "dp", None, None),
        P("tensor", "dp", None, None),
        P("tensor", "dp", None, None),
        P("tensor", "dp", None, None),
        P("tensor", None),
        P("tensor", None),
        P("tensor", None),
        P(),
        P(),
        P(),
    )
    out_specs = (
        P("dp", None),
        P("dp", None),
        P("tensor", "dp", None, None),
        P("tensor", "dp", None, None),
        P("tensor", "dp", None, None),
        P("tensor", "dp", None, None),
        P("tensor", "dp", None, None),
        P("tensor", None),
        P("tensor", None),
        P("tensor", None),
        P("tensor", None),
        P(),
        P(),
        P(),
        P(),
    )
    return jax.shard_map(body, mesh=mesh, in_specs=in_specs, out_specs=out_specs, check_vma=False)
```

```python
import functools

import jax
import jax.numpy as jnp
from jax import lax
from jax.experimental import pallas as pl
from jax.experimental.pallas import tpu as pltpu
from jax.sharding import PartitionSpec as P
import numpy as np

D = 768
HEADS = 12
HEAD = 64
FF = 3072


EPS_NORM = 1e-05
EPS_ADAM = 1e-08
LEARN_RATE = 0.01
VECTOR_RATE = 0.15
MOMENT_DECAY = 0.5
MASKED_SCORE = -1e30
HIGHEST_PRECISION = lax.Precision.HIGHEST


def block_counts(block_edge, head_width, ffn_width):
    return (
        D // block_edge * (3 * head_width // block_edge),
        head_width // block_edge * (D // block_edge),
        D // block_edge * (ffn_width // block_edge),
        ffn_width // block_edge * (D // block_edge),
    )


LOG2E = 1.4426950408889634
LN_TWO = 0.6931471805599453
ROOT_HALF = 0.7071067811865476
PHI_SCALE = 0.3989422804014327
ERF_P = 0.3275911
ERF_A = (0.254829592, -0.284496736, 1.421413741, -1.453152027, 1.061405429)
VMEM_LIMIT = 61 * 1024 * 1024
LANES = 128
VEC_ROWS = 16
GATHER_TURNS = (
    (0, 0), (2, 0), (0, 4), (0, 2), (2, 4), (1, 0), (2, 2), (0, 1), (2, 1), (0, 3), (1, 2), (1, 1), (2, 6), (1,
    6), (1, 3), (2, 3), (1, 5), (1, 7), (2, 5), (2, 8), (2, 7), (1, 11), (2, 10), (1, 9), (0, 5), (0, 7), (1, 8),
    (0, 15), (1, 10), (2, 11), (1, 13), (0, 11), (0, 12), (2, 14), (1, 4), (0, 8), (0, 13), (1, 15), (0, 6), (2,
    9), (2, 12), (0, 10), (1, 14), (0, 9), (0, 14), (1, 12), (2, 13), (2, 15),
)
BF16 = jnp.bfloat16
F32 = jnp.float32


def dot_nn(left, right):
    return lax.dot_general(left, right, (((1,), (0,)), ((), ())), preferred_element_type=F32)


def dot_nt(left, right):
    return lax.dot_general(left, right, (((1,), (1,)), ((), ())), preferred_element_type=F32)


def dot_tn(left, right):
    return lax.dot_general(left, right, (((0,), (0,)), ((), ())), preferred_element_type=F32)


def block_home(pieces):
    d_b, f_b = D // LANES, FF // LANES
    d_p, f_p = d_b // pieces, f_b // pieces
    first = d_b * 3 * d_p
    second = first + d_p * d_b
    third = second + d_b * f_p
    qkv = [
        (n % d_b // d_p, k * 3 * d_p + n // d_b * d_p + n % d_p)
        for k in range(d_b)
        for n in range(3 * d_b)
    ]
    out = [(k // d_p, first + k % d_p * d_b + n) for k in range(d_b) for n in range(d_b)]
    up = [(n // f_p, second + k * f_p + n % f_p) for k in range(d_b) for n in range(f_b)]
    down = [(k // f_p, third + k % f_p * d_b + n) for k in range(f_b) for n in range(d_b)]
    return qkv, out, up, down


def grad_order(pieces):
    d_b, f_b = D // LANES, FF // LANES
    qkv, out, up, down = block_home(pieces)
    f_s, q_s = f_b // d_b, 3
    order = []
    for j in range(d_b):
        order += [down[(j * f_s + k) * d_b + n] for k in range(f_s) for n in range(d_b)]
        order += [up[k * f_b + j * f_s + n] for k in range(d_b) for n in range(f_s)]
        order += [qkv[k * 3 * d_b + j * q_s + n] for k in range(d_b) for n in range(q_s)]
        order += [out[j * d_b + n] for n in range(d_b)]
    return order


def start_blocks(homes, base, rows, cols, source, target, sem):
    def step(index, carry):
        k, n = index // cols, index % cols
        pltpu.make_async_copy(
            source.at[homes[0, base + index]],
            target.at[pl.ds(pl.multiple_of(k * LANES, LANES), LANES), pl.ds(pl.multiple_of(n * LANES, LANES), LANES)],
            sem,
        ).start()
        return carry

    lax.fori_loop(0, rows * cols, step, 0, unroll=6)


def wait_blocks(target, sem):
    pltpu.make_async_copy(target, target, sem).wait()


def mask_bias(ends_ref, row, seq, bias_ref):
    col = lax.broadcasted_iota(jnp.int32, (seq, 1), 0)
    lane = lax.broadcasted_iota(jnp.int32, (1, seq), 1)
    seg_col = jnp.zeros((seq, 1), jnp.int32)
    seg_lane = jnp.zeros((1, seq), jnp.int32)
    end = 0
    for k in range(ends_ref.shape[1] - 1):
        end = end + ends_ref[row, k]
        seg_col = seg_col + (col >= end).astype(jnp.int32)
        seg_lane = seg_lane + (lane >= end).astype(jnp.int32)
    bias_ref[...] = jnp.where(seg_col == seg_lane, 0.0, MASKED_SCORE)


def norm_parts(hidden):
    mean = jnp.mean(hidden, axis=-1, keepdims=True)
    centred = hidden - mean
    var = jnp.mean(centred * centred, axis=-1, keepdims=True)
    inv = lax.rsqrt(var + EPS_NORM)
    return centred * inv, inv


def norm_back(grad, gain, normed, inv):
    scaled = grad * gain
    mean = jnp.mean(scaled, axis=-1, keepdims=True)
    along = jnp.mean(scaled * normed, axis=-1, keepdims=True)
    return inv * (scaled - mean - normed * along)


def put_blocks(ref, value):
    for n in range(ref.shape[0]):
        ref[n] = value[:, n * LANES : (n + 1) * LANES]


def get_blocks(ref):
    return jnp.concatenate([ref[n] for n in range(ref.shape[0])], axis=1)


def gelu_parts(u):
    e = jnp.exp(u * u * -0.5)
    t = 1.0 / (1.0 + (ERF_P * ROOT_HALF) * jnp.abs(u))
    a1, a2, a3, a4, a5 = (0.5 * a for a in ERF_A)
    tail = ((((a5 * t + a4) * t + a3) * t + a2) * t + a1) * t * e
    cdf = jnp.where(u >= 0, 1.0 - tail, tail)
    return u * cdf, cdf + u * e * PHI_SCALE


def forward_kernel(
    homes, pairs, offset, x_any, cot_any, every, qb_ref, vb_ref, bu_ref, rv_ref,
    qkv_out, att_out, lse_ref, out_out, whole_out, nl_out, act_out, dl_out, up_out, al_out, ml_out, g1_out, rg_ref, bg_ref,
    w_ref, wo_ref, wu_ref, wd_ref, x_ref, cot_ref, qkv_ref, att_ref, bias_ref,
    nl_ref, act_ref, dl_ref, up_ref, al_ref, ml_ref, n_ref, inv_ref, acc_ref, in_sem, out_sem,
):
    d_b, f_b = D // LANES, FF // LANES
    total = x_ref.shape[0]
    seq = bias_ref.shape[0]
    row_count = total // seq
    steps = row_count * d_b
    first = pl.multiple_of(offset[0] * seq, seq)
    x_copy = pltpu.make_async_copy(x_any.at[pl.ds(first, total)], x_ref, in_sem.at[0])
    cot_copy = pltpu.make_async_copy(cot_any.at[pl.ds(first, total)], cot_ref, in_sem.at[1])
    x_copy.start()
    start_blocks(homes, 0, d_b, 3 * d_b, every, w_ref, in_sem.at[2])
    cot_copy.start()
    x_copy.wait()
    wait_blocks(w_ref, in_sem.at[2])

    outs = []

    def send(source, target):
        copy = pltpu.make_async_copy(source, target, out_sem.at[len(outs)])
        copy.start()
        outs.append(copy)

    wide = 2 * LANES
    for part in range(3):
        for c in range(0, D, wide):
            y = dot_nn(x_ref[...], w_ref[:, part * D + c : part * D + c + wide])
            if part == 0:
                y = (y + qb_ref[:, c : c + wide]).astype(BF16).astype(F32) * HEAD ** (-0.5)
            if part == 2:
                y = y + vb_ref[:, c : c + wide]
            y = y.astype(BF16)
            for n in range(2):
                qkv_ref[part * d_b + c // LANES + n] = y[:, n * LANES : (n + 1) * LANES]
    send(qkv_ref, qkv_out)
    lane = lax.broadcasted_iota(jnp.int32, (1, LANES), 1)

    def block(base, rows, cols, source, target, sem, index):
        k, n = index // cols, index % cols
        pltpu.make_async_copy(
            every.at[homes[0, base + index]],
            target.at[pl.ds(pl.multiple_of(k * LANES, LANES), LANES), pl.ds(pl.multiple_of(n * LANES, LANES), LANES)],
            sem,
        ).start()

    def fetch(step):
        for base, rows, cols, target, sem in (
            (3 * d_b * d_b, d_b, d_b, wo_ref, 3),
            (4 * d_b * d_b, d_b, f_b, wu_ref, 4),
            (4 * d_b * d_b + d_b * f_b, f_b, d_b, wd_ref, 5),
        ):
            each = rows * cols // steps
            for i in range(each):
                block(base, rows, cols, every, target, in_sem.at[sem], step * each + i)

    for r in range(row_count):
        at = slice(r * seq, (r + 1) * seq)
        mask_bias(pairs, offset[0] + r, seq, bias_ref)

        def pair(n, carry):
            fetch(r * d_b + n)
            q = qkv_ref[n, at]
            k = qkv_ref[d_b + n, at]
            v_t = qkv_ref[2 * d_b + n, at].T
            halves, all_scores = [], []
            for h in range(2):
                keep = (lane < HEAD) if h == 0 else (lane >= HEAD)
                all_scores.append(dot_nt(jnp.where(keep, k, jnp.zeros_like(k)), q) + bias_ref[...])
            for h in range(2):
                scores = all_scores[h]
                top = jnp.max(scores, axis=0, keepdims=True)
                p = jnp.exp(scores - top)
                sums = jnp.sum(p, axis=0, keepdims=True)
                lse_ref[r, 2 * n + h] = (top + jnp.log(sums)).reshape(1, seq)
                mixed = dot_nn(v_t[h * HEAD : (h + 1) * HEAD], p.astype(BF16))
                halves.append(mixed * (1.0 / sums))
            att_ref[n, at] = jnp.concatenate(halves, axis=0).T.astype(BF16)
            return carry

        lax.fori_loop(0, d_b, pair, 0, unroll=2)
    send(att_ref, att_out)
    out_bias, gain_one, shift_one, down_bias, gain_two, shift_two = (
        rv_ref[i : i + 1] for i in range(6)
    )
    rg_ref[...] = jnp.zeros_like(rg_ref)
    tile = total // 4
    tiles = [slice(t * tile, (t + 1) * tile) for t in range(4)]

    def put(ref, at, value):
        for n in range(ref.shape[0]):
            ref[n, at] = value[:, n * LANES : (n + 1) * LANES]

    def get(ref, at):
        return jnp.concatenate([ref[n, at] for n in range(ref.shape[0])], axis=1)

    wait_blocks(wo_ref, in_sem.at[3])
    for at in tiles:
        hidden = dot_nn(get(att_ref, at), wo_ref[...]) + x_ref[at].astype(F32) + out_bias
        n_one, inv_one = norm_parts(hidden)
        n_ref[at] = n_one
        inv_ref[at] = inv_one
        normed = n_one * gain_one + shift_one
        put(nl_ref, at, normed.astype(BF16))
        acc_ref[at] = normed + down_bias
    send(nl_ref, nl_out)
    wait_blocks(wu_ref, in_sem.at[4])
    wait_blocks(wd_ref, in_sem.at[5])
    wide = 768
    per = wide // LANES
    normed_low = get_blocks(nl_ref)
    for c in range(0, FF, wide):
        u = dot_nn(normed_low, wu_ref[:, c : c + wide]) + bu_ref[:, c : c + wide]
        active, slope = gelu_parts(u)
        active = active.astype(BF16)
        slope = slope.astype(BF16)
        for n in range(per):
            act_ref[c // LANES + n] = active[:, n * LANES : (n + 1) * LANES]
            up_ref[c // LANES + n] = slope[:, n * LANES : (n + 1) * LANES]
        acc_ref[...] += dot_nn(active, wd_ref[c : c + wide, :])
    send(act_ref, act_out)
    cot_copy.wait()
    for at in tiles:
        n_two, inv_two = norm_parts(acc_ref[at])
        x_ref[at] = (n_two * gain_two + shift_two).astype(BF16)
        dy = cot_ref[at].astype(F32)
        grad_two = norm_back(dy, gain_two, n_two, inv_two)
        put(dl_ref, at, grad_two.astype(BF16))
        acc_ref[at] = grad_two
        rg_ref[3:4] += jnp.sum(grad_two, axis=0, keepdims=True)
        rg_ref[4:5] += jnp.sum(dy * n_two, axis=0, keepdims=True)
        rg_ref[5:6] += jnp.sum(dy, axis=0, keepdims=True)
    send(x_ref, out_out)
    send(x_ref, whole_out.at[pl.ds(first, total)])
    send(dl_ref, dl_out)
    down_low = get_blocks(dl_ref)
    for c in range(0, FF, wide):
        blocks = range(c // LANES, c // LANES + per)
        slope = jnp.concatenate([up_ref[n] for n in blocks], axis=1).astype(F32)
        up = (dot_nt(down_low, wd_ref[c : c + wide, :]) * slope).astype(BF16)
        for i, n in enumerate(blocks):
            up_ref[n] = up[:, i * LANES : (i + 1) * LANES]
        bg_ref[:, c : c + wide] = jnp.sum(up.astype(F32), axis=0, keepdims=True)
        acc_ref[...] += dot_nt(up, wu_ref[:, c : c + wide])
    send(up_ref, up_out)
    for at in tiles:
        grad_normed = acc_ref[at]
        n_one = n_ref[at]
        rg_ref[1:2] += jnp.sum(grad_normed * n_one, axis=0, keepdims=True)
        rg_ref[2:3] += jnp.sum(grad_normed, axis=0, keepdims=True)
        grad_one = norm_back(grad_normed, gain_one, n_one, inv_ref[at])
        rg_ref[0:1] += jnp.sum(grad_one, axis=0, keepdims=True)
        acc_ref[at] = grad_one
        attn_low = grad_one.astype(BF16)
        put(al_ref, at, attn_low)
        put(ml_ref, at, dot_nt(attn_low, wo_ref[...]).astype(BF16))
    send(acc_ref, g1_out)
    send(al_ref, al_out)
    send(ml_ref, ml_out)
    for copy in outs:
        copy.wait()


def attend_back_kernel(
    homes, pairs, offset, qkv_ref, att_ref, ml_ref, lse_ref, g1_ref, every,
    merged_ref, ig_ref, il_ref, sg_ref, w_ref, bias_ref, sem,
):
    d_b = D // LANES
    row = pl.program_id(0)
    seq = g1_ref.shape[0]

    @pl.when(row == 0)
    def _():
        start_blocks(homes, 0, d_b, 3 * d_b, every, w_ref, sem)
        sg_ref[...] = jnp.zeros_like(sg_ref)

    mask_bias(pairs, offset[0] + row, seq, bias_ref)
    lane = lax.broadcasted_iota(jnp.int32, (1, LANES), 1)

    def pair(n, carry):
        q = qkv_ref[n]
        k = qkv_ref[d_b + n]
        v = qkv_ref[2 * d_b + n]
        g = ml_ref[n]
        k_t = k.T
        both = g.T.astype(F32) * att_ref[n].T.astype(F32)
        zero = jnp.zeros_like(k)
        parts, firsts = [], []
        for h in range(2):
            keep = (lane < HEAD) if h == 0 else (lane >= HEAD)
            scores = dot_nt(jnp.where(keep, k, zero), q) + bias_ref[...]
            firsts.append((scores, dot_nt(jnp.where(keep, v, zero), g)))
        for h in range(2):
            scores, gp = firsts[h]
            spread = jnp.sum(both[h * HEAD : (h + 1) * HEAD], axis=0, keepdims=True)
            p = jnp.exp(scores - lse_ref[0, 2 * n + h].reshape(1, seq))
            low = (p * (gp - spread)).astype(BF16)
            gv = dot_nn(p.astype(BF16), g)
            gk = dot_nn(low, q)
            gq = dot_nn(k_t[h * HEAD : (h + 1) * HEAD], low)
            parts.append((gq, gk, gv))
        gq = (jnp.concatenate([parts[0][0], parts[1][0]], axis=0) * HEAD ** (-0.5)).T
        merged_ref[n] = gq.astype(BF16)
        merged_ref[d_b + n] = jnp.where(lane < HEAD, parts[0][1], parts[1][1]).astype(BF16)
        merged_ref[2 * d_b + n] = jnp.where(lane < HEAD, parts[0][2], parts[1][2]).astype(BF16)
        return carry

    lax.fori_loop(0, d_b, pair, 0, unroll=2)

    @pl.when(row == 0)
    def _():
        wait_blocks(w_ref, sem)

    for n in range(d_b):
        at = slice(n * LANES, (n + 1) * LANES)
        sg_ref[0:1, at] += jnp.sum(merged_ref[n].astype(F32), axis=0, keepdims=True)
        sg_ref[1:2, at] += jnp.sum(merged_ref[2 * d_b + n].astype(F32), axis=0, keepdims=True)
    merged = get_blocks(merged_ref)
    total = g1_ref[...] + dot_nt(merged, w_ref[...])
    ig_ref[...] = total
    il_ref[...] = total.astype(BF16)


def grad_kernel(act_ref, dl_ref, nl_ref, up_ref, x_ref, merged_ref, att_ref, al_ref, g_ref):
    d_b = D // LANES
    f_s = act_ref.shape[0]
    at = 0

    def store(value, at):
        value = value.astype(BF16)
        for k in range(value.shape[0] // LANES):
            for n in range(value.shape[1] // LANES):
                g_ref[at] = value[k * LANES : (k + 1) * LANES, n * LANES : (n + 1) * LANES]
                at += 1
        return at

    at = store(dot_tn(get_blocks(act_ref), get_blocks(dl_ref)), at)
    at = store(dot_tn(get_blocks(nl_ref), get_blocks(up_ref)), at)
    at = store(dot_tn(x_ref[...], get_blocks(merged_ref)), at)
    at = store(dot_tn(att_ref[0], get_blocks(al_ref)), at)


def smem():
    return pl.BlockSpec(memory_space=pltpu.SMEM)


def anywhere():
    return pl.BlockSpec(memory_space=pl.ANY)


def params():
    return pltpu.CompilerParams(vmem_limit_bytes=VMEM_LIMIT, dimension_semantics=("arbitrary",))


def layer_passes(tokens, cotangent, pair_lengths, piece, homes, every, query_bias, value_bias, up_bias, row_vec, row_count, seq):
    d_b, f_b = D // LANES, FF // LANES
    total = row_count * seq
    shape = jax.ShapeDtypeStruct
    offset = (piece * row_count).astype(jnp.int32).reshape(1)
    stack = lambda n: pl.BlockSpec((n, seq, LANES), lambda r, *_: (0, r, 0))
    rows = pl.BlockSpec((seq, D), lambda r, *_: (r, 0))
    own = lambda at: pl.BlockSpec((seq, D), lambda r, *pre: (pre[at][0] + r, 0))
    whole = lambda s: pl.BlockSpec(s, lambda *_: tuple(0 for _ in s))
    lse_spec = pl.BlockSpec((1, HEADS, 1, seq), lambda r, *_: (r, 0, 0, 0))
    vmem = pl.BlockSpec(memory_space=pltpu.VMEM)
    tokens_bf = shape((total, D), BF16)
    stacked = lambda n: shape((n, total, LANES), BF16)
    kept = lambda n: pltpu.VMEM((n, total, LANES), BF16)
    (
        qkv, att, lse, layer_own, layer_whole, normed_low, active_low, down_low, up_low, attn_low, mixed_low, grad_one, row_grad, up_grad
    ) = pl.pallas_call(
        forward_kernel,
        in_specs=[smem()] * 3 + [anywhere()] * 3 + [vmem] * 4,
        out_specs=[anywhere()] * 2 + [vmem] + [anywhere()] * 9 + [vmem] * 2,
        out_shape=[
            stacked(3 * d_b), stacked(d_b), shape((row_count, HEADS, 1, seq), F32), tokens_bf,
            shape(tokens.shape, BF16),
            stacked(d_b), stacked(f_b), stacked(d_b), stacked(f_b), stacked(d_b), stacked(d_b),
            shape((total, D), F32), shape((6, D), F32), shape((1, FF), F32),
        ],
        scratch_shapes=[
            pltpu.VMEM((D, 3 * D), BF16), pltpu.VMEM((D, D), BF16), pltpu.VMEM((D, FF), BF16), pltpu.VMEM((FF, D), BF16),
            pltpu.VMEM((total, D), BF16), pltpu.VMEM((total, D), BF16), kept(3 * d_b), kept(d_b),
            pltpu.VMEM((seq, seq), F32), kept(d_b), kept(f_b), kept(d_b), kept(f_b), kept(d_b), kept(d_b),
            pltpu.VMEM((total, D), F32), pltpu.VMEM((total, 1), F32), pltpu.VMEM((total, D), F32),
            pltpu.SemaphoreType.DMA((6,)), pltpu.SemaphoreType.DMA((11,)),
        ],
        compiler_params=pltpu.CompilerParams(vmem_limit_bytes=VMEM_LIMIT),
        cost_estimate=pl.CostEstimate(flops=64 * total * D * D, bytes_accessed=96 * total * D, transcendentals=0),
        name="forward",
    )(homes, pair_lengths, offset, tokens, cotangent, every, query_bias, value_bias, up_bias, row_vec)
    swap = [(0, 1), (1, 0)]
    layer_other = lax.ppermute(layer_own, "tensor", swap)
    merged, input_whole, input_low, split_grad = pl.pallas_call(
        attend_back_kernel,
        grid_spec=pltpu.PrefetchScalarGridSpec(
            num_scalar_prefetch=3,
            grid=(row_count,),
            in_specs=[stack(3 * d_b), stack(d_b), stack(d_b), lse_spec, rows, anywhere()],
            out_specs=[stack(3 * d_b), own(2), rows, whole((2, D))],
            scratch_shapes=[
                pltpu.VMEM((D, 3 * D), BF16),
                pltpu.VMEM((seq, seq), F32),
                pltpu.SemaphoreType.DMA,
            ],
        ),
        out_shape=[
            shape((3 * d_b, total, LANES), BF16),
            shape(tokens.shape, F32),
            shape((total, D), BF16),
            shape((2, D), F32),
        ],
        compiler_params=params(),
        cost_estimate=pl.CostEstimate(flops=32 * total * D * D, bytes_accessed=40 * total * D, transcendentals=0),
        name="attend_back",
    )(homes, pair_lengths, offset, qkv, att, mixed_low, lse, grad_one, every)
    input_other = lax.ppermute(input_low, "tensor", swap)
    f_s = f_b // d_b
    part = lambda n: pl.BlockSpec((n, total, LANES), lambda j, *_: (j, 0, 0))
    blocks = 2 * f_s * d_b + 4 * d_b
    grads = pl.pallas_call(
        lambda pc, *refs: grad_kernel(*refs),
        grid_spec=pltpu.PrefetchScalarGridSpec(
            num_scalar_prefetch=1,
            grid=(d_b,),
            in_specs=[
                part(f_s), whole((d_b, total, LANES)), whole((d_b, total, LANES)), part(f_s),
                pl.BlockSpec((total, D), lambda j, pc: (pc[0], 0)),
                part(3), part(1), whole((d_b, total, LANES)),
            ],
            out_specs=pl.BlockSpec((blocks, LANES, LANES), lambda j, *_: (j, 0, 0)),
        ),
        out_shape=shape((d_b * blocks, LANES, LANES), BF16),
        compiler_params=params(),
        cost_estimate=pl.CostEstimate(flops=24 * total * D * D, bytes_accessed=40 * total * D, transcendentals=0),
        name="weight_grads",
    )(piece.astype(jnp.int32).reshape(1), active_low, down_low, normed_low, up_low, tokens, merged, att, attn_low)
    return layer_whole, layer_other, input_whole, input_other, grads, row_grad, up_grad, split_grad


def split_slots(orders, counts):
    parts, at = [], 0
    for order, count in zip(orders, counts):
        if count:
            parts.append((order, at, count))
        at += count
    return parts


def index_bits(n_dp):
    dp_bits = list(range(1, n_dp.bit_length() - 1))
    return dp_bits[:1], dp_bits[1:]


def gather_orders(n_dp, spd):
    near, far = index_bits(n_dp)
    first, second = spd * 3 // 14, spd * 4 // 14
    return split_slots(
        ([-1] + near + far, far[:1] + [-1] + far[1:] + near, near + [-1] + far), (first, second, spd - first - second)
    )


def scatter_orders(n_dp, spd):
    near, far = index_bits(n_dp)
    first = spd * 5 // 14
    return split_slots((far[:1] + [-1] + far[1:] + near, near + [-1] + far), (first, spd - first))


def bit_of(number, bit):
    return number // (1 << bit) % 2


def across(bit):
    if bit < 0:
        return {"tensor": 1 - lax.axis_index("tensor")}
    me = lax.axis_index("dp")
    return {"dp": me + (1 - 2 * bit_of(me, bit)) * (1 << bit)}


def place_of(order, code, core):
    dp, tensor = lax.axis_index("dp"), lax.axis_index("tensor")
    place = len(order) - 1
    to_dp, to_tensor = core, tensor
    for bit in order:
        flip = bit_of(code, place)
        if bit < 0:
            to_tensor = (tensor + flip) % 2
        else:
            to_dp = to_dp + (bit_of(dp, bit) + flip) % 2 * (1 << bit)
        place -= 1
    return to_tensor, to_dp


def slot_at(order, code, core, spd, at):
    to_tensor, to_dp = place_of(order, code, core)
    return to_tensor, to_dp * spd + at


def first_slot(order, code, core, n_dp, spd):
    to_tensor, to_dp = place_of(order, code, core)
    return (to_tensor * n_dp + to_dp) * spd


def greet(bits):
    barrier = pltpu.get_barrier_semaphore()
    for bit in bits:
        pl.semaphore_signal(barrier, inc=1, device_id=across(bit), device_id_type=pl.DeviceIdType.MESH)
    pl.semaphore_wait(barrier, len(bits))


def remote(source, target, send, recv, bit):
    return pltpu.make_async_remote_copy(
        src_ref=source, dst_ref=target, send_sem=send, recv_sem=recv,
        device_id=across(bit), device_id_type=pl.DeviceIdType.MESH,
    )


def gather_kernel(
    n_dp, spd, master_ref, vec_ref, col_ref, row_ref, order_ref, grads_ref,
    all_ref, qb_ref, vb_ref, bu_ref, homes_ref, places_ref, own_ref, both_ref, local_sem, send_sem, recv_sem, core_send, core_recv, vec_send, vec_recv):
    parts = gather_orders(n_dp, spd)
    n_bits = len(parts[0][0])
    core = bit_of(lax.axis_index("dp"), 0)
    tensor = lax.axis_index("tensor")
    greet([0] + parts[0][0])
    own_ref[...] = master_ref[0].astype(BF16)
    mine = first_slot(parts[0][0], 0, core, n_dp, spd)
    keep = pltpu.make_async_copy(own_ref, all_ref.at[pl.ds(mine, spd)], local_sem.at[0])
    keep.start()
    keep_vec = pltpu.make_async_copy(vec_ref, both_ref.at[pl.ds(tensor, 1)], local_sem.at[1])
    keep_vec.start()
    vec = remote(vec_ref, both_ref.at[pl.ds(tensor, 1)], vec_send, vec_recv, -1)
    vec.start()

    def piece(part, code, core_of):
        order, at, count = part
        return all_ref.at[pl.ds(first_slot(order, code, core_of, n_dp, spd) + at, count)]

    def forward(p, code, level, source):
        order = parts[p][0]
        for stage in range(level, n_bits):
            remote(
                source, piece(parts[p], code, core), send_sem.at[p, stage, code],
                recv_sem.at[p, code + (1 << stage)], order[n_bits - 1 - stage],
            ).start()
        remote(source, piece(parts[p], code, core), core_send.at[p, code], core_recv.at[p, code], 0).start()

    def turn(p, code, level):
        if isinstance(code, int) and code == 0:
            forward(p, 0, 0, own_ref.at[pl.ds(parts[p][1], parts[p][2])])
        else:
            here = piece(parts[p], code, core)
            pltpu.make_async_copy(here, here, recv_sem.at[p, code]).wait()
            forward(p, code, level + 1, here)

    listed = n_bits == 4 and len(parts) == 3
    opening = [at for at in GATHER_TURNS if at[1] == 0][-1] if listed else None
    if listed:
        cut = GATHER_TURNS.index(opening) + 1
        for p, code in GATHER_TURNS[:cut]:
            turn(p, code, code.bit_length() - 1)
    else:
        for p in range(len(parts)):
            turn(p, 0, -1)
    slots = n_dp * spd
    match = col_ref[...] == order_ref[1:2]
    slot = lax.broadcasted_iota(jnp.int32, match.shape, 0).astype(F32)
    found = jnp.sum(jnp.where(match, slot, 0.0), axis=0, keepdims=True)
    homes_ref[...] = found.astype(jnp.int32) + order_ref[0:1] * slots
    for i in range(places_ref.shape[0]):
        match = (grads_ref[:, 1:2] == row_ref[...]) & (grads_ref[:, 0:1] == i)
        index = lax.broadcasted_iota(jnp.int32, match.shape, 0).astype(F32) + 1.0
        found = jnp.sum(jnp.where(match, index, 0.0), axis=0, keepdims=True)
        places_ref[i : i + 1] = found.astype(jnp.int32) - 1
    if listed:
        for p, code in GATHER_TURNS[cut:]:
            turn(p, code, code.bit_length() - 1)
    for level in range(0 if listed else n_bits):
        def arrive(j, carry):
            for p in range(len(parts)):
                turn(p, (1 << level) + j, level)
            return carry

        lax.fori_loop(0, 1 << level, arrive, 0)

    def drain(code, carry):
        for p, part in enumerate(parts):
            here = piece(part, code, core)
            there = piece(part, code, 1 - core)
            pltpu.make_async_copy(here, here, core_send.at[p, code]).wait()
            pltpu.make_async_copy(there, there, core_recv.at[p, code]).wait()
        return carry

    keep_vec.wait()
    vec.wait()
    pieces = both_ref.shape[0]
    head_w, ffn_w = D // pieces, FF // pieces
    for i in range(pieces):
        row = both_ref[i : i + 1]
        qb_ref[:, i * head_w : (i + 1) * head_w] = row[:, :head_w]
        vb_ref[:, i * head_w : (i + 1) * head_w] = row[:, head_w : 2 * head_w]
        bu_ref[:, i * ffn_w : (i + 1) * ffn_w] = row[:, 2 * head_w :]
    for stage in range(n_bits):
        def sent(code, carry):
            for p, part in enumerate(parts):
                here = piece(part, code, core)
                pltpu.make_async_copy(here, here, send_sem.at[p, stage, code]).wait()
            return carry

        lax.fori_loop(0, 1 << stage, sent, 0)
    lax.fori_loop(0, 1 << n_bits, drain, 0)
    keep.wait()


def gather_all(masters, vec, block_of_slot, n_dp, pieces):
    order = np.array(sum(block_home(pieces), []), np.int32)
    grads_at = np.array(grad_order(pieces), np.int32)
    spd, edge = masters.shape[1], masters.shape[-1]
    parts = gather_orders(n_dp, spd)
    n, n_bits = len(parts), len(parts[0][0])
    dma = pltpu.SemaphoreType.DMA
    vmem = pl.BlockSpec(memory_space=pltpu.VMEM)
    shape = jax.ShapeDtypeStruct
    return pl.pallas_call(
        functools.partial(gather_kernel, n_dp, spd),
        in_specs=[vmem] * 6,
        out_specs=[anywhere()] + [vmem] * 5,
        out_shape=[
            shape((pieces * n_dp * spd, edge, edge), BF16),
            shape((1, D), F32), shape((1, D), F32), shape((1, FF), F32),
            shape((1, len(order)), jnp.int32), shape((pieces, n_dp * spd), jnp.int32),
        ],
        scratch_shapes=[
            pltpu.VMEM((spd, edge, edge), BF16),
            pltpu.VMEM((pieces, vec.shape[1]), F32),
            dma((2,)), dma((n, n_bits, 1 << n_bits)), dma((n, 1 << n_bits)),
            dma((n, 1 << n_bits)), dma((n, 1 << n_bits)), dma, dma,
        ],
        compiler_params=pltpu.CompilerParams(
            vmem_limit_bytes=VMEM_LIMIT, collective_id=0, has_side_effects=True
        ),
        name="gather",
    )(masters, vec, block_of_slot[:, None], block_of_slot[None, :], jnp.asarray(order.T), jnp.asarray(grads_at))


def scatter_kernel(
    n_dp, spd, scale, places, g_any, rg_ref, sg_ref, bg_ref, swapped, out_ref, vec_out,
    g_ref, g_sem, give_ref, sum_ref, in_ref, vec_sum, vec_in,
    core_send, core_recv, send_sem, recv_sem, vec_send, vec_recv,
):
    parts = scatter_orders(n_dp, spd)
    n_bits = len(parts[0][0])
    codes = 1 << n_bits
    core = bit_of(lax.axis_index("dp"), 0)
    vec_bits = [0] + parts[0][0]
    grads = pltpu.make_async_copy(g_any, g_ref, g_sem)
    grads.start()
    greet(vec_bits)

    def term(slot):
        place = places[slot[0], slot[1]]
        return jnp.where(place >= 0, g_ref[jnp.maximum(place, 0)], jnp.zeros(g_ref.shape[1:], BF16))

    def vec_copy(stage):
        return remote(vec_sum.at[stage], vec_in.at[stage], vec_send.at[stage], vec_recv.at[stage], vec_bits[stage])

    def vec_step(stage):
        vec_copy(stage).wait_recv()
        total = vec_sum[stage] + vec_in[stage]
        if stage + 1 < len(vec_bits):
            vec_sum[stage + 1] = total
            vec_copy(stage + 1).start()
        else:
            vec_out[...] = total * scale

    vec_sum[0, 0:6] = rg_ref[...]
    vec_sum[0, 6:8] = sg_ref[...]
    for i in range(FF // D):
        vec_sum[0, 8 + i : 9 + i] = bg_ref[:, i * D : (i + 1) * D]
    vec_sum[0, 8 + FF // D :] = jnp.zeros((VEC_ROWS - 8 - FF // D, D), F32)
    vec_copy(0).start()

    def give(p, code):
        order, at, count = parts[p]
        where = pl.ds(at, count)
        return remote(
            give_ref.at[code, where], sum_ref.at[code, where], core_send.at[p, code], core_recv.at[p, code], 0
        )

    def passed(p, level, code):
        order, at, count = parts[p]
        where = pl.ds(at, count)
        return remote(
            sum_ref.at[code, where], in_ref.at[code - 1, where],
            send_sem.at[p, code], recv_sem.at[p, code - 1], order[n_bits - 1 - level],
        )

    def hand(code):
        for p, (order, at, count) in enumerate(parts):
            start = slot_at(order, code, 1 - core, spd, at)
            for s in range(count):
                give_ref[code, at + s] = term((start[0], start[1] + s))
            give(p, code).start()

    ahead = min(4, codes)
    grads.wait()

    def first_hands(j, carry):
        hand(codes - 1 - j)
        return carry

    lax.fori_loop(0, ahead, first_hands, 0)
    vec_step(0)
    stage = 1

    def total_of(p, code, level, finish):
        order, at, count = parts[p]
        start = slot_at(order, code, core, spd, at)
        give(p, code).wait_recv()
        sources = []
        for stage in range(level + 1, n_bits):
            entry = (1 << stage) - 1 + code
            here = in_ref.at[entry, pl.ds(at, count)]
            pltpu.make_async_copy(here, here, recv_sem.at[p, entry]).wait()
            sources.append(entry)
        for s in range(count):
            value = term((start[0], start[1] + s)).astype(F32) + sum_ref[code, at + s].astype(F32)
            for entry in sources:
                value = value + in_ref[entry, at + s].astype(F32)
            if finish:
                out_ref[at + s] = value * scale
            else:
                sum_ref[code, at + s] = value.astype(BF16)

    for level in reversed(range(n_bits)):
        def onward(j, carry):
            code = (2 << level) - 1 - j
            if (1 << level) >= ahead:
                hand(code - ahead)
            for p in range(len(parts)):
                total_of(p, code, level, False)
                passed(p, level, code).start()
            return carry

        count = 1 << level
        if level == n_bits - 1 and count >= 4:
            lax.fori_loop(0, 1, onward, 0)
            vec_step(1)
            lax.fori_loop(1, 3, onward, 0)
            vec_step(2)
            lax.fori_loop(3, count, onward, 0)
            stage = 3
        else:
            lax.fori_loop(0, count, onward, 0)
        if stage < n_bits:
            vec_step(stage)
            stage += 1
    for p in range(len(parts)):
        total_of(p, 0, -1, True)
    for last in range(stage, n_bits + 1):
        vec_step(last)
    for stage in range(len(vec_bits)):
        vec_copy(stage).wait_send()

    def drain(code, carry):
        for p in range(len(parts)):
            give(p, code).wait_send()
        return carry

    lax.fori_loop(0, codes, drain, 0)
    for level in range(n_bits):
        def drain_level(j, carry):
            for p in range(len(parts)):
                passed(p, level, (1 << level) + j).wait_send()
            return carry

        lax.fori_loop(0, 1 << level, drain_level, 0)


def scatter_all(places, grads, row_grad, qv_grad, up_grad, swapped, n_dp, scale):
    edge = grads.shape[-1]
    spd = places.shape[1] // n_dp
    parts = scatter_orders(n_dp, spd)
    n, n_bits = len(parts), len(parts[0][0])
    codes = 1 << n_bits
    dma = pltpu.SemaphoreType.DMA
    vmem = pl.BlockSpec(memory_space=pltpu.VMEM)
    return pl.pallas_call(
        functools.partial(scatter_kernel, n_dp, spd, scale),
        in_specs=[smem(), anywhere()] + [vmem] * 3 + [anywhere()],
        out_specs=[vmem, vmem],
        out_shape=[
            jax.ShapeDtypeStruct((spd, edge, edge), F32),
            jax.ShapeDtypeStruct((VEC_ROWS, D), F32),
        ],
        scratch_shapes=[
            pltpu.VMEM(grads.shape, BF16),
            dma,
            pltpu.VMEM((codes, spd, edge, edge), BF16),
            pltpu.VMEM((codes, spd, edge, edge), BF16),
            pltpu.VMEM((codes - 1, spd, edge, edge), BF16),
            pltpu.VMEM((n_bits + 1, VEC_ROWS, D), F32),
            pltpu.VMEM((n_bits + 1, VEC_ROWS, D), F32),
            dma((n, codes)), dma((n, codes)), dma((n, codes)), dma((n, codes)),
            dma((n_bits + 1,)), dma((n_bits + 1,)),
        ],
        compiler_params=pltpu.CompilerParams(
            vmem_limit_bytes=VMEM_LIMIT, collective_id=1, has_side_effects=True
        ),
        name="scatter",
    )(places, grads, row_grad, qv_grad, up_grad, swapped)


def adam(grad, first, second, current, outs):
    first = MOMENT_DECAY * first + (1.0 - MOMENT_DECAY) * grad
    second = MOMENT_DECAY * second + (1.0 - MOMENT_DECAY) * grad * grad
    grad_out, new_out, first_out, second_out = outs
    grad_out[...] = grad
    new_out[...] = current - VECTOR_RATE * first / (jnp.sqrt(second) + EPS_ADAM)
    first_out[...] = first
    second_out[...] = second


def update_kernel(
    piece, grad_ref, master_ref, first_ref, second_ref, left_ref, right_ref,
    layer_whole, input_whole, layer_other, input_other, vec_ref, split_ref, sf_ref, ss_ref, row_ref, rf_ref, rs_ref,
    wg_ref, new_ref, nf_ref, ns_ref, low_ref, layer_ref, input_ref, *vec_outs,
):
    step = pl.program_id(0)
    for s in range(grad_ref.shape[0]):
        left, right = left_ref[0, s].astype(BF16), right_ref[0, s].astype(BF16)
        grad = grad_ref[s]
        turned = dot_nn(dot_tn(left, grad.astype(BF16)).astype(BF16), right)
        first = MOMENT_DECAY * first_ref[0, s] + (1.0 - MOMENT_DECAY) * turned
        second = MOMENT_DECAY * second_ref[0, s] + (1.0 - MOMENT_DECAY) * turned * turned
        stepped = first / (jnp.sqrt(second) + EPS_ADAM)
        back = dot_nt(dot_nn(left, stepped.astype(BF16)).astype(BF16), right)
        new = master_ref[0, s] - LEARN_RATE * back
        wg_ref[0, s] = grad
        new_ref[0, s] = new
        nf_ref[0, s] = first
        ns_ref[0, s] = second
        low_ref[0, s] = new.astype(BF16)

    layer_ref[...] = layer_other[...]
    input_ref[...] = input_other[...].astype(F32)

    @pl.when(step == 0)
    def _():
        pieces = (2 * D + FF) // split_ref.shape[1]
        head_w, ffn_w = D // pieces, FF // pieces
        wide = jnp.concatenate([vec_ref[8 + i : 9 + i] for i in range(FF // D)], axis=1)
        grad = jnp.zeros(split_ref.shape, F32)
        for i in range(pieces):
            mine = jnp.concatenate(
                [
                    vec_ref[6:7, i * head_w : (i + 1) * head_w],
                    vec_ref[7:8, i * head_w : (i + 1) * head_w],
                    wide[:, i * ffn_w : (i + 1) * ffn_w],
                ],
                axis=1,
            )
            grad = jnp.where(piece[0] == i, mine, grad)
        adam(grad, sf_ref[...], ss_ref[...], split_ref[...], vec_outs[:4])
        adam(vec_ref[0:6], rf_ref[...], rs_ref[...], row_ref[...], vec_outs[4:])


def update_all(piece, owned, blocks, halves, summed, vectors):
    masters = blocks[0]
    spd, edge = masters.shape[1], masters.shape[-1]
    group = spd // 2
    whole = lambda a: pl.BlockSpec(a.shape, lambda i, p: tuple(0 for _ in a.shape))
    spec = pl.BlockSpec((1, group, edge, edge), lambda i, p: (0, i, 0, 0))
    rows = halves[2].shape[0] // 2
    given = pl.BlockSpec((rows, D), lambda i, p: (i, 0))
    taken = pl.BlockSpec((rows, D), lambda i, p: ((1 - p[0]) * 2 + i, 0))
    shape = jax.ShapeDtypeStruct
    vec_shapes = [shape(vectors[0].shape, F32)] * 4 + [shape(vectors[3].shape, F32)] * 4
    total = halves[0].shape[0]
    return pl.pallas_call(
        update_kernel,
        grid_spec=pltpu.PrefetchScalarGridSpec(
            num_scalar_prefetch=1,
            grid=(2,),
            in_specs=[pl.BlockSpec((group, edge, edge), lambda i, p: (i, 0, 0))]
            + [spec] * 5
            + [anywhere(), anywhere(), given, given]
            + [whole(a) for a in (summed, *vectors)],
            out_specs=[spec] * 5 + [taken, taken] + [whole(a) for a in vec_shapes],
        ),
        out_shape=[shape(masters.shape, F32)] * 4
        + [shape(masters.shape, BF16), shape((total, D), BF16), shape((total, D), F32)]
        + vec_shapes,
        input_output_aliases={7: 5, 8: 6},
        compiler_params=params(),
        name="update",
    )(piece, owned, *blocks, *halves, summed, *vectors)


def body(
    tokens,
    cotangent,
    pair_lengths,
    block_of_slot,
    masters,
    mom_first,
    mom_second,
    left_bases,
    right_bases,
    split_vec,
    split_first,
    split_second,
    row_vec,
    row_first,
    row_second,
):
    pieces = lax.axis_size("tensor")
    piece = lax.axis_index("tensor")
    n_dp = lax.axis_size("dp")
    full_seq = tokens.shape[0] // pair_lengths.shape[0]
    row_count = pair_lengths.shape[0] // pieces
    every, query_bias, value_bias, up_bias, homes, places = gather_all(
        masters, split_vec, block_of_slot, n_dp, pieces
    )
    layer_whole, layer_other, input_whole, input_other, grads, row_local, up_grad, qv_grad = layer_passes(
        tokens, cotangent, pair_lengths, piece, homes, every, query_bias, value_bias, up_bias, row_vec, row_count, full_seq
    )
    mean_scale = 1.0 / (tokens.shape[0] * n_dp)
    owned, summed = scatter_all(places, grads, row_local, qv_grad, up_grad, layer_other, n_dp, mean_scale)
    outs = update_all(
        piece.astype(jnp.int32).reshape(1),
        owned,
        (masters, mom_first, mom_second, left_bases, right_bases),
        (layer_whole, input_whole, layer_other, input_other),
        summed,
        (split_vec, split_first, split_second, row_vec, row_first, row_second),
    )
    return (outs[5], outs[6], *outs[:5], *outs[7:])


def solution(mesh):
    in_specs = (
        P("dp", None),
        P("dp", None),
        P("dp", None),
        P(),
        P("tensor", "dp", None, None),
        P("tensor", "dp", None, None),
        P("tensor", "dp", None, None),
        P("tensor", "dp", None, None),
        P("tensor", "dp", None, None),
        P("tensor", None),
        P("tensor", None),
        P("tensor", None),
        P(),
        P(),
        P(),
    )
    out_specs = (
        P("dp", None),
        P("dp", None),
        P("tensor", "dp", None, None),
        P("tensor", "dp", None, None),
        P("tensor", "dp", None, None),
        P("tensor", "dp", None, None),
        P("tensor", "dp", None, None),
        P("tensor", None),
        P("tensor", None),
        P("tensor", None),
        P("tensor", None),
        P(),
        P(),
        P(),
        P(),
    )
    return jax.shard_map(body, mesh=mesh, in_specs=in_specs, out_specs=out_specs, check_vma=False)
```

```python
import functools

import jax
import jax.numpy as jnp
from jax import lax
from jax.experimental import pallas as pl
from jax.experimental.pallas import tpu as pltpu
from jax.sharding import PartitionSpec as P
import numpy as np

D = 768
HEADS = 12
HEAD = 64
FF = 3072


EPS_NORM = 1e-05
EPS_ADAM = 1e-08
LEARN_RATE = 0.01
VECTOR_RATE = 0.15
MOMENT_DECAY = 0.5
MASKED_SCORE = -1e30
HIGHEST_PRECISION = lax.Precision.HIGHEST


def block_counts(block_edge, head_width, ffn_width):
    return (
        D // block_edge * (3 * head_width // block_edge),
        head_width // block_edge * (D // block_edge),
        D // block_edge * (ffn_width // block_edge),
        ffn_width // block_edge * (D // block_edge),
    )


LOG2E = 1.4426950408889634
LN_TWO = 0.6931471805599453
ROOT_HALF = 0.7071067811865476
PHI_SCALE = 0.3989422804014327
ERF_P = 0.3275911
ERF_A = (0.254829592, -0.284496736, 1.421413741, -1.453152027, 1.061405429)
VMEM_LIMIT = 61 * 1024 * 1024
LANES = 128
VEC_ROWS = 16
GATHER_TURNS = (
    (0, 0), (2, 0), (0, 4), (0, 2), (2, 4), (1, 0), (2, 2), (0, 1), (2, 1), (0, 3), (1, 2), (1, 1), (2, 6), (1,
    6), (1, 3), (2, 3), (1, 5), (1, 7), (2, 5), (2, 8), (2, 7), (1, 11), (2, 10), (1, 9), (0, 5), (0, 7), (1, 8),
    (0, 15), (1, 10), (2, 11), (1, 13), (0, 11), (0, 12), (2, 14), (1, 4), (0, 8), (0, 13), (1, 15), (0, 6), (2,
    9), (2, 12), (0, 10), (1, 14), (0, 9), (0, 14), (1, 12), (2, 13), (2, 15),
)
BF16 = jnp.bfloat16
F32 = jnp.float32


def dot_nn(left, right):
    return lax.dot_general(left, right, (((1,), (0,)), ((), ())), preferred_element_type=F32)


def dot_nt(left, right):
    return lax.dot_general(left, right, (((1,), (1,)), ((), ())), preferred_element_type=F32)


def dot_tn(left, right):
    return lax.dot_general(left, right, (((0,), (0,)), ((), ())), preferred_element_type=F32)


def block_home(pieces):
    d_b, f_b = D // LANES, FF // LANES
    d_p, f_p = d_b // pieces, f_b // pieces
    first = d_b * 3 * d_p
    second = first + d_p * d_b
    third = second + d_b * f_p
    qkv = [
        (n % d_b // d_p, k * 3 * d_p + n // d_b * d_p + n % d_p)
        for k in range(d_b)
        for n in range(3 * d_b)
    ]
    out = [(k // d_p, first + k % d_p * d_b + n) for k in range(d_b) for n in range(d_b)]
    up = [(n // f_p, second + k * f_p + n % f_p) for k in range(d_b) for n in range(f_b)]
    down = [(k // f_p, third + k % f_p * d_b + n) for k in range(f_b) for n in range(d_b)]
    return qkv, out, up, down


def grad_order(pieces):
    d_b, f_b = D // LANES, FF // LANES
    qkv, out, up, down = block_home(pieces)
    f_s, q_s = f_b // d_b, 3
    order = []
    for j in range(d_b):
        order += [down[(j * f_s + k) * d_b + n] for k in range(f_s) for n in range(d_b)]
        order += [up[k * f_b + j * f_s + n] for k in range(d_b) for n in range(f_s)]
        order += [qkv[k * 3 * d_b + j * q_s + n] for k in range(d_b) for n in range(q_s)]
        order += [out[j * d_b + n] for n in range(d_b)]
    return order


def start_blocks(homes, base, rows, cols, source, target, sem):
    def step(index, carry):
        k, n = index // cols, index % cols
        pltpu.make_async_copy(
            source.at[homes[0, base + index]],
            target.at[pl.ds(pl.multiple_of(k * LANES, LANES), LANES), pl.ds(pl.multiple_of(n * LANES, LANES), LANES)],
            sem,
        ).start()
        return carry

    lax.fori_loop(0, rows * cols, step, 0, unroll=6)


def wait_blocks(target, sem):
    pltpu.make_async_copy(target, target, sem).wait()


def mask_bias(ends_ref, row, seq, bias_ref):
    col = lax.broadcasted_iota(jnp.int32, (seq, 1), 0)
    lane = lax.broadcasted_iota(jnp.int32, (1, seq), 1)
    seg_col = jnp.zeros((seq, 1), jnp.int32)
    seg_lane = jnp.zeros((1, seq), jnp.int32)
    end = 0
    for k in range(ends_ref.shape[1] - 1):
        end = end + ends_ref[row, k]
        seg_col = seg_col + (col >= end).astype(jnp.int32)
        seg_lane = seg_lane + (lane >= end).astype(jnp.int32)
    bias_ref[...] = jnp.where(seg_col == seg_lane, 0.0, MASKED_SCORE)


def norm_parts(hidden):
    mean = jnp.mean(hidden, axis=-1, keepdims=True)
    centred = hidden - mean
    var = jnp.mean(centred * centred, axis=-1, keepdims=True)
    inv = lax.rsqrt(var + EPS_NORM)
    return centred * inv, inv


def norm_back(grad, gain, normed, inv):
    scaled = grad * gain
    mean = jnp.mean(scaled, axis=-1, keepdims=True)
    along = jnp.mean(scaled * normed, axis=-1, keepdims=True)
    return inv * (scaled - mean - normed * along)


def put_blocks(ref, value):
    for n in range(ref.shape[0]):
        ref[n] = value[:, n * LANES : (n + 1) * LANES]


def get_blocks(ref):
    return jnp.concatenate([ref[n] for n in range(ref.shape[0])], axis=1)


def gelu_parts(u):
    e = jnp.exp(u * u * -0.5)
    t = 1.0 / (1.0 + (ERF_P * ROOT_HALF) * jnp.abs(u))
    a1, a2, a3, a4, a5 = (0.5 * a for a in ERF_A)
    tail = ((((a5 * t + a4) * t + a3) * t + a2) * t + a1) * t * e
    cdf = jnp.where(u >= 0, 1.0 - tail, tail)
    return u * cdf, cdf + u * e * PHI_SCALE


def forward_kernel(
    homes, pairs, offset, x_any, cot_any, every, qb_ref, vb_ref, bu_ref, rv_ref,
    qkv_out, att_out, lse_ref, out_out, whole_out, nl_out, act_out, dl_out, up_out, al_out, ml_out, g1_out, rg_ref, bg_ref,
    w_ref, wo_ref, wu_ref, wd_ref, x_ref, cot_ref, qkv_ref, att_ref, bias_ref,
    nl_ref, act_ref, dl_ref, up_ref, al_ref, ml_ref, n_ref, inv_ref, acc_ref, in_sem, out_sem,
):
    d_b, f_b = D // LANES, FF // LANES
    total = x_ref.shape[0]
    seq = bias_ref.shape[0]
    row_count = total // seq
    steps = row_count * d_b
    first = pl.multiple_of(offset[0] * seq, seq)
    x_copy = pltpu.make_async_copy(x_any.at[pl.ds(first, total)], x_ref, in_sem.at[0])
    cot_copy = pltpu.make_async_copy(cot_any.at[pl.ds(first, total)], cot_ref, in_sem.at[1])
    x_copy.start()
    start_blocks(homes, 0, d_b, 3 * d_b, every, w_ref, in_sem.at[2])
    cot_copy.start()
    x_copy.wait()
    wait_blocks(w_ref, in_sem.at[2])

    outs = []

    def send(source, target):
        copy = pltpu.make_async_copy(source, target, out_sem.at[len(outs)])
        copy.start()
        outs.append(copy)

    wide = 2 * LANES
    for part in range(3):
        for c in range(0, D, wide):
            y = dot_nn(x_ref[...], w_ref[:, part * D + c : part * D + c + wide])
            if part == 0:
                y = (y + qb_ref[:, c : c + wide]).astype(BF16).astype(F32) * HEAD ** (-0.5)
            if part == 2:
                y = y + vb_ref[:, c : c + wide]
            y = y.astype(BF16)
            for n in range(2):
                qkv_ref[part * d_b + c // LANES + n] = y[:, n * LANES : (n + 1) * LANES]
    send(qkv_ref, qkv_out)
    lane = lax.broadcasted_iota(jnp.int32, (1, LANES), 1)

    def block(base, rows, cols, source, target, sem, index):
        k, n = index // cols, index % cols
        pltpu.make_async_copy(
            every.at[homes[0, base + index]],
            target.at[pl.ds(pl.multiple_of(k * LANES, LANES), LANES), pl.ds(pl.multiple_of(n * LANES, LANES), LANES)],
            sem,
        ).start()

    def fetch(step):
        for base, rows, cols, target, sem in (
            (3 * d_b * d_b, d_b, d_b, wo_ref, 3),
            (4 * d_b * d_b, d_b, f_b, wu_ref, 4),
            (4 * d_b * d_b + d_b * f_b, f_b, d_b, wd_ref, 5),
        ):
            each = rows * cols // steps
            for i in range(each):
                block(base, rows, cols, every, target, in_sem.at[sem], step * each + i)

    for r in range(row_count):
        at = slice(r * seq, (r + 1) * seq)
        mask_bias(pairs, offset[0] + r, seq, bias_ref)

        def pair(n, carry):
            fetch(r * d_b + n)
            q = qkv_ref[n, at]
            k = qkv_ref[d_b + n, at]
            v_t = qkv_ref[2 * d_b + n, at].T
            halves, all_scores = [], []
            for h in range(2):
                keep = (lane < HEAD) if h == 0 else (lane >= HEAD)
                all_scores.append(dot_nt(jnp.where(keep, k, jnp.zeros_like(k)), q) + bias_ref[...])
            for h in range(2):
                scores = all_scores[h]
                top = jnp.max(scores, axis=0, keepdims=True)
                p = jnp.exp(scores - top)
                sums = jnp.sum(p, axis=0, keepdims=True)
                lse_ref[r, 2 * n + h] = (top + jnp.log(sums)).reshape(1, seq)
                mixed = dot_nn(v_t[h * HEAD : (h + 1) * HEAD], p.astype(BF16))
                halves.append(mixed * (1.0 / sums))
            att_ref[n, at] = jnp.concatenate(halves, axis=0).T.astype(BF16)
            return carry

        lax.fori_loop(0, d_b, pair, 0, unroll=2)
    send(att_ref, att_out)
    out_bias, gain_one, shift_one, down_bias, gain_two, shift_two = (
        rv_ref[i : i + 1] for i in range(6)
    )
    rg_ref[...] = jnp.zeros_like(rg_ref)
    tile = total // 4
    tiles = [slice(t * tile, (t + 1) * tile) for t in range(4)]

    def put(ref, at, value):
        for n in range(ref.shape[0]):
            ref[n, at] = value[:, n * LANES : (n + 1) * LANES]

    def get(ref, at):
        return jnp.concatenate([ref[n, at] for n in range(ref.shape[0])], axis=1)

    wait_blocks(wo_ref, in_sem.at[3])
    for at in tiles:
        hidden = dot_nn(get(att_ref, at), wo_ref[...]) + x_ref[at].astype(F32) + out_bias
        n_one, inv_one = norm_parts(hidden)
        n_ref[at] = n_one
        inv_ref[at] = inv_one
        normed = n_one * gain_one + shift_one
        put(nl_ref, at, normed.astype(BF16))
        acc_ref[at] = normed + down_bias
    send(nl_ref, nl_out)
    wait_blocks(wu_ref, in_sem.at[4])
    wait_blocks(wd_ref, in_sem.at[5])
    wide = 768
    per = wide // LANES
    normed_low = get_blocks(nl_ref)
    for c in range(0, FF, wide):
        u = dot_nn(normed_low, wu_ref[:, c : c + wide]) + bu_ref[:, c : c + wide]
        active, slope = gelu_parts(u)
        active = active.astype(BF16)
        slope = slope.astype(BF16)
        for n in range(per):
            act_ref[c // LANES + n] = active[:, n * LANES : (n + 1) * LANES]
            up_ref[c // LANES + n] = slope[:, n * LANES : (n + 1) * LANES]
        acc_ref[...] += dot_nn(active, wd_ref[c : c + wide, :])
    send(act_ref, act_out)
    cot_copy.wait()
    for at in tiles:
        n_two, inv_two = norm_parts(acc_ref[at])
        x_ref[at] = (n_two * gain_two + shift_two).astype(BF16)
        dy = cot_ref[at].astype(F32)
        grad_two = norm_back(dy, gain_two, n_two, inv_two)
        put(dl_ref, at, grad_two.astype(BF16))
        acc_ref[at] = grad_two
        rg_ref[3:4] += jnp.sum(grad_two, axis=0, keepdims=True)
        rg_ref[4:5] += jnp.sum(dy * n_two, axis=0, keepdims=True)
        rg_ref[5:6] += jnp.sum(dy, axis=0, keepdims=True)
    send(x_ref, out_out)
    send(x_ref, whole_out.at[pl.ds(first, total)])
    send(dl_ref, dl_out)
    down_low = get_blocks(dl_ref)
    for c in range(0, FF, wide):
        blocks = range(c // LANES, c // LANES + per)
        slope = jnp.concatenate([up_ref[n] for n in blocks], axis=1).astype(F32)
        up = (dot_nt(down_low, wd_ref[c : c + wide, :]) * slope).astype(BF16)
        for i, n in enumerate(blocks):
            up_ref[n] = up[:, i * LANES : (i + 1) * LANES]
        bg_ref[:, c : c + wide] = jnp.sum(up.astype(F32), axis=0, keepdims=True)
        acc_ref[...] += dot_nt(up, wu_ref[:, c : c + wide])
    send(up_ref, up_out)
    for at in tiles:
        grad_normed = acc_ref[at]
        n_one = n_ref[at]
        rg_ref[1:2] += jnp.sum(grad_normed * n_one, axis=0, keepdims=True)
        rg_ref[2:3] += jnp.sum(grad_normed, axis=0, keepdims=True)
        grad_one = norm_back(grad_normed, gain_one, n_one, inv_ref[at])
        rg_ref[0:1] += jnp.sum(grad_one, axis=0, keepdims=True)
        acc_ref[at] = grad_one
        attn_low = grad_one.astype(BF16)
        put(al_ref, at, attn_low)
        put(ml_ref, at, dot_nt(attn_low, wo_ref[...]).astype(BF16))
    send(acc_ref, g1_out)
    send(al_ref, al_out)
    send(ml_ref, ml_out)
    for copy in outs:
        copy.wait()


def attend_back_kernel(
    homes, pairs, offset, qkv_ref, att_ref, ml_ref, lse_ref, g1_ref, every,
    merged_ref, ig_ref, il_ref, sg_ref, w_ref, bias_ref, sem,
):
    d_b = D // LANES
    row = pl.program_id(0)
    seq = g1_ref.shape[0]

    @pl.when(row == 0)
    def _():
        start_blocks(homes, 0, d_b, 3 * d_b, every, w_ref, sem)
        sg_ref[...] = jnp.zeros_like(sg_ref)

    mask_bias(pairs, offset[0] + row, seq, bias_ref)
    lane = lax.broadcasted_iota(jnp.int32, (1, LANES), 1)

    def pair(n, carry):
        q = qkv_ref[n]
        k = qkv_ref[d_b + n]
        v = qkv_ref[2 * d_b + n]
        g = ml_ref[n]
        k_t = k.T
        both = g.T.astype(F32) * att_ref[n].T.astype(F32)
        zero = jnp.zeros_like(k)
        parts, firsts = [], []
        for h in range(2):
            keep = (lane < HEAD) if h == 0 else (lane >= HEAD)
            scores = dot_nt(jnp.where(keep, k, zero), q) + bias_ref[...]
            firsts.append((scores, dot_nt(jnp.where(keep, v, zero), g)))
        for h in range(2):
            scores, gp = firsts[h]
            spread = jnp.sum(both[h * HEAD : (h + 1) * HEAD], axis=0, keepdims=True)
            p = jnp.exp(scores - lse_ref[0, 2 * n + h].reshape(1, seq))
            low = (p * (gp - spread)).astype(BF16)
            gv = dot_nn(p.astype(BF16), g)
            gk = dot_nn(low, q)
            gq = dot_nn(k_t[h * HEAD : (h + 1) * HEAD], low)
            parts.append((gq, gk, gv))
        gq = (jnp.concatenate([parts[0][0], parts[1][0]], axis=0) * HEAD ** (-0.5)).T
        merged_ref[n] = gq.astype(BF16)
        merged_ref[d_b + n] = jnp.where(lane < HEAD, parts[0][1], parts[1][1]).astype(BF16)
        merged_ref[2 * d_b + n] = jnp.where(lane < HEAD, parts[0][2], parts[1][2]).astype(BF16)
        return carry

    lax.fori_loop(0, d_b, pair, 0, unroll=2)

    @pl.when(row == 0)
    def _():
        wait_blocks(w_ref, sem)

    for n in range(d_b):
        at = slice(n * LANES, (n + 1) * LANES)
        sg_ref[0:1, at] += jnp.sum(merged_ref[n].astype(F32), axis=0, keepdims=True)
        sg_ref[1:2, at] += jnp.sum(merged_ref[2 * d_b + n].astype(F32), axis=0, keepdims=True)
    merged = get_blocks(merged_ref)
    total = g1_ref[...] + dot_nt(merged, w_ref[...])
    ig_ref[...] = total
    il_ref[...] = total.astype(BF16)


def grad_kernel(act_ref, dl_ref, nl_ref, up_ref, x_ref, merged_ref, att_ref, al_ref, g_ref):
    d_b = D // LANES
    f_s = act_ref.shape[0]
    at = 0

    def store(value, at):
        value = value.astype(BF16)
        for k in range(value.shape[0] // LANES):
            for n in range(value.shape[1] // LANES):
                g_ref[at] = value[k * LANES : (k + 1) * LANES, n * LANES : (n + 1) * LANES]
                at += 1
        return at

    at = store(dot_tn(get_blocks(act_ref), get_blocks(dl_ref)), at)
    at = store(dot_tn(get_blocks(nl_ref), get_blocks(up_ref)), at)
    at = store(dot_tn(x_ref[...], get_blocks(merged_ref)), at)
    at = store(dot_tn(att_ref[0], get_blocks(al_ref)), at)


def smem():
    return pl.BlockSpec(memory_space=pltpu.SMEM)


def anywhere():
    return pl.BlockSpec(memory_space=pl.ANY)


def params():
    return pltpu.CompilerParams(vmem_limit_bytes=VMEM_LIMIT, dimension_semantics=("arbitrary",))


def layer_passes(tokens, cotangent, pair_lengths, piece, homes, every, query_bias, value_bias, up_bias, row_vec, row_count, seq):
    d_b, f_b = D // LANES, FF // LANES
    total = row_count * seq
    shape = jax.ShapeDtypeStruct
    offset = (piece * row_count).astype(jnp.int32).reshape(1)
    stack = lambda n: pl.BlockSpec((n, seq, LANES), lambda r, *_: (0, r, 0))
    rows = pl.BlockSpec((seq, D), lambda r, *_: (r, 0))
    own = lambda at: pl.BlockSpec((seq, D), lambda r, *pre: (pre[at][0] + r, 0))
    whole = lambda s: pl.BlockSpec(s, lambda *_: tuple(0 for _ in s))
    lse_spec = pl.BlockSpec((1, HEADS, 1, seq), lambda r, *_: (r, 0, 0, 0))
    vmem = pl.BlockSpec(memory_space=pltpu.VMEM)
    tokens_bf = shape((total, D), BF16)
    stacked = lambda n: shape((n, total, LANES), BF16)
    kept = lambda n: pltpu.VMEM((n, total, LANES), BF16)
    (
        qkv, att, lse, layer_own, layer_whole, normed_low, active_low, down_low, up_low, attn_low, mixed_low, grad_one, row_grad, up_grad
    ) = pl.pallas_call(
        forward_kernel,
        in_specs=[smem()] * 3 + [anywhere()] * 3 + [vmem] * 4,
        out_specs=[anywhere()] * 2 + [vmem] + [anywhere()] * 9 + [vmem] * 2,
        out_shape=[
            stacked(3 * d_b), stacked(d_b), shape((row_count, HEADS, 1, seq), F32), tokens_bf,
            shape(tokens.shape, BF16),
            stacked(d_b), stacked(f_b), stacked(d_b), stacked(f_b), stacked(d_b), stacked(d_b),
            shape((total, D), F32), shape((6, D), F32), shape((1, FF), F32),
        ],
        scratch_shapes=[
            pltpu.VMEM((D, 3 * D), BF16), pltpu.VMEM((D, D), BF16), pltpu.VMEM((D, FF), BF16), pltpu.VMEM((FF, D), BF16),
            pltpu.VMEM((total, D), BF16), pltpu.VMEM((total, D), BF16), kept(3 * d_b), kept(d_b),
            pltpu.VMEM((seq, seq), F32), kept(d_b), kept(f_b), kept(d_b), kept(f_b), kept(d_b), kept(d_b),
            pltpu.VMEM((total, D), F32), pltpu.VMEM((total, 1), F32), pltpu.VMEM((total, D), F32),
            pltpu.SemaphoreType.DMA((6,)), pltpu.SemaphoreType.DMA((11,)),
        ],
        compiler_params=pltpu.CompilerParams(vmem_limit_bytes=VMEM_LIMIT),
        cost_estimate=pl.CostEstimate(flops=64 * total * D * D, bytes_accessed=96 * total * D, transcendentals=0),
        name="forward",
    )(homes, pair_lengths, offset, tokens, cotangent, every, query_bias, value_bias, up_bias, row_vec)
    swap = [(0, 1), (1, 0)]
    layer_other = lax.ppermute(layer_own, "tensor", swap)
    merged, input_whole, input_low, split_grad = pl.pallas_call(
        attend_back_kernel,
        grid_spec=pltpu.PrefetchScalarGridSpec(
            num_scalar_prefetch=3,
            grid=(row_count,),
            in_specs=[stack(3 * d_b), stack(d_b), stack(d_b), lse_spec, rows, anywhere()],
            out_specs=[stack(3 * d_b), own(2), rows, whole((2, D))],
            scratch_shapes=[
                pltpu.VMEM((D, 3 * D), BF16),
                pltpu.VMEM((seq, seq), F32),
                pltpu.SemaphoreType.DMA,
            ],
        ),
        out_shape=[
            shape((3 * d_b, total, LANES), BF16),
            shape(tokens.shape, F32),
            shape((total, D), BF16),
            shape((2, D), F32),
        ],
        compiler_params=params(),
        cost_estimate=pl.CostEstimate(flops=32 * total * D * D, bytes_accessed=40 * total * D, transcendentals=0),
        name="attend_back",
    )(homes, pair_lengths, offset, qkv, att, mixed_low, lse, grad_one, every)
    input_other = lax.ppermute(input_low, "tensor", swap)
    f_s = f_b // d_b
    part = lambda n: pl.BlockSpec((n, total, LANES), lambda j, *_: (j, 0, 0))
    blocks = 2 * f_s * d_b + 4 * d_b
    grads = pl.pallas_call(
        lambda pc, *refs: grad_kernel(*refs),
        grid_spec=pltpu.PrefetchScalarGridSpec(
            num_scalar_prefetch=1,
            grid=(d_b,),
            in_specs=[
                part(f_s), whole((d_b, total, LANES)), whole((d_b, total, LANES)), part(f_s),
                pl.BlockSpec((total, D), lambda j, pc: (pc[0], 0)),
                part(3), part(1), whole((d_b, total, LANES)),
            ],
            out_specs=pl.BlockSpec((blocks, LANES, LANES), lambda j, *_: (j, 0, 0)),
        ),
        out_shape=shape((d_b * blocks, LANES, LANES), BF16),
        compiler_params=params(),
        cost_estimate=pl.CostEstimate(flops=24 * total * D * D, bytes_accessed=40 * total * D, transcendentals=0),
        name="weight_grads",
    )(piece.astype(jnp.int32).reshape(1), active_low, down_low, normed_low, up_low, tokens, merged, att, attn_low)
    return layer_whole, layer_other, input_whole, input_other, grads, row_grad, up_grad, split_grad


def split_slots(orders, counts):
    parts, at = [], 0
    for order, count in zip(orders, counts):
        if count:
            parts.append((order, at, count))
        at += count
    return parts


def index_bits(n_dp):
    dp_bits = list(range(1, n_dp.bit_length() - 1))
    return dp_bits[:1], dp_bits[1:]


def gather_orders(n_dp, spd):
    near, far = index_bits(n_dp)
    first, second = spd * 3 // 14, spd * 4 // 14
    return split_slots(
        ([-1] + near + far, far[:1] + [-1] + far[1:] + near, near + [-1] + far), (first, second, spd - first - second)
    )


def scatter_orders(n_dp, spd):
    near, far = index_bits(n_dp)
    first, last = spd * 5 // 14, spd * 4 // 14
    rest = near + [-1] + far
    return split_slots((far[:1] + [-1] + far[1:] + near, rest, rest), (first, spd - first - last, last))


def bit_of(number, bit):
    return number // (1 << bit) % 2


def across(bit):
    if bit < 0:
        return {"tensor": 1 - lax.axis_index("tensor")}
    me = lax.axis_index("dp")
    return {"dp": me + (1 - 2 * bit_of(me, bit)) * (1 << bit)}


def place_of(order, code, core):
    dp, tensor = lax.axis_index("dp"), lax.axis_index("tensor")
    place = len(order) - 1
    to_dp, to_tensor = core, tensor
    for bit in order:
        flip = bit_of(code, place)
        if bit < 0:
            to_tensor = (tensor + flip) % 2
        else:
            to_dp = to_dp + (bit_of(dp, bit) + flip) % 2 * (1 << bit)
        place -= 1
    return to_tensor, to_dp


def slot_at(order, code, core, spd, at):
    to_tensor, to_dp = place_of(order, code, core)
    return to_tensor, to_dp * spd + at


def first_slot(order, code, core, n_dp, spd):
    to_tensor, to_dp = place_of(order, code, core)
    return (to_tensor * n_dp + to_dp) * spd


def greet(bits):
    barrier = pltpu.get_barrier_semaphore()
    for bit in bits:
        pl.semaphore_signal(barrier, inc=1, device_id=across(bit), device_id_type=pl.DeviceIdType.MESH)
    pl.semaphore_wait(barrier, len(bits))


def remote(source, target, send, recv, bit):
    return pltpu.make_async_remote_copy(
        src_ref=source, dst_ref=target, send_sem=send, recv_sem=recv,
        device_id=across(bit), device_id_type=pl.DeviceIdType.MESH,
    )


def gather_kernel(
    n_dp, spd, master_ref, vec_ref, col_ref, row_ref, order_ref, grads_ref,
    all_ref, qb_ref, vb_ref, bu_ref, homes_ref, places_ref, own_ref, both_ref, local_sem, send_sem, recv_sem, core_send, core_recv, vec_send, vec_recv):
    parts = gather_orders(n_dp, spd)
    n_bits = len(parts[0][0])
    core = bit_of(lax.axis_index("dp"), 0)
    tensor = lax.axis_index("tensor")
    greet([0] + parts[0][0])
    own_ref[...] = master_ref[0].astype(BF16)
    mine = first_slot(parts[0][0], 0, core, n_dp, spd)
    keep = pltpu.make_async_copy(own_ref, all_ref.at[pl.ds(mine, spd)], local_sem.at[0])
    keep.start()
    keep_vec = pltpu.make_async_copy(vec_ref, both_ref.at[pl.ds(tensor, 1)], local_sem.at[1])
    keep_vec.start()
    vec = remote(vec_ref, both_ref.at[pl.ds(tensor, 1)], vec_send, vec_recv, -1)
    vec.start()

    def piece(part, code, core_of):
        order, at, count = part
        return all_ref.at[pl.ds(first_slot(order, code, core_of, n_dp, spd) + at, count)]

    def forward(p, code, level, source):
        order = parts[p][0]
        for stage in range(level, n_bits):
            remote(
                source, piece(parts[p], code, core), send_sem.at[p, stage, code],
                recv_sem.at[p, code + (1 << stage)], order[n_bits - 1 - stage],
            ).start()
        remote(source, piece(parts[p], code, core), core_send.at[p, code], core_recv.at[p, code], 0).start()

    def turn(p, code, level):
        if isinstance(code, int) and code == 0:
            forward(p, 0, 0, own_ref.at[pl.ds(parts[p][1], parts[p][2])])
        else:
            here = piece(parts[p], code, core)
            pltpu.make_async_copy(here, here, recv_sem.at[p, code]).wait()
            forward(p, code, level + 1, here)

    listed = n_bits == 4 and len(parts) == 3
    opening = [at for at in GATHER_TURNS if at[1] == 0][-1] if listed else None
    if listed:
        cut = GATHER_TURNS.index(opening) + 1
        for p, code in GATHER_TURNS[:cut]:
            turn(p, code, code.bit_length() - 1)
    else:
        for p in range(len(parts)):
            turn(p, 0, -1)
    slots = n_dp * spd
    match = col_ref[...] == order_ref[1:2]
    slot = lax.broadcasted_iota(jnp.int32, match.shape, 0).astype(F32)
    found = jnp.sum(jnp.where(match, slot, 0.0), axis=0, keepdims=True)
    homes_ref[...] = found.astype(jnp.int32) + order_ref[0:1] * slots
    for i in range(places_ref.shape[0]):
        match = (grads_ref[:, 1:2] == row_ref[...]) & (grads_ref[:, 0:1] == i)
        index = lax.broadcasted_iota(jnp.int32, match.shape, 0).astype(F32) + 1.0
        found = jnp.sum(jnp.where(match, index, 0.0), axis=0, keepdims=True)
        places_ref[i : i + 1] = found.astype(jnp.int32) - 1
    if listed:
        for p, code in GATHER_TURNS[cut:]:
            turn(p, code, code.bit_length() - 1)
    for level in range(0 if listed else n_bits):
        def arrive(j, carry):
            for p in range(len(parts)):
                turn(p, (1 << level) + j, level)
            return carry

        lax.fori_loop(0, 1 << level, arrive, 0)

    def drain(code, carry):
        for p, part in enumerate(parts):
            here = piece(part, code, core)
            there = piece(part, code, 1 - core)
            pltpu.make_async_copy(here, here, core_send.at[p, code]).wait()
            pltpu.make_async_copy(there, there, core_recv.at[p, code]).wait()
        return carry

    keep_vec.wait()
    vec.wait()
    pieces = both_ref.shape[0]
    head_w, ffn_w = D // pieces, FF // pieces
    for i in range(pieces):
        row = both_ref[i : i + 1]
        qb_ref[:, i * head_w : (i + 1) * head_w] = row[:, :head_w]
        vb_ref[:, i * head_w : (i + 1) * head_w] = row[:, head_w : 2 * head_w]
        bu_ref[:, i * ffn_w : (i + 1) * ffn_w] = row[:, 2 * head_w :]
    for stage in range(n_bits):
        def sent(code, carry):
            for p, part in enumerate(parts):
                here = piece(part, code, core)
                pltpu.make_async_copy(here, here, send_sem.at[p, stage, code]).wait()
            return carry

        lax.fori_loop(0, 1 << stage, sent, 0)
    lax.fori_loop(0, 1 << n_bits, drain, 0)
    keep.wait()


def gather_all(masters, vec, block_of_slot, n_dp, pieces):
    order = np.array(sum(block_home(pieces), []), np.int32)
    grads_at = np.array(grad_order(pieces), np.int32)
    spd, edge = masters.shape[1], masters.shape[-1]
    parts = gather_orders(n_dp, spd)
    n, n_bits = len(parts), len(parts[0][0])
    dma = pltpu.SemaphoreType.DMA
    vmem = pl.BlockSpec(memory_space=pltpu.VMEM)
    shape = jax.ShapeDtypeStruct
    return pl.pallas_call(
        functools.partial(gather_kernel, n_dp, spd),
        in_specs=[vmem] * 6,
        out_specs=[anywhere()] + [vmem] * 5,
        out_shape=[
            shape((pieces * n_dp * spd, edge, edge), BF16),
            shape((1, D), F32), shape((1, D), F32), shape((1, FF), F32),
            shape((1, len(order)), jnp.int32), shape((pieces, n_dp * spd), jnp.int32),
        ],
        scratch_shapes=[
            pltpu.VMEM((spd, edge, edge), BF16),
            pltpu.VMEM((pieces, vec.shape[1]), F32),
            dma((2,)), dma((n, n_bits, 1 << n_bits)), dma((n, 1 << n_bits)),
            dma((n, 1 << n_bits)), dma((n, 1 << n_bits)), dma, dma,
        ],
        compiler_params=pltpu.CompilerParams(
            vmem_limit_bytes=VMEM_LIMIT, collective_id=0, has_side_effects=True
        ),
        name="gather",
    )(masters, vec, block_of_slot[:, None], block_of_slot[None, :], jnp.asarray(order.T), jnp.asarray(grads_at))


def scatter_kernel(
    n_dp, spd, scale, places, g_any, rg_ref, sg_ref, bg_ref, swapped, out_ref, vec_out,
    g_ref, g_sem, give_ref, sum_ref, in_ref, vec_sum, vec_in,
    core_send, core_recv, send_sem, recv_sem, vec_send, vec_recv,
):
    parts = scatter_orders(n_dp, spd)
    n_bits = len(parts[0][0])
    codes = 1 << n_bits
    core = bit_of(lax.axis_index("dp"), 0)
    vec_bits = [0] + parts[0][0]
    grads = pltpu.make_async_copy(g_any, g_ref, g_sem)
    grads.start()
    greet(vec_bits)

    def term(slot):
        place = places[slot[0], slot[1]]
        return jnp.where(place >= 0, g_ref[jnp.maximum(place, 0)], jnp.zeros(g_ref.shape[1:], BF16))

    def vec_copy(stage):
        return remote(vec_sum.at[stage], vec_in.at[stage], vec_send.at[stage], vec_recv.at[stage], vec_bits[stage])

    def vec_step(stage):
        vec_copy(stage).wait_recv()
        total = vec_sum[stage] + vec_in[stage]
        if stage + 1 < len(vec_bits):
            vec_sum[stage + 1] = total
            vec_copy(stage + 1).start()
        else:
            vec_out[...] = total * scale

    vec_sum[0, 0:6] = rg_ref[...]
    vec_sum[0, 6:8] = sg_ref[...]
    for i in range(FF // D):
        vec_sum[0, 8 + i : 9 + i] = bg_ref[:, i * D : (i + 1) * D]
    vec_sum[0, 8 + FF // D :] = jnp.zeros((VEC_ROWS - 8 - FF // D, D), F32)
    vec_copy(0).start()

    def give(p, code):
        order, at, count = parts[p]
        where = pl.ds(at, count)
        return remote(
            give_ref.at[code, where], sum_ref.at[code, where], core_send.at[p, code], core_recv.at[p, code], 0
        )

    def passed(p, level, code):
        order, at, count = parts[p]
        where = pl.ds(at, count)
        return remote(
            sum_ref.at[code, where], in_ref.at[code - 1, where],
            send_sem.at[p, code], recv_sem.at[p, code - 1], order[n_bits - 1 - level],
        )

    def hand(code):
        for p, (order, at, count) in enumerate(parts):
            start = slot_at(order, code, 1 - core, spd, at)
            for s in range(count):
                give_ref[code, at + s] = term((start[0], start[1] + s))
            give(p, code).start()

    ahead = min(4, codes)
    grads.wait()

    def first_hands(j, carry):
        hand(codes - 1 - j)
        return carry

    lax.fori_loop(0, ahead, first_hands, 0)
    vec_step(0)
    stage = 1

    def total_of(p, code, level, finish):
        order, at, count = parts[p]
        start = slot_at(order, code, core, spd, at)
        give(p, code).wait_recv()
        sources = []
        for stage in range(level + 1, n_bits):
            entry = (1 << stage) - 1 + code
            here = in_ref.at[entry, pl.ds(at, count)]
            pltpu.make_async_copy(here, here, recv_sem.at[p, entry]).wait()
            sources.append(entry)
        for s in range(count):
            value = term((start[0], start[1] + s)).astype(F32) + sum_ref[code, at + s].astype(F32)
            for entry in sources:
                value = value + in_ref[entry, at + s].astype(F32)
            if finish:
                out_ref[at + s] = value * scale
            else:
                sum_ref[code, at + s] = value.astype(BF16)

    for level in reversed(range(n_bits)):
        def onward(j, carry):
            code = (2 << level) - 1 - j
            if (1 << level) >= ahead:
                hand(code - ahead)
            for p in range(len(parts)):
                total_of(p, code, level, False)
                passed(p, level, code).start()
            return carry

        count = 1 << level
        if level == n_bits - 1 and count >= 4:
            lax.fori_loop(0, 1, onward, 0)
            vec_step(1)
            lax.fori_loop(1, 3, onward, 0)
            vec_step(2)
            lax.fori_loop(3, count, onward, 0)
            stage = 3
        else:
            lax.fori_loop(0, count, onward, 0)
        if stage < n_bits:
            vec_step(stage)
            stage += 1
    for p in range(len(parts)):
        total_of(p, 0, -1, True)
    for last in range(stage, n_bits + 1):
        vec_step(last)
    for stage in range(len(vec_bits)):
        vec_copy(stage).wait_send()

    def drain(code, carry):
        for p in range(len(parts)):
            give(p, code).wait_send()
        return carry

    lax.fori_loop(0, codes, drain, 0)
    for level in range(n_bits):
        def drain_level(j, carry):
            for p in range(len(parts)):
                passed(p, level, (1 << level) + j).wait_send()
            return carry

        lax.fori_loop(0, 1 << level, drain_level, 0)


def scatter_all(places, grads, row_grad, qv_grad, up_grad, swapped, n_dp, scale):
    edge = grads.shape[-1]
    spd = places.shape[1] // n_dp
    parts = scatter_orders(n_dp, spd)
    n, n_bits = len(parts), len(parts[0][0])
    codes = 1 << n_bits
    dma = pltpu.SemaphoreType.DMA
    vmem = pl.BlockSpec(memory_space=pltpu.VMEM)
    return pl.pallas_call(
        functools.partial(scatter_kernel, n_dp, spd, scale),
        in_specs=[smem(), anywhere()] + [vmem] * 3 + [anywhere()],
        out_specs=[vmem, vmem],
        out_shape=[
            jax.ShapeDtypeStruct((spd, edge, edge), F32),
            jax.ShapeDtypeStruct((VEC_ROWS, D), F32),
        ],
        scratch_shapes=[
            pltpu.VMEM(grads.shape, BF16),
            dma,
            pltpu.VMEM((codes, spd, edge, edge), BF16),
            pltpu.VMEM((codes, spd, edge, edge), BF16),
            pltpu.VMEM((codes - 1, spd, edge, edge), BF16),
            pltpu.VMEM((n_bits + 1, VEC_ROWS, D), F32),
            pltpu.VMEM((n_bits + 1, VEC_ROWS, D), F32),
            dma((n, codes)), dma((n, codes)), dma((n, codes)), dma((n, codes)),
            dma((n_bits + 1,)), dma((n_bits + 1,)),
        ],
        compiler_params=pltpu.CompilerParams(
            vmem_limit_bytes=VMEM_LIMIT, collective_id=1, has_side_effects=True
        ),
        name="scatter",
    )(places, grads, row_grad, qv_grad, up_grad, swapped)


def adam(grad, first, second, current, outs):
    first = MOMENT_DECAY * first + (1.0 - MOMENT_DECAY) * grad
    second = MOMENT_DECAY * second + (1.0 - MOMENT_DECAY) * grad * grad
    grad_out, new_out, first_out, second_out = outs
    grad_out[...] = grad
    new_out[...] = current - VECTOR_RATE * first / (jnp.sqrt(second) + EPS_ADAM)
    first_out[...] = first
    second_out[...] = second


def update_kernel(
    piece, grad_ref, master_ref, first_ref, second_ref, left_ref, right_ref,
    layer_whole, input_whole, layer_other, input_other, vec_ref, split_ref, sf_ref, ss_ref, row_ref, rf_ref, rs_ref,
    wg_ref, new_ref, nf_ref, ns_ref, low_ref, layer_ref, input_ref, *vec_outs,
):
    step = pl.program_id(0)
    for s in range(grad_ref.shape[0]):
        left, right = left_ref[0, s].astype(BF16), right_ref[0, s].astype(BF16)
        grad = grad_ref[s]
        turned = dot_nn(dot_tn(left, grad.astype(BF16)).astype(BF16), right)
        first = MOMENT_DECAY * first_ref[0, s] + (1.0 - MOMENT_DECAY) * turned
        second = MOMENT_DECAY * second_ref[0, s] + (1.0 - MOMENT_DECAY) * turned * turned
        stepped = first / (jnp.sqrt(second) + EPS_ADAM)
        back = dot_nt(dot_nn(left, stepped.astype(BF16)).astype(BF16), right)
        new = master_ref[0, s] - LEARN_RATE * back
        wg_ref[0, s] = grad
        new_ref[0, s] = new
        nf_ref[0, s] = first
        ns_ref[0, s] = second
        low_ref[0, s] = new.astype(BF16)

    layer_ref[...] = layer_other[...]
    input_ref[...] = input_other[...].astype(F32)

    @pl.when(step == 0)
    def _():
        pieces = (2 * D + FF) // split_ref.shape[1]
        head_w, ffn_w = D // pieces, FF // pieces
        wide = jnp.concatenate([vec_ref[8 + i : 9 + i] for i in range(FF // D)], axis=1)
        grad = jnp.zeros(split_ref.shape, F32)
        for i in range(pieces):
            mine = jnp.concatenate(
                [
                    vec_ref[6:7, i * head_w : (i + 1) * head_w],
                    vec_ref[7:8, i * head_w : (i + 1) * head_w],
                    wide[:, i * ffn_w : (i + 1) * ffn_w],
                ],
                axis=1,
            )
            grad = jnp.where(piece[0] == i, mine, grad)
        adam(grad, sf_ref[...], ss_ref[...], split_ref[...], vec_outs[:4])
        adam(vec_ref[0:6], rf_ref[...], rs_ref[...], row_ref[...], vec_outs[4:])


def update_all(piece, owned, blocks, halves, summed, vectors):
    masters = blocks[0]
    spd, edge = masters.shape[1], masters.shape[-1]
    group = spd // 2
    whole = lambda a: pl.BlockSpec(a.shape, lambda i, p: tuple(0 for _ in a.shape))
    spec = pl.BlockSpec((1, group, edge, edge), lambda i, p: (0, i, 0, 0))
    rows = halves[2].shape[0] // 2
    given = pl.BlockSpec((rows, D), lambda i, p: (i, 0))
    taken = pl.BlockSpec((rows, D), lambda i, p: ((1 - p[0]) * 2 + i, 0))
    shape = jax.ShapeDtypeStruct
    vec_shapes = [shape(vectors[0].shape, F32)] * 4 + [shape(vectors[3].shape, F32)] * 4
    total = halves[0].shape[0]
    return pl.pallas_call(
        update_kernel,
        grid_spec=pltpu.PrefetchScalarGridSpec(
            num_scalar_prefetch=1,
            grid=(2,),
            in_specs=[pl.BlockSpec((group, edge, edge), lambda i, p: (i, 0, 0))]
            + [spec] * 5
            + [anywhere(), anywhere(), given, given]
            + [whole(a) for a in (summed, *vectors)],
            out_specs=[spec] * 5 + [taken, taken] + [whole(a) for a in vec_shapes],
        ),
        out_shape=[shape(masters.shape, F32)] * 4
        + [shape(masters.shape, BF16), shape((total, D), BF16), shape((total, D), F32)]
        + vec_shapes,
        input_output_aliases={7: 5, 8: 6},
        compiler_params=params(),
        name="update",
    )(piece, owned, *blocks, *halves, summed, *vectors)


def body(
    tokens,
    cotangent,
    pair_lengths,
    block_of_slot,
    masters,
    mom_first,
    mom_second,
    left_bases,
    right_bases,
    split_vec,
    split_first,
    split_second,
    row_vec,
    row_first,
    row_second,
):
    pieces = lax.axis_size("tensor")
    piece = lax.axis_index("tensor")
    n_dp = lax.axis_size("dp")
    full_seq = tokens.shape[0] // pair_lengths.shape[0]
    row_count = pair_lengths.shape[0] // pieces
    every, query_bias, value_bias, up_bias, homes, places = gather_all(
        masters, split_vec, block_of_slot, n_dp, pieces
    )
    layer_whole, layer_other, input_whole, input_other, grads, row_local, up_grad, qv_grad = layer_passes(
        tokens, cotangent, pair_lengths, piece, homes, every, query_bias, value_bias, up_bias, row_vec, row_count, full_seq
    )
    mean_scale = 1.0 / (tokens.shape[0] * n_dp)
    owned, summed = scatter_all(places, grads, row_local, qv_grad, up_grad, layer_other, n_dp, mean_scale)
    outs = update_all(
        piece.astype(jnp.int32).reshape(1),
        owned,
        (masters, mom_first, mom_second, left_bases, right_bases),
        (layer_whole, input_whole, layer_other, input_other),
        summed,
        (split_vec, split_first, split_second, row_vec, row_first, row_second),
    )
    return (outs[5], outs[6], *outs[:5], *outs[7:])


def solution(mesh):
    in_specs = (
        P("dp", None),
        P("dp", None),
        P("dp", None),
        P(),
        P("tensor", "dp", None, None),
        P("tensor", "dp", None, None),
        P("tensor", "dp", None, None),
        P("tensor", "dp", None, None),
        P("tensor", "dp", None, None),
        P("tensor", None),
        P("tensor", None),
        P("tensor", None),
        P(),
        P(),
        P(),
    )
    out_specs = (
        P("dp", None),
        P("dp", None),
        P("tensor", "dp", None, None),
        P("tensor", "dp", None, None),
        P("tensor", "dp", None, None),
        P("tensor", "dp", None, None),
        P("tensor", "dp", None, None),
        P("tensor", None),
        P("tensor", None),
        P("tensor", None),
        P("tensor", None),
        P(),
        P(),
        P(),
        P(),
    )
    return jax.shard_map(body, mesh=mesh, in_specs=in_specs, out_specs=out_specs, check_vma=False)
```
